32 devices in a mesh: seq: 8 (over z, y), grp: 4 (over x, core).
Axes of the slice: x: 2, y: 2, z: 4, core: 2. Of those that a mesh axis runs over, the one named last changes fastest.
Arguments:
- frames_in: bfloat16 [4, 5120, 512], P('grp', 'seq'), may hold values from -6 to 6
- cond_frames: bfloat16 [4, 5120, 512], P('grp', 'seq'), may hold values from -6 to 6
- step_embed: bfloat16 [4, 512], P('grp'), may hold values from -6 to 6
- prompts: bfloat16 [16, 512, 512], replicated, may hold values from -6 to 6
- prompt_lengths: int32 [16], replicated, may hold values from 1 to 512, 5120 in all
- pairing: int32 [4], P('grp'), may hold values from 0 to 15
- dilations: int32 [2], replicated, may hold values from 1 to 8, as said below
- owners: int32 [34], replicated, may hold values from 0 to 3, as said below
- master: float32 [52, 512, 512], P('grp', 'seq')
- first_moment: float32 [52, 512, 512], P('grp', 'seq'), may hold values from -20 to 20
- second_moment: float32 [52, 512, 512], P('grp', 'seq'), may hold values from 0.8192 to 3.2768
- queries: float32 [2, 32, 512], replicated, may hold values from -6 to 6
- query_first: float32 [2, 32, 512], replicated, may hold values from -4 to 4
- query_second: float32 [2, 32, 512], replicated, may hold values from 0.008192 to 0.032768
- grad_out: bfloat16 [4, 5120, 512], P('grp', 'seq'), may hold values from -6 to 6
- grad_skip: bfloat16 [4, 5120, 512], P('grp', 'seq'), may hold values from -6 to 6
Outputs:
- new_first: float32 [52, 512, 512], P('grp', 'seq')
- new_second: float32 [52, 512, 512], P('grp', 'seq')
- new_master: float32 [52, 512, 512], P('grp', 'seq')
- new_copy: bfloat16 [52, 512, 512], P('grp', 'seq')
- new_query_first: float32 [2, 32, 512], replicated
- new_query_second: float32 [2, 32, 512], replicated
- new_queries: float32 [2, 32, 512], replicated
- block_out: float32 [4, 5120, 512], P('grp', 'seq')
- skip_out: float32 [4, 5120, 512], P('grp', 'seq')
- grad_frames: float32 [4, 5120, 512], P('grp', 'seq')
The draws below stay inside these ranges and needn't reach their ends.
Inputs may be any that keep to these rules, and one draw needn't show every extreme that they name: The owners hold 13, 9, 7 and 5 matrices, in an order that varies. `dilations`: one layer has dilation 8.
All inputs are finite; a program needn't handle non-finite values.
Results may differ from the reference program's by a relative error of at most 0.017.
Values may be sent and summed in bfloat16 or wider, within the bound.
A program may use at most 192 MiB of HBM per device.

```python
import math
import jax
import jax.numpy as jnp
import numpy as np
from jax import lax

C = 512
HEADS = 8
NQ = 32
TOK_DEV = 640
LP = 512
NP = 16
LAYERS = 2
DMAX = 8
CAP = 13
STEP = 10
TILES = 34
SEQLEN = 5120
N_SEQ = 8
N_GRP = 4


def owner_table(key):
    order_key = jax.random.fold_in(key, 101)
    tile_key = jax.random.fold_in(key, 102)
    shortfall = jnp.array([0, 4, 6, 8], jnp.int32)
    counts = CAP - shortfall[jax.random.permutation(order_key, 4)]
    bounds = jnp.cumsum(counts)
    places = jnp.arange(TILES, dtype=jnp.int32)
    owner_at = jnp.sum((places[:, None] >= bounds[None, :]).astype(jnp.int32), axis=1)
    shuffled = jax.random.permutation(tile_key, TILES)
    return jnp.zeros((TILES,), jnp.int32).at[shuffled].set(owner_at)


def draw_owners(key, part):
    return owner_table(key)


def draw_master(key, part):
    owners = owner_table(key)
    key = jax.random.fold_in(key, 7)
    onehot = (owners[:, None] == jnp.arange(N_GRP, dtype=jnp.int32)[None, :]).astype(jnp.int32)
    before = jnp.sum((jnp.cumsum(onehot, axis=0) - onehot) * onehot, axis=1)
    slot_of = owners * CAP + before
    unit_scale = 1.0 / jnp.sqrt(jnp.float32(C))
    kind_scale = jnp.array([3.0 ** (-0.5)] * 6 + [1.0] * 4 + [1.0, 1.0, 3.0] + [2.0] * 2 + [1.0, 1.0], jnp.float32)
    slot_scale = jnp.full((N_GRP * CAP,), 1.0, jnp.float32).at[slot_of].set(jnp.tile(kind_scale, LAYERS)) * unit_scale
    return jax.random.normal(key, (N_GRP * CAP, C, C), jnp.float32) * slot_scale[:, None, None]


def draw_dilations(key, part):
    key = jax.random.fold_in(key, 3)
    second_span = jax.random.randint(jax.random.fold_in(key, 1), (), 1, DMAX + 1)
    widest = jax.random.randint(jax.random.fold_in(key, 2), (), 0, LAYERS)
    return jnp.full((LAYERS,), second_span, jnp.int32).at[widest].set(DMAX)


def place_ends(values, key, least, high):
    spot = [jax.random.randint(jax.random.fold_in(key, axis), (), 0, length) for axis, length in enumerate(values.shape)]
    longest = values.shape.index(max(values.shape))
    next_to = spot[:longest] + [(spot[longest] + 1) % values.shape[longest]] + spot[longest + 1:]
    return values.at[tuple(spot)].set(least).at[tuple(next_to)].set(high)


def levels(stream_key, shape, split, low, top_value):
    def one(dim, parts):
        draws = jax.random.uniform(jax.random.fold_in(jax.random.fold_in(stream_key, 6), dim), (parts,), jnp.float32, low / len(split), top_value / len(split))
        return jnp.repeat(jnp.exp(draws), shape[dim] // parts).reshape((-1,) + (1,) * (len(shape) - dim - 1))

    level = one(*split[0])
    for cut in split[1:]:
        level = level * one(*cut)
    return level


def length_profile(number_of, total, reach, lean):
    loads = [(1 << 20) // math.isqrt(grade ** lean) + 1 for grade in range(2, number_of + 1)]
    rest, holding = total - reach - (number_of - 1), [1] * (number_of - 1)
    while rest > 0:
        movable = [i for i in range(number_of - 1) if holding[i] < reach]
        mass, left = sum([loads[i] for i in movable]), rest
        for i in movable:
            addition = min(reach - holding[i], max(1, left * loads[i] // mass), rest)
            holding[i] = holding[i] + addition
            rest = rest - addition
    return np.array([reach] + holding)


def ragged_sizes(key, number_of, total, limit, slope):
    if number_of == 2:
        one = jax.random.randint(key, (), max(1, total - limit), min(limit, total - 1) + 1)
        return jnp.stack([one, total - one])
    sizes = jnp.asarray(length_profile(number_of, total, limit, slope), jnp.int32)
    couples = (number_of - 1) // 2
    donor, receiver = sizes[1:1 + 2 * couples:2], sizes[2:2 + 2 * couples:2]
    room = jnp.minimum(donor - 1, limit - receiver)
    moved = jax.random.randint(jax.random.fold_in(key, 1), (couples,), 0, 1 << 20) % (room + 1)
    sizes = sizes.at[1:1 + 2 * couples:2].set(donor - moved).at[2:2 + 2 * couples:2].set(receiver + moved)
    return sizes[jax.random.permutation(jax.random.fold_in(key, 2), number_of)]


def centred(own_key, dims, scale, limit, cuts=(), kind=jnp.bfloat16):
    loudness = levels(own_key, dims, cuts, -0.22, 0.18) if cuts else 1.0
    result = jax.random.normal(own_key, dims, jnp.float32) * scale * loudness
    return jnp.minimum(jnp.maximum(result, -limit), limit).astype(kind)


def setup_inputs(seed: int = 0) -> dict:
    key_of = jax.random.split(jax.random.key(seed), 17)
    return {
        "frames_in": centred(key_of[0], (N_GRP, SEQLEN, C), 1.0, 6.0, ((0, 4), (1, 8))),
        "cond_frames": centred(key_of[1], (N_GRP, SEQLEN, C), 1.0, 6.0, ((0, 4), (1, 8))),
        "step_embed": centred(key_of[2], (N_GRP, C), 1.0, 6.0, ((0, 4),)),
        "prompts": centred(key_of[3], (NP, LP, C), 1.0, 6.0),
        "prompt_lengths": ragged_sizes(key_of[4], NP, NP * LP * 5 // 8, LP, 0).astype(jnp.int32),
        "pairing": place_ends(jax.random.randint(key_of[5], (N_GRP,), 0, NP), jax.random.fold_in(key_of[5], 1), 0, NP - 1).astype(jnp.int32),
        "dilations": draw_dilations(jax.random.fold_in(key_of[16], 71), 0),
        "owners": draw_owners(jax.random.fold_in(key_of[16], 71), 0),
        "master": draw_master(jax.random.fold_in(key_of[16], 71), 0),
        "first_moment": centred(key_of[9], (N_GRP * CAP, C, C), (0.022 * (TOK_DEV * N_SEQ * N_GRP) ** 0.5), 20.0, ((0, 4), (1, 8)), jnp.float32),
        "second_moment": jnp.clip(jnp.exp(math.log(3.2768) - 1.3862944 * jax.random.uniform(key_of[10], (N_GRP * CAP, C, C), jnp.float32) ** levels(key_of[10], (N_GRP * CAP, C, C), ((0, 4), (1, 8)), -0.2, 0.2)), 0.8192, 3.2768),
        "queries": centred(key_of[11], (LAYERS, NQ, C), 1.0, 6.0, (), jnp.float32),
        "query_first": centred(key_of[12], (LAYERS, NQ, C), (0.0022 * (TOK_DEV * N_SEQ * N_GRP) ** 0.5), 4.0, (), jnp.float32),
        "query_second": jnp.clip(jnp.exp(jax.random.uniform(key_of[13], (LAYERS, NQ, C), jnp.float32, math.log(0.008192), math.log(0.032768))), 0.008192, 0.032768),
        "grad_out": centred(key_of[14], (N_GRP, SEQLEN, C), 1.0, 6.0, ((0, 4), (1, 8))),
        "grad_skip": centred(key_of[15], (N_GRP, SEQLEN, C), 1.0, 6.0, ((0, 4), (1, 8))),
    }


PRECISE = lax.Precision.HIGHEST
BETA_ONE = 0.9
BETA_TWO = 0.999
EPSILON = 1e-08
WEIGHT_DECAY = 0.01
LEARN_RATE = 0.02
QUERY_RATE = 0.4
HALF_ROOT = 0.7071067811865476
NEGATIVE = -1e+30

@jax.custom_vjp
def low(v):
    return lax.optimization_barrier(v.astype(jnp.bfloat16)).astype(jnp.float32)

@jax.custom_vjp
def low_back(v):
    return v

def low_keep(v):
    return (low(v), None)

def low_pass(kept, grad):
    return (grad,)

def back_keep(v):
    return (v, None)

def back_low(kept, grad):
    return (low(grad),)
low.defvjp(low_keep, low_pass)
low_back.defvjp(back_keep, back_low)

def slot_index(owners):
    onehot = (owners[:, None] == jnp.arange(N_GRP, dtype=jnp.int32)[None, :]).astype(jnp.int32)
    before = jnp.cumsum(onehot, axis=0) - onehot
    return (owners * CAP + lax.optimization_barrier(jnp.sum(before * onehot, axis=1))).astype(jnp.int32)

def film_section(query_rows, key_weight, value_weight, out_weight, film_weight, prompt, length):
    channels = query_rows.shape[1]
    head_size = channels // HEADS
    prompt_rows = prompt.shape[0]
    keys_all = jnp.dot(prompt, key_weight, precision=PRECISE).reshape(prompt_rows, HEADS, head_size)
    values_all = jnp.dot(prompt, value_weight, precision=PRECISE).reshape(prompt_rows, HEADS, head_size)
    query_heads = query_rows.reshape(query_rows.shape[0], HEADS, head_size)
    scores = jnp.einsum('qhd,khd->hqk', query_heads, keys_all, precision=PRECISE) / math.sqrt(head_size)
    live = jnp.arange(prompt_rows) < length
    scores = jnp.where(live[None, None, :], scores, NEGATIVE)
    highest = lax.optimization_barrier(jnp.max(scores, axis=2, keepdims=True))
    expsum = jnp.exp(scores - highest)
    probs = expsum / lax.optimization_barrier(jnp.sum(expsum, axis=2, keepdims=True))
    mixed = jnp.einsum('hqk,khd->qhd', probs, values_all, precision=PRECISE).reshape(query_rows.shape[0], channels)
    pooled = lax.optimization_barrier(jnp.mean(jnp.dot(mixed, out_weight, precision=PRECISE), axis=0))
    film = jnp.dot(pooled, film_weight, precision=PRECISE)
    return (film[:channels], film[channels:])

def layer_parts(weights, layer_index):
    first_tile = 17 * layer_index
    tile_list = [weights[first_tile + number] for number in range(17)]

    def joined(start_tile):
        return jnp.concatenate([tile_list[start_tile], tile_list[start_tile + 1]], axis=1)
    conv_taps = [joined(2 * tap_index) for tap_index in range(3)]
    return (conv_taps, joined(6), joined(8), tile_list[10], tile_list[11], tile_list[12], joined(13), joined(15))

def group_forward(tile_set, query_set, frames, cond_rows, step_vector, prompt, length, dilations):
    weights = low(tile_set)
    channels = frames.shape[1]
    total_frames = frames.shape[0]
    skip_total = jnp.zeros_like(frames)
    for layer_index in range(LAYERS):
        conv_taps, cond_weight, diff_weight, key_weight, value_weight, out_weight, film_weight, branch_weight = layer_parts(weights, layer_index)
        film_scale, film_shift = film_section(query_set[layer_index], key_weight, value_weight, out_weight, film_weight, prompt, length)
        shifted = low(frames * (1.0 + film_scale) + film_shift)
        padded = jnp.pad(shifted, ((DMAX, DMAX), (0, 0)))
        hidden = jnp.dot(cond_rows, cond_weight, precision=PRECISE) + jnp.dot(step_vector[None, :], diff_weight, precision=PRECISE)
        for tap_index in range(3):
            start = (DMAX + (tap_index - 1) * dilations[layer_index]).astype(jnp.int32)
            window = lax.dynamic_slice_in_dim(padded, start, total_frames, 0)
            hidden = hidden + jnp.dot(window, conv_taps[tap_index], precision=PRECISE)
        hidden = low_back(hidden)
        gated = low(jnp.tanh(hidden[:, :channels]) * jax.nn.sigmoid(hidden[:, channels:]))
        branch = low_back(jnp.dot(gated, branch_weight, precision=PRECISE))
        frames = (frames + branch[:, :channels]) * HALF_ROOT
        skip_total = skip_total + branch[:, channels:]
    return (frames, skip_total)

def adam_update(weight, moment_one, moment_two, gradient, step_rate):
    moment_one = BETA_ONE * moment_one + (1.0 - BETA_ONE) * gradient
    moment_two = BETA_TWO * moment_two + (1.0 - BETA_TWO) * gradient * gradient
    normal = moment_one / (1.0 - BETA_ONE ** STEP) / (jnp.sqrt(moment_two / (1.0 - BETA_TWO ** STEP)) + EPSILON)
    return (moment_one, moment_two, weight - step_rate * (normal + WEIGHT_DECAY * weight))

def reference(frames_in, cond_frames, step_embed, prompts, prompt_lengths, pairing, dilations, owners, master, first_moment, second_moment, queries, query_first, query_second, grad_out, grad_skip):
    slot_of = slot_index(owners)
    tiles = jnp.take(master, slot_of, axis=0)

    def one_group(carry, inputs_now):
        frames_group, cond_group, embed_group, chosen, out_group, skip_group = inputs_now
        prompt = prompts[chosen].astype(jnp.float32)
        length = prompt_lengths[chosen]

        def run_group(tile_set, query_set, frames_start):
            return group_forward(tile_set, query_set, frames_start, cond_group.astype(jnp.float32), embed_group.astype(jnp.float32), prompt, length, dilations)
        results, pull_back = jax.vjp(run_group, tiles, queries, frames_group.astype(jnp.float32))
        tile_grad, query_grad, frame_grad = pull_back((out_group.astype(jnp.float32), skip_group.astype(jnp.float32)))
        return ((carry[0] + tile_grad, carry[1] + query_grad), (results[0], results[1], frame_grad))
    start_carry = (jnp.zeros_like(tiles), jnp.zeros_like(queries))
    (tile_total, query_total), (block_out, skip_out, grad_frames) = lax.scan(one_group, start_carry, (frames_in, cond_frames, step_embed, pairing, grad_out, grad_skip))
    occupied = jnp.zeros((N_GRP * CAP,), jnp.float32).at[slot_of].set(1.0)
    slot_grad = jnp.zeros_like(master).at[slot_of].set(tile_total)
    new_first, new_second, new_master = adam_update(master, first_moment, second_moment, slot_grad, LEARN_RATE)
    in_use = occupied[:, None, None] > 0.5
    new_first = jnp.where(in_use, new_first, first_moment)
    new_second = jnp.where(in_use, new_second, second_moment)
    new_master = jnp.where(in_use, new_master, master)
    new_query_first, new_query_second, new_queries = adam_update(queries, query_first, query_second, query_total, QUERY_RATE)
    return (new_first, new_second, new_master, new_master.astype(jnp.bfloat16), new_query_first, new_query_second, new_queries, block_out, skip_out, grad_frames)
```

```python
import functools

import jax
import jax.numpy as jnp
from jax import lax
from jax.experimental import pallas as pl
from jax.experimental.pallas import tpu as pltpu
from jax.sharding import PartitionSpec as P

HEADS = 8
LAYERS = 2
DMAX = 8
CAP = 13
STEP = 10
PER_LAYER = 17
TILES = PER_LAYER * LAYERS

BETA_ONE = 0.9
BETA_TWO = 0.999
EPSILON = 1e-08
WEIGHT_DECAY = 0.01
LEARN_RATE = 0.02
QUERY_RATE = 0.4
HALF_ROOT = 0.7071067811865476
NEGATIVE = -1e30

BF = jnp.bfloat16
F32 = jnp.float32
HALO = 32
WIDE = 256
FILM_ORDER = (10, 11, 12, 13, 14, 8, 9)
FILM = 2 * len(FILM_ORDER)
MAIN = 20
FILM_ALL = FILM * LAYERS
BLOCKS = FILM_ALL + MAIN * LAYERS
PHASES = ((0, FILM_ALL), (FILM_ALL, MAIN), (FILM_ALL + MAIN, MAIN))
MEM = 60 * 1024 * 1024
MESH = pl.DeviceIdType.MESH


def block_table():
    table = []
    for layer in range(LAYERS):
        for tile in FILM_ORDER:
            table += [(PER_LAYER * layer + tile, 0), (PER_LAYER * layer + tile, 1)]
    for layer in range(LAYERS):
        base = PER_LAYER * layer
        for part in range(4):
            for tap in range(4):
                table.append((base + 2 * tap + part // 2, part % 2))
        for part in range(4):
            table.append((base + 15 + part // 2, part % 2))
    return table


BLOCK_OF = {key: place for place, key in enumerate(block_table())}


def mm(a, b):
    return lax.dot_general(a, b, (((1,), (0,)), ((), ())), preferred_element_type=F32)


def mm_nt(a, b):
    return lax.dot_general(a, b, (((1,), (1,)), ((), ())), preferred_element_type=F32)


def split(a):
    high = a.astype(BF)
    return high, (a - high.astype(F32)).astype(BF)


def mm_fine(a, b):
    high, low = split(a)
    return mm(high, b) + mm(low, b)


def mm_nt_fine(a, b):
    high, low = split(a)
    return mm_nt(high, b) + mm_nt(low, b)


def mm_nt_pairs(a, blocks):
    total = None
    for place, block in enumerate(blocks):
        term = mm_nt_fine(a[:, place * WIDE : (place + 1) * WIDE], block)
        total = term if total is None else total + term
    return total


def window(ref, start, count):
    group, rest = lax.div(start, 8), lax.rem(start, 8)
    groups = ref[pl.ds(group, count // 8 + 1)]
    turned = pltpu.roll(groups, lax.rem(8 - rest, 8), 1)
    row = lax.broadcasted_iota(jnp.int32, (1, 8, 1), 1)
    return jnp.where(row < 8 - rest, turned[:-1], turned[1:]).reshape(count, ref.shape[2])


def in_eights(value):
    return value.reshape(value.shape[0] // 8, 8, value.shape[1])


def place_of(n_seq):
    seq, grp = lax.axis_index("seq"), lax.axis_index("grp")
    z, y = lax.div(seq, 2), lax.rem(seq, 2)
    x, c = lax.div(grp, 2), lax.rem(grp, 2)
    return seq, grp, z, y, x, c


def greet(n_seq, seq, grp, groups):
    barrier = pltpu.get_barrier_semaphore()

    def one(k, carry):
        pl.semaphore_signal(
            barrier, inc=1, device_id={"seq": lax.rem(seq + k, n_seq), "grp": grp}, device_id_type=MESH
        )
        return carry

    lax.fori_loop(1, n_seq, one, 0)
    for k in range(1, groups):
        pl.semaphore_signal(
            barrier, inc=1, device_id={"seq": seq, "grp": lax.rem(grp + k, groups)}, device_id_type=MESH
        )
    pl.semaphore_wait(barrier, n_seq - 1 + groups - 1)


def gather_kernel(
    n_seq, owners_ref, master_ref, frames_ref, cond_ref, gout_ref, gskip_ref, w_ref, halo_ref,
    prep, core_in, x_in, fin, send, recv, msend, mrecv, hsend, hrecv, lsem,
):
    seq, grp, z, y, x, c = place_of(n_seq)
    nz = n_seq // 2
    sib, across, other_y = x * 2 + 1 - c, (1 - x) * 2 + c, z * 2 + 1 - y
    greet(n_seq, seq, grp, 4)
    waits = []

    frames = frames_ref.shape[1]
    after, before = lax.rem(seq + 1, n_seq), lax.rem(seq + n_seq - 1, n_seq)
    halos = []
    for place, ref in enumerate((frames_ref, cond_ref, gout_ref, gskip_ref)):
        for side, (start, target) in enumerate(((frames - HALO, after), (0, before))):
            copy = pltpu.make_async_remote_copy(
                src_ref=ref.at[0, pl.ds(start, HALO)],
                dst_ref=halo_ref.at[side, place],
                send_sem=hsend.at[side, place],
                recv_sem=hrecv.at[side, place],
                device_id={"seq": target, "grp": grp},
                device_id_type=MESH,
            )
            copy.start()
            halos.append(copy)

    count = jnp.int32(0)
    for tile in range(TILES):
        own = (owners_ref[tile] == grp).astype(jnp.int32)
        slot = jnp.minimum(count, CAP - 1)
        value = (master_ref[slot] * own.astype(F32)).astype(BF)
        prep[BLOCK_OF[tile, 0]] = value[:, :WIDE]
        prep[BLOCK_OF[tile, 1]] = value[:, WIDE:]
        count = count + own

    def remote(src, dst, sems, index, to_seq, to_grp):
        copy = pltpu.make_async_remote_copy(
            src_ref=src,
            dst_ref=dst,
            send_sem=sems[0].at[index],
            recv_sem=sems[1].at[index],
            device_id={"seq": to_seq, "grp": to_grp},
            device_id_type=MESH,
        )
        copy.start()
        waits.append(copy)
        return copy

    mine, theirs = 2 * c + x, 2 * c + 1 - x
    merge, cross = [], []
    for number, (base, blocks) in enumerate(PHASES):
        each = blocks // 4
        merge.append(
            remote(
                prep.at[pl.ds(base + 2 * (1 - c) * each, 2 * each)],
                core_in.at[pl.ds(base // 2, 2 * each)],
                (msend, mrecv), (0, number), seq, sib,
            )
        )
    for number, (base, blocks) in enumerate(PHASES):
        each = blocks // 4
        merge[number].wait_recv()

        def add(i, carry, base=base, each=each):
            place = base + 2 * c * each + i
            prep[place] = prep[place] + core_in[base // 2 + i]
            return carry

        lax.fori_loop(0, 2 * each, add, 0)
        cross.append(
            remote(
                prep.at[pl.ds(base + theirs * each, each)],
                x_in.at[pl.ds(base // 4, each)],
                (msend, mrecv), (1, number), seq, across,
            )
        )

    class Leg:
        pass

    legs = {}

    def view(number, quarter, source):
        base, blocks = PHASES[number]
        each = blocks // 4
        return w_ref.at[pl.ds(base + quarter * each, each), source]

    def first(number, k):
        leg = Leg()
        zs = lax.rem(z - k + nz, nz)
        leg.a = 1 - lax.div(2 * zs, nz)
        leg.here, leg.there = zs * 2 + y, zs * 2 + 1 - y
        a, b = leg.a, 1 - leg.a
        leg.one = (a * other_y + b * seq, a * grp + b * across)
        leg.two = (a * seq + b * other_y, a * across + b * grp)
        base, blocks = PHASES[number]
        dst = view(number, mine, leg.here)
        src = dst if k else fin.at[pl.ds(base // 4, blocks // 4)]
        sems = (send, recv)
        leg.f1 = remote(src, dst, sems, (1, number, k), *leg.one)
        leg.f2a = remote(src, dst, sems, (2, number, k), *leg.two)
        leg.core = [remote(src, dst, sems, (4, number, k), seq, sib)]
        legs[number, k] = leg

    def second(number, k):
        leg = legs[number, k]
        a, b = leg.a, 1 - leg.a
        leg.f1.wait_recv()
        ref = view(number, a * mine + b * theirs, a * leg.there + b * leg.here)
        leg.f2b = remote(ref, ref, (send, recv), (3, number, k), *leg.two)
        leg.core.append(remote(ref, ref, (send, recv), (5, number, k), seq, sib))

    def third(number, k):
        leg = legs[number, k]
        a, b = leg.a, 1 - leg.a
        leg.f2a.wait_recv()
        ref = view(number, a * theirs + b * mine, a * leg.here + b * leg.there)
        leg.core.append(remote(ref, ref, (send, recv), (6, number, k), seq, sib))
        leg.f2b.wait_recv()
        ref = view(number, theirs, leg.there)
        leg.core.append(remote(ref, ref, (send, recv), (7, number, k), seq, sib))

    zcopies = {}
    locals_ = []
    for number, (base, blocks) in enumerate(PHASES):
        each = blocks // 4
        cross[number].wait_recv()

        def settle(i, carry, base=base, each=each):
            fin[base // 4 + i] = prep[base + mine * each + i] + x_in[base // 4 + i]
            return carry

        lax.fori_loop(0, each, settle, 0)
        src = fin.at[pl.ds(base // 4, each)]
        copy = pltpu.make_async_copy(src, view(number, mine, seq), lsem.at[number])
        copy.start()
        locals_.append(copy)
        for k in range(1, nz):
            zcopies[number, k] = remote(
                src, view(number, mine, seq), (send, recv), (0, number, k),
                lax.rem(z + k, nz) * 2 + y, grp,
            )
        first(number, 0)
    phases = len(PHASES)
    for step in range(phases + 2):
        if step < phases:
            for k in range(1, nz):
                zcopies[step, k].wait_recv()
                first(step, k)
        if 0 <= step - 1 < phases:
            for k in range(nz):
                second(step - 1, k)
        if 0 <= step - 2 < phases:
            for k in range(nz):
                third(step - 2, k)
    for leg in legs.values():
        for copy in leg.core:
            copy.wait_recv()
    for copy in locals_:
        copy.wait()
    for copy in halos:
        copy.wait()
    for copy in waits:
        copy.wait_send()


def any_spec():
    return pl.BlockSpec(memory_space=pl.ANY)


def vmem_spec():
    return pl.BlockSpec(memory_space=pltpu.VMEM)


def smem_spec():
    return pl.BlockSpec(memory_space=pltpu.SMEM)


def gather(n_seq, owners, master, frames_in, cond_frames, grad_out, grad_skip):
    rows = master.shape[1]
    nz = n_seq // 2
    dma = pltpu.SemaphoreType.DMA
    return pl.pallas_call(
        functools.partial(gather_kernel, n_seq),
        out_shape=(
            jax.ShapeDtypeStruct((BLOCKS, n_seq, rows, WIDE), BF),
            jax.ShapeDtypeStruct((2, 4, HALO, frames_in.shape[2]), BF),
        ),
        in_specs=[smem_spec(), vmem_spec()] + [any_spec()] * 4,
        out_specs=(any_spec(), any_spec()),
        scratch_shapes=[
            pltpu.VMEM((BLOCKS, rows, WIDE), BF),
            pltpu.VMEM((BLOCKS // 2, rows, WIDE), BF),
            pltpu.VMEM((BLOCKS // 4, rows, WIDE), BF),
            pltpu.VMEM((BLOCKS // 4, rows, WIDE), BF),
            dma((8, len(PHASES), nz)),
            dma((8, len(PHASES), nz)),
            dma((2, len(PHASES))),
            dma((2, len(PHASES))),
            dma((2, 4)),
            dma((2, 4)),
            dma((len(PHASES),)),
        ],
        compiler_params=pltpu.CompilerParams(
            collective_id=0, has_side_effects=True, vmem_limit_bytes=MEM
        ),
        name="gather",
    )(owners, master, frames_in, cond_frames, grad_out, grad_skip)


def head_mask():
    row = lax.broadcasted_iota(jnp.int32, (HEADS, 512), 0)
    column = lax.broadcasted_iota(jnp.int32, (HEADS, 512), 1)
    return lax.div(column, 512 // HEADS) == row


def block_diagonal(rows):
    column = lax.div(lax.broadcasted_iota(jnp.int32, rows.shape, 1), 512 // HEADS)
    return jnp.concatenate([jnp.where(column == h, rows, 0.0) for h in range(HEADS)], axis=0)


def same_rows(row):
    return jnp.broadcast_to(row, (8, row.shape[1]))


def film_kernel(
    pairing_ref, lengths_ref, queries_ref, embed_ref, prompts_ref, w_ref,
    vec_ref, prompt_ref, probs_ref, left_ref, wf, psem, wsem,
):
    chosen = pairing_ref[0]
    length = lengths_ref[chosen]
    pcopy = pltpu.make_async_copy(prompts_ref.at[chosen], prompt_ref, psem)
    pcopy.start()
    copies = []
    for layer in range(LAYERS):
        copy = pltpu.make_async_copy(
            w_ref.at[pl.ds(layer * FILM, FILM)], wf.at[layer], wsem.at[layer]
        )
        copy.start()
        copies.append(copy)
    pcopy.wait()
    prompt = prompt_ref[...]
    mask = head_mask()
    number = queries_ref.shape[1]
    embed = same_rows(embed_ref[...].astype(F32))
    for layer in range(LAYERS):
        copies[layer].wait()
        blocks = [wf[layer, i] for i in range(FILM)]
        spread = block_diagonal(queries_ref[layer])
        probe = mm_nt_pairs(spread, blocks[0:2])
        scores = mm_nt_fine(probe, prompt) * 0.125
        live = lax.broadcasted_iota(jnp.int32, scores.shape, 1) < length
        scores = jnp.where(live, scores, NEGATIVE)
        weight = jnp.exp(scores - jnp.max(scores, axis=1, keepdims=True))
        probs = weight / jnp.sum(weight, axis=1, keepdims=True)
        probs_ref[layer] = probs
        mean = jnp.concatenate(
            [
                jnp.mean(probs[h * number : (h + 1) * number], axis=0, keepdims=True)
                for h in range(HEADS)
            ],
            axis=0,
        )
        seen = mm_fine(mean, prompt)
        mixed = jnp.concatenate([mm_fine(seen, blocks[2]), mm_fine(seen, blocks[3])], axis=1)
        mixed = same_rows(jnp.sum(jnp.where(mask, mixed, 0.0), axis=0, keepdims=True))
        pooled = jnp.concatenate([mm_fine(mixed, blocks[4]), mm_fine(mixed, blocks[5])], axis=1)
        film = [mm_fine(pooled, blocks[6 + i]) for i in range(4)]
        embed_low = embed.astype(BF)
        steps = [mm(embed_low, blocks[10 + i]) for i in range(4)]
        vec_ref[layer, 0:1] = jnp.concatenate(film[:2], axis=1)[0:1]
        vec_ref[layer, 1:2] = jnp.concatenate(film[2:], axis=1)[0:1]
        vec_ref[layer, 2:3] = jnp.concatenate(steps[:2], axis=1)[0:1]
        vec_ref[layer, 3:4] = jnp.concatenate(steps[2:], axis=1)[0:1]
        vec_ref[layer, 4:8] = jnp.zeros((4, 512), F32)
        left_ref[layer, 0:8] = seen
        left_ref[layer, 8:9] = mixed[0:1]
        left_ref[layer, 9:10] = pooled[0:1]
        left_ref[layer, 10:11] = embed[0:1]
        left_ref[layer, 11:16] = jnp.zeros((5, 512), F32)


def film_forward(pairing, lengths, queries, step_embed, prompts, weights):
    channels = queries.shape[2]
    tall = HEADS * queries.shape[1]
    frames = prompts.shape[1]
    return pl.pallas_call(
        film_kernel,
        out_shape=(
            jax.ShapeDtypeStruct((LAYERS, 8, channels), F32),
            jax.ShapeDtypeStruct((frames, channels), BF),
            jax.ShapeDtypeStruct((LAYERS, tall, frames), F32),
            jax.ShapeDtypeStruct((LAYERS, 16, channels), F32),
        ),
        in_specs=[smem_spec(), smem_spec(), vmem_spec(), vmem_spec(), any_spec(), any_spec()],
        out_specs=(vmem_spec(),) * 4,
        scratch_shapes=[
            pltpu.VMEM((LAYERS, FILM, channels, WIDE), BF),
            pltpu.SemaphoreType.DMA,
            pltpu.SemaphoreType.DMA((LAYERS,)),
        ],
        compiler_params=pltpu.CompilerParams(vmem_limit_bytes=MEM),
        name="film",
    )(pairing, lengths, queries, step_embed, prompts, weights)


def compute_kernel(
    n_seq, dil_ref, vec_ref, frames_ref, cond_ref, gout_ref, gskip_ref, halo_ref, w_ref,
    block_ref, skip_ref, gframes_ref, grad_ref, sums_ref,
    wl, xe, sh, cat, tt, ss, gated, x1, bh, bb, sht, condt, gatt, bx, stage, wsem, gsem,
):
    own = frames_ref.shape[1]
    grid_rows = own + 2 * HALO
    top = HALO + own
    seq = lax.axis_index("seq")
    wcopies = []
    for layer in range(LAYERS):
        copy = pltpu.make_async_copy(
            w_ref.at[pl.ds(FILM_ALL + MAIN * layer, MAIN)], wl.at[layer], wsem.at[layer]
        )
        copy.start()
        wcopies.append(copy)

    def inside(low, number):
        row = lax.broadcasted_iota(jnp.int32, (number, 1), 0) + (low - HALO) + seq * own
        return (row >= 0) & (row < n_seq * own)

    def chunks(low, high, body):
        number = (high - low) // 2
        for part in range(2):
            body(low + part * number, number)

    xe[0:HALO] = halo_ref[0, 0]
    xe[HALO:top] = frames_ref[0]
    xe[top:grid_rows] = halo_ref[1, 0]
    cat[0:HALO, 1536:2048] = halo_ref[0, 1]
    cat[HALO:top, 1536:2048] = cond_ref[0]
    cat[top:grid_rows, 1536:2048] = halo_ref[1, 1]
    condt[...] = jnp.transpose(cond_ref[0].astype(F32)).astype(BF)

    for layer in range(LAYERS):
        low = 0 if layer == 0 else 16
        high = grid_rows - low
        number = high - low
        wcopies[layer].wait()
        scale, shift = 1.0 + vec_ref[layer, 0:1], vec_ref[layer, 1:2]
        here = xe[...].astype(F32) if layer == 0 else x1[...]
        shifted = (here * scale + shift).astype(BF).astype(F32)
        shifted = jnp.where(inside(0, grid_rows), shifted, 0.0)
        groups = grid_rows // 8
        sh[0] = jnp.zeros((8, 512), F32)
        sh[1 : 1 + groups] = in_eights(shifted)
        sh[1 + groups :] = jnp.zeros((3, 8, 512), F32)
        sht[layer] = jnp.transpose(shifted[HALO:top]).astype(BF)
        for tap in range(3):
            start = DMAX + low + (tap - 1) * dil_ref[layer]
            cat[low:high, tap * 512 : (tap + 1) * 512] = window(
                sh, start, number
            ).astype(BF)

        def gates(first, count, layer=layer):
            rows = cat[first : first + count, 0:2048]
            for part in range(2):
                columns = slice(part * WIDE, (part + 1) * WIDE)
                left = mm(rows, wl[layer, part * 4 : part * 4 + 4].reshape(2048, WIDE))
                tangent = jnp.tanh(left + vec_ref[layer, 2:3, columns])
                right = mm(rows, wl[layer, part * 4 + 8 : part * 4 + 12].reshape(2048, WIDE))
                opening = jax.nn.sigmoid(right + vec_ref[layer, 3:4, columns])
                tt[layer, first : first + count, columns] = tangent
                ss[layer, first : first + count, columns] = opening
                gated[first : first + count, columns] = (tangent * opening).astype(BF)

        chunks(low, high, gates)
        gatt[layer] = jnp.transpose(gated[HALO:top].astype(F32)).astype(BF)

        def residual(first, count, layer=layer):
            rows = gated[first : first + count]
            for part in range(2):
                columns = slice(part * WIDE, (part + 1) * WIDE)
                term = mm(rows, wl[layer, 16 + part])
                if layer == 0:
                    base = xe[first : first + count, columns].astype(F32)
                    x1[first : first + count, columns] = (base + term) * HALF_ROOT
                else:
                    base = x1[first : first + count, columns]
                    block_ref[0, first - HALO : first - HALO + count, columns] = (
                        base + term
                    ) * HALF_ROOT

        if layer == 0:
            chunks(0, grid_rows, residual)
        else:
            chunks(HALO, top, residual)

        def skipped(first, count, layer=layer):
            rows = gated[first : first + count]
            place = slice(first - HALO, first - HALO + count)
            for part in range(2):
                columns = slice(part * WIDE, (part + 1) * WIDE)
                term = mm(rows, wl[layer, 18 + part])
                if layer == 0:
                    skip_ref[0, place, columns] = term
                else:
                    skip_ref[0, place, columns] = skip_ref[0, place, columns] + term

        chunks(HALO, top, skipped)

    low, high = 16, grid_rows - 16
    bx[0:HALO] = halo_ref[0, 2].astype(F32)
    bx[HALO:top] = gout_ref[0].astype(F32)
    bx[top:grid_rows] = halo_ref[1, 2].astype(F32)
    bb[0:HALO, 512:1024] = halo_ref[0, 3]
    bb[HALO:top, 512:1024] = gskip_ref[0]
    bb[top:grid_rows, 512:1024] = halo_ref[1, 3]
    edge = 1 + low // 8
    bh[0:edge] = jnp.zeros((edge, 8, 1024), F32)
    bh[1 + high // 8 :] = jnp.zeros((edge + 2, 8, 1024), F32)
    sums_ref[...] = jnp.zeros_like(sums_ref)

    for layer in reversed(range(LAYERS)):
        bb[low:high, 0:512] = (bx[low:high] * HALF_ROOT).astype(BF)
        branch = jnp.concatenate([wl[layer, 16 + part] for part in range(4)], axis=1)

        def gate_grads(first, count, layer=layer, branch=branch):
            rows = slice(first, first + count)
            back = mm_nt(bb[rows], branch)
            tangent, opening = tt[layer, rows], ss[layer, rows]
            keep = inside(first, count)
            slope = back * opening
            one = (slope * (1.0 - tangent * tangent)).astype(BF).astype(F32)
            two = (slope * tangent * (1.0 - opening)).astype(BF).astype(F32)
            place = slice(1 + first // 8, 1 + (first + count) // 8)
            bh[place, :, 0:512] = in_eights(jnp.where(keep, one, 0.0))
            bh[place, :, 512:1024] = in_eights(jnp.where(keep, two, 0.0))

        chunks(low, high, gate_grads)
        total = bh[1 + HALO // 8 : 1 + top // 8].reshape(own, 1024)
        total = jnp.sum(total, axis=0, keepdims=True)
        sums_ref[layer, 2:3] = total[:, 0:512]
        sums_ref[layer, 3:4] = total[:, 512:1024]
        reach, limit = (low, high) if layer else (HALO, top)
        for tap in range(3):
            start = DMAX + reach - (tap - 1) * dil_ref[layer]
            cat[reach:limit, tap * 1024 : (tap + 1) * 1024] = window(
                bh, start, limit - reach
            ).astype(BF)
        taps = jnp.concatenate(
            [wl[layer, part * 4 + tap] for tap in range(3) for part in range(4)], axis=1
        )
        scale = 1.0 + vec_ref[layer, 0:1]

        def frame_grads(first, count, layer=layer, taps=taps, scale=scale):
            rows = slice(first, first + count)
            back = mm_nt(cat[rows], taps)
            if layer:
                here = x1[rows]
                row = lax.broadcasted_iota(jnp.int32, (count, 1), 0) + first
                kept = jnp.where((row >= HALO) & (row < top), back, 0.0)
            else:
                here = xe[rows].astype(F32)
                kept = back
            sums_ref[layer, 0:1] += jnp.sum(kept * here, axis=0, keepdims=True)
            sums_ref[layer, 1:2] += jnp.sum(kept, axis=0, keepdims=True)
            result = bx[rows] * HALF_ROOT + back * scale
            if layer:
                bx[rows] = result
            else:
                gframes_ref[0, first - HALO : first - HALO + count] = result

        chunks(reach, limit, frame_grads)

        def drain(slot, layer=layer):
            for i in range(5):
                pltpu.make_async_copy(
                    stage.at[slot, i], grad_ref.at[layer, i], gsem.at[slot, i]
                ).wait()

        def weight_grads(part, carry, layer=layer):
            slot = lax.rem(part, 2)

            @pl.when(part >= 2)
            def _():
                drain(slot)

            left = sht[layer]
            for i in range(5):
                if i < 3:
                    start = pl.multiple_of(i * 1024 + part * WIDE, WIDE)
                    value = mm(left, cat[HALO:top, pl.ds(start, WIDE)])
                elif i == 3:
                    start = pl.multiple_of(1024 + part * WIDE, WIDE)
                    value = mm(condt[...], cat[HALO:top, pl.ds(start, WIDE)])
                else:
                    start = pl.multiple_of(part * WIDE, WIDE)
                    value = mm(gatt[layer], bb[HALO:top, pl.ds(start, WIDE)])
                stage[slot, i] = value.astype(BF)
                place = part * 4 + i if i < 4 else 16 + part
                pltpu.make_async_copy(
                    stage.at[slot, i], grad_ref.at[layer, place], gsem.at[slot, i]
                ).start()
            return carry

        lax.fori_loop(0, 4, weight_grads, 0)
        drain(0)
        drain(1)


def compute(n_seq, dilations, vec, frames_in, cond_frames, grad_out, grad_skip, halo, weights):
    _, own, channels = frames_in.shape
    rows = own + 2 * HALO
    v = pltpu.VMEM
    frame_out = jax.ShapeDtypeStruct((1, own, channels), F32)
    return pl.pallas_call(
        functools.partial(compute_kernel, n_seq),
        out_shape=(
            frame_out,
            frame_out,
            frame_out,
            jax.ShapeDtypeStruct((LAYERS, MAIN, channels, WIDE), BF),
            jax.ShapeDtypeStruct((LAYERS, 8, channels), F32),
        ),
        in_specs=[smem_spec()] + [vmem_spec()] * 6 + [any_spec()],
        out_specs=(vmem_spec(),) * 3 + (any_spec(), vmem_spec()),
        scratch_shapes=[
            v((LAYERS, MAIN, channels, WIDE), BF),
            v((rows, channels), BF),
            v((rows // 8 + 4, 8, channels), F32),
            v((rows, 6 * channels), BF),
            v((LAYERS, rows, channels), F32),
            v((LAYERS, rows, channels), F32),
            v((rows, channels), BF),
            v((rows, channels), F32),
            v((rows // 8 + 4, 8, 2 * channels), F32),
            v((rows, 2 * channels), BF),
            v((LAYERS, channels, own), BF),
            v((channels, own), BF),
            v((LAYERS, channels, own), BF),
            v((rows, channels), F32),
            v((2, 5, channels, WIDE), BF),
            pltpu.SemaphoreType.DMA((LAYERS,)),
            pltpu.SemaphoreType.DMA((2, 5)),
        ],
        compiler_params=pltpu.CompilerParams(vmem_limit_bytes=MEM),
        name="frames",
    )(dilations, vec, frames_in, cond_frames, grad_out, grad_skip, halo, weights)


def reduce_kernel(
    n_seq, grad_ref, sums_ref, w_ref, prompt_ref, probs_ref, left_ref, queries_ref,
    out_ref, rt_ref, lt_ref, dq_ref,
    mine_in, core_in, chip, one_in, half, two_in, part, z_in, fin, sp, wf, tall, rt, lt, dq,
    osem, send, recv, zsend, zrecv, gsend, grecv, ssend, srecv, bsend, brecv, wsem, lsem,
):
    seq, grp, z, y, x, c = place_of(n_seq)
    nz = n_seq // 2
    rows = fin.shape[2]
    sib, across, other_y = x * 2 + 1 - c, (1 - x) * 2 + c, z * 2 + 1 - y
    wcopies = []
    for layer in range(LAYERS):
        copy = pltpu.make_async_copy(
            w_ref.at[pl.ds(layer * FILM, 10)], wf.at[layer], wsem.at[layer]
        )
        copy.start()
        wcopies.append(copy)
    greet(n_seq, seq, grp, 4)
    waits = []

    def remote(src, dst, one, two, to_seq, to_grp):
        copy = pltpu.make_async_remote_copy(
            src_ref=src,
            dst_ref=dst,
            send_sem=one,
            recv_sem=two,
            device_id={"seq": to_seq, "grp": to_grp},
            device_id_type=MESH,
        )
        copy.start()
        waits.append(copy)
        return copy

    def sums_copy(k):
        return pltpu.make_async_remote_copy(
            src_ref=sums_ref,
            dst_ref=sp.at[seq],
            send_sem=ssend.at[k],
            recv_sem=srecv.at[k],
            device_id={"seq": lax.rem(seq + k, n_seq), "grp": grp},
            device_id_type=MESH,
        )

    def sums_start(k, carry):
        sums_copy(k).start()
        return carry

    lax.fori_loop(1, n_seq, sums_start, 0)
    sp[seq] = sums_ref[...]

    order = [(layer, k) for layer in reversed(range(LAYERS)) for k in reversed(range(nz))]
    targets = {k: lax.rem(z + k, nz) for k in range(nz)}
    core, own = {}, {}
    for layer, k in order:
        spot = pl.ds(2 * targets[k], 2)
        core[layer, k] = remote(
            grad_ref.at[layer, pl.ds(2 * (1 - c), 2), :, spot],
            core_in.at[layer, k],
            send.at[0, layer, k], recv.at[0, layer, k], seq, sib,
        )
        own[layer, k] = pltpu.make_async_copy(
            grad_ref.at[layer, pl.ds(2 * c, 2), :, spot], mine_in.at[layer, k], osem.at[layer, k]
        )
        own[layer, k].start()

    each = MAIN // 4

    def add(a, b):
        return (a.astype(F32) + b.astype(F32)).astype(BF)

    ones, twos, zs = {}, {}, {}

    def stage_one(layer, k):
        own[layer, k].wait()
        core[layer, k].wait_recv()
        a = 1 - lax.div(2 * targets[k], nz)
        b = 1 - a

        def body(i, carry):
            for xx in range(2):
                for yy in range(2):
                    place = a * (2 * xx + yy) + b * (2 * yy + xx)
                    chip[layer, k, place, i] = add(
                        mine_in[layer, k, xx, i, yy], core_in[layer, k, xx, i, yy]
                    )
            return carry

        lax.fori_loop(0, each, body, 0)
        me = a * x + b * y
        ones[layer, k] = remote(
            chip.at[layer, k, pl.ds(2 * (1 - me), 2)],
            one_in.at[layer, k],
            send.at[1, layer, k], recv.at[1, layer, k],
            a * seq + b * other_y, a * across + b * grp,
        )

    def stage_two(layer, k):
        ones[layer, k].wait_recv()
        a = 1 - lax.div(2 * targets[k], nz)
        b = 1 - a
        me, you = a * x + b * y, a * y + b * x

        def body(i, carry):
            for j in range(2):
                half[layer, k, j, i] = add(chip[layer, k, 2 * me + j, i], one_in[layer, k, j, i])
            return carry

        lax.fori_loop(0, each, body, 0)
        twos[layer, k] = remote(
            half.at[layer, k, 1 - you],
            two_in.at[layer, k],
            send.at[2, layer, k], recv.at[2, layer, k],
            a * other_y + b * seq, a * grp + b * across,
        )

    def stage_three(layer, k):
        twos[layer, k].wait_recv()
        a = 1 - lax.div(2 * targets[k], nz)
        you = a * y + (1 - a) * x

        def body(i, carry):
            part[layer, k, i] = add(half[layer, k, you, i], two_in[layer, k, i])
            return carry

        lax.fori_loop(0, each, body, 0)
        if k:
            zs[layer, k] = remote(
                part.at[layer, k], z_in.at[layer, k],
                zsend.at[layer, k], zrecv.at[layer, k], targets[k] * 2 + y, grp,
            )

    finals, lcopies = [], []
    mine = 2 * c + x

    def stage_four(layer):
        for k in range(1, nz):
            zs[layer, k].wait_recv()

        def body(i, carry):
            total = part[layer, 0, i].astype(F32)
            for k in range(1, nz):
                total = total + z_in[layer, k, i].astype(F32)
            fin[layer, i] = total.astype(BF)
            return carry

        lax.fori_loop(0, each, body, 0)
        copy = pltpu.make_async_copy(fin.at[layer], out_ref.at[layer, mine], lsem.at[layer])
        copy.start()
        lcopies.append(copy)
        for k in range(1, 4):
            finals.append(
                remote(
                    fin.at[layer], out_ref.at[layer, mine],
                    gsend.at[layer, k], grecv.at[layer, k], seq, lax.rem(grp + k, 4),
                )
            )

    bundles = []

    def film_backward():
        def sums_wait(k, carry):
            sums_copy(k).wait()
            return carry

        lax.fori_loop(1, n_seq, sums_wait, 0)
        prompt = prompt_ref[...]
        mask = head_mask()
        number = queries_ref.shape[1]
        for layer in range(LAYERS):
            wcopies[layer].wait()
            blocks = [wf[layer, i] for i in range(10)]
            total = sp[0, layer]
            for k in range(1, n_seq):
                total = total + sp[k, layer]
            dfilm = jnp.concatenate([same_rows(total[0:1]), same_rows(total[1:2])], axis=1)
            dpooled = mm_nt_pairs(dfilm, blocks[6:10])
            dmixed = mm_nt_pairs(dpooled, blocks[4:6])
            dseen = mm_nt_pairs(jnp.where(mask, dmixed, 0.0), blocks[2:4])
            dmean = mm_nt_fine(dseen, prompt) * (1.0 / number)
            dprobs = jnp.concatenate(
                [jnp.broadcast_to(dmean[h : h + 1], (number, 512)) for h in range(HEADS)], axis=0
            )
            probs = probs_ref[layer]
            inner = jnp.sum(dprobs * probs, axis=1, keepdims=True)
            dscores = probs * (dprobs - inner) * 0.125
            dprobe = mm_fine(dscores, prompt)
            dspread = jnp.concatenate([mm_fine(dprobe, blocks[0]), mm_fine(dprobe, blocks[1])], axis=1)
            column = lax.div(lax.broadcasted_iota(jnp.int32, (number, 512), 1), 512 // HEADS)
            dquery = jnp.zeros((number, 512), F32)
            for h in range(HEADS):
                dquery = dquery + jnp.where(
                    column == h, dspread[h * number : (h + 1) * number], 0.0
                )
            dq[grp, layer] = dquery.astype(BF)
            tall[layer, :, 0:256] = jnp.transpose(dprobe)
            lefts = jnp.concatenate([left_ref[layer], jnp.zeros((112, 512), F32)], axis=0)
            tall[layer, :, 256:384] = jnp.transpose(lefts)
            start = pl.multiple_of(seq * rows, rows)
            lt[grp, layer] = tall[layer, pl.ds(start, rows), :].astype(BF)
            rt[grp, layer] = jnp.concatenate(
                [total[0:4], dpooled[0:1], dmixed[0:1], jnp.zeros((2, 512), F32)], axis=0
            )
        for k in range(1, 4):
            for j, ref in enumerate((rt, lt, dq)):
                bundles.append(
                    remote(
                        ref.at[grp], ref.at[grp], bsend.at[j, k], brecv.at[j, k],
                        seq, lax.rem(grp + k, 4),
                    )
                )

    stages = len(order)
    for step in range(stages + 2):
        if step < stages:
            stage_one(*order[step])
        if 0 <= step - 1 < stages:
            stage_two(*order[step - 1])
        if 0 <= step - 2 < stages:
            stage_three(*order[step - 2])
        if step == 2:
            film_backward()
        if step == nz + 2:
            stage_four(LAYERS - 1)
    stage_four(0)

    for copy in bundles:
        copy.wait_recv()
    rt_ref[...] = rt[...]
    lt_ref[...] = lt[...]
    total = dq[0].astype(F32)
    for k in range(1, 4):
        total = total + dq[k].astype(F32)
    dq_ref[...] = total
    for copy in finals:
        copy.wait_recv()
    for copy in lcopies:
        copy.wait()
    for copy in waits:
        copy.wait_send()


def reduce_grads(n_seq, rows, grads, sums, weights, prompt, probs, left, queries):
    nz = n_seq // 2
    each = MAIN // 4
    channels = queries.shape[2]
    grads = grads.reshape(LAYERS, 4, each, n_seq, rows, WIDE)
    v = pltpu.VMEM
    dma = pltpu.SemaphoreType.DMA
    number = queries.shape[1]
    return pl.pallas_call(
        functools.partial(reduce_kernel, n_seq),
        out_shape=(
            jax.ShapeDtypeStruct((LAYERS, 4, each, rows, WIDE), BF),
            jax.ShapeDtypeStruct((4, LAYERS, 8, channels), F32),
            jax.ShapeDtypeStruct((4, LAYERS, rows, 384), BF),
            jax.ShapeDtypeStruct((LAYERS, number, channels), F32),
        ),
        in_specs=[any_spec(), vmem_spec(), any_spec()] + [vmem_spec()] * 4,
        out_specs=(any_spec(),) + (vmem_spec(),) * 3,
        scratch_shapes=[
            v((LAYERS, nz, 2, each, 2, rows, WIDE), BF),
            v((LAYERS, nz, 2, each, 2, rows, WIDE), BF),
            v((LAYERS, nz, 4, each, rows, WIDE), BF),
            v((LAYERS, nz, 2, each, rows, WIDE), BF),
            v((LAYERS, nz, 2, each, rows, WIDE), BF),
            v((LAYERS, nz, each, rows, WIDE), BF),
            v((LAYERS, nz, each, rows, WIDE), BF),
            v((LAYERS, nz, each, rows, WIDE), BF),
            v((LAYERS, each, rows, WIDE), BF),
            v((n_seq, LAYERS, 8, channels), F32),
            v((LAYERS, 10, channels, WIDE), BF),
            v((LAYERS, channels, 384), F32),
            v((4, LAYERS, 8, channels), F32),
            v((4, LAYERS, rows, 384), BF),
            v((4, LAYERS, number, channels), BF),
            dma((LAYERS, nz)),
            dma((3, LAYERS, nz)),
            dma((3, LAYERS, nz)),
            dma((LAYERS, nz)),
            dma((LAYERS, nz)),
            dma((LAYERS, 4)),
            dma((LAYERS, 4)),
            dma((n_seq,)),
            dma((n_seq,)),
            dma((3, 4)),
            dma((3, 4)),
            dma((LAYERS,)),
            dma((LAYERS,)),
        ],
        compiler_params=pltpu.CompilerParams(
            collective_id=1, has_side_effects=True, vmem_limit_bytes=MEM
        ),
        name="reduce",
    )(grads, sums, weights, prompt, probs, left, queries)


def adam_update(weight, moment_one, moment_two, gradient, step_rate):
    moment_one = BETA_ONE * moment_one + (1.0 - BETA_ONE) * gradient
    moment_two = BETA_TWO * moment_two + (1.0 - BETA_TWO) * gradient * gradient
    normal = (
        moment_one
        / (1.0 - BETA_ONE**STEP)
        / (jnp.sqrt(moment_two / (1.0 - BETA_TWO**STEP)) + EPSILON)
    )
    return (moment_one, moment_two, weight - step_rate * (normal + WEIGHT_DECAY * weight))


def update_kernel(
    owners_ref, master_ref, first_ref, second_ref, grad_ref, rt_ref, lt_ref,
    queries_ref, qfirst_ref, qsecond_ref, dq_ref,
    nfirst_ref, nsecond_ref, nmaster_ref, ncopy_ref, nqfirst_ref, nqsecond_ref, nqueries_ref,
    tg,
):
    step = pl.program_id(0)
    grp = lax.axis_index("grp")

    @pl.when(step == 0)
    def _():
        one, two, three = adam_update(
            queries_ref[...], qfirst_ref[...], qsecond_ref[...], dq_ref[...], QUERY_RATE
        )
        nqfirst_ref[...] = one
        nqsecond_ref[...] = two
        nqueries_ref[...] = three
        for layer in range(LAYERS):
            base = PER_LAYER * layer
            for place in range(MAIN):
                tile, side = block_table()[FILM_ALL + MAIN * layer + place]
                tg[tile, :, side * WIDE : (side + 1) * WIDE] = grad_ref[
                    layer, place // 5, place % 5
                ].astype(F32)
            spread = block_diagonal(queries_ref[layer])
            probe = lt_ref[0, layer, :, 0:256].astype(F32)
            for k in range(1, 4):
                probe = probe + lt_ref[k, layer, :, 0:256].astype(F32)
            tg[base + 10] = mm(probe.astype(BF), spread.astype(BF))
            mask = head_mask()
            row = lax.broadcasted_iota(jnp.int32, (128, 512), 0)

            def only(vector, at):
                return jnp.where(row == at, vector, 0.0)

            totals = [None] * 6
            for k in range(4):
                left = lt_ref[k, layer, :, 256:384]
                right = rt_ref[k, layer]
                value = jnp.concatenate(
                    [jnp.where(mask, right[5:6], 0.0), jnp.zeros((120, 512), F32)], axis=0
                )
                sides = [
                    value, only(right[4:5], 8), only(right[0:1], 9), only(right[1:2], 9),
                    only(right[2:3], 10), only(right[3:4], 10),
                ]
                for i, side in enumerate(sides):
                    term = mm(left, side.astype(BF))
                    totals[i] = term if totals[i] is None else totals[i] + term
            for i, tile in enumerate((11, 12, 13, 14, 8, 9)):
                tg[base + tile] = totals[i]

    tile, count = jnp.int32(0), jnp.int32(0)
    used = jnp.int32(0)
    for t in range(TILES):
        own = (owners_ref[t] == grp).astype(jnp.int32)
        hit = own * (count == step).astype(jnp.int32)
        tile = tile + hit * t
        used = used + hit
        count = count + own
    gradient = tg[tile]
    master, first, second = master_ref[0], first_ref[0], second_ref[0]
    one, two, three = adam_update(master, first, second, gradient, LEARN_RATE)
    keep = jnp.broadcast_to(used, master.shape) > 0
    three = jnp.where(keep, three, master)
    nfirst_ref[0] = jnp.where(keep, one, first)
    nsecond_ref[0] = jnp.where(keep, two, second)
    nmaster_ref[0] = three
    ncopy_ref[0] = three.astype(BF)


def update(owners, master, first, second, grads, rt, lt, queries, qfirst, qsecond, dq):
    _, rows, channels = master.shape
    slot = pl.BlockSpec((1, rows, channels), lambda i: (i, 0, 0))
    whole = vmem_spec()
    query = jax.ShapeDtypeStruct(queries.shape, F32)
    full = jax.ShapeDtypeStruct(master.shape, F32)
    return pl.pallas_call(
        update_kernel,
        grid=(CAP,),
        out_shape=(full, full, full, jax.ShapeDtypeStruct(master.shape, BF), query, query, query),
        in_specs=[smem_spec(), slot, slot, slot] + [whole] * 7,
        out_specs=(slot, slot, slot, slot, whole, whole, whole),
        scratch_shapes=[pltpu.VMEM((TILES, rows, channels), F32)],
        compiler_params=pltpu.CompilerParams(vmem_limit_bytes=MEM),
        name="update",
    )(owners, master, first, second, grads, rt, lt, queries, qfirst, qsecond, dq)


def on_device(
    n_seq,
    frames_in,
    cond_frames,
    step_embed,
    prompts,
    prompt_lengths,
    pairing,
    dilations,
    owners,
    master,
    first_moment,
    second_moment,
    queries,
    query_first,
    query_second,
    grad_out,
    grad_skip,
):
    rows = master.shape[1]
    channels = master.shape[2]
    gathered, halo = gather(
        n_seq, owners, master, frames_in, cond_frames, grad_out, grad_skip
    )
    weights = gathered.reshape(BLOCKS, channels, WIDE)
    vec, prompt, probs, left = film_forward(
        pairing, prompt_lengths, queries, step_embed, prompts, weights
    )
    block_out, skip_out, grad_frames, grads, sums = compute(
        n_seq, dilations, vec, frames_in, cond_frames, grad_out, grad_skip, halo, weights
    )
    own_grads, rt, lt, dq = reduce_grads(
        n_seq, rows, grads, sums, weights, prompt, probs, left, queries
    )
    new_first, new_second, new_master, new_copy, nqf, nqs, nq = update(
        owners, master, first_moment, second_moment, own_grads, rt, lt,
        queries, query_first, query_second, dq,
    )
    return (
        new_first, new_second, new_master, new_copy, nqf, nqs, nq,
        block_out, skip_out, grad_frames,
    )


def solution(mesh):
    shard = P("grp", "seq", None)
    placed = (
        shard, shard, P("grp", None), P(), P(), P("grp"), P(), P(),
        shard, shard, shard, P(), P(), P(), shard, shard,
    )
    return jax.shard_map(
        functools.partial(on_device, mesh.shape["seq"]),
        mesh=mesh,
        in_specs=placed,
        out_specs=(shard, shard, shard, shard, P(), P(), P(), shard, shard, shard),
        check_vma=False,
    )
```

```python
import functools

import jax
import jax.numpy as jnp
from jax import lax
from jax.experimental import pallas as pl
from jax.experimental.pallas import tpu as pltpu
from jax.sharding import PartitionSpec as P

HEADS = 8
LAYERS = 2
DMAX = 8
CAP = 13
STEP = 10
PER_LAYER = 17
TILES = PER_LAYER * LAYERS

BETA_ONE = 0.9
BETA_TWO = 0.999
EPSILON = 1e-08
WEIGHT_DECAY = 0.01
LEARN_RATE = 0.02
QUERY_RATE = 0.4
HALF_ROOT = 0.7071067811865476
NEGATIVE = -1e30

BF = jnp.bfloat16
F32 = jnp.float32
HALO = 32
WIDE = 256
KEYS = 2 * LAYERS
MAIN = 20
BLOCKS = KEYS + MAIN * LAYERS
PHASES = ((0, KEYS), (KEYS, MAIN), (KEYS + MAIN, MAIN))
FILM_ORDER = (11, 12, 13, 14, 8, 9)
FILM = 2 * len(FILM_ORDER)
LOW_RANK = 1 + len(FILM_ORDER)
HOP_ROWS = (24, 8, 16, 32, 8, 8, 64)
MEM = 64 * 1024 * 1024 - 256 * 1024
MESH = pl.DeviceIdType.MESH


def block_table():
    table = {}
    for layer in range(LAYERS):
        base = PER_LAYER * layer
        for side in range(2):
            table[base + 10, side] = 2 * layer + side
        start = KEYS + MAIN * layer
        for part in range(4):
            for tap in range(4):
                table[base + 2 * tap + part // 2, part % 2] = start + 5 * part + tap
            table[base + 15 + part // 2, part % 2] = start + 5 * part + 4
    return table


BLOCK_OF = block_table()
FILM_OF = {
    (PER_LAYER * layer + tile, side): FILM * layer + 2 * place + side
    for layer in range(LAYERS)
    for place, tile in enumerate(FILM_ORDER)
    for side in range(2)
}


def mm(a, b):
    return lax.dot_general(a, b, (((1,), (0,)), ((), ())), preferred_element_type=F32)


def mm_nt(a, b):
    return lax.dot_general(a, b, (((1,), (1,)), ((), ())), preferred_element_type=F32)


def split(a):
    high = a.astype(BF)
    return high, (a - high.astype(F32)).astype(BF)


def mm_fine(a, b):
    high, low = split(a)
    return mm(high, b) + mm(low, b)


def mm_nt_fine(a, b):
    high, low = split(a)
    return mm_nt(high, b) + mm_nt(low, b)


def mm_nt_pairs(a, blocks):
    total = None
    for place, block in enumerate(blocks):
        term = mm_nt_fine(a[:, place * WIDE : (place + 1) * WIDE], block)
        total = term if total is None else total + term
    return total


def window(ref, start, count, width):
    group, rest = lax.div(start, 8), lax.rem(start, 8)
    groups = ref[pl.ds(group, count // 8 + 1), :, 0:width]
    turned = pltpu.roll(groups, lax.rem(8 - rest, 8), 1)
    row = lax.broadcasted_iota(jnp.int32, (1, 8, 1), 1)
    return jnp.where(row < 8 - rest, turned[:-1], turned[1:]).reshape(count, width)


def in_eights(value):
    return value.reshape(value.shape[0] // 8, 8, value.shape[1])


def place_of(n_seq):
    seq, grp = lax.axis_index("seq"), lax.axis_index("grp")
    z, y = lax.div(seq, 2), lax.rem(seq, 2)
    x, c = lax.div(grp, 2), lax.rem(grp, 2)
    return seq, grp, z, y, x, c


def greet(n_seq, seq, grp, groups):
    barrier = pltpu.get_barrier_semaphore()

    def one(k, carry):
        pl.semaphore_signal(
            barrier, inc=1, device_id={"seq": lax.rem(seq + k, n_seq), "grp": grp}, device_id_type=MESH
        )
        return carry

    lax.fori_loop(1, n_seq, one, 0)
    for k in range(1, groups):
        pl.semaphore_signal(
            barrier, inc=1, device_id={"seq": seq, "grp": lax.rem(grp + k, groups)}, device_id_type=MESH
        )
    pl.semaphore_wait(barrier, n_seq - 1 + groups - 1)


def any_spec():
    return pl.BlockSpec(memory_space=pl.ANY)


def vmem_spec():
    return pl.BlockSpec(memory_space=pltpu.VMEM)


def smem_spec():
    return pl.BlockSpec(memory_space=pltpu.SMEM)


def head_mask():
    row = lax.broadcasted_iota(jnp.int32, (HEADS, 512), 0)
    column = lax.broadcasted_iota(jnp.int32, (HEADS, 512), 1)
    return lax.div(column, 512 // HEADS) == row


def block_diagonal(rows):
    column = lax.div(lax.broadcasted_iota(jnp.int32, rows.shape, 1), 512 // HEADS)
    return jnp.concatenate([jnp.where(column == h, rows, 0.0) for h in range(HEADS)], axis=0)


def same_rows(row):
    return jnp.broadcast_to(row, (8, row.shape[1]))


def pack(vectors):
    pieces = [v[:, 128 * i : 128 * (i + 1)] for v in vectors for i in range(v.shape[1] // 128)]
    spare = -len(pieces) % 8
    if spare:
        pieces.append(jnp.zeros((spare, 128), pieces[0].dtype))
    return jnp.concatenate(pieces, axis=0)


def unpack(rows, place, pieces=4):
    return jnp.concatenate(
        [rows[pieces * place + i : pieces * place + i + 1] for i in range(pieces)], axis=1
    )


def step_kernel(
    n_seq, owners_ref, dil_ref, length_ref, embed_ref, queries_ref, master_hbm, prompt_hbm,
    frames_hbm, cond_hbm, gout_hbm, gskip_hbm,
    block_hbm, skip_hbm, gframes_hbm, out_hbm, low_ref, dquery_ref,
    w, gs, prep, core_in, x_in, fr, fr_in, fx, ff, red_in, one_in, two_in, z_in, fin,
    xe, cat, slopes, gated, x1, bh, bb, sht, condt, gatt, bx, sk, blk,
    master, prompt, probs, left, vec, sums, tall, rt, lt, dq,
    hop_src, hop_in, wide_src, wide_in,
    in_sem, out_sem, hsend, hrecv, send, recv, zsend, zrecv, hop_send, hop_recv,
):
    seq, grp, z, y, x, c = place_of(n_seq)
    nz = n_seq // 2
    rows = prep.shape[1]
    own = frames_hbm.shape[1]
    grid_rows = own + 2 * HALO
    top = HALO + own
    channels = 512
    number = queries_ref.shape[1]
    sib, across, other_y = x * 2 + 1 - c, (1 - x) * 2 + c, z * 2 + 1 - y
    mine, theirs = 2 * c + x, 2 * c + 1 - x

    local_in = [
        pltpu.make_async_copy(a, b, in_sem.at[i])
        for i, (a, b) in enumerate(
            (
                (master_hbm, master),
                (prompt_hbm, prompt),
                (frames_hbm.at[0], xe.at[pl.ds(HALO, own)]),
                (cond_hbm.at[0], cat.at[pl.ds(HALO, own), pl.ds(1536, channels)]),
                (gout_hbm.at[0], bb.at[pl.ds(HALO, own), pl.ds(0, channels)]),
                (gskip_hbm.at[0], bb.at[pl.ds(HALO, own), pl.ds(channels, channels)]),
            )
        )
    ]
    for copy in local_in:
        copy.start()

    greet(n_seq, seq, grp, 4)

    waits = []
    used = [0]

    def remote(src, dst, to_seq, to_grp):
        place = used[0]
        used[0] += 1
        copy = pltpu.make_async_remote_copy(
            src_ref=src,
            dst_ref=dst,
            send_sem=send.at[place],
            recv_sem=recv.at[place],
            device_id={"seq": to_seq, "grp": to_grp},
            device_id_type=MESH,
        )
        copy.start()
        waits.append(copy)
        return copy

    def clear_sends():
        for copy in waits:
            copy.wait_send()
        waits.clear()

    after, before = lax.rem(seq + 1, n_seq), lax.rem(seq + n_seq - 1, n_seq)
    halos = []
    for ref, buffer, column in (
        (frames_hbm, xe, 0),
        (cond_hbm, cat, 1536),
        (gout_hbm, bb, 0),
        (gskip_hbm, bb, channels),
    ):
        for start, at, target in ((own - HALO, 0, after), (0, top, before)):
            place = len(halos)
            copy = pltpu.make_async_remote_copy(
                src_ref=ref.at[0, pl.ds(start, HALO)],
                dst_ref=buffer.at[pl.ds(at, HALO), pl.ds(column, channels)],
                send_sem=hsend.at[place],
                recv_sem=hrecv.at[place],
                device_id={"seq": target, "grp": grp},
                device_id_type=MESH,
            )
            copy.start()
            halos.append(copy)

    slots, flags = [], []
    count = jnp.int32(0)
    for tile in range(TILES):
        flag = (owners_ref[tile] == grp).astype(jnp.int32)
        slots.append(jnp.minimum(count, CAP - 1))
        flags.append(flag.astype(F32))
        count = count + flag

    def rounded(tile):
        return (master[slots[tile]] * flags[tile]).astype(BF)

    def ready(tiles, buffer, table):
        for tile in tiles:
            value = rounded(tile)
            buffer[table[tile, 0]] = value[:, :WIDE]
            buffer[table[tile, 1]] = value[:, WIDE:]

    def merge_start(phase):
        base, blocks = PHASES[phase]
        each = blocks // 4
        return remote(
            prep.at[pl.ds(base + 2 * (1 - c) * each, 2 * each)],
            core_in.at[pl.ds(base // 2, 2 * each)],
            seq, sib,
        )

    def merge_cross(phase, copy):
        base, blocks = PHASES[phase]
        each = blocks // 4
        copy.wait_recv()

        def add(i, carry):
            place = base // 2 + i
            core_in[place] = core_in[place] + prep[base + 2 * c * each + i]
            return carry

        lax.fori_loop(0, 2 * each, add, 0)
        return remote(
            core_in.at[pl.ds(base // 2 + (1 - x) * each, each)],
            x_in.at[pl.ds(base // 4, each)],
            seq, across,
        )

    def view(phase, quarter, source):
        base, blocks = PHASES[phase]
        each = blocks // 4
        return w.at[pl.ds(base + quarter * each, each), source]

    zcopies, legs = {}, {}

    def merge_end(phase, copy):
        base, blocks = PHASES[phase]
        each = blocks // 4
        copy.wait_recv()

        def settle(i, carry):
            w[base + mine * each + i, seq] = (
                core_in[base // 2 + x * each + i] + x_in[base // 4 + i]
            )
            return carry

        lax.fori_loop(0, each, settle, 0)
        ref = view(phase, mine, seq)
        for k in range(1, nz):
            zcopies[phase, k] = remote(ref, ref, lax.rem(z + k, nz) * 2 + y, grp)
        first(phase, 0)

    class Leg:
        pass

    def first(phase, k):
        if k:
            zcopies[phase, k].wait_recv()
        leg = Leg()
        zs = lax.rem(z - k + nz, nz)
        leg.a = 1 - jnp.minimum(lax.div(4 * zs, nz), 1)
        leg.here, leg.there = zs * 2 + y, zs * 2 + 1 - y
        a, b = leg.a, 1 - leg.a
        leg.two = (a * seq + b * other_y, a * across + b * grp)
        ref = view(phase, mine, leg.here)
        leg.f1 = remote(ref, ref, a * other_y + b * seq, a * grp + b * across)
        leg.f2a = remote(ref, ref, *leg.two)
        leg.core = [remote(ref, ref, seq, sib)]
        legs[phase, k] = leg

    def second(phase, k):
        leg = legs[phase, k]
        a, b = leg.a, 1 - leg.a
        leg.f1.wait_recv()
        ref = view(phase, a * mine + b * theirs, a * leg.there + b * leg.here)
        leg.f2b = remote(ref, ref, *leg.two)
        leg.core.append(remote(ref, ref, seq, sib))

    def third(phase, k):
        leg = legs[phase, k]
        a, b = leg.a, 1 - leg.a
        leg.f2a.wait_recv()
        ref = view(phase, a * theirs + b * mine, a * leg.here + b * leg.there)
        leg.core.append(remote(ref, ref, seq, sib))
        leg.f2b.wait_recv()
        ref = view(phase, theirs, leg.there)
        leg.core.append(remote(ref, ref, seq, sib))

    def arrived(phase):
        for k in range(nz):
            for copy in legs[phase, k].core:
                copy.wait_recv()

    def hop_refs(j):
        if j == len(HOP_ROWS) - 1:
            return wide_src, wide_in.at[seq], wide_in
        start = sum(HOP_ROWS[:j])
        spot = pl.ds(start, HOP_ROWS[j])
        return hop_src.at[spot], hop_in.at[seq, spot], hop_in.at[:, spot]

    def hop_copy(j, k):
        src, dst, _ = hop_refs(j)
        return pltpu.make_async_remote_copy(
            src_ref=src,
            dst_ref=dst,
            send_sem=hop_send.at[j, k],
            recv_sem=hop_recv.at[j, k],
            device_id={"seq": lax.rem(seq + k, n_seq), "grp": grp},
            device_id_type=MESH,
        )

    def hop_start(j, value):
        src, dst, _ = hop_refs(j)
        value = value.astype(src.dtype)
        src[...] = value
        dst[...] = value

        def one(k, carry):
            hop_copy(j, k).start()
            return carry

        lax.fori_loop(1, n_seq, one, 0)

    def hop_end(j):
        def one(k, carry):
            hop_copy(j, k).wait()
            return carry

        lax.fori_loop(1, n_seq, one, 0)
        _, _, whole = hop_refs(j)

        def add(i, total):
            return total + whole[i].astype(F32)

        return lax.fori_loop(0, n_seq, add, jnp.zeros((HOP_ROWS[j], 128), F32))

    position = lax.broadcasted_iota(jnp.int32, (channels, rows), 0)
    column = lax.broadcasted_iota(jnp.int32, (channels, rows), 1)
    chosen = jnp.where(position == column + seq * rows, 1.0, 0.0).astype(BF)

    def pick(v):
        return mm_fine(v, chosen)

    def spot_in(p):
        return mm_nt_fine(p, chosen)

    def film_block(layer, place):
        return ff[FILM * layer + place]

    def film_rows(layer, v, places):
        return jnp.concatenate([mm_fine(v, film_block(layer, i)) for i in places], axis=1)

    def film_back(layer, v, places):
        total = None
        for i, place in enumerate(places):
            term = mm_nt_fine(v[:, i * WIDE : (i + 1) * WIDE], film_block(layer, place))
            total = term if total is None else total + term
        return spot_in(total)

    def key_blocks(layer):
        return [w[2 * layer + side].reshape(channels, WIDE) for side in range(2)]

    mask = head_mask()

    def attention(layer):
        spread = block_diagonal(queries_ref[layer])
        probe = mm_nt_pairs(spread, key_blocks(layer))
        pr = prompt[...]
        scores = mm_nt_fine(probe, pr) * 0.125
        live = lax.broadcasted_iota(jnp.int32, scores.shape, 1) < length_ref[0]
        scores = jnp.where(live, scores, NEGATIVE)
        weight = jnp.exp(scores - jnp.max(scores, axis=1, keepdims=True))
        value = weight / jnp.sum(weight, axis=1, keepdims=True)
        probs[layer] = value
        mean = jnp.concatenate(
            [
                jnp.mean(value[h * number : (h + 1) * number], axis=0, keepdims=True)
                for h in range(HEADS)
            ],
            axis=0,
        )
        seen = mm_fine(mean, pr)
        left[layer, 0:8] = seen
        return seen

    def wblock(layer, place):
        return w[KEYS + MAIN * layer + place].reshape(channels, WIDE)

    def inside(low, count):
        row = lax.broadcasted_iota(jnp.int32, (count, 1), 0) + (low - HALO) + seq * own
        return (row >= 0) & (row < n_seq * own)

    def windows_forward(layer):
        low = 16 * layer
        high = grid_rows - low
        scale, shift = 1.0 + vec[layer, 0:1], vec[layer, 1:2]
        here = xe[...].astype(F32) if layer == 0 else x1[...]
        shifted = (here * scale + shift).astype(BF).astype(F32)
        shifted = jnp.where(inside(0, grid_rows), shifted, 0.0)
        groups = grid_rows // 8
        bh[0, :, 0:channels] = jnp.zeros((8, channels), F32)
        bh[1 : 1 + groups, :, 0:channels] = in_eights(shifted)
        bh[1 + groups :, :, 0:channels] = jnp.zeros((3, 8, channels), F32)
        sht[layer] = jnp.transpose(shifted[HALO:top]).astype(BF)
        for tap in range(3):
            start = 8 + low + (tap - 1) * dil_ref[layer]
            cat[low:high, tap * channels : (tap + 1) * channels] = window(
                bh, start, high - low, channels
            ).astype(BF)

    def gates(layer, first_row, rows_now):
        spot = slice(first_row, first_row + rows_now)
        value = cat[spot, 0:2048]
        for part in range(2):
            columns = slice(part * WIDE, (part + 1) * WIDE)
            base = KEYS + MAIN * layer + 5 * part
            lhs = mm(value, w[base : base + 4].reshape(2048, WIDE))
            tangent = jnp.tanh(lhs + vec[layer, 2:3, columns])
            rhs = mm(value, w[base + 10 : base + 14].reshape(2048, WIDE))
            opening = jax.nn.sigmoid(rhs + vec[layer, 3:4, columns])
            gate = tangent * opening
            gated[spot, columns] = gate.astype(BF)
            slopes[layer, spot, columns] = (opening * (1.0 - tangent * tangent)).astype(BF)
            other = slice(channels + part * WIDE, channels + (part + 1) * WIDE)
            slopes[layer, spot, other] = (gate * (1.0 - opening)).astype(BF)

    def residual(layer, first_row, rows_now):
        value = gated[first_row : first_row + rows_now]
        for part in range(2):
            columns = slice(part * WIDE, (part + 1) * WIDE)
            term = mm(value, wblock(layer, 5 * part + 4))
            if layer == 0:
                base = xe[first_row : first_row + rows_now, columns].astype(F32)
                x1[first_row : first_row + rows_now, columns] = (base + term) * HALF_ROOT
            else:
                base = x1[first_row : first_row + rows_now, columns]
                blk[first_row - HALO : first_row - HALO + rows_now, columns] = (
                    base + term
                ) * HALF_ROOT

    def skipped(layer, first_row, rows_now):
        value = gated[first_row : first_row + rows_now]
        spot = slice(first_row - HALO, first_row - HALO + rows_now)
        for part in range(2):
            columns = slice(part * WIDE, (part + 1) * WIDE)
            term = mm(value, wblock(layer, 5 * part + 14))
            if layer == 0:
                sk[spot, columns] = term
            else:
                sk[spot, columns] = sk[spot, columns] + term

    low, high = 16, grid_rows - 16

    def gate_grads(layer, first_row, rows_now):
        spot = slice(first_row, first_row + rows_now)
        bb[spot, 0:channels] = (bx[spot] * HALF_ROOT).astype(BF)
        branch = jnp.concatenate([wblock(layer, 5 * part + 4) for part in range(4)], axis=1)
        back = mm_nt(bb[spot], branch)
        keep = inside(first_row, rows_now)
        place = slice(1 + first_row // 8, 1 + (first_row + rows_now) // 8)
        for side in range(2):
            columns = slice(side * channels, (side + 1) * channels)
            value = (back * slopes[layer, spot, columns].astype(F32)).astype(BF).astype(F32)
            bh[place, :, columns] = in_eights(jnp.where(keep, value, 0.0))

    def windows_backward(layer):
        total = bh[1 + HALO // 8 : 1 + top // 8].reshape(own, 2 * channels)
        total = jnp.sum(total, axis=0, keepdims=True)
        sums[layer, 2:3] = total[:, 0:channels]
        sums[layer, 3:4] = total[:, channels:]
        reach, limit = (low, high) if layer else (HALO, top)
        for tap in range(3):
            start = 8 + reach - (tap - 1) * dil_ref[layer]
            cat[reach:limit, tap * 1024 : (tap + 1) * 1024] = window(
                bh, start, limit - reach, 1024
            ).astype(BF)

    def frame_grads(layer, first_row, rows_now):
        spot = slice(first_row, first_row + rows_now)
        taps = jnp.concatenate(
            [wblock(layer, 5 * part + tap) for tap in range(3) for part in range(4)], axis=1
        )
        back = mm_nt(cat[spot], taps)
        if layer:
            here = x1[spot]
            row = lax.broadcasted_iota(jnp.int32, (rows_now, 1), 0) + first_row
            kept = jnp.where((row >= HALO) & (row < top), back, 0.0)
        else:
            here = xe[spot].astype(F32)
            kept = back
        sums[layer, 0:1] += jnp.sum(kept * here, axis=0, keepdims=True)
        sums[layer, 1:2] += jnp.sum(kept, axis=0, keepdims=True)
        bx[spot] = bx[spot] * HALF_ROOT + back * (1.0 + vec[layer, 0:1])

    def weight_grad(layer, part, i):
        if i < 4:
            tap = i if i < 3 else 1
            start = pl.multiple_of(tap * 1024 + part * WIDE, WIDE)
            lhs = sht[layer] if i < 3 else condt[...]
            return mm(lhs, cat[HALO:top, pl.ds(start, WIDE)])
        start = pl.multiple_of(part * WIDE, WIDE)
        return mm(gatt[layer], bb[HALO:top, pl.ds(start, WIDE)])

    core_sent = {}

    def give(layer, xx):
        part = 2 * (1 - c) + xx
        buffer, base = (gs, 0) if layer else (w, KEYS + MAIN)
        for i in range(5):
            value = weight_grad(layer, part, i).astype(BF)
            buffer[base + 5 * xx + i] = value.reshape(n_seq, rows, WIDE)
        core_sent[layer, xx] = remote(
            buffer.at[pl.ds(base + 5 * xx, 5)], red_in.at[layer, pl.ds(5 * xx, 5)], seq, sib
        )

    def keep(layer, xx):
        part = 2 * c + xx
        core_sent[layer, xx].wait_recv()
        for i in range(5):
            value = weight_grad(layer, part, i).reshape(n_seq, rows, WIDE)
            spot = 5 * xx + i
            red_in[layer, spot] = (red_in[layer, spot].astype(F32) + value).astype(BF)

    ones, twos, zs, targets = {}, {}, {}, {}
    for k in range(nz):
        zd = lax.rem(z + k, nz)
        targets[k] = (zd, 1 - jnp.minimum(lax.div(4 * zd, nz), 1))

    def red_one(layer, k):
        zd, a = targets[k]
        b = 1 - a
        ones[layer, k] = []
        for j in range(2):
            xi, yi = a * (1 - x) + b * j, a * j + b * (1 - y)
            ones[layer, k].append(
                remote(
                    red_in.at[layer, pl.ds(5 * xi, 5), 2 * zd + yi],
                    one_in.at[layer, k, j],
                    a * seq + b * other_y, a * across + b * grp,
                )
            )

    def red_two(layer, k):
        zd, a = targets[k]
        b = 1 - a
        you = a * y + b * x
        for j in range(2):
            ones[layer, k][j].wait_recv()
            xi, yi = a * x + b * j, a * j + b * y

            def body(i, carry, j=j, xi=xi, yi=yi):
                one_in[layer, k, j, i] = (
                    one_in[layer, k, j, i].astype(F32)
                    + red_in[layer, 5 * xi + i, 2 * zd + yi].astype(F32)
                ).astype(BF)
                return carry

            lax.fori_loop(0, 5, body, 0)
        twos[layer, k] = remote(
            one_in.at[layer, k, 1 - you], two_in.at[layer, k],
            a * other_y + b * seq, a * grp + b * across,
        )

    def red_three(layer, k):
        zd, a = targets[k]
        you = a * y + (1 - a) * x
        twos[layer, k].wait_recv()

        def body(i, carry):
            two_in[layer, k, i] = (
                two_in[layer, k, i].astype(F32) + one_in[layer, k, you, i].astype(F32)
            ).astype(BF)
            return carry

        lax.fori_loop(0, 5, body, 0)
        if k:
            zs[layer, k] = remote(two_in.at[layer, k], z_in.at[layer, k], zd * 2 + y, grp)

    lasts = {}
    outs = []

    def local_out(src, dst):
        copy = pltpu.make_async_copy(src, dst, out_sem.at[len(outs)])
        copy.start()
        outs.append(copy)

    def red_four(layer):
        for k in range(1, nz):
            zs[layer, k].wait_recv()

        def body(i, carry):
            total = two_in[layer, 0, i].astype(F32)
            for k in range(1, nz):
                total = total + z_in[layer, k, i].astype(F32)
            fin[layer, i] = total.astype(BF)
            return carry

        lax.fori_loop(0, 5, body, 0)
        src, dst = fin.at[layer], out_hbm.at[layer, mine]
        lasts[layer] = [remote(src, dst, seq, across), remote(src, dst, seq, sib)]
        local_out(src, dst)

    def red_five(layer):
        lasts[layer][0].wait_recv()
        ref = out_hbm.at[layer, theirs]
        lasts[layer].append(remote(ref, ref, seq, sib))

    local_in[0].wait()
    merges = []
    ready([PER_LAYER * layer + 10 for layer in range(LAYERS)], prep, BLOCK_OF)
    merges.append(merge_start(0))
    for layer in range(LAYERS):
        ready([PER_LAYER * layer + t for t in FILM_ORDER], fr, FILM_OF)
    film_core = remote(fr, fr_in, seq, sib)
    main_tiles = (0, 1, 2, 3, 4, 5, 6, 7, 15, 16)
    for layer in range(LAYERS):
        ready([PER_LAYER * layer + t for t in main_tiles], prep, BLOCK_OF)
        merges.append(merge_start(1 + layer))
    crosses = [merge_cross(0, merges[0])]
    film_core.wait_recv()
    fr_in[...] = fr_in[...] + fr[...]
    half = fr.shape[0] // 2
    spot = pl.ds(c * half, half)
    film_cross = remote(fr_in.at[spot], fx, seq, across)
    crosses.append(merge_cross(1, merges[1]))
    merge_end(0, crosses[0])
    crosses.append(merge_cross(2, merges[2]))
    merge_end(1, crosses[1])
    film_cross.wait_recv()
    ff[spot] = fr_in[spot] + fx[...]
    film_last = remote(ff.at[spot], ff.at[spot], seq, sib)
    for k in range(1, nz):
        first(0, k)
    merge_end(2, crosses[2])
    for k in range(nz):
        second(0, k)
    for k in range(1, nz):
        first(1, k)
    for k in range(nz):
        third(0, k)
    local_in[1].wait()
    local_in[3].wait()
    condt[...] = jnp.transpose(cat[HALO:top, 1536:2048].astype(F32)).astype(BF)
    film_last.wait_recv()
    arrived(0)
    embed = same_rows(embed_ref[...].astype(F32))
    seen = [attention(0)]
    for k in range(nz // 2):
        second(1, k)
    seen.append(attention(1))
    vectors = []
    for layer in range(LAYERS):
        mixed = film_rows(layer, pick(seen[layer]), (0, 1))
        vectors.append(jnp.sum(jnp.where(mask, mixed, 0.0), axis=0, keepdims=True))
        steps = film_rows(layer, pick(embed), (8, 9, 10, 11))
        vectors += [steps[0:1, :channels], steps[0:1, channels:]]
    hop_start(0, pack(vectors))
    for k in range(nz // 2, nz):
        second(1, k)
    total = hop_end(0)
    mixed = [unpack(total, 3 * layer) for layer in range(LAYERS)]
    for layer in range(LAYERS):
        vec[layer, 2:3] = unpack(total, 3 * layer + 1)
        vec[layer, 3:4] = unpack(total, 3 * layer + 2)
    hop_start(
        1,
        pack([film_rows(l, pick(same_rows(mixed[l])), (2, 3))[0:1] for l in range(LAYERS)]),
    )
    for k in range(1, nz):
        first(2, k)
    for k in range(nz // 2):
        third(1, k)
    total = hop_end(1)
    pooled = [unpack(total, layer) for layer in range(LAYERS)]
    vectors = []
    for layer in range(LAYERS):
        film = film_rows(layer, pick(same_rows(pooled[layer])), (4, 5, 6, 7))
        vectors += [film[0:1, :channels], film[0:1, channels:]]
        left[layer, 8:9] = mixed[layer]
        left[layer, 9:10] = pooled[layer]
        left[layer, 10:11] = embed[0:1]
        left[layer, 11:16] = jnp.zeros((5, channels), F32)
    hop_start(2, pack(vectors))
    for k in range(nz // 2, nz):
        third(1, k)
    total = hop_end(2)
    for layer in range(LAYERS):
        vec[layer, 0:1] = unpack(total, 2 * layer)
        vec[layer, 1:2] = unpack(total, 2 * layer + 1)
    local_in[2].wait()
    for copy in halos[:4]:
        copy.wait_recv()
    windows_forward(0)
    for k in range(nz // 2):
        second(2, k)
    arrived(1)
    size = grid_rows // 2
    gates(0, 0, size)
    for k in range(nz // 2, nz):
        second(2, k)
    gates(0, size, size)
    for k in range(nz // 2):
        third(2, k)
    residual(0, 0, size)
    residual(0, size, size)
    for k in range(nz // 2, nz):
        third(2, k)
    part_own = own // 2
    for start in (HALO, HALO + part_own):
        skipped(0, start, part_own)
    gatt[0] = jnp.transpose(gated[HALO:top].astype(F32)).astype(BF)
    windows_forward(1)
    local_in[4].wait()
    local_in[5].wait()
    for copy in halos[4:]:
        copy.wait_recv()
    for copy in halos:
        copy.wait_send()
    bx[...] = bb[:, 0:channels].astype(F32)
    arrived(2)
    size = (high - low) // 2
    gates(1, low, size)
    gates(1, low + size, size)
    edge = 1 + low // 8
    bh[0:edge] = jnp.zeros((edge, 8, 1024), F32)
    bh[1 + high // 8 :] = jnp.zeros((edge + 2, 8, 1024), F32)
    sums[...] = jnp.zeros_like(sums)
    gate_grads(1, low, size)
    gate_grads(1, low + size, size)
    gatt[1] = jnp.transpose(gated[HALO:top].astype(F32)).astype(BF)
    windows_backward(1)
    give(1, 0)
    give(1, 1)
    frame_grads(1, low, size)
    keep(1, 0)
    keep(1, 1)
    for k in reversed(range(nz)):
        red_one(1, k)
    clear_sends_early = list(waits)
    frame_grads(1, low + size, size)
    for start in (HALO, HALO + part_own):
        residual(1, start, part_own)
        skipped(1, start, part_own)
    local_out(blk, block_hbm.at[0])
    local_out(sk, skip_hbm.at[0])
    gate_grads(0, low, size)
    red_two(1, nz - 1)
    gate_grads(0, low + size, size)
    windows_backward(0)
    for k in reversed(range(nz // 2, nz - 1)):
        red_two(1, k)
    for copy in clear_sends_early:
        copy.wait_send()
        waits.remove(copy)
    give(0, 0)
    give(0, 1)
    for k in reversed(range(nz // 2)):
        red_two(1, k)
    keep(0, 0)
    keep(0, 1)
    for k in reversed(range(nz)):
        red_one(0, k)
    for start in (HALO, HALO + part_own):
        frame_grads(0, start, part_own)
    local_out(bx.at[pl.ds(HALO, own)], gframes_hbm.at[0])
    hop_start(3, pack([sums[l, i : i + 1] for l in range(LAYERS) for i in range(4)]))
    for k in reversed(range(nz)):
        red_three(1, k)
    total = hop_end(3)
    sides = [[unpack(total, 4 * l + i) for i in range(4)] for l in range(LAYERS)]
    vectors = []
    for layer in range(LAYERS):
        dfilm = same_rows(jnp.concatenate(sides[layer][0:2], axis=1))
        vectors.append(film_back(layer, dfilm, (4, 5, 6, 7))[0:1])
    hop_start(4, pack(vectors))
    red_two(0, nz - 1)
    total = hop_end(4)
    dpooled = [unpack(total, layer) for layer in range(LAYERS)]
    hop_start(
        5, pack([film_back(l, same_rows(dpooled[l]), (2, 3))[0:1] for l in range(LAYERS)])
    )
    red_four(1)
    total = hop_end(5)
    dmixed = [unpack(total, layer) for layer in range(LAYERS)]
    vectors = []
    for layer in range(LAYERS):
        dseen = film_back(layer, jnp.where(mask, dmixed[layer], 0.0), (0, 1))
        vectors += [dseen[h : h + 1] for h in range(HEADS)]
    hop_start(6, pack(vectors))
    for k in reversed(range(nz // 2, nz - 1)):
        red_two(0, k)
    red_three(0, nz - 1)
    total = hop_end(6)
    pr = prompt[...]
    bundles = []
    for layer in range(LAYERS):
        dseen = jnp.concatenate(
            [unpack(total, HEADS * layer + h) for h in range(HEADS)], axis=0
        )
        dmean = mm_nt_fine(dseen, pr) * (1.0 / number)
        dprobs = jnp.concatenate(
            [jnp.broadcast_to(dmean[h : h + 1], (number, channels)) for h in range(HEADS)], axis=0
        )
        value = probs[layer]
        inner = jnp.sum(dprobs * value, axis=1, keepdims=True)
        dprobe = mm_fine(value * (dprobs - inner) * 0.125, pr)
        keys = key_blocks(layer)
        dspread = jnp.concatenate([mm_fine(dprobe, keys[0]), mm_fine(dprobe, keys[1])], axis=1)
        head = lax.div(lax.broadcasted_iota(jnp.int32, (number, channels), 1), channels // HEADS)
        dquery = jnp.zeros((number, channels), F32)
        for h in range(HEADS):
            dquery = dquery + jnp.where(head == h, dspread[h * number : (h + 1) * number], 0.0)
        dq[grp, layer] = dquery.astype(BF)
        tall[:, 0:256] = jnp.transpose(dprobe)
        lefts = jnp.concatenate([left[layer], jnp.zeros((112, channels), F32)], axis=0)
        tall[:, 256:384] = jnp.transpose(lefts)
        start = pl.multiple_of(seq * rows, rows)
        lt[grp, layer] = tall[pl.ds(start, rows), :].astype(BF)
        rt[grp, layer] = jnp.concatenate(
            sides[layer] + [dpooled[layer], dmixed[layer], jnp.zeros((2, channels), F32)], axis=0
        )
        if layer == 0:
            for k in reversed(range(nz // 2)):
                red_two(0, k)
    for k in range(1, 4):
        for ref in (rt, lt, dq):
            bundles.append(remote(ref.at[grp], ref.at[grp], seq, lax.rem(grp + k, 4)))
    for k in reversed(range(nz // 2, nz - 1)):
        red_three(0, k)
    red_five(1)
    for k in reversed(range(nz // 2)):
        red_three(0, k)
    for copy in bundles:
        copy.wait_recv()
    total = dq[0].astype(F32)
    for k in range(1, 4):
        total = total + dq[k].astype(F32)
    dquery_ref[...] = total
    at = lax.broadcasted_iota(jnp.int32, (16, channels), 0)
    for layer in range(LAYERS):
        spread = block_diagonal(queries_ref[layer]).astype(BF)
        probe = lt[0, layer, :, 0:256].astype(F32)
        for k in range(1, 4):
            probe = probe + lt[k, layer, :, 0:256].astype(F32)
        low_ref[layer, 0] = mm(probe.astype(BF), spread).astype(BF)
        total = None
        for k in range(4):
            right = rt[k, layer]
            value = jnp.concatenate(
                [jnp.where(mask, right[5:6], 0.0), jnp.zeros((8, channels), F32)], axis=0
            )
            pieces = [value] + [
                jnp.where(at == row, right[i : i + 1], 0.0)
                for i, row in ((4, 8), (0, 9), (1, 9), (2, 10), (3, 10))
            ]
            side = jnp.concatenate(pieces, axis=1).astype(BF)
            term = mm(lt[k, layer, :, 256:272], side)
            total = term if total is None else total + term
        for i in range(6):
            low_ref[layer, 1 + i] = total[:, i * channels : (i + 1) * channels].astype(BF)
    red_four(0)
    red_five(0)
    for copies in lasts.values():
        copies[1].wait_recv()
        copies[2].wait_recv()
    for copy in outs:
        copy.wait()
    clear_sends()


def train_step(
    n_seq, owners, dilations, length, step_embed, queries, master, prompt,
    frames_in, cond_frames, grad_out, grad_skip,
):
    _, own, channels = frames_in.shape
    rows = master.shape[1]
    number = queries.shape[1]
    grid_rows = own + 2 * HALO
    nz = n_seq // 2
    v = pltpu.VMEM
    dma = pltpu.SemaphoreType.DMA
    frame_out = jax.ShapeDtypeStruct((1, own, channels), F32)
    film = FILM * LAYERS
    copies = 24 + 32 * nz
    return pl.pallas_call(
        functools.partial(step_kernel, n_seq),
        out_shape=(
            frame_out,
            frame_out,
            frame_out,
            jax.ShapeDtypeStruct((LAYERS, 4, 5, rows, WIDE), BF),
            jax.ShapeDtypeStruct((LAYERS, LOW_RANK, rows, channels), BF),
            jax.ShapeDtypeStruct((LAYERS, number, channels), F32),
        ),
        in_specs=[smem_spec()] * 3 + [vmem_spec()] * 2 + [any_spec()] * 6,
        out_specs=(any_spec(),) * 4 + (vmem_spec(),) * 2,
        scratch_shapes=[
            v((BLOCKS, n_seq, rows, WIDE), BF),
            v((10, n_seq, rows, WIDE), BF),
            v((BLOCKS, rows, WIDE), BF),
            v((BLOCKS // 2, rows, WIDE), BF),
            v((BLOCKS // 4, rows, WIDE), BF),
            v((film, rows, WIDE), BF),
            v((film, rows, WIDE), BF),
            v((film // 2, rows, WIDE), BF),
            v((film, rows, WIDE), BF),
            v((LAYERS, 10, n_seq, rows, WIDE), BF),
            v((LAYERS, nz, 2, 5, rows, WIDE), BF),
            v((LAYERS, nz, 5, rows, WIDE), BF),
            v((LAYERS, nz, 5, rows, WIDE), BF),
            v((LAYERS, 5, rows, WIDE), BF),
            v((grid_rows, channels), BF),
            v((grid_rows, 6 * channels), BF),
            v((LAYERS, grid_rows, 2 * channels), BF),
            v((grid_rows, channels), BF),
            v((grid_rows, channels), F32),
            v((grid_rows // 8 + 4, 8, 2 * channels), F32),
            v((grid_rows, 2 * channels), BF),
            v((LAYERS, channels, own), BF),
            v((channels, own), BF),
            v((LAYERS, channels, own), BF),
            v((grid_rows, channels), F32),
            v((own, channels), F32),
            v((own, channels), F32),
            v(master.shape, F32),
            v(prompt.shape, BF),
            v((LAYERS, HEADS * number, prompt.shape[0]), F32),
            v((LAYERS, 16, channels), F32),
            v((LAYERS, 8, channels), F32),
            v((LAYERS, 8, channels), F32),
            v((channels, 384), F32),
            v((4, LAYERS, 8, channels), F32),
            v((4, LAYERS, rows, 384), BF),
            v((4, LAYERS, number, channels), BF),
            v((sum(HOP_ROWS[:-1]), 128), F32),
            v((n_seq, sum(HOP_ROWS[:-1]), 128), F32),
            v((HOP_ROWS[-1], 128), BF),
            v((n_seq, HOP_ROWS[-1], 128), BF),
            dma((6,)),
            dma((8,)),
            dma((8,)),
            dma((8,)),
            dma((copies,)),
            dma((copies,)),
            dma((1,)),
            dma((1,)),
            dma((len(HOP_ROWS), n_seq)),
            dma((len(HOP_ROWS), n_seq)),
        ],
        compiler_params=pltpu.CompilerParams(
            collective_id=0, has_side_effects=True, vmem_limit_bytes=MEM
        ),
        name="train_step",
    )(
        owners, dilations, length, step_embed, queries, master, prompt,
        frames_in, cond_frames, grad_out, grad_skip,
    )


def adam_update(weight, moment_one, moment_two, gradient, step_rate):
    moment_one = BETA_ONE * moment_one + (1.0 - BETA_ONE) * gradient
    moment_two = BETA_TWO * moment_two + (1.0 - BETA_TWO) * gradient * gradient
    normal = (
        moment_one
        / (1.0 - BETA_ONE**STEP)
        / (jnp.sqrt(moment_two / (1.0 - BETA_TWO**STEP)) + EPSILON)
    )
    return (moment_one, moment_two, weight - step_rate * (normal + WEIGHT_DECAY * weight))


def update_kernel(
    owners_ref, master_ref, first_ref, second_ref, grad_ref, low_ref,
    queries_ref, qfirst_ref, qsecond_ref, dq_ref, block_in, skip_in, gframes_in,
    nfirst_ref, nsecond_ref, nmaster_ref, ncopy_ref, nqfirst_ref, nqsecond_ref, nqueries_ref,
    block_out, skip_out, gframes_out,
    tile_of, sem,
):
    step = pl.program_id(0)
    grp = lax.axis_index("grp")
    passed = [
        pltpu.make_async_copy(a, b, sem.at[i])
        for i, (a, b) in enumerate(
            ((block_in, block_out), (skip_in, skip_out), (gframes_in, gframes_out))
        )
    ]

    @pl.when(step == 0)
    def _():
        for copy in passed:
            copy.start()
        for slot in range(CAP + 1):
            tile_of[slot] = TILES
        count = jnp.int32(0)
        for tile in range(TILES):
            own = owners_ref[tile] == grp

            @pl.when(own)
            def _(count=count, tile=tile):
                tile_of[jnp.minimum(count, CAP)] = tile

            count = count + own.astype(jnp.int32)
        one, two, three = adam_update(
            queries_ref[...], qfirst_ref[...], qsecond_ref[...], dq_ref[...], QUERY_RATE
        )
        nqfirst_ref[...] = one
        nqsecond_ref[...] = two
        nqueries_ref[...] = three

    tile = tile_of[step]
    in_use = tile < TILES
    tile = jnp.minimum(tile, TILES - 1)
    layer, kind = lax.div(tile, PER_LAYER), lax.rem(tile, PER_LAYER)
    pair = lax.rem(kind, 2) * (kind < 8) + (kind == 16)
    tap = jnp.where(kind < 8, lax.div(kind, 2), 4)
    block = 10 * pair + tap
    full = jnp.concatenate(
        [
            grad_ref[layer, lax.div(block, 5), lax.rem(block, 5)],
            grad_ref[layer, lax.div(block, 5) + 1, lax.rem(block, 5)],
        ],
        axis=1,
    )
    place = jnp.where(kind < 10, kind - 3, kind - 10)
    place = jnp.clip(place, 0, LOW_RANK - 1)
    thin = low_ref[layer, place]
    is_thin = ((kind >= 8) & (kind <= 14)).astype(jnp.int32)
    gradient = jnp.where(
        jnp.broadcast_to(is_thin, full.shape) > 0, thin.astype(F32), full.astype(F32)
    )
    master, first, second = master_ref[0], first_ref[0], second_ref[0]
    one, two, three = adam_update(master, first, second, gradient, LEARN_RATE)
    keep = jnp.broadcast_to(in_use.astype(jnp.int32), master.shape) > 0
    three = jnp.where(keep, three, master)
    nfirst_ref[0] = jnp.where(keep, one, first)
    nsecond_ref[0] = jnp.where(keep, two, second)
    nmaster_ref[0] = three
    ncopy_ref[0] = three.astype(BF)

    @pl.when(step == pl.num_programs(0) - 1)
    def _():
        for copy in passed:
            copy.wait()


def update(owners, master, first, second, grads, low, queries, qfirst, qsecond, dq, *frames):
    _, rows, channels = master.shape
    slot = pl.BlockSpec((1, rows, channels), lambda i: (i, 0, 0))
    whole = vmem_spec()
    query = jax.ShapeDtypeStruct(queries.shape, F32)
    full = jax.ShapeDtypeStruct(master.shape, F32)
    passed = jax.ShapeDtypeStruct(frames[0].shape, F32)
    return pl.pallas_call(
        update_kernel,
        grid=(CAP,),
        out_shape=(full, full, full, jax.ShapeDtypeStruct(master.shape, BF), query, query, query)
        + (passed,) * 3,
        in_specs=[smem_spec(), slot, slot, slot] + [whole] * 6 + [any_spec()] * 3,
        out_specs=(slot, slot, slot, slot, whole, whole, whole) + (any_spec(),) * 3,
        scratch_shapes=[pltpu.SMEM((CAP + 1,), jnp.int32), pltpu.SemaphoreType.DMA((3,))],
        compiler_params=pltpu.CompilerParams(vmem_limit_bytes=MEM),
        name="update",
    )(owners, master, first, second, grads, low, queries, qfirst, qsecond, dq, *frames)


def on_device(
    n_seq,
    frames_in,
    cond_frames,
    step_embed,
    prompts,
    prompt_lengths,
    pairing,
    dilations,
    owners,
    master,
    first_moment,
    second_moment,
    queries,
    query_first,
    query_second,
    grad_out,
    grad_skip,
):
    prompt = lax.dynamic_index_in_dim(prompts, pairing[0], 0, keepdims=False)
    length = lax.dynamic_index_in_dim(prompt_lengths, pairing[0], 0, keepdims=True)
    block, skip, gframes, own_grads, low, dq = train_step(
        n_seq, owners, dilations, length, step_embed, queries, master, prompt,
        frames_in, cond_frames, grad_out, grad_skip,
    )
    (
        new_first, new_second, new_master, new_copy, nqf, nqs, nq,
        block_out, skip_out, grad_frames,
    ) = update(
        owners, master, first_moment, second_moment, own_grads, low,
        queries, query_first, query_second, dq, block, skip, gframes,
    )
    return (
        new_first, new_second, new_master, new_copy, nqf, nqs, nq,
        block_out, skip_out, grad_frames,
    )


def solution(mesh):
    shard = P("grp", "seq", None)
    placed = (
        shard, shard, P("grp", None), P(), P(), P("grp"), P(), P(),
        shard, shard, shard, P(), P(), P(), shard, shard,
    )
    return jax.shard_map(
        functools.partial(on_device, mesh.shape["seq"]),
        mesh=mesh,
        in_specs=placed,
        out_specs=(shard, shard, shard, shard, P(), P(), P(), shard, shard, shard),
        check_vma=False,
    )
```

```python
import functools

import jax
import jax.numpy as jnp
from jax import lax
from jax.experimental import pallas as pl
from jax.experimental.pallas import tpu as pltpu
from jax.sharding import PartitionSpec as P

HEADS = 8
LAYERS = 2
DMAX = 8
CAP = 13
STEP = 10
PER_LAYER = 17
TILES = PER_LAYER * LAYERS

BETA_ONE = 0.9
BETA_TWO = 0.999
EPSILON = 1e-08
WEIGHT_DECAY = 0.01
LEARN_RATE = 0.02
QUERY_RATE = 0.4
HALF_ROOT = 0.7071067811865476
NEGATIVE = -1e30

BF = jnp.bfloat16
F32 = jnp.float32
HALO = 32
WIDE = 256
KEYS = 2 * LAYERS
MAIN = 20
BLOCKS = KEYS + MAIN * LAYERS
PHASES = ((0, KEYS), (KEYS, MAIN), (KEYS + MAIN, MAIN))
FILM_ORDER = (11, 12, 13, 14, 8, 9)
FILM = 2 * len(FILM_ORDER)
LOW_RANK = 1 + len(FILM_ORDER)
HOP_ROWS = (24, 8, 16, 32, 8, 8, 64)
IN_SPLIT = (2, 2, 2)
OUT_SPLIT = (2, 2)
ORDER = (
    ("prep", 0), ("prep", 1), "fc", ("prep", 2), ("cross", 0), ("cross", 1), ("end", 0),
    ("zs", 0), ("end", 1), ("zs", 1), ("cross", 2), ("first", 0, 1), ("first", 0, 2),
    ("first", 0, 3), "fx", ("second", 0, 2), ("second", 0, 0), ("second", 0, 1), ("second", 0, 3),
    ("third", 0, 1), ("first", 1, 2), "condt", ("first", 1, 1), ("first", 1, 3), "fl", ("end", 2),
    ("third", 0, 0), ("zs", 2), ("third", 0, 2), ("third", 0, 3), ("second", 1, 2),
    ("second", 1, 0), "att0", ("second", 1, 1), "att1", ("second", 1, 3), "hsA", ("first", 2, 1),
    ("first", 2, 2), ("first", 2, 3), ("third", 1, 0), ("third", 1, 1), "heA", "hsB",
    ("third", 1, 2), ("second", 2, 2), ("third", 1, 3), "heB", "hsC", ("second", 2, 0),
    ("second", 2, 1), ("second", 2, 3), "heC", "win0", "gates0a", ("third", 2, 0),
    ("third", 2, 1), ("third", 2, 2), ("third", 2, 3), "gates0b", "res0a", "res0b", "skip0",
    "gatt0", "win1", "gates1a", "gates1b", "gg1a", "gg1b", "gatt1", "winb1", ("give", 1, 0),
    ("give", 1, 1), "fg1a", "fg1b", ("keep", 1, 0), ("keep", 1, 1), ("one", 1, 3), ("one", 1, 2),
    "out1", ("one", 1, 0), ("one", 1, 1), "gg0a", "gg0b", "winb0", ("give", 0, 1), "fg0a",
    ("two", 1, 3), ("two", 1, 2), ("give", 0, 0), "fg0b", ("two", 1, 1), ("two", 1, 0), "hs3",
    ("keep", 0, 0), ("keep", 0, 1), ("three", 1, 3), ("one", 0, 3), ("one", 0, 1),
    ("three", 1, 1), ("one", 0, 0), "he3", ("three", 1, 2), "hs4", ("one", 0, 2), ("three", 1, 0),
    "he4", ("two", 0, 3), "hs5", ("two", 0, 2), ("two", 0, 1), "he5", "hs6", ("three", 0, 1),
    ("four", 1), ("three", 0, 2), ("two", 0, 0), ("three", 0, 3), "he6", "fb1", "fb0", "bundle",
    ("three", 0, 0), ("five", 1), ("four", 0), "low", "end",
)

MEM = 64 * 1024 * 1024 - 256 * 1024
MESH = pl.DeviceIdType.MESH


def block_table():
    table = {}
    for layer in range(LAYERS):
        base = PER_LAYER * layer
        for side in range(2):
            table[base + 10, side] = 2 * layer + side
        start = KEYS + MAIN * layer
        for part in range(4):
            for tap in range(4):
                table[base + 2 * tap + part // 2, part % 2] = start + 5 * part + tap
            table[base + 15 + part // 2, part % 2] = start + 5 * part + 4
    return table


BLOCK_OF = block_table()
FILM_OF = {
    (PER_LAYER * layer + tile, side): FILM * layer + 2 * place + side
    for layer in range(LAYERS)
    for place, tile in enumerate(FILM_ORDER)
    for side in range(2)
}


def mm(a, b):
    return lax.dot_general(a, b, (((1,), (0,)), ((), ())), preferred_element_type=F32)


def mm_nt(a, b):
    return lax.dot_general(a, b, (((1,), (1,)), ((), ())), preferred_element_type=F32)


def split(a):
    high = a.astype(BF)
    return high, (a - high.astype(F32)).astype(BF)


def mm_fine(a, b):
    high, low = split(a)
    return mm(high, b) + mm(low, b)


def mm_nt_fine(a, b):
    high, low = split(a)
    return mm_nt(high, b) + mm_nt(low, b)


def mm_nt_pairs(a, blocks):
    total = None
    for place, block in enumerate(blocks):
        term = mm_nt_fine(a[:, place * WIDE : (place + 1) * WIDE], block)
        total = term if total is None else total + term
    return total


def window(ref, start, count, width):
    group, rest = lax.div(start, 8), lax.rem(start, 8)
    groups = ref[pl.ds(group, count // 8 + 1), :, 0:width]
    turned = pltpu.roll(groups, lax.rem(8 - rest, 8), 1)
    row = lax.broadcasted_iota(jnp.int32, (1, 8, 1), 1)
    return jnp.where(row < 8 - rest, turned[:-1], turned[1:]).reshape(count, width)


def in_eights(value):
    return value.reshape(value.shape[0] // 8, 8, value.shape[1])


def place_of(n_seq):
    seq, grp = lax.axis_index("seq"), lax.axis_index("grp")
    z, y = lax.div(seq, 2), lax.rem(seq, 2)
    x, c = lax.div(grp, 2), lax.rem(grp, 2)
    return seq, grp, z, y, x, c


def greet(n_seq, seq, grp, groups):
    barrier = pltpu.get_barrier_semaphore()

    def one(k, carry):
        pl.semaphore_signal(
            barrier, inc=1, device_id={"seq": lax.rem(seq + k, n_seq), "grp": grp}, device_id_type=MESH
        )
        return carry

    lax.fori_loop(1, n_seq, one, 0)
    for k in range(1, groups):
        pl.semaphore_signal(
            barrier, inc=1, device_id={"seq": seq, "grp": lax.rem(grp + k, groups)}, device_id_type=MESH
        )
    pl.semaphore_wait(barrier, n_seq - 1 + groups - 1)


def any_spec():
    return pl.BlockSpec(memory_space=pl.ANY)


def vmem_spec():
    return pl.BlockSpec(memory_space=pltpu.VMEM)


def smem_spec():
    return pl.BlockSpec(memory_space=pltpu.SMEM)


def head_mask():
    row = lax.broadcasted_iota(jnp.int32, (HEADS, 512), 0)
    column = lax.broadcasted_iota(jnp.int32, (HEADS, 512), 1)
    return lax.div(column, 512 // HEADS) == row


def block_diagonal(rows):
    column = lax.div(lax.broadcasted_iota(jnp.int32, rows.shape, 1), 512 // HEADS)
    return jnp.concatenate([jnp.where(column == h, rows, 0.0) for h in range(HEADS)], axis=0)


def same_rows(row):
    return jnp.broadcast_to(row, (8, row.shape[1]))


def pack(vectors):
    pieces = [v[:, 128 * i : 128 * (i + 1)] for v in vectors for i in range(v.shape[1] // 128)]
    spare = -len(pieces) % 8
    if spare:
        pieces.append(jnp.zeros((spare, 128), pieces[0].dtype))
    return jnp.concatenate(pieces, axis=0)


def unpack(rows, place, pieces=4):
    return jnp.concatenate(
        [rows[pieces * place + i : pieces * place + i + 1] for i in range(pieces)], axis=1
    )


def step_kernel(
    n_seq, owners_ref, dil_ref, length_ref, embed_ref, queries_ref, master_hbm, prompt_hbm,
    frames_hbm, cond_hbm, gout_hbm, gskip_hbm,
    block_hbm, skip_hbm, gframes_hbm, out_hbm, low_ref, dquery_ref,
    w, gs, prep, core_in, x_in, fr, fr_in, fx, ff, red_in, one_in, two_in, z_in, fin,
    xe, cat, slopes, gated, x1, bh, bb, sht, condt, gatt, bx, sk, blk,
    master, prompt, probs, left, vec, sums, tall, rt, lt, dq,
    hop_src, hop_in, wide_src, wide_in,
    in_sem, out_sem, hsend, hrecv, send, recv, zsend, zrecv, hop_send, hop_recv,
):
    seq, grp, z, y, x, c = place_of(n_seq)
    nz = n_seq // 2
    rows = prep.shape[1]
    own = frames_hbm.shape[1]
    grid_rows = own + 2 * HALO
    top = HALO + own
    channels = 512
    number = queries_ref.shape[1]
    sib, across, other_y = x * 2 + 1 - c, (1 - x) * 2 + c, z * 2 + 1 - y
    mine, theirs = 2 * c + x, 2 * c + 1 - x

    local_in = [
        pltpu.make_async_copy(a, b, in_sem.at[i])
        for i, (a, b) in enumerate(
            (
                (master_hbm, master),
                (prompt_hbm, prompt),
                (frames_hbm.at[0], xe.at[pl.ds(HALO, own)]),
                (cond_hbm.at[0], cat.at[pl.ds(HALO, own), pl.ds(1536, channels)]),
                (gout_hbm.at[0], bb.at[pl.ds(HALO, own), pl.ds(0, channels)]),
                (gskip_hbm.at[0], bb.at[pl.ds(HALO, own), pl.ds(channels, channels)]),
            )
        )
    ]
    for copy in local_in:
        copy.start()

    greet(n_seq, seq, grp, 4)

    waits = []
    used = [0]

    def remote(src, dst, to_seq, to_grp):
        place = used[0]
        used[0] += 1
        copy = pltpu.make_async_remote_copy(
            src_ref=src,
            dst_ref=dst,
            send_sem=send.at[place],
            recv_sem=recv.at[place],
            device_id={"seq": to_seq, "grp": to_grp},
            device_id_type=MESH,
        )
        copy.start()
        waits.append(copy)
        return copy

    gathering = []

    def spread(*args):
        copy = remote(*args)
        gathering.append(copy)
        return copy

    after, before = lax.rem(seq + 1, n_seq), lax.rem(seq + n_seq - 1, n_seq)
    halos = []
    for ref, buffer, column in (
        (frames_hbm, xe, 0),
        (cond_hbm, cat, 1536),
        (gout_hbm, bb, 0),
        (gskip_hbm, bb, channels),
    ):
        for start, at, target in ((own - HALO, 0, after), (0, top, before)):
            place = len(halos)
            copy = pltpu.make_async_remote_copy(
                src_ref=ref.at[0, pl.ds(start, HALO)],
                dst_ref=buffer.at[pl.ds(at, HALO), pl.ds(column, channels)],
                send_sem=hsend.at[place],
                recv_sem=hrecv.at[place],
                device_id={"seq": target, "grp": grp},
                device_id_type=MESH,
            )
            copy.start()
            halos.append(copy)

    slots, flags = [], []
    count = jnp.int32(0)
    for tile in range(TILES):
        flag = (owners_ref[tile] == grp).astype(jnp.int32)
        slots.append(jnp.minimum(count, CAP - 1))
        flags.append(flag.astype(F32))
        count = count + flag

    def rounded(tile):
        return (master[slots[tile]] * flags[tile]).astype(BF)

    def ready(tiles, buffer, table):
        for tile in tiles:
            value = rounded(tile)
            buffer[table[tile, 0]] = value[:, :WIDE]
            buffer[table[tile, 1]] = value[:, WIDE:]

    def merge_start(phase):
        base, blocks = PHASES[phase]
        each = blocks // 4
        return remote(
            prep.at[pl.ds(base + 2 * (1 - c) * each, 2 * each)],
            core_in.at[pl.ds(base // 2, 2 * each)],
            seq, sib,
        )

    def merge_cross(phase, copy):
        base, blocks = PHASES[phase]
        each = blocks // 4
        copy.wait_recv()

        def add(i, carry):
            place = base // 2 + i
            core_in[place] = core_in[place] + prep[base + 2 * c * each + i]
            return carry

        lax.fori_loop(0, 2 * each, add, 0)
        return remote(
            core_in.at[pl.ds(base // 2 + (1 - x) * each, each)],
            x_in.at[pl.ds(base // 4, each)],
            seq, across,
        )

    def view(phase, quarter, source):
        base, blocks = PHASES[phase]
        each = blocks // 4
        return w.at[pl.ds(base + quarter * each, each), source]

    zcopies, legs = {}, {}

    def merge_end(phase, copy):
        base, blocks = PHASES[phase]
        each = blocks // 4
        copy.wait_recv()

        def settle(i, carry):
            w[base + mine * each + i, seq] = (
                core_in[base // 2 + x * each + i] + x_in[base // 4 + i]
            )
            return carry

        lax.fori_loop(0, each, settle, 0)
        first(phase, 0)

    def spread_z(phase):
        ref = view(phase, mine, seq)
        for k in range(1, nz):
            zcopies[phase, k] = spread(ref, ref, lax.rem(z + k, nz) * 2 + y, grp)

    class Leg:
        pass

    def y_first(zz, quarters):
        return 1 - jnp.minimum(lax.div(4 * zz, quarters * nz), 1)

    def first(phase, k):
        if k:
            zcopies[phase, k].wait_recv()
        leg = Leg()
        zs = lax.rem(z - k + nz, nz)
        leg.a = y_first(zs, IN_SPLIT[phase])
        leg.here, leg.there = zs * 2 + y, zs * 2 + 1 - y
        a, b = leg.a, 1 - leg.a
        leg.two = (a * seq + b * other_y, a * across + b * grp)
        ref = view(phase, mine, leg.here)
        leg.f1 = spread(ref, ref, a * other_y + b * seq, a * grp + b * across)
        leg.f2a = spread(ref, ref, *leg.two)
        leg.core = [spread(ref, ref, seq, sib)]
        legs[phase, k] = leg

    def second(phase, k):
        leg = legs[phase, k]
        a, b = leg.a, 1 - leg.a
        leg.f1.wait_recv()
        ref = view(phase, a * mine + b * theirs, a * leg.there + b * leg.here)
        leg.f2b = spread(ref, ref, *leg.two)
        leg.core.append(spread(ref, ref, seq, sib))

    def third(phase, k):
        leg = legs[phase, k]
        a, b = leg.a, 1 - leg.a
        leg.f2a.wait_recv()
        ref = view(phase, a * theirs + b * mine, a * leg.here + b * leg.there)
        leg.core.append(spread(ref, ref, seq, sib))
        leg.f2b.wait_recv()
        ref = view(phase, theirs, leg.there)
        leg.core.append(spread(ref, ref, seq, sib))

    def arrived(phase):
        for k in range(nz):
            for copy in legs[phase, k].core:
                copy.wait_recv()

    def hop_refs(j):
        if j == len(HOP_ROWS) - 1:
            return wide_src, wide_in.at[seq], wide_in
        start = sum(HOP_ROWS[:j])
        spot = pl.ds(start, HOP_ROWS[j])
        return hop_src.at[spot], hop_in.at[seq, spot], hop_in.at[:, spot]

    def hop_copy(j, k):
        src, dst, _ = hop_refs(j)
        return pltpu.make_async_remote_copy(
            src_ref=src,
            dst_ref=dst,
            send_sem=hop_send.at[j, k],
            recv_sem=hop_recv.at[j, k],
            device_id={"seq": lax.rem(seq + k, n_seq), "grp": grp},
            device_id_type=MESH,
        )

    def hop_start(j, value):
        src, dst, _ = hop_refs(j)
        value = value.astype(src.dtype)
        src[...] = value
        dst[...] = value

        def one(k, carry):
            hop_copy(j, k).start()
            return carry

        lax.fori_loop(1, n_seq, one, 0)

    def hop_end(j):
        def one(k, carry):
            hop_copy(j, k).wait()
            return carry

        lax.fori_loop(1, n_seq, one, 0)
        _, _, whole = hop_refs(j)

        def add(i, total):
            return total + whole[i].astype(F32)

        return lax.fori_loop(0, n_seq, add, jnp.zeros((HOP_ROWS[j], 128), F32))

    position = lax.broadcasted_iota(jnp.int32, (channels, rows), 0)
    column = lax.broadcasted_iota(jnp.int32, (channels, rows), 1)
    chosen = jnp.where(position == column + seq * rows, 1.0, 0.0).astype(BF)

    def pick(v):
        return mm_fine(v, chosen)

    def spot_in(p):
        return mm_nt_fine(p, chosen)

    def film_block(layer, place):
        return ff[FILM * layer + place]

    def film_rows(layer, v, places):
        return jnp.concatenate([mm_fine(v, film_block(layer, i)) for i in places], axis=1)

    def film_back(layer, v, places):
        total = None
        for i, place in enumerate(places):
            term = mm_nt_fine(v[:, i * WIDE : (i + 1) * WIDE], film_block(layer, place))
            total = term if total is None else total + term
        return spot_in(total)

    def key_blocks(layer):
        return [w[2 * layer + side].reshape(channels, WIDE) for side in range(2)]

    mask = head_mask()

    def attention(layer):
        spread = block_diagonal(queries_ref[layer])
        probe = mm_nt_pairs(spread, key_blocks(layer))
        pr = prompt[...]
        scores = mm_nt_fine(probe, pr) * 0.125
        live = lax.broadcasted_iota(jnp.int32, scores.shape, 1) < length_ref[0]
        scores = jnp.where(live, scores, NEGATIVE)
        weight = jnp.exp(scores - jnp.max(scores, axis=1, keepdims=True))
        value = weight / jnp.sum(weight, axis=1, keepdims=True)
        probs[layer] = value
        mean = jnp.concatenate(
            [
                jnp.mean(value[h * number : (h + 1) * number], axis=0, keepdims=True)
                for h in range(HEADS)
            ],
            axis=0,
        )
        seen = mm_fine(mean, pr)
        left[layer, 0:8] = seen
        return seen

    def wblock(layer, place):
        return w[KEYS + MAIN * layer + place].reshape(channels, WIDE)

    def inside(low, count):
        row = lax.broadcasted_iota(jnp.int32, (count, 1), 0) + (low - HALO) + seq * own
        return (row >= 0) & (row < n_seq * own)

    def windows_forward(layer):
        low = 16 * layer
        high = grid_rows - low
        scale, shift = 1.0 + vec[layer, 0:1], vec[layer, 1:2]
        here = xe[...].astype(F32) if layer == 0 else x1[...]
        shifted = (here * scale + shift).astype(BF).astype(F32)
        shifted = jnp.where(inside(0, grid_rows), shifted, 0.0)
        groups = grid_rows // 8
        bh[0, :, 0:channels] = jnp.zeros((8, channels), F32)
        bh[1 : 1 + groups, :, 0:channels] = in_eights(shifted)
        bh[1 + groups :, :, 0:channels] = jnp.zeros((3, 8, channels), F32)
        sht[layer] = jnp.transpose(shifted[HALO:top]).astype(BF)
        for tap in range(3):
            start = 8 + low + (tap - 1) * dil_ref[layer]
            cat[low:high, tap * channels : (tap + 1) * channels] = window(
                bh, start, high - low, channels
            ).astype(BF)

    def gates(layer, first_row, rows_now):
        spot = slice(first_row, first_row + rows_now)
        value = cat[spot, 0:2048]
        for part in range(2):
            columns = slice(part * WIDE, (part + 1) * WIDE)
            base = KEYS + MAIN * layer + 5 * part
            lhs = mm(value, w[base : base + 4].reshape(2048, WIDE))
            tangent = jnp.tanh(lhs + vec[layer, 2:3, columns])
            rhs = mm(value, w[base + 10 : base + 14].reshape(2048, WIDE))
            opening = jax.nn.sigmoid(rhs + vec[layer, 3:4, columns])
            gate = tangent * opening
            gated[spot, columns] = gate.astype(BF)
            slopes[layer, spot, columns] = (opening * (1.0 - tangent * tangent)).astype(BF)
            other = slice(channels + part * WIDE, channels + (part + 1) * WIDE)
            slopes[layer, spot, other] = (gate * (1.0 - opening)).astype(BF)

    def residual(layer, first_row, rows_now):
        value = gated[first_row : first_row + rows_now]
        for part in range(2):
            columns = slice(part * WIDE, (part + 1) * WIDE)
            term = mm(value, wblock(layer, 5 * part + 4))
            if layer == 0:
                base = xe[first_row : first_row + rows_now, columns].astype(F32)
                x1[first_row : first_row + rows_now, columns] = (base + term) * HALF_ROOT
            else:
                base = x1[first_row : first_row + rows_now, columns]
                blk[first_row - HALO : first_row - HALO + rows_now, columns] = (
                    base + term
                ) * HALF_ROOT

    def skipped(layer, first_row, rows_now):
        value = gated[first_row : first_row + rows_now]
        spot = slice(first_row - HALO, first_row - HALO + rows_now)
        for part in range(2):
            columns = slice(part * WIDE, (part + 1) * WIDE)
            term = mm(value, wblock(layer, 5 * part + 14))
            if layer == 0:
                sk[spot, columns] = term
            else:
                sk[spot, columns] = sk[spot, columns] + term

    low, high = 16, grid_rows - 16

    def gate_grads(layer, first_row, rows_now):
        spot = slice(first_row, first_row + rows_now)
        bb[spot, 0:channels] = (bx[spot] * HALF_ROOT).astype(BF)
        branch = jnp.concatenate([wblock(layer, 5 * part + 4) for part in range(4)], axis=1)
        back = mm_nt(bb[spot], branch)
        keep = inside(first_row, rows_now)
        place = slice(1 + first_row // 8, 1 + (first_row + rows_now) // 8)
        for side in range(2):
            columns = slice(side * channels, (side + 1) * channels)
            value = (back * slopes[layer, spot, columns].astype(F32)).astype(BF).astype(F32)
            bh[place, :, columns] = in_eights(jnp.where(keep, value, 0.0))

    def windows_backward(layer):
        total = bh[1 + HALO // 8 : 1 + top // 8].reshape(own, 2 * channels)
        total = jnp.sum(total, axis=0, keepdims=True)
        sums[layer, 2:3] = total[:, 0:channels]
        sums[layer, 3:4] = total[:, channels:]
        reach, limit = (low, high) if layer else (HALO, top)
        for tap in range(3):
            start = 8 + reach - (tap - 1) * dil_ref[layer]
            cat[reach:limit, tap * 1024 : (tap + 1) * 1024] = window(
                bh, start, limit - reach, 1024
            ).astype(BF)

    def frame_grads(layer, first_row, rows_now):
        spot = slice(first_row, first_row + rows_now)
        taps = jnp.concatenate(
            [wblock(layer, 5 * part + tap) for tap in range(3) for part in range(4)], axis=1
        )
        back = mm_nt(cat[spot], taps)
        if layer:
            here = x1[spot]
            row = lax.broadcasted_iota(jnp.int32, (rows_now, 1), 0) + first_row
            kept = jnp.where((row >= HALO) & (row < top), back, 0.0)
        else:
            here = xe[spot].astype(F32)
            kept = back
        sums[layer, 0:1] += jnp.sum(kept * here, axis=0, keepdims=True)
        sums[layer, 1:2] += jnp.sum(kept, axis=0, keepdims=True)
        bx[spot] = bx[spot] * HALF_ROOT + back * (1.0 + vec[layer, 0:1])

    def weight_grad(layer, part, i):
        if i < 4:
            tap = i if i < 3 else 1
            start = pl.multiple_of(tap * 1024 + part * WIDE, WIDE)
            lhs = sht[layer] if i < 3 else condt[...]
            return mm(lhs, cat[HALO:top, pl.ds(start, WIDE)])
        start = pl.multiple_of(part * WIDE, WIDE)
        return mm(gatt[layer], bb[HALO:top, pl.ds(start, WIDE)])

    core_sent = {}

    def give(layer, xx):
        part = 2 * (1 - c) + xx
        buffer, base = (gs, 0) if layer else (w, KEYS + MAIN)
        for i in range(5):
            value = weight_grad(layer, part, i).astype(BF)
            buffer[base + 5 * xx + i] = value.reshape(n_seq, rows, WIDE)
        core_sent[layer, xx] = remote(
            buffer.at[pl.ds(base + 5 * xx, 5)], red_in.at[layer, pl.ds(5 * xx, 5)], seq, sib
        )

    def keep(layer, xx):
        part = 2 * c + xx
        core_sent[layer, xx].wait_recv()
        for i in range(5):
            value = weight_grad(layer, part, i).reshape(n_seq, rows, WIDE)
            spot = 5 * xx + i
            red_in[layer, spot] = (red_in[layer, spot].astype(F32) + value).astype(BF)

    ones, twos, zs, targets = {}, {}, {}, {}
    for layer in range(LAYERS):
        for k in range(nz):
            zd = lax.rem(z + k, nz)
            targets[layer, k] = (zd, y_first(zd, OUT_SPLIT[layer]))

    def red_one(layer, k):
        zd, a = targets[layer, k]
        b = 1 - a
        ones[layer, k] = []
        for j in range(2):
            xi, yi = a * (1 - x) + b * j, a * j + b * (1 - y)
            ones[layer, k].append(
                remote(
                    red_in.at[layer, pl.ds(5 * xi, 5), 2 * zd + yi],
                    one_in.at[layer, k, j],
                    a * seq + b * other_y, a * across + b * grp,
                )
            )

    def red_two(layer, k):
        zd, a = targets[layer, k]
        b = 1 - a
        you = a * y + b * x
        for j in range(2):
            ones[layer, k][j].wait_recv()
            xi, yi = a * x + b * j, a * j + b * y

            def body(i, carry, j=j, xi=xi, yi=yi):
                one_in[layer, k, j, i] = (
                    one_in[layer, k, j, i].astype(F32)
                    + red_in[layer, 5 * xi + i, 2 * zd + yi].astype(F32)
                ).astype(BF)
                return carry

            lax.fori_loop(0, 5, body, 0)
        twos[layer, k] = remote(
            one_in.at[layer, k, 1 - you], two_in.at[layer, k],
            a * other_y + b * seq, a * grp + b * across,
        )

    def red_three(layer, k):
        zd, a = targets[layer, k]
        you = a * y + (1 - a) * x
        twos[layer, k].wait_recv()

        def body(i, carry):
            two_in[layer, k, i] = (
                two_in[layer, k, i].astype(F32) + one_in[layer, k, you, i].astype(F32)
            ).astype(BF)
            return carry

        lax.fori_loop(0, 5, body, 0)
        if k:
            zs[layer, k] = remote(two_in.at[layer, k], z_in.at[layer, k], zd * 2 + y, grp)

    lasts = {}
    outs = []

    def local_out(src, dst):
        copy = pltpu.make_async_copy(src, dst, out_sem.at[len(outs)])
        copy.start()
        outs.append(copy)

    def red_four(layer):
        for k in range(1, nz):
            zs[layer, k].wait_recv()

        def body(i, carry):
            total = two_in[layer, 0, i].astype(F32)
            for k in range(1, nz):
                total = total + z_in[layer, k, i].astype(F32)
            fin[layer, i] = total.astype(BF)
            return carry

        lax.fori_loop(0, 5, body, 0)
        src, dst = fin.at[layer], out_hbm.at[layer, mine]
        lasts[layer] = [remote(src, dst, seq, across), remote(src, dst, seq, sib)]
        if not layer:
            lasts[layer].append(remote(src, dst, seq, (1 - x) * 2 + 1 - c))
        local_out(src, dst)

    def red_five(layer):
        lasts[layer][0].wait_recv()
        ref = out_hbm.at[layer, theirs]
        lasts[layer].append(remote(ref, ref, seq, sib))

    ops = {}

    def op(*key):
        def keep_op(body):
            ops[key] = body
            return body

        return keep_op

    def quarter(j):
        return range(j * nz // 4, (j + 1) * nz // 4)

    main_tiles = (0, 1, 2, 3, 4, 5, 6, 7, 15, 16)
    merges, crosses, film_sent, kept, seen, hops = {}, {}, {}, {}, {}, {}
    half = fr.shape[0] // 2
    half_spot = pl.ds(c * half, half)
    size_all, size_mid, size_own = grid_rows // 2, (high - low) // 2, own // 2
    embed = same_rows(embed_ref[...].astype(F32))

    for phase in range(3):

        @op("prep", phase)
        def _(phase=phase):
            if phase:
                tiles = [PER_LAYER * (phase - 1) + t for t in main_tiles]
            else:
                tiles = [PER_LAYER * layer + 10 for layer in range(LAYERS)]
            ready(tiles, prep, BLOCK_OF)
            merges[phase] = merge_start(phase)

        @op("cross", phase)
        def _(phase=phase):
            crosses[phase] = merge_cross(phase, merges[phase])

        @op("end", phase)
        def _(phase=phase):
            merge_end(phase, crosses[phase])

        @op("zs", phase)
        def _(phase=phase):
            spread_z(phase)
            for k in quarter(0):
                if k:
                    first(phase, k)

        for j in range(4):

            @op("first", phase, j)
            def _(phase=phase, j=j):
                for k in quarter(j):
                    first(phase, k)

            @op("second", phase, j)
            def _(phase=phase, j=j):
                for k in quarter(j):
                    second(phase, k)

            @op("third", phase, j)
            def _(phase=phase, j=j):
                for k in quarter(j):
                    third(phase, k)

    @op("fc")
    def _():
        for layer in range(LAYERS):
            ready([PER_LAYER * layer + t for t in FILM_ORDER], fr, FILM_OF)
        film_sent[0] = remote(fr, fr_in, seq, sib)

    @op("fx")
    def _():
        film_sent[0].wait_recv()
        fr_in[...] = fr_in[...] + fr[...]
        film_sent[1] = remote(fr_in.at[half_spot], fx, seq, across)

    @op("fl")
    def _():
        film_sent[1].wait_recv()
        ff[half_spot] = fr_in[half_spot] + fx[...]
        film_sent[2] = remote(ff.at[half_spot], ff.at[half_spot], seq, sib)

    @op("condt")
    def _():
        local_in[3].wait()
        condt[...] = jnp.transpose(cat[HALO:top, 1536:2048].astype(F32)).astype(BF)

    @op("att0")
    def _():
        local_in[1].wait()
        arrived(0)
        seen[0] = attention(0)

    @op("att1")
    def _():
        seen[1] = attention(1)

    @op("hsA")
    def _():
        film_sent[2].wait_recv()
        vectors = []
        for layer in range(LAYERS):
            mixed = film_rows(layer, pick(seen[layer]), (0, 1))
            vectors.append(jnp.sum(jnp.where(mask, mixed, 0.0), axis=0, keepdims=True))
            steps = film_rows(layer, pick(embed), (8, 9, 10, 11))
            vectors += [steps[0:1, :channels], steps[0:1, channels:]]
        hop_start(0, pack(vectors))

    @op("heA")
    def _():
        total = hop_end(0)
        hops["mixed"] = [unpack(total, 3 * layer) for layer in range(LAYERS)]
        for layer in range(LAYERS):
            vec[layer, 2:3] = unpack(total, 3 * layer + 1)
            vec[layer, 3:4] = unpack(total, 3 * layer + 2)

    @op("hsB")
    def _():
        mixed = hops["mixed"]
        hop_start(
            1,
            pack([film_rows(l, pick(same_rows(mixed[l])), (2, 3))[0:1] for l in range(LAYERS)]),
        )

    @op("heB")
    def _():
        total = hop_end(1)
        hops["pooled"] = [unpack(total, layer) for layer in range(LAYERS)]

    @op("hsC")
    def _():
        vectors = []
        for layer in range(LAYERS):
            pooled = hops["pooled"][layer]
            film = film_rows(layer, pick(same_rows(pooled)), (4, 5, 6, 7))
            vectors += [film[0:1, :channels], film[0:1, channels:]]
        hop_start(2, pack(vectors))

    @op("heC")
    def _():
        total = hop_end(2)
        for layer in range(LAYERS):
            vec[layer, 0:1] = unpack(total, 2 * layer)
            vec[layer, 1:2] = unpack(total, 2 * layer + 1)
            left[layer, 8:9] = hops["mixed"][layer]
            left[layer, 9:10] = hops["pooled"][layer]
            left[layer, 10:11] = embed[0:1]
            left[layer, 11:16] = jnp.zeros((5, channels), F32)

    @op("win0")
    def _():
        local_in[2].wait()
        for copy in halos[:4]:
            copy.wait_recv()
        windows_forward(0)

    @op("win1")
    def _():
        local_in[4].wait()
        local_in[5].wait()
        for copy in halos[4:]:
            copy.wait_recv()
        bx[...] = bb[:, 0:channels].astype(F32)
        windows_forward(1)

    for layer in range(LAYERS):
        start, size = (low, size_mid) if layer else (0, size_all)
        for part, name in enumerate("ab"):
            first_row = start + part * size

            @op(f"gates{layer}{name}")
            def _(layer=layer, first_row=first_row, size=size, part=part):
                if not part:
                    arrived(1 + layer)
                gates(layer, first_row, size)

        @op(f"gatt{layer}")
        def _(layer=layer):
            gatt[layer] = jnp.transpose(gated[HALO:top].astype(F32)).astype(BF)

    @op("res0a")
    def _():
        residual(0, 0, size_all)

    @op("res0b")
    def _():
        residual(0, size_all, size_all)

    @op("skip0")
    def _():
        for part in range(2):
            skipped(0, HALO + part * size_own, size_own)

    @op("out1")
    def _():
        for part in range(2):
            residual(1, HALO + part * size_own, size_own)
            skipped(1, HALO + part * size_own, size_own)
        local_out(blk, block_hbm.at[0])
        local_out(sk, skip_hbm.at[0])

    for layer in range(LAYERS):
        for part, name in enumerate("ab"):

            @op(f"gg{layer}{name}")
            def _(layer=layer, part=part):
                if layer and not part:
                    edge = 1 + low // 8
                    bh[0:edge] = jnp.zeros((edge, 8, 1024), F32)
                    bh[1 + high // 8 :] = jnp.zeros((edge + 2, 8, 1024), F32)
                    sums[...] = jnp.zeros_like(sums)
                gate_grads(layer, low + part * size_mid, size_mid)

            @op(f"fg{layer}{name}")
            def _(layer=layer, part=part):
                if layer:
                    frame_grads(1, low + part * size_mid, size_mid)
                else:
                    frame_grads(0, HALO + part * size_own, size_own)

        @op(f"winb{layer}")
        def _(layer=layer):
            windows_backward(layer)

        for xx in range(2):

            @op("give", layer, xx)
            def _(layer=layer, xx=xx):
                if not layer and not kept:
                    for copy in gathering:
                        copy.wait_send()
                    kept[0] = True
                give(layer, xx)

            @op("keep", layer, xx)
            def _(layer=layer, xx=xx):
                keep(layer, xx)

        for j in range(4):
            for name, body in (("one", red_one), ("two", red_two), ("three", red_three)):

                @op(name, layer, j)
                def _(layer=layer, j=j, body=body):
                    for k in quarter(j):
                        body(layer, k)

        @op("four", layer)
        def _(layer=layer):
            red_four(layer)

    @op("five", 1)
    def _():
        red_five(1)

    @op("hs3")
    def _():
        local_out(bx.at[pl.ds(HALO, own)], gframes_hbm.at[0])
        hop_start(3, pack([sums[l, i : i + 1] for l in range(LAYERS) for i in range(4)]))

    @op("he3")
    def _():
        total = hop_end(3)
        hops["sides"] = [[unpack(total, 4 * l + i) for i in range(4)] for l in range(LAYERS)]

    @op("hs4")
    def _():
        vectors = []
        for layer in range(LAYERS):
            dfilm = same_rows(jnp.concatenate(hops["sides"][layer][0:2], axis=1))
            vectors.append(film_back(layer, dfilm, (4, 5, 6, 7))[0:1])
        hop_start(4, pack(vectors))

    @op("he4")
    def _():
        total = hop_end(4)
        hops["dpooled"] = [unpack(total, layer) for layer in range(LAYERS)]

    @op("hs5")
    def _():
        value = hops["dpooled"]
        hop_start(
            5, pack([film_back(l, same_rows(value[l]), (2, 3))[0:1] for l in range(LAYERS)])
        )

    @op("he5")
    def _():
        total = hop_end(5)
        hops["dmixed"] = [unpack(total, layer) for layer in range(LAYERS)]

    @op("hs6")
    def _():
        vectors = []
        for layer in range(LAYERS):
            dseen = film_back(layer, jnp.where(mask, hops["dmixed"][layer], 0.0), (0, 1))
            vectors += [dseen[h : h + 1] for h in range(HEADS)]
        hop_start(6, pack(vectors))

    @op("he6")
    def _():
        hops["dseen"] = hop_end(6)

    def attention_back(layer):
        total = hops["dseen"]
        pr = prompt[...]
        dseen = jnp.concatenate(
            [unpack(total, HEADS * layer + h) for h in range(HEADS)], axis=0
        )
        dmean = mm_nt_fine(dseen, pr) * (1.0 / number)
        dprobs = jnp.concatenate(
            [jnp.broadcast_to(dmean[h : h + 1], (number, channels)) for h in range(HEADS)], axis=0
        )
        value = probs[layer]
        inner = jnp.sum(dprobs * value, axis=1, keepdims=True)
        dprobe = mm_fine(value * (dprobs - inner) * 0.125, pr)
        keys = key_blocks(layer)
        dspread = jnp.concatenate([mm_fine(dprobe, keys[0]), mm_fine(dprobe, keys[1])], axis=1)
        head = lax.div(lax.broadcasted_iota(jnp.int32, (number, channels), 1), channels // HEADS)
        dquery = jnp.zeros((number, channels), F32)
        for h in range(HEADS):
            dquery = dquery + jnp.where(head == h, dspread[h * number : (h + 1) * number], 0.0)
        dq[grp, layer] = dquery.astype(BF)
        tall[:, 0:256] = jnp.transpose(dprobe)
        lefts = jnp.concatenate([left[layer], jnp.zeros((112, channels), F32)], axis=0)
        tall[:, 256:384] = jnp.transpose(lefts)
        start = pl.multiple_of(seq * rows, rows)
        lt[grp, layer] = tall[pl.ds(start, rows), :].astype(BF)
        rt[grp, layer] = jnp.concatenate(
            hops["sides"][layer]
            + [hops["dpooled"][layer], hops["dmixed"][layer], jnp.zeros((2, channels), F32)],
            axis=0,
        )

    @op("fb1")
    def _():
        attention_back(1)

    @op("fb0")
    def _():
        attention_back(0)

    bundles = []

    @op("bundle")
    def _():
        for k in range(1, 4):
            for ref in (rt, lt, dq):
                bundles.append(remote(ref.at[grp], ref.at[grp], seq, lax.rem(grp + k, 4)))

    @op("low")
    def _():
        for copy in bundles:
            copy.wait_recv()
        total = dq[0].astype(F32)
        for k in range(1, 4):
            total = total + dq[k].astype(F32)
        dquery_ref[...] = total
        at = lax.broadcasted_iota(jnp.int32, (16, channels), 0)
        for layer in range(LAYERS):
            spread = block_diagonal(queries_ref[layer]).astype(BF)
            probe = lt[0, layer, :, 0:256].astype(F32)
            for k in range(1, 4):
                probe = probe + lt[k, layer, :, 0:256].astype(F32)
            low_ref[layer, 0] = mm(probe.astype(BF), spread).astype(BF)
            total = None
            for k in range(4):
                right = rt[k, layer]
                value = jnp.concatenate(
                    [jnp.where(mask, right[5:6], 0.0), jnp.zeros((8, channels), F32)], axis=0
                )
                pieces = [value] + [
                    jnp.where(at == row, right[i : i + 1], 0.0)
                    for i, row in ((4, 8), (0, 9), (1, 9), (2, 10), (3, 10))
                ]
                side = jnp.concatenate(pieces, axis=1).astype(BF)
                term = mm(lt[k, layer, :, 256:272], side)
                total = term if total is None else total + term
            for i in range(6):
                low_ref[layer, 1 + i] = total[:, i * channels : (i + 1) * channels].astype(BF)

    @op("end")
    def _():
        for copies in lasts.values():
            for copy in copies[1:]:
                copy.wait_recv()
        lasts[0][0].wait_recv()
        for copy in outs:
            copy.wait()
        for copy in halos:
            copy.wait_send()
        for copy in waits:
            if not any(copy is done for done in gathering):
                copy.wait_send()

    local_in[0].wait()
    for key in ORDER:
        ops[key if isinstance(key, tuple) else (key,)]()


def train_step(
    n_seq, owners, dilations, length, step_embed, queries, master, prompt,
    frames_in, cond_frames, grad_out, grad_skip,
):
    _, own, channels = frames_in.shape
    rows = master.shape[1]
    number = queries.shape[1]
    grid_rows = own + 2 * HALO
    nz = n_seq // 2
    v = pltpu.VMEM
    dma = pltpu.SemaphoreType.DMA
    frame_out = jax.ShapeDtypeStruct((1, own, channels), F32)
    film = FILM * LAYERS
    copies = 24 + 32 * nz
    return pl.pallas_call(
        functools.partial(step_kernel, n_seq),
        out_shape=(
            frame_out,
            frame_out,
            frame_out,
            jax.ShapeDtypeStruct((LAYERS, 4, 5, rows, WIDE), BF),
            jax.ShapeDtypeStruct((LAYERS, LOW_RANK, rows, channels), BF),
            jax.ShapeDtypeStruct((LAYERS, number, channels), F32),
        ),
        in_specs=[smem_spec()] * 3 + [vmem_spec()] * 2 + [any_spec()] * 6,
        out_specs=(any_spec(),) * 4 + (vmem_spec(),) * 2,
        scratch_shapes=[
            v((BLOCKS, n_seq, rows, WIDE), BF),
            v((10, n_seq, rows, WIDE), BF),
            v((BLOCKS, rows, WIDE), BF),
            v((BLOCKS // 2, rows, WIDE), BF),
            v((BLOCKS // 4, rows, WIDE), BF),
            v((film, rows, WIDE), BF),
            v((film, rows, WIDE), BF),
            v((film // 2, rows, WIDE), BF),
            v((film, rows, WIDE), BF),
            v((LAYERS, 10, n_seq, rows, WIDE), BF),
            v((LAYERS, nz, 2, 5, rows, WIDE), BF),
            v((LAYERS, nz, 5, rows, WIDE), BF),
            v((LAYERS, nz, 5, rows, WIDE), BF),
            v((LAYERS, 5, rows, WIDE), BF),
            v((grid_rows, channels), BF),
            v((grid_rows, 6 * channels), BF),
            v((LAYERS, grid_rows, 2 * channels), BF),
            v((grid_rows, channels), BF),
            v((grid_rows, channels), F32),
            v((grid_rows // 8 + 4, 8, 2 * channels), F32),
            v((grid_rows, 2 * channels), BF),
            v((LAYERS, channels, own), BF),
            v((channels, own), BF),
            v((LAYERS, channels, own), BF),
            v((grid_rows, channels), F32),
            v((own, channels), F32),
            v((own, channels), F32),
            v(master.shape, F32),
            v(prompt.shape, BF),
            v((LAYERS, HEADS * number, prompt.shape[0]), F32),
            v((LAYERS, 16, channels), F32),
            v((LAYERS, 8, channels), F32),
            v((LAYERS, 8, channels), F32),
            v((channels, 384), F32),
            v((4, LAYERS, 8, channels), F32),
            v((4, LAYERS, rows, 384), BF),
            v((4, LAYERS, number, channels), BF),
            v((sum(HOP_ROWS[:-1]), 128), F32),
            v((n_seq, sum(HOP_ROWS[:-1]), 128), F32),
            v((HOP_ROWS[-1], 128), BF),
            v((n_seq, HOP_ROWS[-1], 128), BF),
            dma((6,)),
            dma((8,)),
            dma((8,)),
            dma((8,)),
            dma((copies,)),
            dma((copies,)),
            dma((1,)),
            dma((1,)),
            dma((len(HOP_ROWS), n_seq)),
            dma((len(HOP_ROWS), n_seq)),
        ],
        compiler_params=pltpu.CompilerParams(
            collective_id=0, has_side_effects=True, vmem_limit_bytes=MEM
        ),
        name="train_step",
    )(
        owners, dilations, length, step_embed, queries, master, prompt,
        frames_in, cond_frames, grad_out, grad_skip,
    )


def adam_update(weight, moment_one, moment_two, gradient, step_rate):
    moment_one = BETA_ONE * moment_one + (1.0 - BETA_ONE) * gradient
    moment_two = BETA_TWO * moment_two + (1.0 - BETA_TWO) * gradient * gradient
    normal = (
        moment_one
        / (1.0 - BETA_ONE**STEP)
        / (jnp.sqrt(moment_two / (1.0 - BETA_TWO**STEP)) + EPSILON)
    )
    return (moment_one, moment_two, weight - step_rate * (normal + WEIGHT_DECAY * weight))


def update_kernel(
    owners_ref, master_ref, first_ref, second_ref, grad_ref, low_ref,
    queries_ref, qfirst_ref, qsecond_ref, dq_ref, block_in, skip_in, gframes_in,
    nfirst_ref, nsecond_ref, nmaster_ref, ncopy_ref, nqfirst_ref, nqsecond_ref, nqueries_ref,
    block_out, skip_out, gframes_out,
    tile_of,
):
    step = pl.program_id(0)
    grp = lax.axis_index("grp")
    block_out[...] = block_in[...]
    skip_out[...] = skip_in[...]
    gframes_out[...] = gframes_in[...]

    @pl.when(step == 0)
    def _():
        for slot in range(CAP + 1):
            tile_of[slot] = TILES
        count = jnp.int32(0)
        for tile in range(TILES):
            own = owners_ref[tile] == grp

            @pl.when(own)
            def _(count=count, tile=tile):
                tile_of[jnp.minimum(count, CAP)] = tile

            count = count + own.astype(jnp.int32)
        one, two, three = adam_update(
            queries_ref[...], qfirst_ref[...], qsecond_ref[...], dq_ref[...], QUERY_RATE
        )
        nqfirst_ref[...] = one
        nqsecond_ref[...] = two
        nqueries_ref[...] = three

    tile = tile_of[step]
    in_use = tile < TILES
    tile = jnp.minimum(tile, TILES - 1)
    layer, kind = lax.div(tile, PER_LAYER), lax.rem(tile, PER_LAYER)
    pair = lax.rem(kind, 2) * (kind < 8) + (kind == 16)
    tap = jnp.where(kind < 8, lax.div(kind, 2), 4)
    block = 10 * pair + tap
    full = jnp.concatenate(
        [
            grad_ref[layer, lax.div(block, 5), lax.rem(block, 5)],
            grad_ref[layer, lax.div(block, 5) + 1, lax.rem(block, 5)],
        ],
        axis=1,
    )
    place = jnp.where(kind < 10, kind - 3, kind - 10)
    place = jnp.clip(place, 0, LOW_RANK - 1)
    thin = low_ref[layer, place]
    is_thin = ((kind >= 8) & (kind <= 14)).astype(jnp.int32)
    gradient = jnp.where(
        jnp.broadcast_to(is_thin, full.shape) > 0, thin.astype(F32), full.astype(F32)
    )
    master, first, second = master_ref[0], first_ref[0], second_ref[0]
    one, two, three = adam_update(master, first, second, gradient, LEARN_RATE)
    keep = jnp.broadcast_to(in_use.astype(jnp.int32), master.shape) > 0
    three = jnp.where(keep, three, master)
    nfirst_ref[0] = jnp.where(keep, one, first)
    nsecond_ref[0] = jnp.where(keep, two, second)
    nmaster_ref[0] = three
    ncopy_ref[0] = three.astype(BF)


def update(owners, master, first, second, grads, low, queries, qfirst, qsecond, dq, *frames):
    _, rows, channels = master.shape
    slot = pl.BlockSpec((1, rows, channels), lambda i: (i, 0, 0))
    whole = vmem_spec()
    query = jax.ShapeDtypeStruct(queries.shape, F32)
    full = jax.ShapeDtypeStruct(master.shape, F32)
    passed = jax.ShapeDtypeStruct(frames[0].shape, F32)
    pieces = 10
    piece = pl.BlockSpec(
        (1, passed.shape[1] // pieces, channels), lambda i: (0, jnp.minimum(i, pieces - 1), 0)
    )
    return pl.pallas_call(
        update_kernel,
        grid=(CAP,),
        out_shape=(full, full, full, jax.ShapeDtypeStruct(master.shape, BF), query, query, query)
        + (passed,) * 3,
        in_specs=[smem_spec(), slot, slot, slot] + [whole] * 6 + [piece] * 3,
        out_specs=(slot, slot, slot, slot, whole, whole, whole) + (piece,) * 3,
        scratch_shapes=[pltpu.SMEM((CAP + 1,), jnp.int32)],
        compiler_params=pltpu.CompilerParams(vmem_limit_bytes=MEM),
        name="update",
    )(owners, master, first, second, grads, low, queries, qfirst, qsecond, dq, *frames)


def on_device(
    n_seq,
    frames_in,
    cond_frames,
    step_embed,
    prompts,
    prompt_lengths,
    pairing,
    dilations,
    owners,
    master,
    first_moment,
    second_moment,
    queries,
    query_first,
    query_second,
    grad_out,
    grad_skip,
):
    prompt = lax.dynamic_index_in_dim(prompts, pairing[0], 0, keepdims=False)
    length = lax.dynamic_index_in_dim(prompt_lengths, pairing[0], 0, keepdims=True)
    block, skip, gframes, own_grads, low, dq = train_step(
        n_seq, owners, dilations, length, step_embed, queries, master, prompt,
        frames_in, cond_frames, grad_out, grad_skip,
    )
    (
        new_first, new_second, new_master, new_copy, nqf, nqs, nq,
        block_out, skip_out, grad_frames,
    ) = update(
        owners, master, first_moment, second_moment, own_grads, low,
        queries, query_first, query_second, dq, block, skip, gframes,
    )
    return (
        new_first, new_second, new_master, new_copy, nqf, nqs, nq,
        block_out, skip_out, grad_frames,
    )


def solution(mesh):
    shard = P("grp", "seq", None)
    placed = (
        shard, shard, P("grp", None), P(), P(), P("grp"), P(), P(),
        shard, shard, shard, P(), P(), P(), shard, shard,
    )
    return jax.shard_map(
        functools.partial(on_device, mesh.shape["seq"]),
        mesh=mesh,
        in_specs=placed,
        out_specs=(shard, shard, shard, shard, P(), P(), P(), shard, shard, shard),
        check_vma=False,
    )
```

```python
import functools

import jax
import jax.numpy as jnp
from jax import lax
from jax.experimental import pallas as pl
from jax.experimental.pallas import tpu as pltpu
from jax.sharding import PartitionSpec as P

HEADS = 8
LAYERS = 2
DMAX = 8
CAP = 13
STEP = 10
PER_LAYER = 17
TILES = PER_LAYER * LAYERS

BETA_ONE = 0.9
BETA_TWO = 0.999
EPSILON = 1e-08
WEIGHT_DECAY = 0.01
LEARN_RATE = 0.02
QUERY_RATE = 0.4
HALF_ROOT = 0.7071067811865476
NEGATIVE = -1e30

BF = jnp.bfloat16
F32 = jnp.float32
HALO = 32
WIDE = 256
KEYS = 2 * LAYERS
MAIN = 20
LAZY = KEYS + MAIN * LAYERS
LAZY_EACH = 8
BLOCKS = LAZY + LAZY_EACH * LAYERS
PHASES = ((0, KEYS), (KEYS, MAIN), (KEYS + MAIN, MAIN), (LAZY, LAZY_EACH * LAYERS))
FILM_ORDER = (11, 12, 13, 14, 8, 9)
FILM = 2 * len(FILM_ORDER)
LOW_RANK = 1 + len(FILM_ORDER)
HOP_ROWS = (24, 8, 16, 32)
ORDER = (
    ("prep", 0), ("prep", 1), ("cross", 0), "fc", ("cross", 1), ("prep", 2), ("end", 0),
    ("end", 1), ("first", 0), "fx", ("cross", 2), ("second", 0), ("first", 1), ("third", 0),
    ("pr", 0), ("pr", 1), "fl", ("pr", 2), ("pr", 3), ("end", 2), "att0", "att1", ("second", 1),
    "hsA", "condt", ("first", 2), ("end", 3), "heA", "hsB", ("third", 1), "heB", "hsC",
    ("second", 2), "heC", ("first", 3), "win0", "gates0a", ("third", 2), "gates0b", "res0",
    "gatt0", "skip0", "win1", "gates1a", "gates1b", "gg1a", "gatt1", "gg1b", "winb1",
    ("give", 1, 1), "fg1b", ("give", 1, 0), "fg1a", "out1", ("keep", 1, 1), ("second", 3),
    ("keep", 1, 0), ("one", 1), "gg0a", "gg0b", "winb0", ("give", 0, 1), "fg0b", ("give", 0, 0),
    "fg0a", "hs3", ("two", 1), ("keep", 0, 1), ("keep", 0, 0), ("one", 0), ("third", 3), "he3",
    ("three", 1), ("two", 0), "fb1", ("four", 1), ("three", 0), "fb0", "bundle", ("four", 0),
    ("five", 1), "low", "end",
)

MEM = 64 * 1024 * 1024 - 256 * 1024
MESH = pl.DeviceIdType.MESH


def block_table():
    table = {}
    for layer in range(LAYERS):
        base = PER_LAYER * layer
        for side in range(2):
            table[base + 10, side] = 2 * layer + side
        start = KEYS + MAIN * layer
        for part in range(4):
            for tap in range(4):
                table[base + 2 * tap + part // 2, part % 2] = start + 5 * part + tap
            table[base + 15 + part // 2, part % 2] = start + 5 * part + 4
    return table


BLOCK_OF = block_table()
FILM_OF = {
    (PER_LAYER * layer + tile, side): FILM * layer + 2 * place + side
    for layer in range(LAYERS)
    for place, tile in enumerate(FILM_ORDER)
    for side in range(2)
}


def mm(a, b):
    return lax.dot_general(a, b, (((1,), (0,)), ((), ())), preferred_element_type=F32)


def mm_nt(a, b):
    return lax.dot_general(a, b, (((1,), (1,)), ((), ())), preferred_element_type=F32)


def split(a):
    high = a.astype(BF)
    return high, (a - high.astype(F32)).astype(BF)


def mm_fine(a, b):
    high, low = split(a)
    return mm(high, b) + mm(low, b)


def mm_nt_fine(a, b):
    high, low = split(a)
    return mm_nt(high, b) + mm_nt(low, b)


def mm_nt_pairs(a, blocks):
    total = None
    for place, block in enumerate(blocks):
        term = mm_nt_fine(a[:, place * WIDE : (place + 1) * WIDE], block)
        total = term if total is None else total + term
    return total


def window(ref, start, count, width):
    group, rest = lax.div(start, 8), lax.rem(start, 8)
    groups = ref[pl.ds(group, count // 8 + 1), :, 0:width]
    turned = pltpu.roll(groups, lax.rem(8 - rest, 8), 1)
    row = lax.broadcasted_iota(jnp.int32, (1, 8, 1), 1)
    return jnp.where(row < 8 - rest, turned[:-1], turned[1:]).reshape(count, width)


def in_eights(value):
    return value.reshape(value.shape[0] // 8, 8, value.shape[1])


def place_of(n_seq):
    seq, grp = lax.axis_index("seq"), lax.axis_index("grp")
    z, y = lax.div(seq, 2), lax.rem(seq, 2)
    x, c = lax.div(grp, 2), lax.rem(grp, 2)
    return seq, grp, z, y, x, c


def greet(n_seq, seq, grp, groups):
    barrier = pltpu.get_barrier_semaphore()

    def one(k, carry):
        pl.semaphore_signal(
            barrier, inc=1, device_id={"seq": lax.rem(seq + k, n_seq), "grp": grp}, device_id_type=MESH
        )
        return carry

    lax.fori_loop(1, n_seq, one, 0)
    for k in range(1, groups):
        pl.semaphore_signal(
            barrier, inc=1, device_id={"seq": seq, "grp": lax.rem(grp + k, groups)}, device_id_type=MESH
        )
    pl.semaphore_wait(barrier, n_seq - 1 + groups - 1)


def any_spec():
    return pl.BlockSpec(memory_space=pl.ANY)


def vmem_spec():
    return pl.BlockSpec(memory_space=pltpu.VMEM)


def smem_spec():
    return pl.BlockSpec(memory_space=pltpu.SMEM)


def head_mask():
    row = lax.broadcasted_iota(jnp.int32, (HEADS, 512), 0)
    column = lax.broadcasted_iota(jnp.int32, (HEADS, 512), 1)
    return lax.div(column, 512 // HEADS) == row


def block_diagonal(rows):
    column = lax.div(lax.broadcasted_iota(jnp.int32, rows.shape, 1), 512 // HEADS)
    return jnp.concatenate([jnp.where(column == h, rows, 0.0) for h in range(HEADS)], axis=0)


def same_rows(row):
    return jnp.broadcast_to(row, (8, row.shape[1]))


def pack(vectors):
    pieces = [v[:, 128 * i : 128 * (i + 1)] for v in vectors for i in range(v.shape[1] // 128)]
    spare = -len(pieces) % 8
    if spare:
        pieces.append(jnp.zeros((spare, 128), pieces[0].dtype))
    return jnp.concatenate(pieces, axis=0)


def unpack(rows, place, pieces=4):
    return jnp.concatenate(
        [rows[pieces * place + i : pieces * place + i + 1] for i in range(pieces)], axis=1
    )


def step_kernel(
    n_seq, owners_ref, dil_ref, lengths_ref, pairing_ref, embed_ref, queries_ref, master_hbm,
    prompts_hbm, frames_hbm, cond_hbm, gout_hbm, gskip_hbm,
    block_hbm, skip_hbm, gframes_hbm, out_hbm, low_ref, dquery_ref,
    w, gs, prep, core_in, x_in, fr, fr_in, fx, ff, red_in, one_a, one_b, two_in, z_in, fin,
    xe, cat, slopes, gated, x1, bh, bb, sht, condt, gatt, bx, sk,
    master, prompt, probs, left, vec, sums, bundle,
    hop_src, hop_in,
    in_sem, prompt_sem, out_sem, hsend, hrecv, send, recv, zsend, zrecv, hop_send, hop_recv,
):
    seq, grp, z, y, x, c = place_of(n_seq)
    nz = n_seq // 2
    rows = prep.shape[1]
    own = frames_hbm.shape[1]
    grid_rows = own + 2 * HALO
    top = HALO + own
    channels = 512
    number = queries_ref.shape[1]
    sib, across, other_y = x * 2 + 1 - c, (1 - x) * 2 + c, z * 2 + 1 - y
    mine, theirs = 2 * c + x, 2 * c + 1 - x

    local_in = [
        pltpu.make_async_copy(a, b, in_sem.at[i])
        for i, (a, b) in enumerate(
            (
                (master_hbm, master),
                (frames_hbm.at[0], xe.at[pl.ds(HALO, own)]),
                (cond_hbm.at[0], cat.at[pl.ds(HALO, own), pl.ds(1536, channels)]),
                (gout_hbm.at[0], bb.at[pl.ds(HALO, own), pl.ds(0, channels)]),
                (gskip_hbm.at[0], bb.at[pl.ds(HALO, own), pl.ds(channels, channels)]),
            )
        )
    ]
    for copy in local_in:
        copy.start()

    def prompt_copy(turn, i):
        rows_now, columns = pl.ds(0, prompt.shape[0]), pl.ds((i % 2) * channels, channels)
        return pltpu.make_async_copy(
            prompts_hbm.at[4 * turn + i], slopes.at[i // 2, rows_now, columns], prompt_sem.at[i]
        )

    for i in range(4):
        prompt_copy(0, i).start()

    greet(n_seq, seq, grp, 4)

    waits = []
    used = [0]

    def remote(src, dst, to_seq, to_grp, sent=None):
        place = used[0]
        used[0] += 1
        copy = pltpu.make_async_remote_copy(
            src_ref=src,
            dst_ref=dst,
            send_sem=send.at[place],
            recv_sem=recv.at[place],
            device_id={"seq": to_seq, "grp": to_grp},
            device_id_type=MESH,
        )
        copy.start()
        (waits if sent is None else sent).append(copy)
        return copy

    after, before = lax.rem(seq + 1, n_seq), lax.rem(seq + n_seq - 1, n_seq)
    halos = []
    for ref, buffer, column in (
        (frames_hbm, xe, 0),
        (cond_hbm, cat, 1536),
        (gout_hbm, bb, 0),
        (gskip_hbm, bb, channels),
    ):
        for start, at, target in ((own - HALO, 0, after), (0, top, before)):
            place = len(halos)
            copy = pltpu.make_async_remote_copy(
                src_ref=ref.at[0, pl.ds(start, HALO)],
                dst_ref=buffer.at[pl.ds(at, HALO), pl.ds(column, channels)],
                send_sem=hsend.at[place],
                recv_sem=hrecv.at[place],
                device_id={"seq": target, "grp": grp},
                device_id_type=MESH,
            )
            copy.start()
            halos.append(copy)

    slots, flags = [], []
    count = jnp.int32(0)
    for tile in range(TILES):
        flag = (owners_ref[tile] == grp).astype(jnp.int32)
        slots.append(jnp.minimum(count, CAP - 1))
        flags.append(flag.astype(F32))
        count = count + flag

    def rounded(tile):
        return (master[slots[tile]] * flags[tile]).astype(BF)

    def ready(tiles, buffer, table):
        for tile in tiles:
            value = rounded(tile)
            buffer[table[tile, 0]] = value[:, :WIDE]
            buffer[table[tile, 1]] = value[:, WIDE:]

    def merge_start(phase):
        base, blocks = PHASES[phase]
        each = blocks // 4
        return remote(
            prep.at[pl.ds(base + 2 * (1 - c) * each, 2 * each)],
            core_in.at[pl.ds(base // 2, 2 * each)],
            seq, sib,
        )

    def merge_cross(phase, copy):
        base, blocks = PHASES[phase]
        each = blocks // 4
        copy.wait_recv()

        def add(i, carry):
            place = base // 2 + i
            core_in[place] = core_in[place] + prep[base + 2 * c * each + i]
            return carry

        lax.fori_loop(0, 2 * each, add, 0)
        return remote(
            core_in.at[pl.ds(base // 2 + (1 - x) * each, each)],
            x_in.at[pl.ds(base // 4, each)],
            seq, across,
        )

    def view(phase, quarter, zz, yy):
        base, blocks = PHASES[phase]
        each = blocks // 4
        return w.at[pl.ds(base + quarter * each, each), zz, yy]

    low_z, high_z = pl.ds(0, nz // 2), pl.ds(nz // 2, nz - nz // 2)
    all_z = pl.ds(0, nz)
    gathering, legs = [], {}

    def spread(ref, to_seq, to_grp):
        return remote(ref, ref, to_seq, to_grp, gathering)

    def merge_end(phase, copy):
        base, blocks = PHASES[phase]
        each = blocks // 4
        copy.wait_recv()

        def settle(i, carry):
            w[base + mine * each + i, z, y] = (
                core_in[base // 2 + x * each + i] + x_in[base // 4 + i]
            )
            return carry

        lax.fori_loop(0, each, settle, 0)

    def spread_z(phase):
        ref = view(phase, mine, z, y)
        legs[phase] = [spread(ref, lax.rem(z + k, nz) * 2 + y, grp) for k in range(1, nz)]

    core_legs = {}

    def first(phase):
        for copy in legs[phase]:
            copy.wait_recv()
        lower, upper = view(phase, mine, low_z, y), view(phase, mine, high_z, y)
        one = [spread(lower, other_y, grp), spread(upper, seq, across)]
        two = [spread(lower, seq, across), spread(upper, other_y, grp)]
        legs[phase] = (one, two)
        core_legs[phase] = [spread(view(phase, mine, all_z, y), seq, sib)]

    def second(phase):
        one, two = legs[phase]
        for copy in one:
            copy.wait_recv()
        lower, upper = view(phase, mine, low_z, 1 - y), view(phase, theirs, high_z, y)
        two += [spread(lower, seq, across), spread(upper, other_y, grp)]
        core_legs[phase] += [spread(lower, seq, sib), spread(upper, seq, sib)]

    def third(phase):
        for copy in legs[phase][1]:
            copy.wait_recv()
        core_legs[phase] += [
            spread(view(phase, theirs, low_z, pl.ds(0, 2)), seq, sib),
            spread(view(phase, mine, high_z, 1 - y), seq, sib),
            spread(view(phase, theirs, high_z, 1 - y), seq, sib),
        ]

    def arrived(phase):
        for copy in core_legs[phase]:
            copy.wait_recv()

    def hop_refs(j):
        start = sum(HOP_ROWS[:j])
        spot = pl.ds(start, HOP_ROWS[j])
        return hop_src.at[spot], hop_in.at[seq, spot], hop_in.at[:, spot]

    def hop_copy(j, k):
        src, dst, _ = hop_refs(j)
        return pltpu.make_async_remote_copy(
            src_ref=src,
            dst_ref=dst,
            send_sem=hop_send.at[j, k],
            recv_sem=hop_recv.at[j, k],
            device_id={"seq": lax.rem(seq + k, n_seq), "grp": grp},
            device_id_type=MESH,
        )

    def hop_start(j, value):
        src, dst, _ = hop_refs(j)
        value = value.astype(src.dtype)
        src[...] = value
        dst[...] = value

        def one(k, carry):
            hop_copy(j, k).start()
            return carry

        lax.fori_loop(1, n_seq, one, 0)

    def hop_end(j):
        def one(k, carry):
            hop_copy(j, k).wait()
            return carry

        lax.fori_loop(1, n_seq, one, 0)
        _, _, whole = hop_refs(j)

        def add(i, total):
            return total + whole[i].astype(F32)

        return lax.fori_loop(0, n_seq, add, jnp.zeros((HOP_ROWS[j], 128), F32))

    position = lax.broadcasted_iota(jnp.int32, (channels, rows), 0)
    column = lax.broadcasted_iota(jnp.int32, (channels, rows), 1)
    chosen = jnp.where(position == column + seq * rows, 1.0, 0.0).astype(BF)

    def pick(v):
        return mm_fine(v, chosen)

    def film_block(layer, place):
        return ff[FILM * layer + place]

    def film_rows(layer, v, places):
        return jnp.concatenate([mm_fine(v, film_block(layer, i)) for i in places], axis=1)

    def film_back(layer, v, places):
        total = None
        for i, place in enumerate(places):
            high, rest = split(v[:, i * WIDE : (i + 1) * WIDE])
            both = jnp.concatenate([high.astype(F32), rest.astype(F32)], axis=0).astype(BF)
            whole = w[LAZY + LAZY_EACH * layer + place].reshape(channels, WIDE)
            term = mm_nt(both, whole)
            total = term if total is None else total + term
        return total[:8] + total[8:]

    def key_blocks(layer):
        return [w[2 * layer + side].reshape(channels, WIDE) for side in range(2)]

    mask = head_mask()

    def attention(layer):
        spread = block_diagonal(queries_ref[layer])
        probe = mm_nt_pairs(spread, key_blocks(layer))
        pr = prompt[...]
        scores = mm_nt_fine(probe, pr) * 0.125
        live = lax.broadcasted_iota(jnp.int32, scores.shape, 1) < lengths_ref[pairing_ref[0]]
        scores = jnp.where(live, scores, NEGATIVE)
        weight = jnp.exp(scores - jnp.max(scores, axis=1, keepdims=True))
        value = weight / jnp.sum(weight, axis=1, keepdims=True)
        probs[layer] = value.astype(BF)
        mean = jnp.concatenate(
            [
                jnp.mean(value[h * number : (h + 1) * number], axis=0, keepdims=True)
                for h in range(HEADS)
            ],
            axis=0,
        )
        seen = mm_fine(mean, pr)
        left[layer, 0:8] = seen
        return seen

    def wblock(layer, place):
        return w[KEYS + MAIN * layer + place].reshape(channels, WIDE)

    def inside(low, count):
        row = lax.broadcasted_iota(jnp.int32, (count, 1), 0) + (low - HALO) + seq * own
        return (row >= 0) & (row < n_seq * own)

    def windows_forward(layer):
        low = 16 * layer
        high = grid_rows - low
        scale, shift = 1.0 + vec[layer, 0:1], vec[layer, 1:2]
        here = xe[...].astype(F32) if layer == 0 else x1[...]
        shifted = (here * scale + shift).astype(BF).astype(F32)
        shifted = jnp.where(inside(0, grid_rows), shifted, 0.0)
        groups = grid_rows // 8
        bh[0] = jnp.zeros((8, channels), F32)
        bh[1 : 1 + groups] = in_eights(shifted)
        bh[1 + groups :] = jnp.zeros((3, 8, channels), F32)
        sht[layer] = jnp.transpose(shifted[HALO:top]).astype(BF)
        for tap in range(3):
            start = 8 + low + (tap - 1) * dil_ref[layer]
            cat[low:high, tap * channels : (tap + 1) * channels] = window(
                bh, start, high - low, channels
            ).astype(BF)

    def gates(layer, first_row, rows_now):
        spot = slice(first_row, first_row + rows_now)
        value = cat[spot, 0:2048]
        for part in range(2):
            columns = slice(part * WIDE, (part + 1) * WIDE)
            base = KEYS + MAIN * layer + 5 * part
            lhs = mm(value, w[base : base + 4].reshape(2048, WIDE))
            tangent = jnp.tanh(lhs + vec[layer, 2:3, columns])
            rhs = mm(value, w[base + 10 : base + 14].reshape(2048, WIDE))
            opening = jax.nn.sigmoid(rhs + vec[layer, 3:4, columns])
            gate = tangent * opening
            gated[spot, columns] = gate.astype(BF)
            slopes[layer, spot, columns] = (opening * (1.0 - tangent * tangent)).astype(BF)
            other = slice(channels + part * WIDE, channels + (part + 1) * WIDE)
            slopes[layer, spot, other] = (gate * (1.0 - opening)).astype(BF)

    def residual(layer, first_row, rows_now):
        value = gated[first_row : first_row + rows_now]
        for part in range(2):
            columns = slice(part * WIDE, (part + 1) * WIDE)
            term = mm(value, wblock(layer, 5 * part + 4))
            if layer == 0:
                base = xe[first_row : first_row + rows_now, columns].astype(F32)
                x1[first_row : first_row + rows_now, columns] = (base + term) * HALF_ROOT
            else:
                base = x1[first_row : first_row + rows_now, columns]
                x1[first_row : first_row + rows_now, columns] = (base + term) * HALF_ROOT

    def skipped(layer, first_row, rows_now):
        value = gated[first_row : first_row + rows_now]
        spot = slice(first_row - HALO, first_row - HALO + rows_now)
        for part in range(2):
            columns = slice(part * WIDE, (part + 1) * WIDE)
            term = mm(value, wblock(layer, 5 * part + 14))
            if layer == 0:
                sk[spot, columns] = term
            else:
                sk[spot, columns] = sk[spot, columns] + term

    low, high = 16, grid_rows - 16

    def gate_grads(layer, first_row, rows_now):
        spot = slice(first_row, first_row + rows_now)
        bb[spot, 0:channels] = (bx[spot] * HALF_ROOT).astype(BF)
        branch = jnp.concatenate([wblock(layer, 5 * part + 4) for part in range(4)], axis=1)
        back = mm_nt(bb[spot], branch)
        keep = inside(first_row, rows_now)
        for side in range(2):
            columns = slice(side * channels, (side + 1) * channels)
            value = back * slopes[layer, spot, columns].astype(F32)
            middle = slice((2 + side) * channels, (3 + side) * channels)
            cat[spot, middle] = jnp.where(keep, value, 0.0).astype(BF)

    def windows_backward(layer):
        reach, limit = (low, high) if layer else (HALO, top)
        edge = 1 + low // 8
        bh[0:edge] = jnp.zeros((edge, 8, channels), F32)
        bh[1 + high // 8 :] = jnp.zeros((edge + 2, 8, channels), F32)
        for side in range(2):
            middle = slice((2 + side) * channels, (3 + side) * channels)
            value = cat[low:high, middle].astype(F32)
            bh[edge : 1 + high // 8] = in_eights(value)
            total = jnp.sum(value[HALO - low : top - low], axis=0, keepdims=True)
            sums[layer, 2 + side : 3 + side] = total
            for tap in (0, 2):
                start = 8 + reach - (tap - 1) * dil_ref[layer]
                columns = slice((2 * tap + side) * channels, (2 * tap + side + 1) * channels)
                cat[reach:limit, columns] = window(bh, start, limit - reach, channels).astype(BF)

    def frame_grads(layer, first_row, rows_now):
        spot = slice(first_row, first_row + rows_now)
        taps = jnp.concatenate(
            [wblock(layer, 5 * part + tap) for tap in range(3) for part in range(4)], axis=1
        )
        back = mm_nt(cat[spot], taps)
        if layer:
            here = x1[spot]
            row = lax.broadcasted_iota(jnp.int32, (rows_now, 1), 0) + first_row
            kept = jnp.where((row >= HALO) & (row < top), back, 0.0)
        else:
            here = xe[spot].astype(F32)
            kept = back
        sums[layer, 0:1] += jnp.sum(kept * here, axis=0, keepdims=True)
        sums[layer, 1:2] += jnp.sum(kept, axis=0, keepdims=True)
        bx[spot] = bx[spot] * HALF_ROOT + back * (1.0 + vec[layer, 0:1])

    def weight_grad(layer, part, i):
        if i < 4:
            tap = i if i < 3 else 1
            start = pl.multiple_of(tap * 1024 + part * WIDE, WIDE)
            lhs = sht[layer] if i < 3 else condt[...]
            return mm(lhs, cat[HALO:top, pl.ds(start, WIDE)])
        start = pl.multiple_of(part * WIDE, WIDE)
        return mm(gatt[layer], bb[HALO:top, pl.ds(start, WIDE)])

    core_sent = {}

    def give(layer, xx):
        part = 2 * (1 - c) + xx
        buffer, base = (gs, 0) if layer else (w, KEYS + MAIN)
        for i in range(5):
            value = weight_grad(layer, part, i).astype(BF)
            buffer[base + 5 * xx + i] = value.reshape(nz, 2, rows, WIDE)
        core_sent[layer, xx] = remote(
            buffer.at[pl.ds(base + 5 * xx, 5)], red_in.at[layer, pl.ds(5 * xx, 5)], seq, sib
        )

    def keep(layer, xx):
        part = 2 * c + xx
        core_sent[layer, xx].wait_recv()
        for i in range(5):
            value = weight_grad(layer, part, i).reshape(nz, 2, rows, WIDE)
            spot = 5 * xx + i
            red_in[layer, spot] = (red_in[layer, spot].astype(F32) + value).astype(BF)

    ones, twos, zs = {}, {}, {}
    near = nz // 2

    def red_one(layer):
        ones[layer] = [
            remote(red_in.at[layer, pl.ds(5 * (1 - x), 5), low_z], one_a.at[layer], seq, across),
            remote(red_in.at[layer, :, high_z, 1 - y], one_b.at[layer], other_y, grp),
        ]

    def plus(a, b):
        return (a.astype(F32) + b.astype(F32)).astype(BF)

    def red_two(layer):
        for copy in ones[layer]:
            copy.wait_recv()

        def lower(i, carry):
            one_a[layer, i] = plus(one_a[layer, i], red_in[layer, 5 * x + i, 0:near])
            return carry

        lax.fori_loop(0, 5, lower, 0)
        twos[layer] = [
            remote(one_a.at[layer, :, :, 1 - y], two_in.at[layer, :, low_z], other_y, grp)
        ]

        def upper(i, carry):
            one_b[layer, i] = plus(one_b[layer, i], red_in[layer, i, near:nz, y])
            return carry

        lax.fori_loop(0, 10, upper, 0)
        twos[layer].append(
            remote(
                one_b.at[layer, pl.ds(5 * (1 - x), 5)], two_in.at[layer, :, high_z], seq, across
            )
        )

    def red_three(layer):
        for copy in twos[layer]:
            copy.wait_recv()

        def body(i, carry):
            two_in[layer, i, 0:near] = plus(two_in[layer, i, 0:near], one_a[layer, i, :, y])
            two_in[layer, i, near:nz] = plus(two_in[layer, i, near:nz], one_b[layer, 5 * x + i])
            return carry

        lax.fori_loop(0, 5, body, 0)
        zs[layer] = []
        for k in range(1, nz):
            zd = lax.rem(z + k, nz)
            zs[layer].append(remote(two_in.at[layer, :, zd], z_in.at[layer, k - 1], zd * 2 + y, grp))

    lasts = {}
    outs = []

    def local_out(src, dst):
        copy = pltpu.make_async_copy(src, dst, out_sem.at[len(outs)])
        copy.start()
        outs.append(copy)

    def red_four(layer):
        for copy in zs[layer]:
            copy.wait_recv()

        def body(i, carry):
            total = two_in[layer, i, z].astype(F32)
            for k in range(1, nz):
                total = total + z_in[layer, k - 1, i].astype(F32)
            fin[layer, i] = total.astype(BF)
            return carry

        lax.fori_loop(0, 5, body, 0)
        src, dst = fin.at[layer], out_hbm.at[layer, mine]
        lasts[layer] = [remote(src, dst, seq, across), remote(src, dst, seq, sib)]
        if not layer:
            lasts[layer].append(remote(src, dst, seq, (1 - x) * 2 + 1 - c))
        local_out(src, dst)

    def red_five(layer):
        lasts[layer][0].wait_recv()
        ref = out_hbm.at[layer, theirs]
        lasts[layer].append(remote(ref, ref, seq, sib))

    ops = {}

    def op(*key):
        def keep_op(body):
            ops[key] = body
            return body

        return keep_op

    main_tiles = (0, 1, 2, 3, 4, 5, 6, 7, 15, 16)
    merges, crosses, film_sent, seen, hops = {}, {}, {}, {}, {}
    half = fr.shape[0] // 2
    half_spot = pl.ds(c * half, half)
    size_all, size_mid, size_own = grid_rows // 2, (high - low) // 2, own // 2
    embed = same_rows(embed_ref[...].astype(F32))

    for phase in range(3):

        @op("prep", phase)
        def _(phase=phase):
            if phase:
                tiles = [PER_LAYER * (phase - 1) + t for t in main_tiles]
            else:
                tiles = [PER_LAYER * layer + 10 for layer in range(LAYERS)]
            ready(tiles, prep, BLOCK_OF)
            merges[phase] = merge_start(phase)

        @op("cross", phase)
        def _(phase=phase):
            crosses[phase] = merge_cross(phase, merges[phase])

        @op("end", phase)
        def _(phase=phase):
            merge_end(phase, crosses[phase])
            spread_z(phase)

    for phase in range(4):
        for name, body in (("first", first), ("second", second), ("third", third)):

            @op(name, phase)
            def _(phase=phase, body=body):
                body(phase)

    @op("end", 3)
    def _():
        film_rows_here()
        base, each = PHASES[3][0], PHASES[3][1] // 4

        def settle(i, carry):
            w[base + mine * each + i, z, y] = ff[FILM * c + each * x + i]
            return carry

        lax.fori_loop(0, each, settle, 0)
        spread_z(3)

    @op("fc")
    def _():
        for layer in range(LAYERS):
            ready([PER_LAYER * layer + t for t in FILM_ORDER], fr, FILM_OF)
        film_sent[0] = remote(fr.at[pl.ds((1 - c) * half, half)], fr_in, seq, sib)

    @op("fx")
    def _():
        film_sent[0].wait_recv()
        fr_in[...] = fr_in[...] + fr[half_spot]
        film_sent[1] = remote(fr_in, fx, seq, across)

    @op("fl")
    def _():
        film_sent[1].wait_recv()
        ff[half_spot] = fr_in[...] + fx[...]
        film_sent[2] = remote(ff.at[half_spot], ff.at[half_spot], seq, sib)

    for turn in range(4):

        @op("pr", turn)
        def _(turn=turn):
            total = prompt[...] if turn else None
            for i in range(4):
                prompt_copy(turn, i).wait()
                flag = (pairing_ref[0] == 4 * turn + i).astype(F32).astype(BF)
                part = slice((i % 2) * channels, (i % 2 + 1) * channels)
                term = slopes[i // 2, 0 : prompt.shape[0], part] * flag
                total = term if total is None else total + term
            prompt[...] = total
            if turn < 3:
                for i in range(4):
                    prompt_copy(turn + 1, i).start()

    def gathered():
        while gathering:
            gathering.pop().wait_send()

    def film_rows_here():
        if 3 not in film_sent:
            film_sent[2].wait_recv()
            film_sent[3] = True

    @op("condt")
    def _():
        local_in[2].wait()
        condt[...] = jnp.transpose(cat[HALO:top, 1536:2048].astype(F32)).astype(BF)

    @op("att0")
    def _():
        arrived(0)
        seen[0] = attention(0)

    @op("att1")
    def _():
        seen[1] = attention(1)

    @op("hsA")
    def _():
        film_rows_here()
        vectors = []
        for layer in range(LAYERS):
            mixed = film_rows(layer, pick(seen[layer]), (0, 1))
            vectors.append(jnp.sum(jnp.where(mask, mixed, 0.0), axis=0, keepdims=True))
            steps = film_rows(layer, pick(embed), (8, 9, 10, 11))
            vectors += [steps[0:1, :channels], steps[0:1, channels:]]
        hop_start(0, pack(vectors))

    @op("heA")
    def _():
        total = hop_end(0)
        hops["mixed"] = [unpack(total, 3 * layer) for layer in range(LAYERS)]
        for layer in range(LAYERS):
            vec[layer, 2:3] = unpack(total, 3 * layer + 1)
            vec[layer, 3:4] = unpack(total, 3 * layer + 2)

    @op("hsB")
    def _():
        mixed = hops["mixed"]
        hop_start(
            1,
            pack([film_rows(l, pick(same_rows(mixed[l])), (2, 3))[0:1] for l in range(LAYERS)]),
        )

    @op("heB")
    def _():
        total = hop_end(1)
        hops["pooled"] = [unpack(total, layer) for layer in range(LAYERS)]

    @op("hsC")
    def _():
        vectors = []
        for layer in range(LAYERS):
            pooled = hops["pooled"][layer]
            film = film_rows(layer, pick(same_rows(pooled)), (4, 5, 6, 7))
            vectors += [film[0:1, :channels], film[0:1, channels:]]
        hop_start(2, pack(vectors))

    @op("heC")
    def _():
        total = hop_end(2)
        for layer in range(LAYERS):
            vec[layer, 0:1] = unpack(total, 2 * layer)
            vec[layer, 1:2] = unpack(total, 2 * layer + 1)
            left[layer, 8:9] = hops["mixed"][layer]
            left[layer, 9:10] = hops["pooled"][layer]
            left[layer, 10:11] = embed[0:1]
            left[layer, 11:16] = jnp.zeros((5, channels), F32)

    @op("win0")
    def _():
        local_in[1].wait()
        for copy in halos[:4]:
            copy.wait_recv()
        windows_forward(0)

    @op("win1")
    def _():
        local_in[3].wait()
        local_in[4].wait()
        for copy in halos[4:]:
            copy.wait_recv()
        bx[...] = bb[:, 0:channels].astype(F32)
        windows_forward(1)

    for layer in range(LAYERS):
        start, size = (low, size_mid) if layer else (0, size_all)
        for part, name in enumerate("ab"):
            first_row = start + part * size

            @op(f"gates{layer}{name}")
            def _(layer=layer, first_row=first_row, size=size, part=part):
                if not part:
                    arrived(1 + layer)
                gates(layer, first_row, size)

        @op(f"gatt{layer}")
        def _(layer=layer):
            gatt[layer] = jnp.transpose(gated[HALO:top].astype(F32)).astype(BF)

    @op("res0")
    def _():
        for part in range(2):
            residual(0, part * size_all, size_all)

    @op("skip0")
    def _():
        for part in range(2):
            skipped(0, HALO + part * size_own, size_own)

    @op("out1")
    def _():
        for part in range(2):
            residual(1, HALO + part * size_own, size_own)
            skipped(1, HALO + part * size_own, size_own)
        local_out(x1.at[pl.ds(HALO, own)], block_hbm.at[0])
        local_out(sk, skip_hbm.at[0])

    for layer in range(LAYERS):
        for part, name in enumerate("ab"):

            @op(f"gg{layer}{name}")
            def _(layer=layer, part=part):
                if layer and not part:
                    sums[...] = jnp.zeros_like(sums)
                gate_grads(layer, low + part * size_mid, size_mid)

            @op(f"fg{layer}{name}")
            def _(layer=layer, part=part):
                if layer:
                    frame_grads(1, low + part * size_mid, size_mid)
                else:
                    frame_grads(0, HALO + part * size_own, size_own)

        @op(f"winb{layer}")
        def _(layer=layer):
            windows_backward(layer)

        for xx in range(2):

            @op("give", layer, xx)
            def _(layer=layer, xx=xx):
                if not layer:
                    gathered()
                give(layer, xx)

            @op("keep", layer, xx)
            def _(layer=layer, xx=xx):
                keep(layer, xx)

        for name, body in (("one", red_one), ("two", red_two), ("three", red_three)):

            @op(name, layer)
            def _(layer=layer, body=body):
                body(layer)

        @op("four", layer)
        def _(layer=layer):
            red_four(layer)

    @op("five", 1)
    def _():
        red_five(1)

    @op("hs3")
    def _():
        local_out(bx.at[pl.ds(HALO, own)], gframes_hbm.at[0])
        hop_start(3, pack([sums[l, i : i + 1] for l in range(LAYERS) for i in range(4)]))

    @op("he3")
    def _():
        total = hop_end(3)
        hops["sides"] = [[unpack(total, 4 * l + i) for i in range(4)] for l in range(LAYERS)]

    rt_at, dq_at, lt_at = 0, 16 * LAYERS, (16 + number) * LAYERS

    def attention_back(layer):
        pr = prompt[...]
        sides = hops["sides"][layer]
        dfilm = same_rows(jnp.concatenate(sides[0:2], axis=1))
        dpooled = film_back(layer, dfilm, (4, 5, 6, 7))
        dmixed = film_back(layer, dpooled, (2, 3))
        dseen = film_back(layer, jnp.where(mask, dmixed, 0.0), (0, 1))
        dmean = mm_nt_fine(dseen, pr) * (1.0 / number)
        dprobs = jnp.concatenate(
            [jnp.broadcast_to(dmean[h : h + 1], (number, channels)) for h in range(HEADS)], axis=0
        )
        value = probs[layer].astype(F32)
        inner = jnp.sum(dprobs * value, axis=1, keepdims=True)
        dprobe = mm_fine(value * (dprobs - inner) * 0.125, pr)
        keys = key_blocks(layer)
        dspread = jnp.concatenate([mm_fine(dprobe, keys[0]), mm_fine(dprobe, keys[1])], axis=1)
        head = lax.div(lax.broadcasted_iota(jnp.int32, (number, channels), 1), channels // HEADS)
        dquery = jnp.zeros((number, channels), F32)
        for h in range(HEADS):
            dquery = dquery + jnp.where(head == h, dspread[h * number : (h + 1) * number], 0.0)
        start = dq_at + number * layer
        bundle[grp, start : start + number] = dquery.astype(BF)
        lefts = jnp.concatenate([left[layer], jnp.zeros((112, channels), F32)], axis=0)
        bh[0 : channels // 8, :, 0:256] = in_eights(jnp.transpose(dprobe))
        bh[0 : channels // 8, :, 256:384] = in_eights(jnp.transpose(lefts))
        eights = pl.ds(seq * (rows // 8), rows // 8)
        place = lt_at + rows * layer
        bundle[grp, place : place + rows, 0:384] = bh[eights, :, 0:384].reshape(rows, 384).astype(BF)
        place = rt_at + 16 * layer
        bundle[grp, place : place + 16] = jnp.concatenate(
            sides + [dpooled[0:1], dmixed[0:1], jnp.zeros((10, channels), F32)], axis=0
        ).astype(BF)

    @op("fb1")
    def _():
        arrived(3)
        attention_back(1)

    @op("fb0")
    def _():
        attention_back(0)

    bundles = []

    @op("bundle")
    def _():
        for k in range(1, 4):
            ref = bundle.at[grp]
            bundles.append(remote(ref, ref, seq, lax.rem(grp + k, 4)))

    @op("low")
    def _():
        for copy in bundles:
            copy.wait_recv()
        for layer in range(LAYERS):
            spot = slice(dq_at + number * layer, dq_at + number * (layer + 1))
            total = bundle[0, spot].astype(F32)
            for k in range(1, 4):
                total = total + bundle[k, spot].astype(F32)
            dquery_ref[layer] = total
        at = lax.broadcasted_iota(jnp.int32, (16, channels), 0)
        for layer in range(LAYERS):
            spread_rows = block_diagonal(queries_ref[layer]).astype(BF)
            spot = slice(lt_at + rows * layer, lt_at + rows * (layer + 1))
            probe = bundle[0, spot, 0:256].astype(F32)
            for k in range(1, 4):
                probe = probe + bundle[k, spot, 0:256].astype(F32)
            low_ref[layer, 0] = mm(probe.astype(BF), spread_rows).astype(BF)
            total = None
            for k in range(4):
                right = bundle[k, 16 * layer : 16 * layer + 16].astype(F32)
                value = jnp.concatenate(
                    [jnp.where(mask, right[5:6], 0.0), jnp.zeros((8, channels), F32)], axis=0
                )
                pieces = [value] + [
                    jnp.where(at == row, right[i : i + 1], 0.0)
                    for i, row in ((4, 8), (0, 9), (1, 9), (2, 10), (3, 10))
                ]
                side = jnp.concatenate(pieces, axis=1).astype(BF)
                term = mm(bundle[k, spot, 256:272], side)
                total = term if total is None else total + term
            for i in range(6):
                low_ref[layer, 1 + i] = total[:, i * channels : (i + 1) * channels].astype(BF)

    @op("end")
    def _():
        for copies in lasts.values():
            for copy in copies[1:]:
                copy.wait_recv()
        lasts[0][0].wait_recv()
        for copy in outs:
            copy.wait()
        for copy in halos:
            copy.wait_send()
        gathered()
        for copy in waits:
            copy.wait_send()

    local_in[0].wait()
    for key in ORDER:
        ops[key if isinstance(key, tuple) else (key,)]()


def train_step(
    n_seq, owners, dilations, lengths, pairing, step_embed, queries, master, prompts,
    frames_in, cond_frames, grad_out, grad_skip,
):
    _, own, channels = frames_in.shape
    rows = master.shape[1]
    number = queries.shape[1]
    grid_rows = own + 2 * HALO
    nz = n_seq // 2
    v = pltpu.VMEM
    dma = pltpu.SemaphoreType.DMA
    frame_out = jax.ShapeDtypeStruct((1, own, channels), F32)
    film = FILM * LAYERS
    copies = 80 + 6 * nz
    return pl.pallas_call(
        functools.partial(step_kernel, n_seq),
        out_shape=(
            frame_out,
            frame_out,
            frame_out,
            jax.ShapeDtypeStruct((LAYERS, 4, 5, rows, WIDE), BF),
            jax.ShapeDtypeStruct((LAYERS, LOW_RANK, rows, channels), BF),
            jax.ShapeDtypeStruct((LAYERS, number, channels), F32),
        ),
        in_specs=[smem_spec()] * 4 + [vmem_spec()] * 2 + [any_spec()] * 6,
        out_specs=(any_spec(),) * 4 + (vmem_spec(),) * 2,
        scratch_shapes=[
            v((BLOCKS, nz, 2, rows, WIDE), BF),
            v((10, nz, 2, rows, WIDE), BF),
            v((LAZY, rows, WIDE), BF),
            v((LAZY // 2, rows, WIDE), BF),
            v((LAZY // 4, rows, WIDE), BF),
            v((film, rows, WIDE), BF),
            v((film // 2, rows, WIDE), BF),
            v((film // 2, rows, WIDE), BF),
            v((film, rows, WIDE), BF),
            v((LAYERS, 10, nz, 2, rows, WIDE), BF),
            v((LAYERS, 5, nz // 2, 2, rows, WIDE), BF),
            v((LAYERS, 10, nz - nz // 2, rows, WIDE), BF),
            v((LAYERS, 5, nz, rows, WIDE), BF),
            v((LAYERS, nz - 1, 5, rows, WIDE), BF),
            v((LAYERS, 5, rows, WIDE), BF),
            v((grid_rows, channels), BF),
            v((grid_rows, 6 * channels), BF),
            v((LAYERS, grid_rows, 2 * channels), BF),
            v((grid_rows, channels), BF),
            v((grid_rows, channels), F32),
            v((grid_rows // 8 + 4, 8, channels), F32),
            v((grid_rows, 2 * channels), BF),
            v((LAYERS, channels, own), BF),
            v((channels, own), BF),
            v((LAYERS, channels, own), BF),
            v((grid_rows, channels), F32),
            v((own, channels), F32),
            v(master.shape, F32),
            v(prompts.shape[1:], BF),
            v((LAYERS, HEADS * number, prompts.shape[1]), BF),
            v((LAYERS, 16, channels), F32),
            v((LAYERS, 8, channels), F32),
            v((LAYERS, 8, channels), F32),
            v((4, (16 + number + rows) * LAYERS, channels), BF),
            v((sum(HOP_ROWS), 128), F32),
            v((n_seq, sum(HOP_ROWS), 128), F32),
            dma((5,)),
            dma((4,)),
            dma((8,)),
            dma((8,)),
            dma((8,)),
            dma((copies,)),
            dma((copies,)),
            dma((1,)),
            dma((1,)),
            dma((len(HOP_ROWS), n_seq)),
            dma((len(HOP_ROWS), n_seq)),
        ],
        compiler_params=pltpu.CompilerParams(
            collective_id=0, has_side_effects=True, vmem_limit_bytes=MEM
        ),
        name="train_step",
    )(
        owners, dilations, lengths, pairing, step_embed, queries, master, prompts,
        frames_in, cond_frames, grad_out, grad_skip,
    )


def adam_update(weight, moment_one, moment_two, gradient, step_rate):
    moment_one = BETA_ONE * moment_one + (1.0 - BETA_ONE) * gradient
    moment_two = BETA_TWO * moment_two + (1.0 - BETA_TWO) * gradient * gradient
    normal = (
        moment_one
        / (1.0 - BETA_ONE**STEP)
        / (jnp.sqrt(moment_two / (1.0 - BETA_TWO**STEP)) + EPSILON)
    )
    return (moment_one, moment_two, weight - step_rate * (normal + WEIGHT_DECAY * weight))


def update_kernel(
    owners_ref, master_hbm, first_hbm, second_hbm, grad_hbm, low_hbm,
    queries_ref, qfirst_ref, qsecond_ref, dq_ref, block_in, skip_in, gframes_in,
    nfirst_hbm, nsecond_hbm, nmaster_hbm, ncopy_hbm, nqfirst_ref, nqsecond_ref, nqueries_ref,
    block_out, skip_out, gframes_out,
    master, first, second, grad, low, three, one, two, copied, frames,
    tile_of, grad_sem, in_sem, out_sem, frame_sem,
):
    grp = lax.axis_index("grp")
    grads_in = [
        pltpu.make_async_copy(a, b, grad_sem.at[i])
        for i, (a, b) in enumerate(((grad_hbm, grad), (low_hbm, low)))
    ]
    spots = [pl.ds(start, count) for start, count in CHUNKS]
    slots_in = [
        [
            pltpu.make_async_copy(a.at[spot], b.at[spot], in_sem.at[i, j])
            for j, (a, b) in enumerate(
                ((master_hbm, master), (first_hbm, first), (second_hbm, second))
            )
        ]
        for i, spot in enumerate(spots)
    ]
    frames_in = [
        pltpu.make_async_copy(a, frames.at[i], frame_sem.at[0, i])
        for i, a in enumerate((block_in, skip_in, gframes_in))
    ]
    for copy in grads_in + slots_in[0]:
        copy.start()
    for copies in slots_in[1:]:
        for copy in copies:
            copy.start()
    for copy in frames_in:
        copy.start()

    for slot in range(CAP + 1):
        tile_of[slot] = TILES
    count = jnp.int32(0)
    for tile in range(TILES):
        own = owners_ref[tile] == grp

        @pl.when(own)
        def _(count=count, tile=tile):
            tile_of[jnp.minimum(count, CAP)] = tile

        count = count + own.astype(jnp.int32)
    news = adam_update(
        queries_ref[...], qfirst_ref[...], qsecond_ref[...], dq_ref[...], QUERY_RATE
    )
    nqfirst_ref[...], nqsecond_ref[...], nqueries_ref[...] = news

    def slot_update(slot, carry):
        tile = tile_of[slot]
        used = (tile < TILES).astype(jnp.int32)
        tile = jnp.minimum(tile, TILES - 1)
        layer, kind = lax.div(tile, PER_LAYER), lax.rem(tile, PER_LAYER)
        plain = kind < 8
        pair = jnp.where(plain, lax.rem(kind, 2), (kind == 16).astype(jnp.int32))
        tap = jnp.where(plain, lax.div(kind, 2), 4)
        full = jnp.concatenate([grad[layer, 2 * pair, tap], grad[layer, 2 * pair + 1, tap]], axis=1)
        place = jnp.where(kind < 10, kind - 3, kind - 10)
        thin = low[layer, jnp.clip(place, 0, LOW_RANK - 1)]
        is_thin = ((kind >= 8) & (kind <= 14)).astype(jnp.int32)
        gradient = jnp.where(
            jnp.broadcast_to(is_thin, full.shape) > 0, thin.astype(F32), full.astype(F32)
        )
        old, old_first, old_second = master[slot], first[slot], second[slot]
        new_first, new_second, new = adam_update(old, old_first, old_second, gradient, LEARN_RATE)
        keep = jnp.broadcast_to(used, old.shape) > 0
        new = jnp.where(keep, new, old)
        one[slot] = jnp.where(keep, new_first, old_first)
        two[slot] = jnp.where(keep, new_second, old_second)
        three[slot] = new
        copied[slot] = new.astype(BF)
        return carry

    for copy in grads_in:
        copy.wait()
    outs = []
    for i, (start, number) in enumerate(CHUNKS):
        for copy in slots_in[i]:
            copy.wait()
        lax.fori_loop(start, start + number, slot_update, 0)
        for j, (a, b) in enumerate(
            ((one, nfirst_hbm), (two, nsecond_hbm), (three, nmaster_hbm), (copied, ncopy_hbm))
        ):
            copy = pltpu.make_async_copy(a.at[spots[i]], b.at[spots[i]], out_sem.at[i, j])
            copy.start()
            outs.append(copy)
    for i, target in enumerate((block_out, skip_out, gframes_out)):
        frames_in[i].wait()
        copy = pltpu.make_async_copy(frames.at[i], target, frame_sem.at[1, i])
        copy.start()
        outs.append(copy)
    for copy in outs:
        copy.wait()


CHUNKS = ((0, 3), (3, 3), (6, 3), (9, 4))


def update(owners, master, first, second, grads, low, queries, qfirst, qsecond, dq, *frames):
    any_, whole = any_spec(), vmem_spec()
    query = jax.ShapeDtypeStruct(queries.shape, F32)
    full = jax.ShapeDtypeStruct(master.shape, F32)
    passed = jax.ShapeDtypeStruct(frames[0].shape, F32)
    v = pltpu.VMEM
    slots = v(master.shape, F32)
    return pl.pallas_call(
        update_kernel,
        out_shape=(full, full, full, jax.ShapeDtypeStruct(master.shape, BF), query, query, query)
        + (passed,) * 3,
        in_specs=[smem_spec()] + [any_] * 5 + [whole] * 4 + [any_] * 3,
        out_specs=(any_,) * 4 + (whole,) * 3 + (any_,) * 3,
        scratch_shapes=[
            slots, slots, slots, v(grads.shape, BF), v(low.shape, BF),
            slots, slots, slots, v(master.shape, BF), v((3,) + passed.shape, F32),
            pltpu.SMEM((CAP + 1,), jnp.int32),
            pltpu.SemaphoreType.DMA((2,)),
            pltpu.SemaphoreType.DMA((len(CHUNKS), 3)),
            pltpu.SemaphoreType.DMA((len(CHUNKS), 4)),
            pltpu.SemaphoreType.DMA((2, 3)),
        ],
        compiler_params=pltpu.CompilerParams(vmem_limit_bytes=MEM),
        name="update",
    )(owners, master, first, second, grads, low, queries, qfirst, qsecond, dq, *frames)


def on_device(
    n_seq,
    frames_in,
    cond_frames,
    step_embed,
    prompts,
    prompt_lengths,
    pairing,
    dilations,
    owners,
    master,
    first_moment,
    second_moment,
    queries,
    query_first,
    query_second,
    grad_out,
    grad_skip,
):
    block, skip, gframes, own_grads, low, dq = train_step(
        n_seq, owners, dilations, prompt_lengths, pairing, step_embed, queries, master, prompts,
        frames_in, cond_frames, grad_out, grad_skip,
    )
    (
        new_first, new_second, new_master, new_copy, nqf, nqs, nq,
        block_out, skip_out, grad_frames,
    ) = update(
        owners, master, first_moment, second_moment, own_grads, low,
        queries, query_first, query_second, dq, block, skip, gframes,
    )
    return (
        new_first, new_second, new_master, new_copy, nqf, nqs, nq,
        block_out, skip_out, grad_frames,
    )


def solution(mesh):
    shard = P("grp", "seq", None)
    placed = (
        shard, shard, P("grp", None), P(), P(), P("grp"), P(), P(),
        shard, shard, shard, P(), P(), P(), shard, shard,
    )
    return jax.shard_map(
        functools.partial(on_device, mesh.shape["seq"]),
        mesh=mesh,
        in_specs=placed,
        out_specs=(shard, shard, shard, shard, P(), P(), P(), shard, shard, shard),
        check_vma=False,
    )
```

```python
import functools

import jax
import jax.numpy as jnp
from jax import lax
from jax.experimental import pallas as pl
from jax.experimental.pallas import tpu as pltpu
from jax.sharding import PartitionSpec as P

HEADS = 8
LAYERS = 2
DMAX = 8
CAP = 13
STEP = 10
PER_LAYER = 17
TILES = PER_LAYER * LAYERS

BETA_ONE = 0.9
BETA_TWO = 0.999
EPSILON = 1e-08
WEIGHT_DECAY = 0.01
LEARN_RATE = 0.02
QUERY_RATE = 0.4
HALF_ROOT = 0.7071067811865476
NEGATIVE = -1e30

BF = jnp.bfloat16
F32 = jnp.float32
HALO = 32
WIDE = 256
KEYS = 2 * LAYERS
MAIN = 20
LAZY = KEYS + MAIN * LAYERS
LAZY_EACH = 8
BLOCKS = LAZY + LAZY_EACH * LAYERS
PHASES = ((0, KEYS), (KEYS, MAIN), (KEYS + MAIN, MAIN), (LAZY, LAZY_EACH * LAYERS))
FILM_ORDER = (11, 12, 13, 14, 8, 9)
FILM = 2 * len(FILM_ORDER)
LOW_RANK = 1 + len(FILM_ORDER)
HOP_ROWS = (24, 8, 16, 32)
ORDER = (
    ("prep", 0), ("prep", 1), ("cross", 0), "fc", ("cross", 1), ("prep", 2), ("end", 0),
    ("end", 1), ("first", 0), "fx", ("cross", 2), ("second", 0), ("first", 1), ("third", 0),
    ("pr", 0), ("pr", 1), "fl", ("pr", 2), ("pr", 3), ("end", 2), "att0", "att1", ("second", 1),
    "hsA", "condt", ("first", 2), ("end", 3), "heA", "hsB", ("third", 1), "heB", "hsC",
    ("second", 2), "heC", ("first", 3), "win0", "gates0a", ("third", 2), "gates0b", "res0",
    "gatt0", "skip0", "win1", "gates1a", "gates1b", "gg1a", "gatt1", "gg1b", "winb1",
    ("give", 1, 1), "fg1b", ("give", 1, 0), "fg1a", "out1", ("keep", 1, 1), ("second", 3),
    ("keep", 1, 0), ("one", 1), "gg0a", "gg0b", "winb0", ("give", 0, 1), "fg0b", ("give", 0, 0),
    "fg0a", "hs3", ("two", 1), ("keep", 0, 1), ("keep", 0, 0), ("one", 0), ("third", 3), "he3",
    ("three", 1), ("two", 0), "fb1", ("four", 1), ("three", 0), "fb0", "bundle", ("four", 0),
    ("five", 1), "low", "end",
)

MEM = 64 * 1024 * 1024 - 256 * 1024
MESH = pl.DeviceIdType.MESH


def block_table():
    table = {}
    for layer in range(LAYERS):
        base = PER_LAYER * layer
        for side in range(2):
            table[base + 10, side] = 2 * layer + side
        start = KEYS + MAIN * layer
        for part in range(4):
            for tap in range(4):
                table[base + 2 * tap + part // 2, part % 2] = start + 5 * part + tap
            table[base + 15 + part // 2, part % 2] = start + 5 * part + 4
    return table


BLOCK_OF = block_table()
FILM_OF = {
    (PER_LAYER * layer + tile, side): FILM * layer + 2 * place + side
    for layer in range(LAYERS)
    for place, tile in enumerate(FILM_ORDER)
    for side in range(2)
}


def mm(a, b):
    return lax.dot_general(a, b, (((1,), (0,)), ((), ())), preferred_element_type=F32)


def mm_nt(a, b):
    return lax.dot_general(a, b, (((1,), (1,)), ((), ())), preferred_element_type=F32)


def mm_nt_fine(a, b):
    high = a.astype(BF)
    return mm_nt(high, b) + mm_nt((a - high.astype(F32)).astype(BF), b)


def mm_low(a, b):
    return mm(a.astype(BF), b)


def mm_nt_low(a, b):
    return mm_nt(a.astype(BF), b)


def mm_nt_pairs(a, blocks):
    total = None
    for place, block in enumerate(blocks):
        term = mm_nt_fine(a[:, place * WIDE : (place + 1) * WIDE], block)
        total = term if total is None else total + term
    return total


def window(ref, start, count, width):
    group, rest = lax.div(start, 8), lax.rem(start, 8)
    groups = ref[pl.ds(group, count // 8 + 1), :, 0:width]
    turned = pltpu.roll(groups, lax.rem(8 - rest, 8), 1)
    row = lax.broadcasted_iota(jnp.int32, (1, 8, 1), 1)
    return jnp.where(row < 8 - rest, turned[:-1], turned[1:]).reshape(count, width)


def in_eights(value):
    return value.reshape(value.shape[0] // 8, 8, value.shape[1])


def place_of(n_seq):
    seq, grp = lax.axis_index("seq"), lax.axis_index("grp")
    z, y = lax.div(seq, 2), lax.rem(seq, 2)
    x, c = lax.div(grp, 2), lax.rem(grp, 2)
    return seq, grp, z, y, x, c


def greet(n_seq, seq, grp, groups):
    barrier = pltpu.get_barrier_semaphore()

    def one(k, carry):
        pl.semaphore_signal(
            barrier, inc=1, device_id={"seq": lax.rem(seq + k, n_seq), "grp": grp}, device_id_type=MESH
        )
        return carry

    lax.fori_loop(1, n_seq, one, 0)
    for k in range(1, groups):
        pl.semaphore_signal(
            barrier, inc=1, device_id={"seq": seq, "grp": lax.rem(grp + k, groups)}, device_id_type=MESH
        )
    pl.semaphore_wait(barrier, n_seq - 1 + groups - 1)


def any_spec():
    return pl.BlockSpec(memory_space=pl.ANY)


def vmem_spec():
    return pl.BlockSpec(memory_space=pltpu.VMEM)


def smem_spec():
    return pl.BlockSpec(memory_space=pltpu.SMEM)


def head_mask():
    row = lax.broadcasted_iota(jnp.int32, (HEADS, 512), 0)
    column = lax.broadcasted_iota(jnp.int32, (HEADS, 512), 1)
    return lax.div(column, 512 // HEADS) == row


def block_diagonal(rows):
    column = lax.div(lax.broadcasted_iota(jnp.int32, rows.shape, 1), 512 // HEADS)
    return jnp.concatenate([jnp.where(column == h, rows, 0.0) for h in range(HEADS)], axis=0)


def same_rows(row):
    return jnp.broadcast_to(row, (8, row.shape[1]))


def pack(vectors):
    pieces = [v[:, 128 * i : 128 * (i + 1)] for v in vectors for i in range(v.shape[1] // 128)]
    spare = -len(pieces) % 8
    if spare:
        pieces.append(jnp.zeros((spare, 128), pieces[0].dtype))
    return jnp.concatenate(pieces, axis=0)


def unpack(rows, place, pieces=4):
    return jnp.concatenate(
        [rows[pieces * place + i : pieces * place + i + 1] for i in range(pieces)], axis=1
    )


def step_kernel(
    n_seq, owners_ref, dil_ref, lengths_ref, pairing_ref, embed_ref, queries_ref, master_hbm,
    prompts_hbm, frames_hbm, cond_hbm, gout_hbm, gskip_hbm,
    block_hbm, skip_hbm, gframes_hbm, out_hbm, low_ref, dquery_ref,
    w, gs, prep, core_in, x_in, fr, fr_in, fx, ff, red_in, one_a, one_b, two_in, z_in, fin,
    xe, cat, slopes, gated, x1, bh, bb, sht, condt, gatt, bx, sk,
    master, prompt, probs, left, vec, sums, bundle,
    hop_src, hop_in,
    in_sem, prompt_sem, out_sem, hsend, hrecv, send, recv, zsend, zrecv, hop_send, hop_recv,
):
    seq, grp, z, y, x, c = place_of(n_seq)
    nz = n_seq // 2
    rows = prep.shape[1]
    own = frames_hbm.shape[1]
    grid_rows = own + 2 * HALO
    top = HALO + own
    channels = 512
    number = queries_ref.shape[1]
    sib, across, other_y = x * 2 + 1 - c, (1 - x) * 2 + c, z * 2 + 1 - y
    mine, theirs = 2 * c + x, 2 * c + 1 - x

    local_in = [
        pltpu.make_async_copy(a, b, in_sem.at[i])
        for i, (a, b) in enumerate(
            (
                (master_hbm, master),
                (frames_hbm.at[0], xe.at[pl.ds(HALO, own)]),
                (cond_hbm.at[0], cat.at[pl.ds(HALO, own), pl.ds(1536, channels)]),
                (gout_hbm.at[0], bb.at[pl.ds(HALO, own), pl.ds(0, channels)]),
                (gskip_hbm.at[0], bb.at[pl.ds(HALO, own), pl.ds(channels, channels)]),
            )
        )
    ]
    for copy in local_in:
        copy.start()

    def prompt_copy(turn, i):
        rows_now, columns = pl.ds(0, prompt.shape[0]), pl.ds((i % 2) * channels, channels)
        return pltpu.make_async_copy(
            prompts_hbm.at[4 * turn + i], slopes.at[i // 2, rows_now, columns], prompt_sem.at[i]
        )

    for i in range(4):
        prompt_copy(0, i).start()

    greet(n_seq, seq, grp, 4)

    waits = []
    used = [0]

    def remote(src, dst, to_seq, to_grp, sent=None):
        place = used[0]
        used[0] += 1
        copy = pltpu.make_async_remote_copy(
            src_ref=src,
            dst_ref=dst,
            send_sem=send.at[place],
            recv_sem=recv.at[place],
            device_id={"seq": to_seq, "grp": to_grp},
            device_id_type=MESH,
        )
        copy.start()
        (waits if sent is None else sent).append(copy)
        return copy

    after, before = lax.rem(seq + 1, n_seq), lax.rem(seq + n_seq - 1, n_seq)
    halos = []
    for ref, buffer, column in (
        (frames_hbm, xe, 0),
        (cond_hbm, cat, 1536),
        (gout_hbm, bb, 0),
        (gskip_hbm, bb, channels),
    ):
        for start, at, target in ((own - HALO, 0, after), (0, top, before)):
            place = len(halos)
            copy = pltpu.make_async_remote_copy(
                src_ref=ref.at[0, pl.ds(start, HALO)],
                dst_ref=buffer.at[pl.ds(at, HALO), pl.ds(column, channels)],
                send_sem=hsend.at[place],
                recv_sem=hrecv.at[place],
                device_id={"seq": target, "grp": grp},
                device_id_type=MESH,
            )
            copy.start()
            halos.append(copy)

    slots, flags = [], []
    count = jnp.int32(0)
    for tile in range(TILES):
        flag = (owners_ref[tile] == grp).astype(jnp.int32)
        slots.append(jnp.minimum(count, CAP - 1))
        flags.append(flag.astype(F32))
        count = count + flag

    def rounded(tile):
        return (master[slots[tile]] * flags[tile]).astype(BF)

    def ready(tiles, buffer, table):
        for tile in tiles:
            value = rounded(tile)
            buffer[table[tile, 0]] = value[:, :WIDE]
            buffer[table[tile, 1]] = value[:, WIDE:]

    def merge_start(phase):
        base, blocks = PHASES[phase]
        each = blocks // 4
        return remote(
            prep.at[pl.ds(base + 2 * (1 - c) * each, 2 * each)],
            core_in.at[pl.ds(base // 2, 2 * each)],
            seq, sib,
        )

    def merge_cross(phase, copy):
        base, blocks = PHASES[phase]
        each = blocks // 4
        copy.wait_recv()

        def add(i, carry):
            place = base // 2 + i
            core_in[place] = core_in[place] + prep[base + 2 * c * each + i]
            return carry

        lax.fori_loop(0, 2 * each, add, 0)
        return remote(
            core_in.at[pl.ds(base // 2 + (1 - x) * each, each)],
            x_in.at[pl.ds(base // 4, each)],
            seq, across,
        )

    def view(phase, quarter, zz, yy):
        base, blocks = PHASES[phase]
        each = blocks // 4
        return w.at[pl.ds(base + quarter * each, each), zz, yy]

    low_z, high_z = pl.ds(0, nz // 2), pl.ds(nz // 2, nz - nz // 2)
    all_z = pl.ds(0, nz)
    gathering, legs = [], {}

    def spread(ref, to_seq, to_grp):
        return remote(ref, ref, to_seq, to_grp, gathering)

    def merge_end(phase, copy):
        base, blocks = PHASES[phase]
        each = blocks // 4
        copy.wait_recv()

        def settle(i, carry):
            w[base + mine * each + i, z, y] = (
                core_in[base // 2 + x * each + i] + x_in[base // 4 + i]
            )
            return carry

        lax.fori_loop(0, each, settle, 0)

    def spread_z(phase):
        ref = view(phase, mine, z, y)
        legs[phase] = [spread(ref, lax.rem(z + k, nz) * 2 + y, grp) for k in range(1, nz)]

    core_legs = {}

    def first(phase):
        for copy in legs[phase]:
            copy.wait_recv()
        lower, upper = view(phase, mine, low_z, y), view(phase, mine, high_z, y)
        one = [spread(lower, other_y, grp), spread(upper, seq, across)]
        two = [spread(lower, seq, across), spread(upper, other_y, grp)]
        legs[phase] = (one, two)
        core_legs[phase] = [spread(view(phase, mine, all_z, y), seq, sib)]

    def second(phase):
        one, two = legs[phase]
        for copy in one:
            copy.wait_recv()
        lower, upper = view(phase, mine, low_z, 1 - y), view(phase, theirs, high_z, y)
        two += [spread(lower, seq, across), spread(upper, other_y, grp)]
        core_legs[phase] += [spread(lower, seq, sib), spread(upper, seq, sib)]

    def third(phase):
        for copy in legs[phase][1]:
            copy.wait_recv()
        core_legs[phase] += [
            spread(view(phase, theirs, low_z, pl.ds(0, 2)), seq, sib),
            spread(view(phase, mine, high_z, 1 - y), seq, sib),
            spread(view(phase, theirs, high_z, 1 - y), seq, sib),
        ]

    def arrived(phase):
        for copy in core_legs[phase]:
            copy.wait_recv()

    def hop_refs(j):
        start = sum(HOP_ROWS[:j])
        spot = pl.ds(start, HOP_ROWS[j])
        return hop_src.at[spot], hop_in.at[seq, spot], hop_in.at[:, spot]

    def hop_copy(j, k):
        src, dst, _ = hop_refs(j)
        return pltpu.make_async_remote_copy(
            src_ref=src,
            dst_ref=dst,
            send_sem=hop_send.at[j, k],
            recv_sem=hop_recv.at[j, k],
            device_id={"seq": lax.rem(seq + k, n_seq), "grp": grp},
            device_id_type=MESH,
        )

    def hop_start(j, value):
        src, dst, _ = hop_refs(j)
        value = value.astype(src.dtype)
        src[...] = value
        dst[...] = value

        def one(k, carry):
            hop_copy(j, k).start()
            return carry

        lax.fori_loop(1, n_seq, one, 0)

    def hop_end(j):
        def one(k, carry):
            hop_copy(j, k).wait()
            return carry

        lax.fori_loop(1, n_seq, one, 0)
        _, _, whole = hop_refs(j)

        def add(i, total):
            return total + whole[i].astype(F32)

        return lax.fori_loop(0, n_seq, add, jnp.zeros((HOP_ROWS[j], 128), F32))

    position = lax.broadcasted_iota(jnp.int32, (channels, rows), 0)
    column = lax.broadcasted_iota(jnp.int32, (channels, rows), 1)
    chosen = jnp.where(position == column + seq * rows, 1.0, 0.0).astype(BF)

    def pick(v):
        return mm_low(v, chosen)

    def film_block(layer, place):
        return ff[FILM * layer + place]

    def film_rows(layer, v, places):
        return jnp.concatenate([mm_low(v, film_block(layer, i)) for i in places], axis=1)

    def film_back(layer, v, places):
        total = None
        for i, place in enumerate(places):
            whole = w[LAZY + LAZY_EACH * layer + place].reshape(channels, WIDE)
            term = mm_nt(v[:, i * WIDE : (i + 1) * WIDE].astype(BF), whole)
            total = term if total is None else total + term
        return total

    def key_blocks(layer):
        return [w[2 * layer + side].reshape(channels, WIDE) for side in range(2)]

    mask = head_mask()

    def attention(layer):
        spread = block_diagonal(queries_ref[layer])
        probe = mm_nt_pairs(spread, key_blocks(layer))
        pr = prompt[...]
        scores = mm_nt_fine(probe, pr) * 0.125
        live = lax.broadcasted_iota(jnp.int32, scores.shape, 1) < lengths_ref[pairing_ref[0]]
        scores = jnp.where(live, scores, NEGATIVE)
        weight = jnp.exp(scores - jnp.max(scores, axis=1, keepdims=True))
        value = weight / jnp.sum(weight, axis=1, keepdims=True)
        probs[layer] = value.astype(BF)
        mean = jnp.concatenate(
            [
                jnp.mean(value[h * number : (h + 1) * number], axis=0, keepdims=True)
                for h in range(HEADS)
            ],
            axis=0,
        )
        seen = mm_low(mean, pr)
        left[layer, 0:8] = seen
        return seen

    def wblock(layer, place):
        return w[KEYS + MAIN * layer + place].reshape(channels, WIDE)

    def inside(low, count):
        row = lax.broadcasted_iota(jnp.int32, (count, 1), 0) + (low - HALO) + seq * own
        return (row >= 0) & (row < n_seq * own)

    def windows_forward(layer):
        low = 16 * layer
        high = grid_rows - low
        scale, shift = 1.0 + vec[layer, 0:1], vec[layer, 1:2]
        here = xe[...].astype(F32) if layer == 0 else x1[...]
        shifted = (here * scale + shift).astype(BF).astype(F32)
        shifted = jnp.where(inside(0, grid_rows), shifted, 0.0)
        groups = grid_rows // 8
        bh[0] = jnp.zeros((8, channels), F32)
        bh[1 : 1 + groups] = in_eights(shifted)
        bh[1 + groups :] = jnp.zeros((3, 8, channels), F32)
        sht[layer] = jnp.transpose(shifted[HALO:top]).astype(BF)
        cat[low:high, channels : 2 * channels] = shifted[low:high].astype(BF)
        for tap in (0, 2):
            start = 8 + low + (tap - 1) * dil_ref[layer]
            cat[low:high, tap * channels : (tap + 1) * channels] = window(
                bh, start, high - low, channels
            ).astype(BF)

    def gates(layer, first_row, rows_now):
        spot = slice(first_row, first_row + rows_now)
        value = cat[spot, 0:2048]
        for part in range(2):
            columns = slice(part * WIDE, (part + 1) * WIDE)
            base = KEYS + MAIN * layer + 5 * part
            lhs = mm(value, w[base : base + 4].reshape(2048, WIDE))
            tangent = jnp.tanh(lhs + vec[layer, 2:3, columns])
            rhs = mm(value, w[base + 10 : base + 14].reshape(2048, WIDE))
            opening = jax.nn.sigmoid(rhs + vec[layer, 3:4, columns])
            gate = tangent * opening
            gated[spot, columns] = gate.astype(BF)
            slopes[layer, spot, columns] = (opening * (1.0 - tangent * tangent)).astype(BF)
            other = slice(channels + part * WIDE, channels + (part + 1) * WIDE)
            slopes[layer, spot, other] = (gate * (1.0 - opening)).astype(BF)

    def residual(layer, first_row, rows_now):
        value = gated[first_row : first_row + rows_now]
        for part in range(2):
            columns = slice(part * WIDE, (part + 1) * WIDE)
            term = mm(value, wblock(layer, 5 * part + 4))
            if layer == 0:
                base = xe[first_row : first_row + rows_now, columns].astype(F32)
                x1[first_row : first_row + rows_now, columns] = (base + term) * HALF_ROOT
            else:
                base = x1[first_row : first_row + rows_now, columns]
                x1[first_row : first_row + rows_now, columns] = (base + term) * HALF_ROOT

    def skipped(layer, first_row, rows_now):
        value = gated[first_row : first_row + rows_now]
        spot = slice(first_row - HALO, first_row - HALO + rows_now)
        for part in range(2):
            columns = slice(part * WIDE, (part + 1) * WIDE)
            term = mm(value, wblock(layer, 5 * part + 14))
            if layer == 0:
                sk[spot, columns] = term
            else:
                sk[spot, columns] = sk[spot, columns] + term

    low, high = 16, grid_rows - 16

    def gate_grads(layer, first_row, rows_now):
        spot = slice(first_row, first_row + rows_now)
        bb[spot, 0:channels] = (bx[spot] * HALF_ROOT).astype(BF)
        branch = jnp.concatenate([wblock(layer, 5 * part + 4) for part in range(4)], axis=1)
        back = mm_nt(bb[spot], branch)
        keep = inside(first_row, rows_now)
        for side in range(2):
            columns = slice(side * channels, (side + 1) * channels)
            value = back * slopes[layer, spot, columns].astype(F32)
            middle = slice((2 + side) * channels, (3 + side) * channels)
            cat[spot, middle] = jnp.where(keep, value, 0.0).astype(BF)

    def windows_backward(layer):
        reach, limit = (low, high) if layer else (HALO, top)
        edge = 1 + low // 8
        bh[0:edge] = jnp.zeros((edge, 8, channels), F32)
        bh[1 + high // 8 :] = jnp.zeros((edge + 2, 8, channels), F32)
        for side in range(2):
            middle = slice((2 + side) * channels, (3 + side) * channels)
            value = cat[low:high, middle].astype(F32)
            bh[edge : 1 + high // 8] = in_eights(value)
            total = jnp.sum(value[HALO - low : top - low], axis=0, keepdims=True)
            sums[layer, 2 + side : 3 + side] = total
            for tap in (0, 2):
                start = 8 + reach - (tap - 1) * dil_ref[layer]
                columns = slice((2 * tap + side) * channels, (2 * tap + side + 1) * channels)
                cat[reach:limit, columns] = window(bh, start, limit - reach, channels).astype(BF)

    def frame_grads(layer, first_row, rows_now):
        spot = slice(first_row, first_row + rows_now)
        taps = jnp.concatenate(
            [wblock(layer, 5 * part + tap) for tap in range(3) for part in range(4)], axis=1
        )
        back = mm_nt(cat[spot], taps)
        if layer:
            here = x1[spot]
            row = lax.broadcasted_iota(jnp.int32, (rows_now, 1), 0) + first_row
            kept = jnp.where((row >= HALO) & (row < top), back, 0.0)
        else:
            here = xe[spot].astype(F32)
            kept = back
        sums[layer, 0:1] += jnp.sum(kept * here, axis=0, keepdims=True)
        sums[layer, 1:2] += jnp.sum(kept, axis=0, keepdims=True)
        bx[spot] = bx[spot] * HALF_ROOT + back * (1.0 + vec[layer, 0:1])

    def weight_grad(layer, part, i):
        if i < 4:
            tap = i if i < 3 else 1
            start = pl.multiple_of(tap * 1024 + part * WIDE, WIDE)
            lhs = sht[layer] if i < 3 else condt[...]
            return mm(lhs, cat[HALO:top, pl.ds(start, WIDE)])
        start = pl.multiple_of(part * WIDE, WIDE)
        return mm(gatt[layer], bb[HALO:top, pl.ds(start, WIDE)])

    core_sent = {}

    def give(layer, xx):
        part = 2 * (1 - c) + xx
        buffer, base = (gs, 0) if layer else (w, KEYS + MAIN)
        for i in range(5):
            value = weight_grad(layer, part, i).astype(BF)
            buffer[base + 5 * xx + i] = value.reshape(nz, 2, rows, WIDE)
        core_sent[layer, xx] = remote(
            buffer.at[pl.ds(base + 5 * xx, 5)], red_in.at[layer, pl.ds(5 * xx, 5)], seq, sib
        )

    def keep(layer, xx):
        part = 2 * c + xx
        core_sent[layer, xx].wait_recv()
        for i in range(5):
            value = weight_grad(layer, part, i).reshape(nz, 2, rows, WIDE)
            spot = 5 * xx + i
            red_in[layer, spot] = (red_in[layer, spot].astype(F32) + value).astype(BF)

    ones, twos, zs = {}, {}, {}
    near = nz // 2

    def red_one(layer):
        ones[layer] = [
            remote(red_in.at[layer, pl.ds(5 * (1 - x), 5), low_z], one_a.at[layer], seq, across),
            remote(red_in.at[layer, :, high_z, 1 - y], one_b.at[layer], other_y, grp),
        ]

    def plus(a, b):
        return a + b

    def red_two(layer):
        for copy in ones[layer]:
            copy.wait_recv()

        def lower(i, carry):
            one_a[layer, i] = plus(one_a[layer, i], red_in[layer, 5 * x + i, 0:near])
            return carry

        lax.fori_loop(0, 5, lower, 0)
        twos[layer] = [
            remote(one_a.at[layer, :, :, 1 - y], two_in.at[layer, :, low_z], other_y, grp)
        ]

        def upper(i, carry):
            one_b[layer, i] = plus(one_b[layer, i], red_in[layer, i, near:nz, y])
            return carry

        lax.fori_loop(0, 10, upper, 0)
        twos[layer].append(
            remote(
                one_b.at[layer, pl.ds(5 * (1 - x), 5)], two_in.at[layer, :, high_z], seq, across
            )
        )

    def red_three(layer):
        for copy in twos[layer]:
            copy.wait_recv()

        def body(i, carry):
            two_in[layer, i, 0:near] = plus(two_in[layer, i, 0:near], one_a[layer, i, :, y])
            two_in[layer, i, near:nz] = plus(two_in[layer, i, near:nz], one_b[layer, 5 * x + i])
            return carry

        lax.fori_loop(0, 5, body, 0)
        zs[layer] = []
        for k in range(1, nz):
            zd = lax.rem(z + k, nz)
            zs[layer].append(remote(two_in.at[layer, :, zd], z_in.at[layer, k - 1], zd * 2 + y, grp))

    lasts = {}
    outs = []

    def local_out(src, dst):
        copy = pltpu.make_async_copy(src, dst, out_sem.at[len(outs)])
        copy.start()
        outs.append(copy)

    def red_four(layer):
        for copy in zs[layer]:
            copy.wait_recv()

        def body(i, carry):
            total = two_in[layer, i, z].astype(F32)
            for k in range(1, nz):
                total = total + z_in[layer, k - 1, i].astype(F32)
            fin[layer, i] = total.astype(BF)
            return carry

        lax.fori_loop(0, 5, body, 0)
        src, dst = fin.at[layer], out_hbm.at[layer, mine]
        lasts[layer] = [remote(src, dst, seq, across), remote(src, dst, seq, sib)]
        if not layer:
            lasts[layer].append(remote(src, dst, seq, (1 - x) * 2 + 1 - c))
        local_out(src, dst)

    def red_five(layer):
        lasts[layer][0].wait_recv()
        ref = out_hbm.at[layer, theirs]
        lasts[layer].append(remote(ref, ref, seq, sib))

    ops = {}

    def op(*key):
        def keep_op(body):
            ops[key] = body
            return body

        return keep_op

    main_tiles = (0, 1, 2, 3, 4, 5, 6, 7, 15, 16)
    merges, crosses, film_sent, seen, hops = {}, {}, {}, {}, {}
    half = fr.shape[0] // 2
    half_spot = pl.ds(c * half, half)
    size_all, size_mid, size_own = grid_rows // 2, (high - low) // 2, own // 2
    embed = same_rows(embed_ref[...].astype(F32))

    for phase in range(3):

        @op("prep", phase)
        def _(phase=phase):
            if phase:
                tiles = [PER_LAYER * (phase - 1) + t for t in main_tiles]
            else:
                tiles = [PER_LAYER * layer + 10 for layer in range(LAYERS)]
            ready(tiles, prep, BLOCK_OF)
            merges[phase] = merge_start(phase)

        @op("cross", phase)
        def _(phase=phase):
            crosses[phase] = merge_cross(phase, merges[phase])

        @op("end", phase)
        def _(phase=phase):
            merge_end(phase, crosses[phase])
            spread_z(phase)

    for phase in range(4):
        for name, body in (("first", first), ("second", second), ("third", third)):

            @op(name, phase)
            def _(phase=phase, body=body):
                body(phase)

    @op("end", 3)
    def _():
        film_rows_here()
        base, each = PHASES[3][0], PHASES[3][1] // 4

        def settle(i, carry):
            w[base + mine * each + i, z, y] = ff[FILM * c + each * x + i]
            return carry

        lax.fori_loop(0, each, settle, 0)
        spread_z(3)

    @op("fc")
    def _():
        for layer in range(LAYERS):
            ready([PER_LAYER * layer + t for t in FILM_ORDER], fr, FILM_OF)
        film_sent[0] = remote(fr.at[pl.ds((1 - c) * half, half)], fr_in, seq, sib)

    @op("fx")
    def _():
        film_sent[0].wait_recv()
        fr_in[...] = fr_in[...] + fr[half_spot]
        film_sent[1] = remote(fr_in, fx, seq, across)

    @op("fl")
    def _():
        film_sent[1].wait_recv()
        ff[half_spot] = fr_in[...] + fx[...]
        film_sent[2] = remote(ff.at[half_spot], ff.at[half_spot], seq, sib)

    for turn in range(4):

        @op("pr", turn)
        def _(turn=turn):
            total = prompt[...] if turn else None
            for i in range(4):
                prompt_copy(turn, i).wait()
                flag = (pairing_ref[0] == 4 * turn + i).astype(F32).astype(BF)
                part = slice((i % 2) * channels, (i % 2 + 1) * channels)
                term = slopes[i // 2, 0 : prompt.shape[0], part] * flag
                total = term if total is None else total + term
            prompt[...] = total
            if turn < 3:
                for i in range(4):
                    prompt_copy(turn + 1, i).start()

    def gathered():
        while gathering:
            gathering.pop().wait_send()

    def film_rows_here():
        if 3 not in film_sent:
            film_sent[2].wait_recv()
            film_sent[3] = True

    @op("condt")
    def _():
        local_in[2].wait()
        condt[...] = jnp.transpose(cat[HALO:top, 1536:2048].astype(F32)).astype(BF)

    @op("att0")
    def _():
        arrived(0)
        seen[0] = attention(0)

    @op("att1")
    def _():
        seen[1] = attention(1)

    @op("hsA")
    def _():
        film_rows_here()
        vectors = []
        embed_here = pick(embed)
        for layer in range(LAYERS):
            mixed = film_rows(layer, pick(seen[layer]), (0, 1))
            vectors.append(jnp.sum(jnp.where(mask, mixed, 0.0), axis=0, keepdims=True))
            steps = film_rows(layer, embed_here, (8, 9, 10, 11))
            vectors += [steps[0:1, :channels], steps[0:1, channels:]]
        hop_start(0, pack(vectors))

    @op("heA")
    def _():
        total = hop_end(0)
        hops["mixed"] = [unpack(total, 3 * layer) for layer in range(LAYERS)]
        for layer in range(LAYERS):
            vec[layer, 2:3] = unpack(total, 3 * layer + 1)
            vec[layer, 3:4] = unpack(total, 3 * layer + 2)

    @op("hsB")
    def _():
        mixed = hops["mixed"]
        hop_start(
            1,
            pack([film_rows(l, pick(same_rows(mixed[l])), (2, 3))[0:1] for l in range(LAYERS)]),
        )

    @op("heB")
    def _():
        total = hop_end(1)
        hops["pooled"] = [unpack(total, layer) for layer in range(LAYERS)]

    @op("hsC")
    def _():
        vectors = []
        for layer in range(LAYERS):
            pooled = hops["pooled"][layer]
            film = film_rows(layer, pick(same_rows(pooled)), (4, 5, 6, 7))
            vectors += [film[0:1, :channels], film[0:1, channels:]]
        hop_start(2, pack(vectors))

    @op("heC")
    def _():
        total = hop_end(2)
        for layer in range(LAYERS):
            vec[layer, 0:1] = unpack(total, 2 * layer)
            vec[layer, 1:2] = unpack(total, 2 * layer + 1)
            left[layer, 8:9] = hops["mixed"][layer]
            left[layer, 9:10] = hops["pooled"][layer]
            left[layer, 10:11] = embed[0:1]
            left[layer, 11:16] = jnp.zeros((5, channels), F32)

    @op("win0")
    def _():
        local_in[1].wait()
        for copy in halos[:4]:
            copy.wait_recv()
        windows_forward(0)

    @op("win1")
    def _():
        local_in[3].wait()
        local_in[4].wait()
        for copy in halos[4:]:
            copy.wait_recv()
        bx[...] = bb[:, 0:channels].astype(F32)
        windows_forward(1)

    for layer in range(LAYERS):
        start, size = (low, size_mid) if layer else (0, size_all)
        for part, name in enumerate("ab"):
            first_row = start + part * size

            @op(f"gates{layer}{name}")
            def _(layer=layer, first_row=first_row, size=size, part=part):
                if not part:
                    arrived(1 + layer)
                gates(layer, first_row, size)

        @op(f"gatt{layer}")
        def _(layer=layer):
            gatt[layer] = jnp.transpose(gated[HALO:top].astype(F32)).astype(BF)

    @op("res0")
    def _():
        for part in range(2):
            residual(0, part * size_all, size_all)

    @op("skip0")
    def _():
        for part in range(2):
            skipped(0, HALO + part * size_own, size_own)

    @op("out1")
    def _():
        for part in range(2):
            residual(1, HALO + part * size_own, size_own)
            skipped(1, HALO + part * size_own, size_own)
        local_out(x1.at[pl.ds(HALO, own)], block_hbm.at[0])
        local_out(sk, skip_hbm.at[0])

    for layer in range(LAYERS):
        for part, name in enumerate("ab"):

            @op(f"gg{layer}{name}")
            def _(layer=layer, part=part):
                if layer and not part:
                    sums[...] = jnp.zeros_like(sums)
                gate_grads(layer, low + part * size_mid, size_mid)

            @op(f"fg{layer}{name}")
            def _(layer=layer, part=part):
                if layer:
                    frame_grads(1, low + part * size_mid, size_mid)
                else:
                    frame_grads(0, HALO + part * size_own, size_own)

        @op(f"winb{layer}")
        def _(layer=layer):
            windows_backward(layer)

        for xx in range(2):

            @op("give", layer, xx)
            def _(layer=layer, xx=xx):
                if not layer:
                    gathered()
                give(layer, xx)

            @op("keep", layer, xx)
            def _(layer=layer, xx=xx):
                keep(layer, xx)

        for name, body in (("one", red_one), ("two", red_two), ("three", red_three)):

            @op(name, layer)
            def _(layer=layer, body=body):
                body(layer)

        @op("four", layer)
        def _(layer=layer):
            red_four(layer)

    @op("five", 1)
    def _():
        red_five(1)

    @op("hs3")
    def _():
        local_out(bx.at[pl.ds(HALO, own)], gframes_hbm.at[0])
        hop_start(3, pack([sums[l, i : i + 1] for l in range(LAYERS) for i in range(4)]))

    @op("he3")
    def _():
        total = hop_end(3)
        hops["sides"] = [[unpack(total, 4 * l + i) for i in range(4)] for l in range(LAYERS)]

    rt_at, dq_at, lt_at = 0, 16 * LAYERS, (16 + number) * LAYERS

    def attention_back(layer):
        pr = prompt[...]
        sides = hops["sides"][layer]
        dfilm = same_rows(jnp.concatenate(sides[0:2], axis=1))
        dpooled = film_back(layer, dfilm, (4, 5, 6, 7))
        dmixed = film_back(layer, dpooled, (2, 3))
        dseen = film_back(layer, jnp.where(mask, dmixed, 0.0), (0, 1))
        dmean = mm_nt_low(dseen, pr) * (1.0 / number)
        dprobs = jnp.concatenate(
            [jnp.broadcast_to(dmean[h : h + 1], (number, channels)) for h in range(HEADS)], axis=0
        )
        value = probs[layer].astype(F32)
        inner = jnp.sum(dprobs * value, axis=1, keepdims=True)
        dprobe = mm_low(value * (dprobs - inner) * 0.125, pr)
        keys = key_blocks(layer)
        dspread = jnp.concatenate([mm_low(dprobe, keys[0]), mm_low(dprobe, keys[1])], axis=1)
        head = lax.div(lax.broadcasted_iota(jnp.int32, (number, channels), 1), channels // HEADS)
        dquery = jnp.zeros((number, channels), F32)
        for h in range(HEADS):
            dquery = dquery + jnp.where(head == h, dspread[h * number : (h + 1) * number], 0.0)
        start = dq_at + number * layer
        bundle[grp, start : start + number] = dquery.astype(BF)
        lefts = jnp.concatenate([left[layer], jnp.zeros((112, channels), F32)], axis=0)
        bh[0 : channels // 8, :, 0:256] = in_eights(jnp.transpose(dprobe))
        bh[0 : channels // 8, :, 256:384] = in_eights(jnp.transpose(lefts))
        eights = pl.ds(seq * (rows // 8), rows // 8)
        place = lt_at + rows * layer
        bundle[grp, place : place + rows, 0:384] = bh[eights, :, 0:384].reshape(rows, 384).astype(BF)
        place = rt_at + 16 * layer
        bundle[grp, place : place + 16] = jnp.concatenate(
            sides + [dpooled[0:1], dmixed[0:1], jnp.zeros((10, channels), F32)], axis=0
        ).astype(BF)

    @op("fb1")
    def _():
        arrived(3)
        attention_back(1)

    @op("fb0")
    def _():
        attention_back(0)

    bundles = []

    @op("bundle")
    def _():
        for k in range(1, 4):
            ref = bundle.at[grp]
            bundles.append(remote(ref, ref, seq, lax.rem(grp + k, 4)))

    @op("low")
    def _():
        for copy in bundles:
            copy.wait_recv()
        for layer in range(LAYERS):
            spot = slice(dq_at + number * layer, dq_at + number * (layer + 1))
            total = bundle[0, spot].astype(F32)
            for k in range(1, 4):
                total = total + bundle[k, spot].astype(F32)
            dquery_ref[layer] = total
        at = lax.broadcasted_iota(jnp.int32, (16, channels), 0)
        for layer in range(LAYERS):
            spread_rows = block_diagonal(queries_ref[layer]).astype(BF)
            spot = slice(lt_at + rows * layer, lt_at + rows * (layer + 1))
            probe = bundle[0, spot, 0:256].astype(F32)
            for k in range(1, 4):
                probe = probe + bundle[k, spot, 0:256].astype(F32)
            low_ref[layer, 0] = mm(probe.astype(BF), spread_rows).astype(BF)
            lefts, sides = [], []
            for k in range(4):
                right = bundle[k, 16 * layer : 16 * layer + 16].astype(F32)
                value = jnp.concatenate(
                    [jnp.where(mask, right[5:6], 0.0), jnp.zeros((8, channels), F32)], axis=0
                )
                pieces = [value] + [
                    jnp.where(at == row, right[i : i + 1], 0.0)
                    for i, row in ((4, 8), (0, 9), (1, 9), (2, 10), (3, 10))
                ]
                sides.append(jnp.concatenate(pieces, axis=1))
                lefts.append(bundle[k, spot, 256:272])
            total = mm(
                jnp.concatenate(lefts, axis=1), jnp.concatenate(sides, axis=0).astype(BF)
            )
            for i in range(6):
                low_ref[layer, 1 + i] = total[:, i * channels : (i + 1) * channels].astype(BF)

    @op("end")
    def _():
        for copies in lasts.values():
            for copy in copies[1:]:
                copy.wait_recv()
        lasts[0][0].wait_recv()
        for copy in outs:
            copy.wait()
        for copy in halos:
            copy.wait_send()
        gathered()
        for copy in waits:
            copy.wait_send()

    local_in[0].wait()
    for key in ORDER:
        ops[key if isinstance(key, tuple) else (key,)]()


def train_step(
    n_seq, owners, dilations, lengths, pairing, step_embed, queries, master, prompts,
    frames_in, cond_frames, grad_out, grad_skip,
):
    _, own, channels = frames_in.shape
    rows = master.shape[1]
    number = queries.shape[1]
    grid_rows = own + 2 * HALO
    nz = n_seq // 2
    v = pltpu.VMEM
    dma = pltpu.SemaphoreType.DMA
    frame_out = jax.ShapeDtypeStruct((1, own, channels), F32)
    film = FILM * LAYERS
    copies = 80 + 6 * nz
    return pl.pallas_call(
        functools.partial(step_kernel, n_seq),
        out_shape=(
            frame_out,
            frame_out,
            frame_out,
            jax.ShapeDtypeStruct((LAYERS, 4, 5, rows, WIDE), BF),
            jax.ShapeDtypeStruct((LAYERS, LOW_RANK, rows, channels), BF),
            jax.ShapeDtypeStruct((LAYERS, number, channels), F32),
        ),
        in_specs=[smem_spec()] * 4 + [vmem_spec()] * 2 + [any_spec()] * 6,
        out_specs=(any_spec(),) * 4 + (vmem_spec(),) * 2,
        scratch_shapes=[
            v((BLOCKS, nz, 2, rows, WIDE), BF),
            v((10, nz, 2, rows, WIDE), BF),
            v((LAZY, rows, WIDE), BF),
            v((LAZY // 2, rows, WIDE), BF),
            v((LAZY // 4, rows, WIDE), BF),
            v((film, rows, WIDE), BF),
            v((film // 2, rows, WIDE), BF),
            v((film // 2, rows, WIDE), BF),
            v((film, rows, WIDE), BF),
            v((LAYERS, 10, nz, 2, rows, WIDE), BF),
            v((LAYERS, 5, nz // 2, 2, rows, WIDE), BF),
            v((LAYERS, 10, nz - nz // 2, rows, WIDE), BF),
            v((LAYERS, 5, nz, rows, WIDE), BF),
            v((LAYERS, nz - 1, 5, rows, WIDE), BF),
            v((LAYERS, 5, rows, WIDE), BF),
            v((grid_rows, channels), BF),
            v((grid_rows, 6 * channels), BF),
            v((LAYERS, grid_rows, 2 * channels), BF),
            v((grid_rows, channels), BF),
            v((grid_rows, channels), F32),
            v((grid_rows // 8 + 4, 8, channels), F32),
            v((grid_rows, 2 * channels), BF),
            v((LAYERS, channels, own), BF),
            v((channels, own), BF),
            v((LAYERS, channels, own), BF),
            v((grid_rows, channels), F32),
            v((own, channels), F32),
            v(master.shape, F32),
            v(prompts.shape[1:], BF),
            v((LAYERS, HEADS * number, prompts.shape[1]), BF),
            v((LAYERS, 16, channels), F32),
            v((LAYERS, 8, channels), F32),
            v((LAYERS, 8, channels), F32),
            v((4, (16 + number + rows) * LAYERS, channels), BF),
            v((sum(HOP_ROWS), 128), F32),
            v((n_seq, sum(HOP_ROWS), 128), F32),
            dma((5,)),
            dma((4,)),
            dma((8,)),
            dma((8,)),
            dma((8,)),
            dma((copies,)),
            dma((copies,)),
            dma((1,)),
            dma((1,)),
            dma((len(HOP_ROWS), n_seq)),
            dma((len(HOP_ROWS), n_seq)),
        ],
        compiler_params=pltpu.CompilerParams(
            collective_id=0, has_side_effects=True, vmem_limit_bytes=MEM
        ),
        name="train_step",
    )(
        owners, dilations, lengths, pairing, step_embed, queries, master, prompts,
        frames_in, cond_frames, grad_out, grad_skip,
    )


def adam_update(weight, moment_one, moment_two, gradient, step_rate):
    moment_one = BETA_ONE * moment_one + (1.0 - BETA_ONE) * gradient
    moment_two = BETA_TWO * moment_two + (1.0 - BETA_TWO) * gradient * gradient
    normal = (
        moment_one
        / (1.0 - BETA_ONE**STEP)
        / (jnp.sqrt(moment_two / (1.0 - BETA_TWO**STEP)) + EPSILON)
    )
    return (moment_one, moment_two, weight - step_rate * (normal + WEIGHT_DECAY * weight))


def update_kernel(
    owners_ref, master_hbm, first_hbm, second_hbm, grad_hbm, low_hbm,
    queries_ref, qfirst_ref, qsecond_ref, dq_ref, block_in, skip_in, gframes_in,
    nfirst_hbm, nsecond_hbm, nmaster_hbm, ncopy_hbm, nqfirst_ref, nqsecond_ref, nqueries_ref,
    block_out, skip_out, gframes_out,
    master, first, second, grad, low, three, one, two, copied, frames,
    tile_of, grad_sem, in_sem, out_sem, frame_sem,
):
    grp = lax.axis_index("grp")
    grads_in = [
        pltpu.make_async_copy(a, b, grad_sem.at[i])
        for i, (a, b) in enumerate(((grad_hbm, grad), (low_hbm, low)))
    ]
    spots = [pl.ds(start, count) for start, count in CHUNKS]
    slots_in = [
        [
            pltpu.make_async_copy(a.at[spot], b.at[spot], in_sem.at[i, j])
            for j, (a, b) in enumerate(
                ((master_hbm, master), (first_hbm, first), (second_hbm, second))
            )
        ]
        for i, spot in enumerate(spots)
    ]
    frames_in = [
        pltpu.make_async_copy(a, frames.at[i], frame_sem.at[0, i])
        for i, a in enumerate((block_in, skip_in, gframes_in))
    ]
    for copy in grads_in + slots_in[0]:
        copy.start()
    for copies in slots_in[1:]:
        for copy in copies:
            copy.start()
    for copy in frames_in:
        copy.start()

    for slot in range(CAP + 1):
        tile_of[slot] = TILES
    count = jnp.int32(0)
    for tile in range(TILES):
        own = owners_ref[tile] == grp

        @pl.when(own)
        def _(count=count, tile=tile):
            tile_of[jnp.minimum(count, CAP)] = tile

        count = count + own.astype(jnp.int32)
    news = adam_update(
        queries_ref[...], qfirst_ref[...], qsecond_ref[...], dq_ref[...], QUERY_RATE
    )
    nqfirst_ref[...], nqsecond_ref[...], nqueries_ref[...] = news

    def slot_update(slot, carry):
        tile = tile_of[slot]
        used = (tile < TILES).astype(jnp.int32)
        tile = jnp.minimum(tile, TILES - 1)
        layer, kind = lax.div(tile, PER_LAYER), lax.rem(tile, PER_LAYER)
        plain = kind < 8
        pair = jnp.where(plain, lax.rem(kind, 2), (kind == 16).astype(jnp.int32))
        tap = jnp.where(plain, lax.div(kind, 2), 4)
        full = jnp.concatenate([grad[layer, 2 * pair, tap], grad[layer, 2 * pair + 1, tap]], axis=1)
        place = jnp.where(kind < 10, kind - 3, kind - 10)
        thin = low[layer, jnp.clip(place, 0, LOW_RANK - 1)]
        is_thin = ((kind >= 8) & (kind <= 14)).astype(jnp.int32)
        gradient = jnp.where(
            jnp.broadcast_to(is_thin, full.shape) > 0, thin.astype(F32), full.astype(F32)
        )
        old, old_first, old_second = master[slot], first[slot], second[slot]
        new_first, new_second, new = adam_update(old, old_first, old_second, gradient, LEARN_RATE)
        keep = jnp.broadcast_to(used, old.shape) > 0
        new = jnp.where(keep, new, old)
        one[slot] = jnp.where(keep, new_first, old_first)
        two[slot] = jnp.where(keep, new_second, old_second)
        three[slot] = new
        copied[slot] = new.astype(BF)
        return carry

    for copy in grads_in:
        copy.wait()
    outs = []
    for i, (start, number) in enumerate(CHUNKS):
        for copy in slots_in[i]:
            copy.wait()
        lax.fori_loop(start, start + number, slot_update, 0)
        for j, (a, b) in enumerate(
            ((one, nfirst_hbm), (two, nsecond_hbm), (three, nmaster_hbm), (copied, ncopy_hbm))
        ):
            copy = pltpu.make_async_copy(a.at[spots[i]], b.at[spots[i]], out_sem.at[i, j])
            copy.start()
            outs.append(copy)
    for i, target in enumerate((block_out, skip_out, gframes_out)):
        frames_in[i].wait()
        copy = pltpu.make_async_copy(frames.at[i], target, frame_sem.at[1, i])
        copy.start()
        outs.append(copy)
    for copy in outs:
        copy.wait()


CHUNKS = ((0, 3), (3, 3), (6, 3), (9, 4))


def update(owners, master, first, second, grads, low, queries, qfirst, qsecond, dq, *frames):
    any_, whole = any_spec(), vmem_spec()
    query = jax.ShapeDtypeStruct(queries.shape, F32)
    full = jax.ShapeDtypeStruct(master.shape, F32)
    passed = jax.ShapeDtypeStruct(frames[0].shape, F32)
    v = pltpu.VMEM
    slots = v(master.shape, F32)
    return pl.pallas_call(
        update_kernel,
        out_shape=(full, full, full, jax.ShapeDtypeStruct(master.shape, BF), query, query, query)
        + (passed,) * 3,
        in_specs=[smem_spec()] + [any_] * 5 + [whole] * 4 + [any_] * 3,
        out_specs=(any_,) * 4 + (whole,) * 3 + (any_,) * 3,
        scratch_shapes=[
            slots, slots, slots, v(grads.shape, BF), v(low.shape, BF),
            slots, slots, slots, v(master.shape, BF), v((3,) + passed.shape, F32),
            pltpu.SMEM((CAP + 1,), jnp.int32),
            pltpu.SemaphoreType.DMA((2,)),
            pltpu.SemaphoreType.DMA((len(CHUNKS), 3)),
            pltpu.SemaphoreType.DMA((len(CHUNKS), 4)),
            pltpu.SemaphoreType.DMA((2, 3)),
        ],
        compiler_params=pltpu.CompilerParams(vmem_limit_bytes=MEM),
        name="update",
    )(owners, master, first, second, grads, low, queries, qfirst, qsecond, dq, *frames)


def on_device(
    n_seq,
    frames_in,
    cond_frames,
    step_embed,
    prompts,
    prompt_lengths,
    pairing,
    dilations,
    owners,
    master,
    first_moment,
    second_moment,
    queries,
    query_first,
    query_second,
    grad_out,
    grad_skip,
):
    block, skip, gframes, own_grads, low, dq = train_step(
        n_seq, owners, dilations, prompt_lengths, pairing, step_embed, queries, master, prompts,
        frames_in, cond_frames, grad_out, grad_skip,
    )
    (
        new_first, new_second, new_master, new_copy, nqf, nqs, nq,
        block_out, skip_out, grad_frames,
    ) = update(
        owners, master, first_moment, second_moment, own_grads, low,
        queries, query_first, query_second, dq, block, skip, gframes,
    )
    return (
        new_first, new_second, new_master, new_copy, nqf, nqs, nq,
        block_out, skip_out, grad_frames,
    )


def solution(mesh):
    shard = P("grp", "seq", None)
    placed = (
        shard, shard, P("grp", None), P(), P(), P("grp"), P(), P(),
        shard, shard, shard, P(), P(), P(), shard, shard,
    )
    return jax.shard_map(
        functools.partial(on_device, mesh.shape["seq"]),
        mesh=mesh,
        in_specs=placed,
        out_specs=(shard, shard, shard, shard, P(), P(), P(), shard, shard, shard),
        check_vma=False,
    )
```

```python
import functools

import jax
import jax.numpy as jnp
from jax import lax
from jax.experimental import pallas as pl
from jax.experimental.pallas import tpu as pltpu
from jax.sharding import PartitionSpec as P

HEADS = 8
LAYERS = 2
DMAX = 8
CAP = 13
STEP = 10
PER_LAYER = 17
TILES = PER_LAYER * LAYERS

BETA_ONE = 0.9
BETA_TWO = 0.999
EPSILON = 1e-08
WEIGHT_DECAY = 0.01
LEARN_RATE = 0.02
QUERY_RATE = 0.4
HALF_ROOT = 0.7071067811865476
NEGATIVE = -1e30

BF = jnp.bfloat16
F32 = jnp.float32
HALO = 32
WIDE = 256
MAIN = 20
BLOCKS = MAIN * LAYERS
PHASES = (None, (0, MAIN), (MAIN, MAIN))
FILM_ORDER = (10, 11, 12, 13, 14, 8, 9)
FILM = 2 * len(FILM_ORDER)
LOW_RANK = len(FILM_ORDER)
HOP_ROWS = (24, 16, 32, 8, 8)
ORDER = (
    "fc", ("pr", 0), ("prep", 2), ("prep", 1), "fx", ("cross", 1), "fl", "hsK", ("cross", 2),
    ("pr", 1), ("end", 1), ("first", 1, 0), "heK", ("pr", 2), ("pr", 3), "att", "hsB", ("end", 2),
    ("first", 2, 0), ("first", 1, 2), ("first", 1, 3), ("first", 1, 1), ("second", 1, 2),
    ("second", 1, 3), ("second", 1, 0), ("second", 1, 1), "heB", "hsC", ("third", 1, 2),
    ("first", 2, 3), ("first", 2, 2), ("third", 1, 1), "heC", ("first", 2, 1), ("third", 1, 0),
    ("third", 1, 3), ("second", 2, 3), ("second", 2, 2), ("second", 2, 0), "win0", "condt",
    "gates0a", ("second", 2, 1), "gates0b", "res0", "skip0", ("third", 2, 3), ("third", 2, 0),
    ("third", 2, 2), "gatt0", ("third", 2, 1), "win1", "gates1a", "gates1b", "gatt1", "gg1a",
    "gg1b", "winb1", ("give", 1, 0), "fg1a", ("give", 1, 1), ("keep", 1, 0), ("keep", 1, 1),
    ("one", 1, 3), ("one", 1, 1), "fg1b", "gg0a", ("one", 1, 2), "gg0b", ("one", 1, 0), "winb0",
    "fg0b", "out1", ("give", 0, 0), "fg0a", ("give", 0, 1), ("two", 1, 3), "hs3", ("two", 1, 1),
    ("keep", 0, 0), ("two", 1, 2), ("two", 1, 0), ("keep", 0, 1), ("one", 0, 2), ("one", 0, 0),
    ("three", 1, 3), "he3", "hs4", ("three", 1, 2), ("three", 1, 1), ("one", 0, 3), ("one", 0, 1),
    ("two", 0, 2), ("two", 0, 0), "he4", "fb", "hs5", ("three", 1, 0), ("two", 0, 3), ("four", 1),
    ("two", 0, 1), ("three", 0, 2), "he5", ("three", 0, 3), ("three", 0, 0), "bundle",
    ("three", 0, 1), ("four", 0), ("five", 1), "low", "end",
)

MEM = 64 * 1024 * 1024 - 256 * 1024
MESH = pl.DeviceIdType.MESH


def block_table():
    table = {}
    for layer in range(LAYERS):
        base = PER_LAYER * layer
        start = MAIN * layer
        for part in range(4):
            for tap in range(4):
                table[base + 2 * tap + part // 2, part % 2] = start + 5 * part + tap
            table[base + 15 + part // 2, part % 2] = start + 5 * part + 4
    return table


BLOCK_OF = block_table()
FILM_OF = {
    (PER_LAYER * layer + tile, side): FILM * layer + 2 * place + side
    for layer in range(LAYERS)
    for place, tile in enumerate(FILM_ORDER)
    for side in range(2)
}


def mm(a, b):
    return lax.dot_general(a, b, (((1,), (0,)), ((), ())), preferred_element_type=F32)


def mm_nt(a, b):
    return lax.dot_general(a, b, (((1,), (1,)), ((), ())), preferred_element_type=F32)


def mm_nt_fine(a, b):
    high = a.astype(BF)
    return mm_nt(high, b) + mm_nt((a - high.astype(F32)).astype(BF), b)


def mm_low(a, b):
    return mm(a.astype(BF), b)


def mm_nt_low(a, b):
    return mm_nt(a.astype(BF), b)


def mm_nt_pairs(a, blocks):
    total = None
    for place, block in enumerate(blocks):
        term = mm_nt_fine(a[:, place * WIDE : (place + 1) * WIDE], block)
        total = term if total is None else total + term
    return total


def window(ref, start, count, width):
    group, rest = lax.div(start, 8), lax.rem(start, 8)
    groups = ref[pl.ds(group, count // 8 + 1), :, 0:width]
    turned = pltpu.roll(groups, lax.rem(8 - rest, 8), 1)
    row = lax.broadcasted_iota(jnp.int32, (1, 8, 1), 1)
    return jnp.where(row < 8 - rest, turned[:-1], turned[1:]).reshape(count, width)


def in_eights(value):
    return value.reshape(value.shape[0] // 8, 8, value.shape[1])


def place_of(n_seq):
    seq, grp = lax.axis_index("seq"), lax.axis_index("grp")
    z, y = lax.div(seq, 2), lax.rem(seq, 2)
    x, c = lax.div(grp, 2), lax.rem(grp, 2)
    return seq, grp, z, y, x, c


def greet(n_seq, seq, grp, groups):
    barrier = pltpu.get_barrier_semaphore()

    def one(k, carry):
        pl.semaphore_signal(
            barrier, inc=1, device_id={"seq": lax.rem(seq + k, n_seq), "grp": grp}, device_id_type=MESH
        )
        return carry

    lax.fori_loop(1, n_seq, one, 0)
    for k in range(1, groups):
        pl.semaphore_signal(
            barrier, inc=1, device_id={"seq": seq, "grp": lax.rem(grp + k, groups)}, device_id_type=MESH
        )
    pl.semaphore_wait(barrier, n_seq - 1 + groups - 1)


def any_spec():
    return pl.BlockSpec(memory_space=pl.ANY)


def vmem_spec():
    return pl.BlockSpec(memory_space=pltpu.VMEM)


def smem_spec():
    return pl.BlockSpec(memory_space=pltpu.SMEM)


def head_mask():
    row = lax.broadcasted_iota(jnp.int32, (HEADS, 512), 0)
    column = lax.broadcasted_iota(jnp.int32, (HEADS, 512), 1)
    return lax.div(column, 512 // HEADS) == row


def block_diagonal(rows):
    column = lax.div(lax.broadcasted_iota(jnp.int32, rows.shape, 1), 512 // HEADS)
    return jnp.concatenate([jnp.where(column == h, rows, 0.0) for h in range(HEADS)], axis=0)


def same_rows(row):
    return jnp.broadcast_to(row, (8, row.shape[1]))


def pack(vectors):
    pieces = [v[:, 128 * i : 128 * (i + 1)] for v in vectors for i in range(v.shape[1] // 128)]
    spare = -len(pieces) % 8
    if spare:
        pieces.append(jnp.zeros((spare, 128), pieces[0].dtype))
    return jnp.concatenate(pieces, axis=0)


def unpack(rows, place, pieces=4):
    return jnp.concatenate(
        [rows[pieces * place + i : pieces * place + i + 1] for i in range(pieces)], axis=1
    )


def step_kernel(
    n_seq, owners_ref, dil_ref, lengths_ref, pairing_ref, embed_ref, queries_ref, master_hbm,
    prompts_hbm, frames_hbm, cond_hbm, gout_hbm, gskip_hbm,
    block_hbm, skip_hbm, gframes_hbm, out_hbm, low_ref, dquery_ref,
    w, gs, prep, core_in, x_in, fr, fr_in, fx, ff, red_in, one_in, two_in, z_in, fin,
    xe, cat, slopes, gated, x1, bh, bb, sht, condt, gatt, bx, sk,
    master, prompt, probs, left, vec, sums, bundle,
    kv_out, kv_in, at_out, at_in, small_out, small_in, hop_src, hop_in,
    in_sem, prompt_sem, out_sem, hsend, hrecv, send, recv, hop_send, hop_recv, each_send, each_recv,
):
    seq, grp, z, y, x, c = place_of(n_seq)
    nz = n_seq // 2
    rows = prep.shape[1]
    own = frames_hbm.shape[1]
    grid_rows = own + 2 * HALO
    top = HALO + own
    channels = 512
    number = queries_ref.shape[1]
    sib, across, other_y = x * 2 + 1 - c, (1 - x) * 2 + c, z * 2 + 1 - y
    mine, theirs = 2 * c + x, 2 * c + 1 - x

    local_in = [
        pltpu.make_async_copy(a, b, in_sem.at[i])
        for i, (a, b) in enumerate(
            (
                (master_hbm, master),
                (frames_hbm.at[0], xe.at[pl.ds(HALO, own)]),
                (cond_hbm.at[0], cat.at[pl.ds(HALO, own), pl.ds(1536, channels)]),
                (gout_hbm.at[0], bb.at[pl.ds(HALO, own), pl.ds(0, channels)]),
                (gskip_hbm.at[0], bb.at[pl.ds(HALO, own), pl.ds(channels, channels)]),
            )
        )
    ]
    for copy in local_in:
        copy.start()

    def prompt_copy(turn, i):
        rows_now, columns = pl.ds(0, prompt.shape[0]), pl.ds((i % 2) * channels, channels)
        return pltpu.make_async_copy(
            prompts_hbm.at[4 * turn + i], slopes.at[i // 2, rows_now, columns], prompt_sem.at[i]
        )

    for i in range(4):
        prompt_copy(0, i).start()

    greet(n_seq, seq, grp, 4)

    waits = []
    used = [0]

    def remote(src, dst, to_seq, to_grp, sent=None):
        place = used[0]
        used[0] += 1
        copy = pltpu.make_async_remote_copy(
            src_ref=src,
            dst_ref=dst,
            send_sem=send.at[place],
            recv_sem=recv.at[place],
            device_id={"seq": to_seq, "grp": to_grp},
            device_id_type=MESH,
        )
        copy.start()
        (waits if sent is None else sent).append(copy)
        return copy

    after, before = lax.rem(seq + 1, n_seq), lax.rem(seq + n_seq - 1, n_seq)
    halos = []
    for ref, buffer, column in (
        (frames_hbm, xe, 0),
        (cond_hbm, cat, 1536),
        (gout_hbm, bb, 0),
        (gskip_hbm, bb, channels),
    ):
        for start, at, target in ((own - HALO, 0, after), (0, top, before)):
            place = len(halos)
            copy = pltpu.make_async_remote_copy(
                src_ref=ref.at[0, pl.ds(start, HALO)],
                dst_ref=buffer.at[pl.ds(at, HALO), pl.ds(column, channels)],
                send_sem=hsend.at[place],
                recv_sem=hrecv.at[place],
                device_id={"seq": target, "grp": grp},
                device_id_type=MESH,
            )
            copy.start()
            halos.append(copy)

    slots, flags = [], []
    count = jnp.int32(0)
    for tile in range(TILES):
        flag = (owners_ref[tile] == grp).astype(jnp.int32)
        slots.append(jnp.minimum(count, CAP - 1))
        flags.append(flag.astype(F32))
        count = count + flag

    def rounded(tile):
        return (master[slots[tile]] * flags[tile]).astype(BF)

    def ready(tiles, buffer, table):
        for tile in tiles:
            value = rounded(tile)
            buffer[table[tile, 0]] = value[:, :WIDE]
            buffer[table[tile, 1]] = value[:, WIDE:]

    def merge_start(phase):
        base, blocks = PHASES[phase]
        each = blocks // 4
        return remote(
            prep.at[pl.ds(base + 2 * (1 - c) * each, 2 * each)],
            core_in.at[pl.ds(base // 2, 2 * each)],
            seq, sib,
        )

    def merge_cross(phase, copy):
        base, blocks = PHASES[phase]
        each = blocks // 4
        copy.wait_recv()

        def add(i, carry):
            place = base // 2 + i
            core_in[place] = core_in[place] + prep[base + 2 * c * each + i]
            return carry

        lax.fori_loop(0, 2 * each, add, 0)
        return remote(
            core_in.at[pl.ds(base // 2 + (1 - x) * each, each)],
            x_in.at[pl.ds(base // 4, each)],
            seq, across,
        )

    def view(phase, quarter, zz, yy):
        base, blocks = PHASES[phase]
        each = blocks // 4
        return w.at[pl.ds(base + quarter * each, each), zz, yy]

    gathering, legs = [], {}

    def spread(ref, to_seq, to_grp):
        return remote(ref, ref, to_seq, to_grp, gathering)

    def merge_end(phase, copy):
        base, blocks = PHASES[phase]
        each = blocks // 4
        copy.wait_recv()

        def settle(i, carry):
            w[base + mine * each + i, z, y] = (
                core_in[base // 2 + x * each + i] + x_in[base // 4 + i]
            )
            return carry

        lax.fori_loop(0, each, settle, 0)

    def y_first(zz):
        return 1 - jnp.minimum(lax.div(2 * zz, nz), 1)

    def spread_z(phase):
        ref = view(phase, mine, z, y)
        for k in range(1, nz):
            legs[phase, k] = spread(ref, lax.rem(z + k, nz) * 2 + y, grp)

    core_legs = {phase: [] for phase in (1, 2)}

    def first(phase, k):
        zs = lax.rem(z - k + nz, nz)
        a = y_first(zs)
        b = 1 - a
        if k:
            legs[phase, k].wait_recv()
        ref = view(phase, mine, zs, y)
        one = spread(ref, a * other_y + b * seq, a * grp + b * across)
        two = spread(ref, a * seq + b * other_y, a * across + b * grp)
        core_legs[phase].append(spread(ref, seq, sib))
        legs[phase, k] = (zs, a, one, two)

    def second(phase, k):
        zs, a, one, two = legs[phase, k]
        b = 1 - a
        one.wait_recv()
        ref = view(phase, a * mine + b * theirs, zs, a * (1 - y) + b * y)
        last = spread(ref, a * seq + b * other_y, a * across + b * grp)
        core_legs[phase].append(spread(ref, seq, sib))
        legs[phase, k] = (zs, a, two, last)

    def third(phase, k):
        zs, a, two, last = legs[phase, k]
        b = 1 - a
        two.wait_recv()
        ref = view(phase, a * theirs + b * mine, zs, a * y + b * (1 - y))
        core_legs[phase].append(spread(ref, seq, sib))
        last.wait_recv()
        core_legs[phase].append(spread(view(phase, theirs, zs, 1 - y), seq, sib))

    def arrived(phase):
        for copy in core_legs[phase]:
            copy.wait_recv()

    def hop_refs(j):
        start = sum(HOP_ROWS[:j])
        spot = pl.ds(start, HOP_ROWS[j])
        return hop_src.at[spot], hop_in.at[seq, spot], hop_in.at[:, spot]

    def hop_copy(j, k):
        src, dst, _ = hop_refs(j)
        return pltpu.make_async_remote_copy(
            src_ref=src,
            dst_ref=dst,
            send_sem=hop_send.at[j, k],
            recv_sem=hop_recv.at[j, k],
            device_id={"seq": lax.rem(seq + k, n_seq), "grp": grp},
            device_id_type=MESH,
        )

    def hop_start(j, value):
        src, dst, _ = hop_refs(j)
        value = value.astype(src.dtype)
        src[...] = value
        dst[...] = value

        def one(k, carry):
            hop_copy(j, k).start()
            return carry

        lax.fori_loop(1, n_seq, one, 0)

    def hop_end(j):
        def one(k, carry):
            hop_copy(j, k).wait()
            return carry

        lax.fori_loop(1, n_seq, one, 0)
        _, _, whole = hop_refs(j)

        def add(i, total):
            return total + whole[i].astype(F32)

        return lax.fori_loop(0, n_seq, add, jnp.zeros((HOP_ROWS[j], 128), F32))

    position = lax.broadcasted_iota(jnp.int32, (channels, rows), 0)
    column = lax.broadcasted_iota(jnp.int32, (channels, rows), 1)
    chosen = jnp.where(position == column + seq * rows, 1.0, 0.0).astype(BF)

    def pick(v):
        return mm_low(v, chosen)

    def film_block(layer, place):
        return ff[FILM * layer + place]

    def film_rows(layer, v, places):
        return jnp.concatenate([mm_low(v, film_block(layer, i)) for i in places], axis=1)

    def film_back(layer, v, places):
        total = None
        for i, place in enumerate(places):
            term = mm_nt_low(v[:, i * WIDE : (i + 1) * WIDE], film_block(layer, place))
            total = term if total is None else total + term
        return mm_nt_low(total, chosen)

    wide_head = channels // HEADS
    copies_of = n_seq // HEADS
    head = lax.div(seq, copies_of)
    lane = lax.broadcasted_iota(jnp.int32, (channels, 128), 1)
    at_row = lax.broadcasted_iota(jnp.int32, (channels, 128), 0)
    of_head = at_row == head * wide_head + lax.rem(lane, wide_head)
    head_columns = jnp.where(of_head, 1.0, 0.0).astype(BF)
    own_half = lax.div(lax.broadcasted_iota(jnp.int32, (8, 128), 1), wide_head) == (
        lax.broadcasted_iota(jnp.int32, (8, 128), 0)
    )

    def exchange(index, source, target):
        def copy(k):
            dest = lax.rem(seq + k, n_seq)
            return pltpu.make_async_remote_copy(
                src_ref=source(dest),
                dst_ref=target,
                send_sem=each_send.at[index, k],
                recv_sem=each_recv.at[index, k],
                device_id={"seq": dest, "grp": grp},
                device_id_type=MESH,
            )

        def begin():
            def one(k, carry):
                copy(k).start()
                return carry

            lax.fori_loop(1, n_seq, one, 0)

        def finish():
            def one(k, carry):
                copy(k).wait()
                return carry

            lax.fori_loop(1, n_seq, one, 0)

        return begin, finish

    kv_begin, kv_finish = exchange(
        0, lambda dest: kv_out.at[lax.div(dest, copies_of)], kv_in.at[seq]
    )
    at_begin, at_finish = exchange(1, lambda dest: at_out.at[dest], at_in.at[seq])
    small_begin, small_finish = exchange(2, lambda dest: small_out, small_in.at[seq])

    def head_weights():
        value = kv_in[...].reshape(channels, WIDE)
        return value[:, 0:128], value[:, 128:256]

    def attention():
        keys, values = head_weights()
        pieces = []
        for layer in range(LAYERS):
            high = queries_ref[layer].astype(BF)
            rest = (queries_ref[layer] - high.astype(F32)).astype(BF)
            both = mm(high, head_columns) + mm(rest, head_columns)
            half = lax.div(lax.broadcasted_iota(jnp.int32, both.shape, 1), wide_head)
            pieces.append(jnp.where(half == layer, both, 0.0))
        probe = mm_nt_fine(jnp.concatenate(pieces, axis=0), keys)
        pr = prompt[...]
        scores = mm_nt_fine(probe, pr) * 0.125
        live = lax.broadcasted_iota(jnp.int32, scores.shape, 1) < lengths_ref[pairing_ref[0]]
        scores = jnp.where(live, scores, NEGATIVE)
        weight = jnp.exp(scores - jnp.max(scores, axis=1, keepdims=True))
        value = weight / jnp.sum(weight, axis=1, keepdims=True)
        probs[...] = value
        mean = jnp.concatenate(
            [
                jnp.mean(value[l * number : (l + 1) * number], axis=0, keepdims=True)
                for l in range(LAYERS)
            ]
            + [jnp.zeros((8 - LAYERS, value.shape[1]), F32)],
            axis=0,
        )
        seen = mm_low(mean, pr)
        mixed = jnp.where(own_half, mm_low(seen, values), 0.0)
        left[0:8] = seen
        left[8:16] = mm_nt_low(mixed, head_columns)

    def wblock(layer, place):
        return w[MAIN * layer + place].reshape(channels, WIDE)

    def inside(low, count):
        row = lax.broadcasted_iota(jnp.int32, (count, 1), 0) + (low - HALO) + seq * own
        return (row >= 0) & (row < n_seq * own)

    def windows_forward(layer):
        low = 16 * layer
        high = grid_rows - low
        scale, shift = 1.0 + vec[layer, 0:1], vec[layer, 1:2]
        here = xe[...].astype(F32) if layer == 0 else x1[...]
        shifted = (here * scale + shift).astype(BF).astype(F32)
        shifted = jnp.where(inside(0, grid_rows), shifted, 0.0)
        groups = grid_rows // 8
        bh[0] = jnp.zeros((8, channels), F32)
        bh[1 : 1 + groups] = in_eights(shifted)
        bh[1 + groups :] = jnp.zeros((3, 8, channels), F32)
        sht[layer] = jnp.transpose(shifted[HALO:top]).astype(BF)
        cat[low:high, channels : 2 * channels] = shifted[low:high].astype(BF)
        for tap in (0, 2):
            start = 8 + low + (tap - 1) * dil_ref[layer]
            cat[low:high, tap * channels : (tap + 1) * channels] = window(
                bh, start, high - low, channels
            ).astype(BF)

    def gates(layer, first_row, rows_now):
        spot = slice(first_row, first_row + rows_now)
        value = cat[spot, 0:2048]
        for part in range(2):
            columns = slice(part * WIDE, (part + 1) * WIDE)
            base = MAIN * layer + 5 * part
            lhs = mm(value, w[base : base + 4].reshape(2048, WIDE))
            tangent = jnp.tanh(lhs + vec[layer, 2:3, columns])
            rhs = mm(value, w[base + 10 : base + 14].reshape(2048, WIDE))
            opening = jax.nn.sigmoid(rhs + vec[layer, 3:4, columns])
            gate = tangent * opening
            gated[spot, columns] = gate.astype(BF)
            slopes[layer, spot, columns] = (opening * (1.0 - tangent * tangent)).astype(BF)
            other = slice(channels + part * WIDE, channels + (part + 1) * WIDE)
            slopes[layer, spot, other] = (gate * (1.0 - opening)).astype(BF)

    def residual(layer, first_row, rows_now):
        value = gated[first_row : first_row + rows_now]
        for part in range(2):
            columns = slice(part * WIDE, (part + 1) * WIDE)
            term = mm(value, wblock(layer, 5 * part + 4))
            if layer == 0:
                base = xe[first_row : first_row + rows_now, columns].astype(F32)
                x1[first_row : first_row + rows_now, columns] = (base + term) * HALF_ROOT
            else:
                base = x1[first_row : first_row + rows_now, columns]
                x1[first_row : first_row + rows_now, columns] = (base + term) * HALF_ROOT

    def skipped(layer, first_row, rows_now):
        value = gated[first_row : first_row + rows_now]
        spot = slice(first_row - HALO, first_row - HALO + rows_now)
        for part in range(2):
            columns = slice(part * WIDE, (part + 1) * WIDE)
            term = mm(value, wblock(layer, 5 * part + 14))
            if layer == 0:
                sk[spot, columns] = term
            else:
                sk[spot, columns] = sk[spot, columns] + term

    low, high = 16, grid_rows - 16

    def gate_grads(layer, first_row, rows_now):
        spot = slice(first_row, first_row + rows_now)
        bb[spot, 0:channels] = (bx[spot] * HALF_ROOT).astype(BF)
        branch = jnp.concatenate([wblock(layer, 5 * part + 4) for part in range(4)], axis=1)
        back = mm_nt(bb[spot], branch)
        keep = inside(first_row, rows_now)
        for side in range(2):
            columns = slice(side * channels, (side + 1) * channels)
            value = back * slopes[layer, spot, columns].astype(F32)
            middle = slice((2 + side) * channels, (3 + side) * channels)
            cat[spot, middle] = jnp.where(keep, value, 0.0).astype(BF)

    def windows_backward(layer):
        reach, limit = (low, high) if layer else (HALO, top)
        edge = 1 + low // 8
        bh[0:edge] = jnp.zeros((edge, 8, channels), F32)
        bh[1 + high // 8 :] = jnp.zeros((edge + 2, 8, channels), F32)
        for side in range(2):
            middle = slice((2 + side) * channels, (3 + side) * channels)
            value = cat[low:high, middle].astype(F32)
            bh[edge : 1 + high // 8] = in_eights(value)
            total = jnp.sum(value[HALO - low : top - low], axis=0, keepdims=True)
            sums[layer, 2 + side : 3 + side] = total
            for tap in (0, 2):
                start = 8 + reach - (tap - 1) * dil_ref[layer]
                columns = slice((2 * tap + side) * channels, (2 * tap + side + 1) * channels)
                cat[reach:limit, columns] = window(bh, start, limit - reach, channels).astype(BF)

    def frame_grads(layer, first_row, rows_now):
        spot = slice(first_row, first_row + rows_now)
        taps = jnp.concatenate(
            [wblock(layer, 5 * part + tap) for tap in range(3) for part in range(4)], axis=1
        )
        back = mm_nt(cat[spot], taps)
        if layer:
            here = x1[spot]
            row = lax.broadcasted_iota(jnp.int32, (rows_now, 1), 0) + first_row
            kept = jnp.where((row >= HALO) & (row < top), back, 0.0)
        else:
            here = xe[spot].astype(F32)
            kept = back
        sums[layer, 0:1] += jnp.sum(kept * here, axis=0, keepdims=True)
        sums[layer, 1:2] += jnp.sum(kept, axis=0, keepdims=True)
        bx[spot] = bx[spot] * HALF_ROOT + back * (1.0 + vec[layer, 0:1])

    def weight_grad(layer, part, i):
        if i < 4:
            tap = i if i < 3 else 1
            start = pl.multiple_of(tap * 1024 + part * WIDE, WIDE)
            lhs = sht[layer] if i < 3 else condt[...]
            return mm(lhs, cat[HALO:top, pl.ds(start, WIDE)])
        start = pl.multiple_of(part * WIDE, WIDE)
        return mm(gatt[layer], bb[HALO:top, pl.ds(start, WIDE)])

    core_sent = {}

    def give(layer, xx):
        part = 2 * (1 - c) + xx
        buffer, base = (gs, 0) if layer else (w, MAIN)
        for i in range(5):
            value = weight_grad(layer, part, i).astype(BF)
            buffer[base + 5 * xx + i] = value.reshape(nz, 2, rows, WIDE)
        core_sent[layer, xx] = remote(
            buffer.at[pl.ds(base + 5 * xx, 5)], red_in.at[layer, pl.ds(5 * xx, 5)], seq, sib
        )

    def keep(layer, xx):
        part = 2 * c + xx
        core_sent[layer, xx].wait_recv()
        for i in range(5):
            value = weight_grad(layer, part, i).reshape(nz, 2, rows, WIDE)
            spot = 5 * xx + i
            red_in[layer, spot] = (red_in[layer, spot].astype(F32) + value).astype(BF)

    ones, twos, zs, targets = {}, {}, {}, {}
    for k in range(nz):
        zd = lax.rem(z + k, nz)
        targets[k] = (zd, y_first(zd))

    def red_one(layer, k):
        zd, a = targets[k]
        b = 1 - a
        ones[layer, k] = []
        for j in range(2):
            xi, yi = a * (1 - x) + b * j, a * j + b * (1 - y)
            ones[layer, k].append(
                remote(
                    red_in.at[layer, pl.ds(5 * xi, 5), zd, yi],
                    one_in.at[layer, k, j],
                    a * seq + b * other_y, a * across + b * grp,
                )
            )

    def red_two(layer, k):
        zd, a = targets[k]
        b = 1 - a
        you = a * y + b * x
        for j in range(2):
            ones[layer, k][j].wait_recv()
            xi, yi = a * x + b * j, a * j + b * y

            def body(i, carry, j=j, xi=xi, yi=yi):
                one_in[layer, k, j, i] = (
                    one_in[layer, k, j, i] + red_in[layer, 5 * xi + i, zd, yi]
                )
                return carry

            lax.fori_loop(0, 5, body, 0)
        twos[layer, k] = remote(
            one_in.at[layer, k, 1 - you], two_in.at[layer, k],
            a * other_y + b * seq, a * grp + b * across,
        )

    def red_three(layer, k):
        zd, a = targets[k]
        you = a * y + (1 - a) * x
        twos[layer, k].wait_recv()

        def body(i, carry):
            two_in[layer, k, i] = two_in[layer, k, i] + one_in[layer, k, you, i]
            return carry

        lax.fori_loop(0, 5, body, 0)
        if k:
            zs[layer, k] = remote(two_in.at[layer, k], z_in.at[layer, k - 1], zd * 2 + y, grp)

    lasts = {}
    outs = []

    def local_out(src, dst):
        copy = pltpu.make_async_copy(src, dst, out_sem.at[len(outs)])
        copy.start()
        outs.append(copy)

    def red_four(layer):
        for k in range(1, nz):
            zs[layer, k].wait_recv()

        def body(i, carry):
            total = two_in[layer, 0, i].astype(F32)
            for k in range(1, nz):
                total = total + z_in[layer, k - 1, i].astype(F32)
            fin[layer, i] = total.astype(BF)
            return carry

        lax.fori_loop(0, 5, body, 0)
        src, dst = fin.at[layer], out_hbm.at[layer, mine]
        lasts[layer] = [remote(src, dst, seq, across), remote(src, dst, seq, sib)]
        if not layer:
            lasts[layer].append(remote(src, dst, seq, (1 - x) * 2 + 1 - c))
        local_out(src, dst)

    def red_five(layer):
        lasts[layer][0].wait_recv()
        ref = out_hbm.at[layer, theirs]
        lasts[layer].append(remote(ref, ref, seq, sib))

    ops = {}

    def op(*key):
        def keep_op(body):
            ops[key] = body
            return body

        return keep_op

    main_tiles = (0, 1, 2, 3, 4, 5, 6, 7, 15, 16)
    merges, crosses, film_sent, seen, hops = {}, {}, {}, {}, {}
    half = fr.shape[0] // 2
    half_spot = pl.ds(c * half, half)
    size_all, size_mid, size_own = grid_rows // 2, (high - low) // 2, own // 2
    embed = same_rows(embed_ref[...].astype(F32))

    for phase in (1, 2):

        @op("prep", phase)
        def _(phase=phase):
            ready([PER_LAYER * (phase - 1) + t for t in main_tiles], prep, BLOCK_OF)
            merges[phase] = merge_start(phase)

        @op("cross", phase)
        def _(phase=phase):
            crosses[phase] = merge_cross(phase, merges[phase])

        @op("end", phase)
        def _(phase=phase):
            merge_end(phase, crosses[phase])
            spread_z(phase)

    def quarter(j):
        return range(j * nz // 4, (j + 1) * nz // 4)

    for phase in (1, 2):
        for j in range(4):
            for name, body in (("first", first), ("second", second), ("third", third)):

                @op(name, phase, j)
                def _(phase=phase, j=j, body=body):
                    for k in quarter(j):
                        body(phase, k)

    @op("fc")
    def _():
        for layer in range(LAYERS):
            ready([PER_LAYER * layer + t for t in FILM_ORDER], fr, FILM_OF)
        film_sent[0] = remote(fr.at[pl.ds((1 - c) * half, half)], fr_in, seq, sib)

    @op("fx")
    def _():
        film_sent[0].wait_recv()
        fr_in[...] = fr_in[...] + fr[half_spot]
        film_sent[1] = remote(fr_in, fx, seq, across)

    @op("fl")
    def _():
        film_sent[1].wait_recv()
        ff[half_spot] = fr_in[...] + fx[...]
        film_sent[2] = remote(ff.at[half_spot], ff.at[half_spot], seq, sib)

    for turn in range(4):

        @op("pr", turn)
        def _(turn=turn):
            total = prompt[...] if turn else None
            for i in range(4):
                prompt_copy(turn, i).wait()
                flag = (pairing_ref[0] == 4 * turn + i).astype(F32).astype(BF)
                part = slice((i % 2) * channels, (i % 2 + 1) * channels)
                term = slopes[i // 2, 0 : prompt.shape[0], part] * flag
                total = term if total is None else total + term
            prompt[...] = total
            if turn < 3:
                for i in range(4):
                    prompt_copy(turn + 1, i).start()

    def gathered():
        while gathering:
            gathering.pop().wait_send()

    def film_rows_here():
        if 3 not in film_sent:
            film_sent[2].wait_recv()
            film_sent[3] = True

    @op("condt")
    def _():
        local_in[2].wait()
        condt[...] = jnp.transpose(cat[HALO:top, 1536:2048].astype(F32)).astype(BF)

    @op("hsK")
    def _():
        film_rows_here()
        for h in range(HEADS):
            columns = slice((h % 4) * wide_head, (h % 4 + 1) * wide_head)
            pieces = [
                film_block(layer, place + h // 4).astype(F32)[:, columns]
                for place in (0, 2)
                for layer in range(LAYERS)
            ]
            kv_out[h] = jnp.concatenate(pieces, axis=1).astype(BF)
        kv_in[seq] = kv_out[head]
        kv_begin()

    @op("heK")
    def _():
        kv_finish()

    @op("att")
    def _():
        attention()

    @op("hsB")
    def _():
        vectors = []
        embed_here, mixed = pick(embed), pick(left[8:16])
        for layer in range(LAYERS):
            vectors.append(film_rows(layer, mixed, (4, 5))[layer : layer + 1])
            steps = film_rows(layer, embed_here, (10, 11, 12, 13))
            vectors += [steps[0:1, :channels], steps[0:1, channels:]]
        hop_start(0, pack(vectors))

    @op("heB")
    def _():
        total = hop_end(0)
        hops["pooled"] = [unpack(total, 3 * layer) for layer in range(LAYERS)]
        for layer in range(LAYERS):
            vec[layer, 2:3] = unpack(total, 3 * layer + 1)
            vec[layer, 3:4] = unpack(total, 3 * layer + 2)

    @op("hsC")
    def _():
        vectors = []
        for layer in range(LAYERS):
            pooled = hops["pooled"][layer]
            film = film_rows(layer, pick(same_rows(pooled)), (6, 7, 8, 9))
            vectors += [film[0:1, :channels], film[0:1, channels:]]
        hop_start(1, pack(vectors))

    @op("heC")
    def _():
        total = hop_end(1)
        for layer in range(LAYERS):
            vec[layer, 0:1] = unpack(total, 2 * layer)
            vec[layer, 1:2] = unpack(total, 2 * layer + 1)

    @op("win0")
    def _():
        local_in[1].wait()
        for copy in halos[:4]:
            copy.wait_recv()
        windows_forward(0)

    @op("win1")
    def _():
        local_in[3].wait()
        local_in[4].wait()
        for copy in halos[4:]:
            copy.wait_recv()
        bx[...] = bb[:, 0:channels].astype(F32)
        windows_forward(1)

    for layer in range(LAYERS):
        start, size = (low, size_mid) if layer else (0, size_all)
        for part, name in enumerate("ab"):
            first_row = start + part * size

            @op(f"gates{layer}{name}")
            def _(layer=layer, first_row=first_row, size=size, part=part):
                if not part:
                    arrived(1 + layer)
                gates(layer, first_row, size)

        @op(f"gatt{layer}")
        def _(layer=layer):
            gatt[layer] = jnp.transpose(gated[HALO:top].astype(F32)).astype(BF)

    @op("res0")
    def _():
        for part in range(2):
            residual(0, part * size_all, size_all)

    @op("skip0")
    def _():
        for part in range(2):
            skipped(0, HALO + part * size_own, size_own)

    @op("out1")
    def _():
        for part in range(2):
            residual(1, HALO + part * size_own, size_own)
            skipped(1, HALO + part * size_own, size_own)
        local_out(x1.at[pl.ds(HALO, own)], block_hbm.at[0])
        local_out(sk, skip_hbm.at[0])

    for layer in range(LAYERS):
        for part, name in enumerate("ab"):

            @op(f"gg{layer}{name}")
            def _(layer=layer, part=part):
                if layer and not part:
                    sums[...] = jnp.zeros_like(sums)
                gate_grads(layer, low + part * size_mid, size_mid)

            @op(f"fg{layer}{name}")
            def _(layer=layer, part=part):
                if layer:
                    frame_grads(1, low + part * size_mid, size_mid)
                else:
                    frame_grads(0, HALO + part * size_own, size_own)

        @op(f"winb{layer}")
        def _(layer=layer):
            windows_backward(layer)

        for xx in range(2):

            @op("give", layer, xx)
            def _(layer=layer, xx=xx):
                if not layer:
                    gathered()
                give(layer, xx)

            @op("keep", layer, xx)
            def _(layer=layer, xx=xx):
                keep(layer, xx)

        for j in range(4):
            for name, body in (("one", red_one), ("two", red_two), ("three", red_three)):

                @op(name, layer, j)
                def _(layer=layer, j=j, body=body):
                    for k in quarter(j):
                        body(layer, k)

        @op("four", layer)
        def _(layer=layer):
            red_four(layer)

    @op("five", 1)
    def _():
        red_five(1)

    @op("hs3")
    def _():
        local_out(bx.at[pl.ds(HALO, own)], gframes_hbm.at[0])
        hop_start(2, pack([sums[l, i : i + 1] for l in range(LAYERS) for i in range(4)]))

    @op("he3")
    def _():
        total = hop_end(2)
        hops["sides"] = [[unpack(total, 4 * l + i) for i in range(4)] for l in range(LAYERS)]

    @op("hs4")
    def _():
        vectors = []
        for layer in range(LAYERS):
            dfilm = same_rows(jnp.concatenate(hops["sides"][layer][0:2], axis=1))
            vectors.append(film_back(layer, dfilm, (6, 7, 8, 9))[0:1])
        hop_start(3, pack(vectors))

    @op("he4")
    def _():
        total = hop_end(3)
        hops["dpooled"] = [unpack(total, layer) for layer in range(LAYERS)]

    rt_at, dq_at, lt_at = 0, 16 * LAYERS, (16 + number) * LAYERS

    @op("fb")
    def _():
        vectors = [
            film_back(l, same_rows(hops["dpooled"][l]), (4, 5))[0:1] for l in range(LAYERS)
        ]
        if copies_of > 1:
            hop_start(4, pack(vectors))
            total = hop_end(4)
            vectors = [unpack(total, layer) for layer in range(LAYERS)]
        dmixed = jnp.concatenate(vectors + [jnp.zeros((8 - LAYERS, channels), F32)], axis=0)
        dmixed = jnp.where(own_half, mm_low(dmixed, head_columns), 0.0)
        keys, values = head_weights()
        pr = prompt[...]
        dmean = mm_nt_low(mm_nt_low(dmixed, values), pr) * (1.0 / number)
        dprobs = jnp.concatenate(
            [jnp.broadcast_to(dmean[l : l + 1], (number, channels)) for l in range(LAYERS)], axis=0
        )
        value = probs[...]
        inner = jnp.sum(dprobs * value, axis=1, keepdims=True)
        dprobe = mm_low(value * (dprobs - inner) * 0.125, pr)
        dqueries = mm_low(dprobe, keys)
        half = lax.div(lax.broadcasted_iota(jnp.int32, (number, 128), 1), wide_head)
        dquery = jnp.where(half == 0, dqueries[0:number], dqueries[number : 2 * number])
        small_out[...] = jnp.concatenate(
            [dquery, dmixed, jnp.zeros((8, 128), F32)], axis=0
        ).astype(BF)
        lefts = jnp.concatenate(
            [dprobe, left[0:2], left[8:10]]
            + [hops["pooled"][layer] for layer in range(LAYERS)]
            + [embed[0:1], jnp.zeros((128 - 2 * number - 7, channels), F32)],
            axis=0,
        )
        at_out[...] = jnp.transpose(lefts).astype(BF).reshape(n_seq, rows, 128)

    @op("hs5")
    def _():
        small_in[seq] = small_out[...]
        at_in[seq] = at_out[seq]
        small_begin()
        at_begin()

    @op("he5")
    def _():
        small_finish()
        at_finish()

        def halves(one, two):
            wanted = lax.broadcasted_iota(jnp.int32, one.shape, 1) < wide_head
            return (
                jnp.where(wanted, one, pltpu.roll(two, wide_head, 1)),
                jnp.where(wanted, pltpu.roll(one, wide_head, 1), two),
            )

        blocks = [[], []]
        for h in range(0, HEADS, 2):
            pair = halves(
                small_in[h * copies_of].astype(F32), small_in[(h + 1) * copies_of].astype(F32)
            )
            for layer in range(LAYERS):
                blocks[layer].append(pair[layer])
        for layer in range(LAYERS):
            full = jnp.concatenate(blocks[layer], axis=1)
            start = dq_at + number * layer
            bundle[grp, start : start + number, 0:channels] = full[0:number].astype(BF)
            dmixed = full[number + layer : number + layer + 1]
            place = rt_at + 16 * layer
            bundle[grp, place : place + 16, 0:channels] = jnp.concatenate(
                hops["sides"][layer]
                + [hops["dpooled"][layer], dmixed, jnp.zeros((10, channels), F32)],
                axis=0,
            ).astype(BF)
        spot = slice(lt_at, lt_at + rows)
        at = lax.broadcasted_iota(jnp.int32, (rows, 128), 1)
        thin = jnp.where(at >= 66, at_in[seq].astype(F32), 0.0)
        for h in range(0, HEADS, 2):
            one, two = at_in[h * copies_of].astype(F32), at_in[(h + 1) * copies_of].astype(F32)
            pair = jnp.where(at < wide_head, one, pltpu.roll(two, wide_head, 1))
            bundle[grp, spot, h * wide_head : (h + 2) * wide_head] = pair.astype(BF)
            for k, value in ((h, one), (h + 1, two)):
                turned = pltpu.roll(value, wide_head + 2 * k, 1)
                thin = jnp.where(lax.div(at, 2) == k, turned, thin)
        bundle[grp, spot, channels : channels + 128] = thin.astype(BF)

    bundles = []

    @op("bundle")
    def _():
        for k in range(1, 4):
            ref = bundle.at[grp]
            bundles.append(remote(ref, ref, seq, lax.rem(grp + k, 4)))

    @op("low")
    def _():
        for copy in bundles:
            copy.wait_recv()
        for layer in range(LAYERS):
            spot = slice(dq_at + number * layer, dq_at + number * (layer + 1))
            total = bundle[0, spot, 0:channels].astype(F32)
            for k in range(1, 4):
                total = total + bundle[k, spot, 0:channels].astype(F32)
            dquery_ref[layer] = total
        mask = head_mask()
        at = lax.broadcasted_iota(jnp.int32, (8, channels), 0)
        spot = slice(lt_at, lt_at + rows)
        probe = bundle[0, spot, 0:channels].astype(F32)
        for k in range(1, 4):
            probe = probe + bundle[k, spot, 0:channels].astype(F32)
        probe = probe.astype(BF)
        blank = jnp.zeros((number, channels), F32)
        column = lax.div(lax.broadcasted_iota(jnp.int32, (number, channels), 1), wide_head)
        for layer in range(LAYERS):
            side = []
            for h in range(HEADS):
                one = jnp.where(column == h, queries_ref[layer], 0.0)
                side += [blank, one] if layer else [one, blank]
            low_ref[layer, 0] = mm(probe, jnp.concatenate(side, axis=0).astype(BF)).astype(BF)
            total = None
            for k in range(4):
                right = bundle[k, 16 * layer : 16 * layer + 16, 0:channels].astype(F32)
                dmixed = jnp.where(mask, right[5:6], 0.0)
                nothing = jnp.zeros((1, channels), F32)
                rows_of = []
                for h in range(HEADS):
                    one = dmixed[h : h + 1]
                    rows_of += [nothing, one] if layer else [one, nothing]
                value = jnp.concatenate(rows_of, axis=0)
                gap = jnp.zeros((48, channels), F32)
                rest = jnp.zeros((56, channels), F32)
                pieces = [jnp.concatenate([value, gap, jnp.zeros((64, channels), F32)], axis=0)]
                for i, row in ((4, 2), (0, 4), (1, 4), (2, 6), (3, 6)):
                    row = row + (layer if row < 6 else 0)
                    one = jnp.where(at == row, right[i : i + 1], 0.0)
                    pieces.append(
                        jnp.concatenate([jnp.zeros((64, channels), F32), one, rest], axis=0)
                    )
                term = mm(
                    bundle[k, spot, channels : channels + 128],
                    jnp.concatenate(pieces, axis=1).astype(BF),
                )
                total = term if total is None else total + term
            for i in range(6):
                low_ref[layer, 1 + i] = total[:, i * channels : (i + 1) * channels].astype(BF)

    @op("end")
    def _():
        for copies in lasts.values():
            for copy in copies[1:]:
                copy.wait_recv()
        lasts[0][0].wait_recv()
        for copy in outs:
            copy.wait()
        for copy in halos:
            copy.wait_send()
        gathered()
        for copy in waits:
            copy.wait_send()

    local_in[0].wait()
    for key in ORDER:
        ops[key if isinstance(key, tuple) else (key,)]()


def train_step(
    n_seq, owners, dilations, lengths, pairing, step_embed, queries, master, prompts,
    frames_in, cond_frames, grad_out, grad_skip,
):
    _, own, channels = frames_in.shape
    rows = master.shape[1]
    number = queries.shape[1]
    grid_rows = own + 2 * HALO
    nz = n_seq // 2
    v = pltpu.VMEM
    dma = pltpu.SemaphoreType.DMA
    frame_out = jax.ShapeDtypeStruct((1, own, channels), F32)
    film = FILM * LAYERS
    copies = 40 + 24 * nz
    return pl.pallas_call(
        functools.partial(step_kernel, n_seq),
        out_shape=(
            frame_out,
            frame_out,
            frame_out,
            jax.ShapeDtypeStruct((LAYERS, 4, 5, rows, WIDE), BF),
            jax.ShapeDtypeStruct((LAYERS, LOW_RANK, rows, channels), BF),
            jax.ShapeDtypeStruct((LAYERS, number, channels), F32),
        ),
        in_specs=[smem_spec()] * 4 + [vmem_spec()] * 2 + [any_spec()] * 6,
        out_specs=(any_spec(),) * 4 + (vmem_spec(),) * 2,
        scratch_shapes=[
            v((BLOCKS, nz, 2, rows, WIDE), BF),
            v((10, nz, 2, rows, WIDE), BF),
            v((BLOCKS, rows, WIDE), BF),
            v((BLOCKS // 2, rows, WIDE), BF),
            v((BLOCKS // 4, rows, WIDE), BF),
            v((film, rows, WIDE), BF),
            v((film // 2, rows, WIDE), BF),
            v((film // 2, rows, WIDE), BF),
            v((film, rows, WIDE), BF),
            v((LAYERS, 10, nz, 2, rows, WIDE), BF),
            v((LAYERS, nz, 2, 5, rows, WIDE), BF),
            v((LAYERS, nz, 5, rows, WIDE), BF),
            v((LAYERS, nz - 1, 5, rows, WIDE), BF),
            v((LAYERS, 5, rows, WIDE), BF),
            v((grid_rows, channels), BF),
            v((grid_rows, 6 * channels), BF),
            v((LAYERS, grid_rows, 2 * channels), BF),
            v((grid_rows, channels), BF),
            v((grid_rows, channels), F32),
            v((grid_rows // 8 + 4, 8, channels), F32),
            v((grid_rows, 2 * channels), BF),
            v((LAYERS, channels, own), BF),
            v((channels, own), BF),
            v((LAYERS, channels, own), BF),
            v((grid_rows, channels), F32),
            v((own, channels), F32),
            v(master.shape, F32),
            v(prompts.shape[1:], BF),
            v((LAYERS * number, prompts.shape[1]), F32),
            v((16, channels), F32),
            v((LAYERS, 8, channels), F32),
            v((LAYERS, 8, channels), F32),
            v((4, (16 + number) * LAYERS + rows, channels + 128), BF),
            v((HEADS, rows, WIDE), BF),
            v((n_seq, rows, WIDE), BF),
            v((n_seq, rows, 128), BF),
            v((n_seq, rows, 128), BF),
            v((number + 16, 128), BF),
            v((n_seq, number + 16, 128), BF),
            v((sum(HOP_ROWS), 128), F32),
            v((n_seq, sum(HOP_ROWS), 128), F32),
            dma((5,)),
            dma((4,)),
            dma((8,)),
            dma((8,)),
            dma((8,)),
            dma((copies,)),
            dma((copies,)),
            dma((len(HOP_ROWS), n_seq)),
            dma((len(HOP_ROWS), n_seq)),
            dma((3, n_seq)),
            dma((3, n_seq)),
        ],
        compiler_params=pltpu.CompilerParams(
            collective_id=0, has_side_effects=True, vmem_limit_bytes=MEM
        ),
        name="train_step",
    )(
        owners, dilations, lengths, pairing, step_embed, queries, master, prompts,
        frames_in, cond_frames, grad_out, grad_skip,
    )


def adam_update(weight, moment_one, moment_two, gradient, step_rate):
    moment_one = BETA_ONE * moment_one + (1.0 - BETA_ONE) * gradient
    moment_two = BETA_TWO * moment_two + (1.0 - BETA_TWO) * gradient * gradient
    normal = (
        moment_one
        / (1.0 - BETA_ONE**STEP)
        / (jnp.sqrt(moment_two / (1.0 - BETA_TWO**STEP)) + EPSILON)
    )
    return (moment_one, moment_two, weight - step_rate * (normal + WEIGHT_DECAY * weight))


def update_kernel(
    owners_ref, master_hbm, first_hbm, second_hbm, grad_hbm, low_hbm,
    queries_ref, qfirst_ref, qsecond_ref, dq_ref, block_in, skip_in, gframes_in,
    nfirst_hbm, nsecond_hbm, nmaster_hbm, ncopy_hbm, nqfirst_ref, nqsecond_ref, nqueries_ref,
    block_out, skip_out, gframes_out,
    master, first, second, grad, low, three, one, two, copied, frames,
    tile_of, grad_sem, in_sem, out_sem, frame_sem,
):
    grp = lax.axis_index("grp")
    grads_in = [
        pltpu.make_async_copy(a, b, grad_sem.at[i])
        for i, (a, b) in enumerate(((grad_hbm, grad), (low_hbm, low)))
    ]
    spots = [pl.ds(start, count) for start, count in CHUNKS]
    slots_in = [
        [
            pltpu.make_async_copy(a.at[spot], b.at[spot], in_sem.at[i, j])
            for j, (a, b) in enumerate(
                ((master_hbm, master), (first_hbm, first), (second_hbm, second))
            )
        ]
        for i, spot in enumerate(spots)
    ]
    frames_in = [
        pltpu.make_async_copy(a, frames.at[i], frame_sem.at[0, i])
        for i, a in enumerate((block_in, skip_in, gframes_in))
    ]
    for copy in grads_in + slots_in[0]:
        copy.start()
    for copies in slots_in[1:]:
        for copy in copies:
            copy.start()
    for copy in frames_in:
        copy.start()

    for slot in range(CAP + 1):
        tile_of[slot] = TILES
    count = jnp.int32(0)
    for tile in range(TILES):
        own = owners_ref[tile] == grp

        @pl.when(own)
        def _(count=count, tile=tile):
            tile_of[jnp.minimum(count, CAP)] = tile

        count = count + own.astype(jnp.int32)
    news = adam_update(
        queries_ref[...], qfirst_ref[...], qsecond_ref[...], dq_ref[...], QUERY_RATE
    )
    nqfirst_ref[...], nqsecond_ref[...], nqueries_ref[...] = news

    def slot_update(slot, carry):
        tile = tile_of[slot]
        used = (tile < TILES).astype(jnp.int32)
        tile = jnp.minimum(tile, TILES - 1)
        layer, kind = lax.div(tile, PER_LAYER), lax.rem(tile, PER_LAYER)
        plain = kind < 8
        pair = jnp.where(plain, lax.rem(kind, 2), (kind == 16).astype(jnp.int32))
        tap = jnp.where(plain, lax.div(kind, 2), 4)
        full = jnp.concatenate([grad[layer, 2 * pair, tap], grad[layer, 2 * pair + 1, tap]], axis=1)
        place = jnp.where(kind < 10, kind - 3, kind - 10)
        thin = low[layer, jnp.clip(place, 0, LOW_RANK - 1)]
        is_thin = ((kind >= 8) & (kind <= 14)).astype(jnp.int32)
        gradient = jnp.where(
            jnp.broadcast_to(is_thin, full.shape) > 0, thin.astype(F32), full.astype(F32)
        )
        old, old_first, old_second = master[slot], first[slot], second[slot]
        new_first, new_second, new = adam_update(old, old_first, old_second, gradient, LEARN_RATE)
        keep = jnp.broadcast_to(used, old.shape) > 0
        new = jnp.where(keep, new, old)
        one[slot] = jnp.where(keep, new_first, old_first)
        two[slot] = jnp.where(keep, new_second, old_second)
        three[slot] = new
        copied[slot] = new.astype(BF)
        return carry

    for copy in grads_in:
        copy.wait()
    outs = []
    for i, (start, number) in enumerate(CHUNKS):
        for copy in slots_in[i]:
            copy.wait()
        lax.fori_loop(start, start + number, slot_update, 0)
        for j, (a, b) in enumerate(
            ((one, nfirst_hbm), (two, nsecond_hbm), (three, nmaster_hbm), (copied, ncopy_hbm))
        ):
            copy = pltpu.make_async_copy(a.at[spots[i]], b.at[spots[i]], out_sem.at[i, j])
            copy.start()
            outs.append(copy)
    for i, target in enumerate((block_out, skip_out, gframes_out)):
        frames_in[i].wait()
        copy = pltpu.make_async_copy(frames.at[i], target, frame_sem.at[1, i])
        copy.start()
        outs.append(copy)
    for copy in outs:
        copy.wait()


CHUNKS = ((0, 3), (3, 3), (6, 3), (9, 4))


def update(owners, master, first, second, grads, low, queries, qfirst, qsecond, dq, *frames):
    any_, whole = any_spec(), vmem_spec()
    query = jax.ShapeDtypeStruct(queries.shape, F32)
    full = jax.ShapeDtypeStruct(master.shape, F32)
    passed = jax.ShapeDtypeStruct(frames[0].shape, F32)
    v = pltpu.VMEM
    slots = v(master.shape, F32)
    return pl.pallas_call(
        update_kernel,
        out_shape=(full, full, full, jax.ShapeDtypeStruct(master.shape, BF), query, query, query)
        + (passed,) * 3,
        in_specs=[smem_spec()] + [any_] * 5 + [whole] * 4 + [any_] * 3,
        out_specs=(any_,) * 4 + (whole,) * 3 + (any_,) * 3,
        scratch_shapes=[
            slots, slots, slots, v(grads.shape, BF), v(low.shape, BF),
            slots, slots, slots, v(master.shape, BF), v((3,) + passed.shape, F32),
            pltpu.SMEM((CAP + 1,), jnp.int32),
            pltpu.SemaphoreType.DMA((2,)),
            pltpu.SemaphoreType.DMA((len(CHUNKS), 3)),
            pltpu.SemaphoreType.DMA((len(CHUNKS), 4)),
            pltpu.SemaphoreType.DMA((2, 3)),
        ],
        compiler_params=pltpu.CompilerParams(vmem_limit_bytes=MEM),
        name="update",
    )(owners, master, first, second, grads, low, queries, qfirst, qsecond, dq, *frames)


def on_device(
    n_seq,
    frames_in,
    cond_frames,
    step_embed,
    prompts,
    prompt_lengths,
    pairing,
    dilations,
    owners,
    master,
    first_moment,
    second_moment,
    queries,
    query_first,
    query_second,
    grad_out,
    grad_skip,
):
    block, skip, gframes, own_grads, low, dq = train_step(
        n_seq, owners, dilations, prompt_lengths, pairing, step_embed, queries, master, prompts,
        frames_in, cond_frames, grad_out, grad_skip,
    )
    (
        new_first, new_second, new_master, new_copy, nqf, nqs, nq,
        block_out, skip_out, grad_frames,
    ) = update(
        owners, master, first_moment, second_moment, own_grads, low,
        queries, query_first, query_second, dq, block, skip, gframes,
    )
    return (
        new_first, new_second, new_master, new_copy, nqf, nqs, nq,
        block_out, skip_out, grad_frames,
    )


def solution(mesh):
    shard = P("grp", "seq", None)
    placed = (
        shard, shard, P("grp", None), P(), P(), P("grp"), P(), P(),
        shard, shard, shard, P(), P(), P(), shard, shard,
    )
    return jax.shard_map(
        functools.partial(on_device, mesh.shape["seq"]),
        mesh=mesh,
        in_specs=placed,
        out_specs=(shard, shard, shard, shard, P(), P(), P(), shard, shard, shard),
        check_vma=False,
    )
```

```python
import functools

import jax
import jax.numpy as jnp
from jax import lax
from jax.experimental import pallas as pl
from jax.experimental.pallas import tpu as pltpu
from jax.sharding import PartitionSpec as P

HEADS = 8
LAYERS = 2
DMAX = 8
CAP = 13
STEP = 10
PER_LAYER = 17
TILES = PER_LAYER * LAYERS

BETA_ONE = 0.9
BETA_TWO = 0.999
EPSILON = 1e-08
WEIGHT_DECAY = 0.01
LEARN_RATE = 0.02
QUERY_RATE = 0.4
HALF_ROOT = 0.7071067811865476
NEGATIVE = -1e30

BF = jnp.bfloat16
F32 = jnp.float32
HALO = 32
WIDE = 256
MAIN = 20
BLOCKS = MAIN * LAYERS
PHASES = (None, (0, MAIN), (MAIN, MAIN))
FILM_ORDER = (10, 11, 12, 13, 14, 8, 9)
FILM = 2 * len(FILM_ORDER)
LOW_RANK = len(FILM_ORDER)
KEY_VALUE = 4 * LAYERS
HOP_ROWS = (24, 16, 32, 8, 8)
IN_SPLIT = (2, 2, 2)
OUT_SPLIT = (2, 2)
LAST_DIRECT = True
ORDER = (
    ("prep", 1), "fcK", "fcR", ("pr", 0), ("prep", 2), ("cross", 1), "fxK", ("pr", 1),
    ("cross", 2), "fxR", ("end", 1), ("first", 1, 0), "flK", ("pr", 2), "hsK", ("end", 2),
    ("first", 2, 0), ("first", 1, 2), ("first", 1, 1), ("pr", 3), ("first", 1, 3), "flR",
    ("second", 1, 2), ("second", 1, 0), "heK", ("second", 2, 0), "att", ("second", 1, 1), "hsB",
    ("second", 1, 3), ("first", 2, 2), ("first", 2, 3), ("third", 1, 3), ("third", 2, 0), "heB",
    ("third", 1, 2), "hsC", ("third", 1, 1), ("third", 1, 0), ("first", 2, 1), ("second", 2, 2),
    "heC", ("second", 2, 3), "win0", "condt", ("second", 2, 1), "gates0a", "gates0b",
    ("third", 2, 2), "res0", ("third", 2, 3), ("third", 2, 1), "gatt0", "skip0", "win1",
    "gates1a", "gates1b", "gatt1", "gg1a", "gg1b", "winb1", ("give", 1, 1), ("give", 1, 0),
    "fg1a", ("keep", 1, 1), "fg1b", ("keep", 1, 0), ("one", 1, 3), "gg0a", ("one", 1, 1), "gg0b",
    "winb0", "out1", "fg0b", ("one", 1, 0), ("one", 1, 2), ("give", 0, 0), "fg0a", "hs3",
    ("two", 1, 3), ("give", 0, 1), ("two", 1, 1), ("keep", 0, 0), ("two", 1, 2), ("two", 1, 0),
    ("keep", 0, 1), "he3", ("one", 0, 2), ("one", 0, 0), "hs4", ("three", 1, 1), ("one", 0, 1),
    ("three", 1, 2), ("one", 0, 3), ("three", 1, 3), ("two", 0, 2), "he4", "fb", "dq1", "hs5",
    ("two", 0, 0), ("three", 1, 0), ("two", 0, 1), ("two", 0, 3), ("three", 0, 2),
    ("three", 0, 0), ("three", 0, 1), ("three", 0, 3), "he5", "bundle", ("four", 1), "dq2",
    ("four", 0), ("five", 1), "dq3", "low", "end",
)

MEM = 64 * 1024 * 1024 - 256 * 1024
MESH = pl.DeviceIdType.MESH


def block_table():
    table = {}
    for layer in range(LAYERS):
        base = PER_LAYER * layer
        start = MAIN * layer
        for part in range(4):
            for tap in range(4):
                table[base + 2 * tap + part // 2, part % 2] = start + 5 * part + tap
            table[base + 15 + part // 2, part % 2] = start + 5 * part + 4
    return table


BLOCK_OF = block_table()
FILM_OF = {
    (PER_LAYER * layer + tile, side): (
        4 * layer + 2 * place + side
        if place < 2
        else KEY_VALUE + (FILM - 4) * layer + 2 * (place - 2) + side
    )
    for layer in range(LAYERS)
    for place, tile in enumerate(FILM_ORDER)
    for side in range(2)
}


def mm(a, b):
    return lax.dot_general(a, b, (((1,), (0,)), ((), ())), preferred_element_type=F32)


def mm_nt(a, b):
    return lax.dot_general(a, b, (((1,), (1,)), ((), ())), preferred_element_type=F32)


def mm_nt_fine(a, b):
    high = a.astype(BF)
    return mm_nt(high, b) + mm_nt((a - high.astype(F32)).astype(BF), b)


def mm_low(a, b):
    return mm(a.astype(BF), b)


def mm_nt_low(a, b):
    return mm_nt(a.astype(BF), b)


def mm_nt_pairs(a, blocks):
    total = None
    for place, block in enumerate(blocks):
        term = mm_nt_fine(a[:, place * WIDE : (place + 1) * WIDE], block)
        total = term if total is None else total + term
    return total


def window(ref, start, count, width):
    group, rest = lax.div(start, 8), lax.rem(start, 8)
    groups = ref[pl.ds(group, count // 8 + 1), :, 0:width]
    turned = pltpu.roll(groups, lax.rem(8 - rest, 8), 1)
    row = lax.broadcasted_iota(jnp.int32, (1, 8, 1), 1)
    return jnp.where(row < 8 - rest, turned[:-1], turned[1:]).reshape(count, width)


def in_eights(value):
    return value.reshape(value.shape[0] // 8, 8, value.shape[1])


def place_of(n_seq):
    seq, grp = lax.axis_index("seq"), lax.axis_index("grp")
    z, y = lax.div(seq, 2), lax.rem(seq, 2)
    x, c = lax.div(grp, 2), lax.rem(grp, 2)
    return seq, grp, z, y, x, c


def greet(n_seq, seq, grp, groups):
    barrier = pltpu.get_barrier_semaphore()

    def one(k, carry):
        pl.semaphore_signal(
            barrier, inc=1, device_id={"seq": lax.rem(seq + k, n_seq), "grp": grp}, device_id_type=MESH
        )
        return carry

    lax.fori_loop(1, n_seq, one, 0)
    for k in range(1, groups):
        pl.semaphore_signal(
            barrier, inc=1, device_id={"seq": seq, "grp": lax.rem(grp + k, groups)}, device_id_type=MESH
        )
    pl.semaphore_wait(barrier, n_seq - 1 + groups - 1)


def any_spec():
    return pl.BlockSpec(memory_space=pl.ANY)


def vmem_spec():
    return pl.BlockSpec(memory_space=pltpu.VMEM)


def smem_spec():
    return pl.BlockSpec(memory_space=pltpu.SMEM)


def head_mask():
    row = lax.broadcasted_iota(jnp.int32, (HEADS, 512), 0)
    column = lax.broadcasted_iota(jnp.int32, (HEADS, 512), 1)
    return lax.div(column, 512 // HEADS) == row


def block_diagonal(rows):
    column = lax.div(lax.broadcasted_iota(jnp.int32, rows.shape, 1), 512 // HEADS)
    return jnp.concatenate([jnp.where(column == h, rows, 0.0) for h in range(HEADS)], axis=0)


def same_rows(row):
    return jnp.broadcast_to(row, (8, row.shape[1]))


def pack(vectors):
    pieces = [v[:, 128 * i : 128 * (i + 1)] for v in vectors for i in range(v.shape[1] // 128)]
    spare = -len(pieces) % 8
    if spare:
        pieces.append(jnp.zeros((spare, 128), pieces[0].dtype))
    return jnp.concatenate(pieces, axis=0)


def unpack(rows, place, pieces=4):
    return jnp.concatenate(
        [rows[pieces * place + i : pieces * place + i + 1] for i in range(pieces)], axis=1
    )


def step_kernel(
    n_seq, owners_ref, dil_ref, lengths_ref, pairing_ref, embed_ref, queries_ref, master_hbm,
    prompts_hbm, frames_hbm, cond_hbm, gout_hbm, gskip_hbm,
    block_hbm, skip_hbm, gframes_hbm, out_hbm, low_ref, dquery_ref,
    w, gs, prep, core_in, x_in, fr, fr_in, fx, ff, red_in, one_in, two_in, z_in, fin,
    xe, cat, slopes, gated, x1, bh, bb, sht, condt, gatt, bx, sk,
    master, prompt, probs, left, vec, sums, bundle, wide, dq_in,
    kv_out, kv_in, at_out, at_in, small_out, small_in, dq_out, dq_all, hop_src, hop_in,
    in_sem, prompt_sem, out_sem, hsend, hrecv, send, recv, hop_send, hop_recv, each_send, each_recv,
):
    seq, grp, z, y, x, c = place_of(n_seq)
    nz = n_seq // 2
    rows = prep.shape[1]
    own = frames_hbm.shape[1]
    grid_rows = own + 2 * HALO
    top = HALO + own
    channels = 512
    number = queries_ref.shape[1]
    sib, across, other_y = x * 2 + 1 - c, (1 - x) * 2 + c, z * 2 + 1 - y
    mine, theirs = 2 * c + x, 2 * c + 1 - x

    local_in = [
        pltpu.make_async_copy(a, b, in_sem.at[i])
        for i, (a, b) in enumerate(
            (
                (master_hbm, master),
                (frames_hbm.at[0], xe.at[pl.ds(HALO, own)]),
                (cond_hbm.at[0], cat.at[pl.ds(HALO, own), pl.ds(1536, channels)]),
                (gout_hbm.at[0], bb.at[pl.ds(HALO, own), pl.ds(0, channels)]),
                (gskip_hbm.at[0], bb.at[pl.ds(HALO, own), pl.ds(channels, channels)]),
            )
        )
    ]
    for copy in local_in:
        copy.start()

    def prompt_copy(turn, i):
        rows_now, columns = pl.ds(0, prompt.shape[0]), pl.ds((i % 2) * channels, channels)
        return pltpu.make_async_copy(
            prompts_hbm.at[4 * turn + i], slopes.at[i // 2, rows_now, columns], prompt_sem.at[i]
        )

    for i in range(4):
        prompt_copy(0, i).start()

    greet(n_seq, seq, grp, 4)

    waits = []
    used = [0]

    def remote(src, dst, to_seq, to_grp, sent=None):
        place = used[0]
        used[0] += 1
        copy = pltpu.make_async_remote_copy(
            src_ref=src,
            dst_ref=dst,
            send_sem=send.at[place],
            recv_sem=recv.at[place],
            device_id={"seq": to_seq, "grp": to_grp},
            device_id_type=MESH,
        )
        copy.start()
        (waits if sent is None else sent).append(copy)
        return copy

    after, before = lax.rem(seq + 1, n_seq), lax.rem(seq + n_seq - 1, n_seq)
    halos = []
    for ref, buffer, column in (
        (frames_hbm, xe, 0),
        (cond_hbm, cat, 1536),
        (gout_hbm, bb, 0),
        (gskip_hbm, bb, channels),
    ):
        for start, at, target in ((own - HALO, 0, after), (0, top, before)):
            place = len(halos)
            copy = pltpu.make_async_remote_copy(
                src_ref=ref.at[0, pl.ds(start, HALO)],
                dst_ref=buffer.at[pl.ds(at, HALO), pl.ds(column, channels)],
                send_sem=hsend.at[place],
                recv_sem=hrecv.at[place],
                device_id={"seq": target, "grp": grp},
                device_id_type=MESH,
            )
            copy.start()
            halos.append(copy)

    slots, flags = [], []
    count = jnp.int32(0)
    for tile in range(TILES):
        flag = (owners_ref[tile] == grp).astype(jnp.int32)
        slots.append(jnp.minimum(count, CAP - 1))
        flags.append(flag.astype(F32))
        count = count + flag

    def rounded(tile):
        return (master[slots[tile]] * flags[tile]).astype(BF)

    def ready(tiles, buffer, table):
        for tile in tiles:
            value = rounded(tile)
            buffer[table[tile, 0]] = value[:, :WIDE]
            buffer[table[tile, 1]] = value[:, WIDE:]

    def merge_start(phase):
        base, blocks = PHASES[phase]
        each = blocks // 4
        return remote(
            prep.at[pl.ds(base + 2 * (1 - c) * each, 2 * each)],
            core_in.at[pl.ds(base // 2, 2 * each)],
            seq, sib,
        )

    def merge_cross(phase, copy):
        base, blocks = PHASES[phase]
        each = blocks // 4
        copy.wait_recv()

        def add(i, carry):
            place = base // 2 + i
            core_in[place] = core_in[place] + prep[base + 2 * c * each + i]
            return carry

        lax.fori_loop(0, 2 * each, add, 0)
        return remote(
            core_in.at[pl.ds(base // 2 + (1 - x) * each, each)],
            x_in.at[pl.ds(base // 4, each)],
            seq, across,
        )

    def view(phase, quarter, zz, yy):
        base, blocks = PHASES[phase]
        each = blocks // 4
        return w.at[pl.ds(base + quarter * each, each), zz, yy]

    gathering, legs = [], {}

    def spread(ref, to_seq, to_grp):
        return remote(ref, ref, to_seq, to_grp, gathering)

    def merge_end(phase, copy):
        base, blocks = PHASES[phase]
        each = blocks // 4
        copy.wait_recv()

        def settle(i, carry):
            w[base + mine * each + i, z, y] = (
                core_in[base // 2 + x * each + i] + x_in[base // 4 + i]
            )
            return carry

        lax.fori_loop(0, each, settle, 0)

    def y_first(zz, quarters):
        return 1 - jnp.minimum(lax.div(4 * zz, quarters * nz), 1)

    def spread_z(phase):
        ref = view(phase, mine, z, y)
        for k in range(1, nz):
            legs[phase, k] = spread(ref, lax.rem(z + k, nz) * 2 + y, grp)

    core_legs = {phase: [] for phase in (1, 2)}

    def first(phase, k):
        zs = lax.rem(z - k + nz, nz)
        a = y_first(zs, IN_SPLIT[phase])
        b = 1 - a
        if k:
            legs[phase, k].wait_recv()
        ref = view(phase, mine, zs, y)
        one = spread(ref, a * other_y + b * seq, a * grp + b * across)
        two = spread(ref, a * seq + b * other_y, a * across + b * grp)
        core_legs[phase].append(spread(ref, seq, sib))
        legs[phase, k] = (zs, a, one, two)

    def second(phase, k):
        zs, a, one, two = legs[phase, k]
        b = 1 - a
        one.wait_recv()
        ref = view(phase, a * mine + b * theirs, zs, a * (1 - y) + b * y)
        last = spread(ref, a * seq + b * other_y, a * across + b * grp)
        core_legs[phase].append(spread(ref, seq, sib))
        legs[phase, k] = (zs, a, two, last)

    def third(phase, k):
        zs, a, two, last = legs[phase, k]
        b = 1 - a
        two.wait_recv()
        ref = view(phase, a * theirs + b * mine, zs, a * y + b * (1 - y))
        core_legs[phase].append(spread(ref, seq, sib))
        last.wait_recv()
        core_legs[phase].append(spread(view(phase, theirs, zs, 1 - y), seq, sib))

    def arrived(phase):
        for copy in core_legs[phase]:
            copy.wait_recv()

    def hop_refs(j):
        start = sum(HOP_ROWS[:j])
        spot = pl.ds(start, HOP_ROWS[j])
        return hop_src.at[spot], hop_in.at[seq, spot], hop_in.at[:, spot]

    def hop_copy(j, k):
        src, dst, _ = hop_refs(j)
        return pltpu.make_async_remote_copy(
            src_ref=src,
            dst_ref=dst,
            send_sem=hop_send.at[j, k],
            recv_sem=hop_recv.at[j, k],
            device_id={"seq": lax.rem(seq + k, n_seq), "grp": grp},
            device_id_type=MESH,
        )

    def hop_start(j, value):
        src, dst, _ = hop_refs(j)
        value = value.astype(src.dtype)
        src[...] = value
        dst[...] = value

        def one(k, carry):
            hop_copy(j, k).start()
            return carry

        lax.fori_loop(1, n_seq, one, 0)

    def hop_end(j):
        def one(k, carry):
            hop_copy(j, k).wait()
            return carry

        lax.fori_loop(1, n_seq, one, 0)
        _, _, whole = hop_refs(j)

        def add(i, total):
            return total + whole[i].astype(F32)

        return lax.fori_loop(0, n_seq, add, jnp.zeros((HOP_ROWS[j], 128), F32))

    position = lax.broadcasted_iota(jnp.int32, (channels, rows), 0)
    column = lax.broadcasted_iota(jnp.int32, (channels, rows), 1)
    chosen = jnp.where(position == column + seq * rows, 1.0, 0.0).astype(BF)

    def pick(v):
        return mm_low(v, chosen)

    def film_block(layer, place):
        if place < 4:
            return ff[4 * layer + place]
        return ff[KEY_VALUE + (FILM - 4) * layer + place - 4]

    def film_rows(layer, v, places):
        return jnp.concatenate([mm_low(v, film_block(layer, i)) for i in places], axis=1)

    def film_back(layer, v, places):
        total = None
        for i, place in enumerate(places):
            term = mm_nt_low(v[:, i * WIDE : (i + 1) * WIDE], film_block(layer, place))
            total = term if total is None else total + term
        return mm_nt_low(total, chosen)

    wide_head = channels // HEADS
    copies_of = n_seq // HEADS
    head = lax.div(seq, copies_of)
    lane = lax.broadcasted_iota(jnp.int32, (channels, 128), 1)
    at_row = lax.broadcasted_iota(jnp.int32, (channels, 128), 0)
    of_head = at_row == head * wide_head + lax.rem(lane, wide_head)
    head_columns = jnp.where(of_head, 1.0, 0.0).astype(BF)
    own_half = lax.div(lax.broadcasted_iota(jnp.int32, (8, 128), 1), wide_head) == (
        lax.broadcasted_iota(jnp.int32, (8, 128), 0)
    )

    def exchange(index, source, target):
        def copy(k):
            dest = lax.rem(seq + k, n_seq)
            return pltpu.make_async_remote_copy(
                src_ref=source(dest),
                dst_ref=target,
                send_sem=each_send.at[index, k],
                recv_sem=each_recv.at[index, k],
                device_id={"seq": dest, "grp": grp},
                device_id_type=MESH,
            )

        def begin():
            def one(k, carry):
                copy(k).start()
                return carry

            lax.fori_loop(1, n_seq, one, 0)

        def finish():
            def one(k, carry):
                copy(k).wait()
                return carry

            lax.fori_loop(1, n_seq, one, 0)

        return begin, finish

    kv_begin, kv_finish = exchange(
        0, lambda dest: kv_out.at[lax.div(dest, copies_of)], kv_in.at[seq]
    )
    at_begin, at_finish = exchange(1, lambda dest: at_out.at[dest], at_in.at[seq])
    dq_begin, dq_finish = exchange(3, lambda dest: dq_out, dq_all.at[seq])
    small_begin, small_finish = exchange(2, lambda dest: small_out, small_in.at[seq])

    def head_weights():
        value = kv_in[...].reshape(channels, WIDE)
        return value[:, 0:128], value[:, 128:256]

    def attention():
        keys, values = head_weights()
        pieces = []
        for layer in range(LAYERS):
            high = queries_ref[layer].astype(BF)
            rest = (queries_ref[layer] - high.astype(F32)).astype(BF)
            both = mm(high, head_columns) + mm(rest, head_columns)
            half = lax.div(lax.broadcasted_iota(jnp.int32, both.shape, 1), wide_head)
            pieces.append(jnp.where(half == layer, both, 0.0))
        probe = mm_nt_fine(jnp.concatenate(pieces, axis=0), keys)
        pr = prompt[...]
        scores = mm_nt_fine(probe, pr) * 0.125
        live = lax.broadcasted_iota(jnp.int32, scores.shape, 1) < lengths_ref[pairing_ref[0]]
        scores = jnp.where(live, scores, NEGATIVE)
        weight = jnp.exp(scores - jnp.max(scores, axis=1, keepdims=True))
        value = weight / jnp.sum(weight, axis=1, keepdims=True)
        probs[...] = value
        mean = jnp.concatenate(
            [
                jnp.mean(value[l * number : (l + 1) * number], axis=0, keepdims=True)
                for l in range(LAYERS)
            ]
            + [jnp.zeros((8 - LAYERS, value.shape[1]), F32)],
            axis=0,
        )
        seen = mm_low(mean, pr)
        mixed = jnp.where(own_half, mm_low(seen, values), 0.0)
        left[0:8] = seen
        left[8:16] = mm_nt_low(mixed, head_columns)

    def wblock(layer, place):
        return w[MAIN * layer + place].reshape(channels, WIDE)

    def inside(low, count):
        row = lax.broadcasted_iota(jnp.int32, (count, 1), 0) + (low - HALO) + seq * own
        return (row >= 0) & (row < n_seq * own)

    def windows_forward(layer):
        low = 16 * layer
        high = grid_rows - low
        scale, shift = 1.0 + vec[layer, 0:1], vec[layer, 1:2]
        here = xe[...].astype(F32) if layer == 0 else x1[...]
        shifted = (here * scale + shift).astype(BF).astype(F32)
        shifted = jnp.where(inside(0, grid_rows), shifted, 0.0)
        groups = grid_rows // 8
        bh[0] = jnp.zeros((8, channels), F32)
        bh[1 : 1 + groups] = in_eights(shifted)
        bh[1 + groups :] = jnp.zeros((3, 8, channels), F32)
        sht[layer] = jnp.transpose(shifted[HALO:top]).astype(BF)
        cat[low:high, channels : 2 * channels] = shifted[low:high].astype(BF)
        for tap in (0, 2):
            start = 8 + low + (tap - 1) * dil_ref[layer]
            cat[low:high, tap * channels : (tap + 1) * channels] = window(
                bh, start, high - low, channels
            ).astype(BF)

    def gates(layer, first_row, rows_now):
        spot = slice(first_row, first_row + rows_now)
        value = cat[spot, 0:2048]
        for part in range(2):
            columns = slice(part * WIDE, (part + 1) * WIDE)
            base = MAIN * layer + 5 * part
            lhs = mm(value, w[base : base + 4].reshape(2048, WIDE))
            tangent = jnp.tanh(lhs + vec[layer, 2:3, columns])
            rhs = mm(value, w[base + 10 : base + 14].reshape(2048, WIDE))
            opening = jax.nn.sigmoid(rhs + vec[layer, 3:4, columns])
            gate = tangent * opening
            gated[spot, columns] = gate.astype(BF)
            slopes[layer, spot, columns] = (opening * (1.0 - tangent * tangent)).astype(BF)
            other = slice(channels + part * WIDE, channels + (part + 1) * WIDE)
            slopes[layer, spot, other] = (gate * (1.0 - opening)).astype(BF)

    def residual(layer, first_row, rows_now):
        value = gated[first_row : first_row + rows_now]
        for part in range(2):
            columns = slice(part * WIDE, (part + 1) * WIDE)
            term = mm(value, wblock(layer, 5 * part + 4))
            if layer == 0:
                base = xe[first_row : first_row + rows_now, columns].astype(F32)
                x1[first_row : first_row + rows_now, columns] = (base + term) * HALF_ROOT
            else:
                base = x1[first_row : first_row + rows_now, columns]
                x1[first_row : first_row + rows_now, columns] = (base + term) * HALF_ROOT

    def skipped(layer, first_row, rows_now):
        value = gated[first_row : first_row + rows_now]
        spot = slice(first_row - HALO, first_row - HALO + rows_now)
        for part in range(2):
            columns = slice(part * WIDE, (part + 1) * WIDE)
            term = mm(value, wblock(layer, 5 * part + 14))
            if layer == 0:
                sk[spot, columns] = term
            else:
                sk[spot, columns] = sk[spot, columns] + term

    low, high = 16, grid_rows - 16

    def gate_grads(layer, first_row, rows_now):
        spot = slice(first_row, first_row + rows_now)
        bb[spot, 0:channels] = (bx[spot] * HALF_ROOT).astype(BF)
        branch = jnp.concatenate([wblock(layer, 5 * part + 4) for part in range(4)], axis=1)
        back = mm_nt(bb[spot], branch)
        keep = inside(first_row, rows_now)
        for side in range(2):
            columns = slice(side * channels, (side + 1) * channels)
            value = back * slopes[layer, spot, columns].astype(F32)
            middle = slice((2 + side) * channels, (3 + side) * channels)
            cat[spot, middle] = jnp.where(keep, value, 0.0).astype(BF)

    def windows_backward(layer):
        reach, limit = (low, high) if layer else (HALO, top)
        edge = 1 + low // 8
        bh[0:edge] = jnp.zeros((edge, 8, channels), F32)
        bh[1 + high // 8 :] = jnp.zeros((edge + 2, 8, channels), F32)
        for side in range(2):
            middle = slice((2 + side) * channels, (3 + side) * channels)
            value = cat[low:high, middle].astype(F32)
            bh[edge : 1 + high // 8] = in_eights(value)
            total = jnp.sum(value[HALO - low : top - low], axis=0, keepdims=True)
            sums[layer, 2 + side : 3 + side] = total
            for tap in (0, 2):
                start = 8 + reach - (tap - 1) * dil_ref[layer]
                columns = slice((2 * tap + side) * channels, (2 * tap + side + 1) * channels)
                cat[reach:limit, columns] = window(bh, start, limit - reach, channels).astype(BF)

    def frame_grads(layer, first_row, rows_now):
        spot = slice(first_row, first_row + rows_now)
        taps = jnp.concatenate(
            [wblock(layer, 5 * part + tap) for tap in range(3) for part in range(4)], axis=1
        )
        back = mm_nt(cat[spot], taps)
        if layer:
            here = x1[spot]
            row = lax.broadcasted_iota(jnp.int32, (rows_now, 1), 0) + first_row
            kept = jnp.where((row >= HALO) & (row < top), back, 0.0)
        else:
            here = xe[spot].astype(F32)
            kept = back
        sums[layer, 0:1] += jnp.sum(kept * here, axis=0, keepdims=True)
        sums[layer, 1:2] += jnp.sum(kept, axis=0, keepdims=True)
        bx[spot] = bx[spot] * HALF_ROOT + back * (1.0 + vec[layer, 0:1])

    def weight_grad(layer, part, i):
        if i < 4:
            tap = i if i < 3 else 1
            start = pl.multiple_of(tap * 1024 + part * WIDE, WIDE)
            lhs = sht[layer] if i < 3 else condt[...]
            return mm(lhs, cat[HALO:top, pl.ds(start, WIDE)])
        start = pl.multiple_of(part * WIDE, WIDE)
        return mm(gatt[layer], bb[HALO:top, pl.ds(start, WIDE)])

    core_sent = {}

    def give(layer, xx):
        part = 2 * (1 - c) + xx
        buffer, base = (gs, 0) if layer else (w, MAIN)
        for i in range(5):
            value = weight_grad(layer, part, i).astype(BF)
            buffer[base + 5 * xx + i] = value.reshape(nz, 2, rows, WIDE)
        core_sent[layer, xx] = remote(
            buffer.at[pl.ds(base + 5 * xx, 5)], red_in.at[layer, pl.ds(5 * xx, 5)], seq, sib
        )

    def keep(layer, xx):
        part = 2 * c + xx
        core_sent[layer, xx].wait_recv()
        for i in range(5):
            value = weight_grad(layer, part, i).reshape(nz, 2, rows, WIDE)
            spot = 5 * xx + i
            red_in[layer, spot] = (red_in[layer, spot].astype(F32) + value).astype(BF)

    ones, twos, zs, targets = {}, {}, {}, {}
    for layer in range(LAYERS):
        for k in range(nz):
            zd = lax.rem(z + k, nz)
            targets[layer, k] = (zd, y_first(zd, OUT_SPLIT[layer]))

    def red_one(layer, k):
        zd, a = targets[layer, k]
        b = 1 - a
        ones[layer, k] = []
        for j in range(2):
            xi, yi = a * (1 - x) + b * j, a * j + b * (1 - y)
            ones[layer, k].append(
                remote(
                    red_in.at[layer, pl.ds(5 * xi, 5), zd, yi],
                    one_in.at[layer, k, j],
                    a * seq + b * other_y, a * across + b * grp,
                )
            )

    def red_two(layer, k):
        zd, a = targets[layer, k]
        b = 1 - a
        you = a * y + b * x
        for j in range(2):
            ones[layer, k][j].wait_recv()
            xi, yi = a * x + b * j, a * j + b * y

            def body(i, carry, j=j, xi=xi, yi=yi):
                one_in[layer, k, j, i] = (
                    one_in[layer, k, j, i] + red_in[layer, 5 * xi + i, zd, yi]
                )
                return carry

            lax.fori_loop(0, 5, body, 0)
        twos[layer, k] = remote(
            one_in.at[layer, k, 1 - you], two_in.at[layer, k],
            a * other_y + b * seq, a * grp + b * across,
        )

    def red_three(layer, k):
        zd, a = targets[layer, k]
        you = a * y + (1 - a) * x
        twos[layer, k].wait_recv()

        def body(i, carry):
            two_in[layer, k, i] = two_in[layer, k, i] + one_in[layer, k, you, i]
            return carry

        lax.fori_loop(0, 5, body, 0)
        if k:
            zs[layer, k] = remote(two_in.at[layer, k], z_in.at[layer, k - 1], zd * 2 + y, grp)

    lasts = {}
    outs = []

    def local_out(src, dst):
        copy = pltpu.make_async_copy(src, dst, out_sem.at[len(outs)])
        copy.start()
        outs.append(copy)

    def red_four(layer):
        for k in range(1, nz):
            zs[layer, k].wait_recv()

        def body(i, carry):
            total = two_in[layer, 0, i].astype(F32)
            for k in range(1, nz):
                total = total + z_in[layer, k - 1, i].astype(F32)
            fin[layer, i] = total.astype(BF)
            return carry

        lax.fori_loop(0, 5, body, 0)
        src, dst = fin.at[layer], out_hbm.at[layer, mine]
        lasts[layer] = [remote(src, dst, seq, across), remote(src, dst, seq, sib)]
        if not layer and LAST_DIRECT:
            lasts[layer].append(remote(src, dst, seq, (1 - x) * 2 + 1 - c))
        local_out(src, dst)

    def red_five(layer):
        lasts[layer][0].wait_recv()
        ref = out_hbm.at[layer, theirs]
        lasts[layer].append(remote(ref, ref, seq, sib))

    ops = {}

    def op(*key):
        def keep_op(body):
            ops[key] = body
            return body

        return keep_op

    main_tiles = (0, 1, 2, 3, 4, 5, 6, 7, 15, 16)
    merges, crosses, film_sent, seen, hops = {}, {}, {}, {}, {}
    size_all, size_mid, size_own = grid_rows // 2, (high - low) // 2, own // 2
    embed = same_rows(embed_ref[...].astype(F32))

    for phase in (1, 2):

        @op("prep", phase)
        def _(phase=phase):
            ready([PER_LAYER * (phase - 1) + t for t in main_tiles], prep, BLOCK_OF)
            merges[phase] = merge_start(phase)

        @op("cross", phase)
        def _(phase=phase):
            crosses[phase] = merge_cross(phase, merges[phase])

        @op("end", phase)
        def _(phase=phase):
            merge_end(phase, crosses[phase])
            spread_z(phase)

    def quarter(j):
        return range(j * nz // 4, (j + 1) * nz // 4)

    for phase in (1, 2):
        for j in range(4):
            for name, body in (("first", first), ("second", second), ("third", third)):

                @op(name, phase, j)
                def _(phase=phase, j=j, body=body):
                    for k in quarter(j):
                        body(phase, k)

    parts = {"K": (0, KEY_VALUE), "R": (KEY_VALUE, FILM * LAYERS - KEY_VALUE)}
    for name, (begin, blocks) in parts.items():
        half = blocks // 2
        own_half_at = begin + c * half

        @op("fc" + name)
        def _(name=name, begin=begin, half=half):
            order = FILM_ORDER[:2] if name == "K" else FILM_ORDER[2:]
            for layer in range(LAYERS):
                ready([PER_LAYER * layer + t for t in order], fr, FILM_OF)
            film_sent[name, 0] = remote(
                fr.at[pl.ds(begin + (1 - c) * half, half)],
                fr_in.at[pl.ds(begin // 2, half)],
                seq, sib,
            )

        @op("fx" + name)
        def _(name=name, begin=begin, half=half, own_half_at=own_half_at):
            film_sent[name, 0].wait_recv()
            spot = slice(begin // 2, begin // 2 + half)
            fr_in[spot] = fr_in[spot] + fr[pl.ds(own_half_at, half)]
            ref = pl.ds(begin // 2, half)
            film_sent[name, 1] = remote(fr_in.at[ref], fx.at[ref], seq, across)

        @op("fl" + name)
        def _(name=name, begin=begin, half=half, own_half_at=own_half_at):
            film_sent[name, 1].wait_recv()
            spot = slice(begin // 2, begin // 2 + half)
            ref = pl.ds(own_half_at, half)
            ff[ref] = fr_in[spot] + fx[spot]
            film_sent[name, 2] = remote(ff.at[ref], ff.at[ref], seq, sib)

    for turn in range(4):

        @op("pr", turn)
        def _(turn=turn):
            total = prompt[...] if turn else None
            for i in range(4):
                prompt_copy(turn, i).wait()
                flag = (pairing_ref[0] == 4 * turn + i).astype(F32).astype(BF)
                part = slice((i % 2) * channels, (i % 2 + 1) * channels)
                term = slopes[i // 2, 0 : prompt.shape[0], part] * flag
                total = term if total is None else total + term
            prompt[...] = total
            if turn < 3:
                for i in range(4):
                    prompt_copy(turn + 1, i).start()

    def gathered():
        while gathering:
            gathering.pop().wait_send()

    @op("condt")
    def _():
        local_in[2].wait()
        condt[...] = jnp.transpose(cat[HALO:top, 1536:2048].astype(F32)).astype(BF)

    @op("hsK")
    def _():
        film_sent["K", 2].wait_recv()
        for h in range(HEADS):
            columns = slice((h % 4) * wide_head, (h % 4 + 1) * wide_head)
            pieces = [
                film_block(layer, place + h // 4).astype(F32)[:, columns]
                for place in (0, 2)
                for layer in range(LAYERS)
            ]
            kv_out[h] = jnp.concatenate(pieces, axis=1).astype(BF)
        kv_in[seq] = kv_out[head]
        kv_begin()

    @op("heK")
    def _():
        kv_finish()

    @op("att")
    def _():
        attention()

    @op("hsB")
    def _():
        film_sent["R", 2].wait_recv()
        vectors = []
        embed_here, mixed = pick(embed), pick(left[8:16])
        for layer in range(LAYERS):
            vectors.append(film_rows(layer, mixed, (4, 5))[layer : layer + 1])
            steps = film_rows(layer, embed_here, (10, 11, 12, 13))
            vectors += [steps[0:1, :channels], steps[0:1, channels:]]
        hop_start(0, pack(vectors))

    @op("heB")
    def _():
        total = hop_end(0)
        hops["pooled"] = [unpack(total, 3 * layer) for layer in range(LAYERS)]
        for layer in range(LAYERS):
            vec[layer, 2:3] = unpack(total, 3 * layer + 1)
            vec[layer, 3:4] = unpack(total, 3 * layer + 2)

    @op("hsC")
    def _():
        vectors = []
        for layer in range(LAYERS):
            pooled = hops["pooled"][layer]
            film = film_rows(layer, pick(same_rows(pooled)), (6, 7, 8, 9))
            vectors += [film[0:1, :channels], film[0:1, channels:]]
        hop_start(1, pack(vectors))

    @op("heC")
    def _():
        total = hop_end(1)
        for layer in range(LAYERS):
            vec[layer, 0:1] = unpack(total, 2 * layer)
            vec[layer, 1:2] = unpack(total, 2 * layer + 1)

    @op("win0")
    def _():
        local_in[1].wait()
        for copy in halos[:4]:
            copy.wait_recv()
        windows_forward(0)

    @op("win1")
    def _():
        local_in[3].wait()
        local_in[4].wait()
        for copy in halos[4:]:
            copy.wait_recv()
        bx[...] = bb[:, 0:channels].astype(F32)
        windows_forward(1)

    for layer in range(LAYERS):
        start, size = (low, size_mid) if layer else (0, size_all)
        for part, name in enumerate("ab"):
            first_row = start + part * size

            @op(f"gates{layer}{name}")
            def _(layer=layer, first_row=first_row, size=size, part=part):
                if not part:
                    arrived(1 + layer)
                gates(layer, first_row, size)

        @op(f"gatt{layer}")
        def _(layer=layer):
            gatt[layer] = jnp.transpose(gated[HALO:top].astype(F32)).astype(BF)

    @op("res0")
    def _():
        for part in range(2):
            residual(0, part * size_all, size_all)

    @op("skip0")
    def _():
        for part in range(2):
            skipped(0, HALO + part * size_own, size_own)

    @op("out1")
    def _():
        for part in range(2):
            residual(1, HALO + part * size_own, size_own)
            skipped(1, HALO + part * size_own, size_own)
        local_out(x1.at[pl.ds(HALO, own)], block_hbm.at[0])
        local_out(sk, skip_hbm.at[0])

    for layer in range(LAYERS):
        for part, name in enumerate("ab"):

            @op(f"gg{layer}{name}")
            def _(layer=layer, part=part):
                if layer and not part:
                    sums[...] = jnp.zeros_like(sums)
                gate_grads(layer, low + part * size_mid, size_mid)

            @op(f"fg{layer}{name}")
            def _(layer=layer, part=part):
                if layer:
                    frame_grads(1, low + part * size_mid, size_mid)
                else:
                    frame_grads(0, HALO + part * size_own, size_own)

        @op(f"winb{layer}")
        def _(layer=layer):
            windows_backward(layer)

        for xx in range(2):

            @op("give", layer, xx)
            def _(layer=layer, xx=xx):
                if not layer:
                    gathered()
                give(layer, xx)

            @op("keep", layer, xx)
            def _(layer=layer, xx=xx):
                keep(layer, xx)

        for j in range(4):
            for name, body in (("one", red_one), ("two", red_two), ("three", red_three)):

                @op(name, layer, j)
                def _(layer=layer, j=j, body=body):
                    for k in quarter(j):
                        body(layer, k)

        @op("four", layer)
        def _(layer=layer):
            red_four(layer)

        @op("five", layer)
        def _(layer=layer):
            red_five(layer)

    @op("hs3")
    def _():
        local_out(bx.at[pl.ds(HALO, own)], gframes_hbm.at[0])
        hop_start(2, pack([sums[l, i : i + 1] for l in range(LAYERS) for i in range(4)]))

    @op("he3")
    def _():
        total = hop_end(2)
        hops["sides"] = [[unpack(total, 4 * l + i) for i in range(4)] for l in range(LAYERS)]

    @op("hs4")
    def _():
        vectors = []
        for layer in range(LAYERS):
            dfilm = same_rows(jnp.concatenate(hops["sides"][layer][0:2], axis=1))
            vectors.append(film_back(layer, dfilm, (6, 7, 8, 9))[0:1])
        hop_start(3, pack(vectors))

    @op("he4")
    def _():
        total = hop_end(3)
        hops["dpooled"] = [unpack(total, layer) for layer in range(LAYERS)]


    @op("fb")
    def _():
        vectors = [
            film_back(l, same_rows(hops["dpooled"][l]), (4, 5))[0:1] for l in range(LAYERS)
        ]
        if copies_of > 1:
            hop_start(4, pack(vectors))
            total = hop_end(4)
            vectors = [unpack(total, layer) for layer in range(LAYERS)]
        dmixed = jnp.concatenate(vectors + [jnp.zeros((8 - LAYERS, channels), F32)], axis=0)
        dmixed = jnp.where(own_half, mm_low(dmixed, head_columns), 0.0)
        keys, values = head_weights()
        pr = prompt[...]
        dmean = mm_nt_low(mm_nt_low(dmixed, values), pr) * (1.0 / number)
        dprobs = jnp.concatenate(
            [jnp.broadcast_to(dmean[l : l + 1], (number, channels)) for l in range(LAYERS)], axis=0
        )
        value = probs[...]
        inner = jnp.sum(dprobs * value, axis=1, keepdims=True)
        dprobe = mm_low(value * (dprobs - inner) * 0.125, pr)
        dqueries = mm_low(dprobe, keys)
        half = lax.div(lax.broadcasted_iota(jnp.int32, (number, 128), 1), wide_head)
        dquery = jnp.where(half == 0, dqueries[0:number], dqueries[number : 2 * number])
        dq_in[grp] = dquery.astype(BF)
        small_out[...] = jnp.concatenate([dmixed, jnp.zeros((8, 128), F32)], axis=0).astype(BF)
        lefts = jnp.concatenate(
            [dprobe, left[0:2], left[8:10]]
            + [hops["pooled"][layer] for layer in range(LAYERS)]
            + [embed[0:1], jnp.zeros((128 - 2 * number - 7, channels), F32)],
            axis=0,
        )
        at_out[...] = jnp.transpose(lefts).astype(BF).reshape(n_seq, rows, 128)

    @op("hs5")
    def _():
        small_in[seq] = small_out[...]
        at_in[seq] = at_out[seq]
        small_begin()
        at_begin()

    def halves(one, two):
        wanted = lax.broadcasted_iota(jnp.int32, one.shape, 1) < wide_head
        return (
            jnp.where(wanted, one, pltpu.roll(two, wide_head, 1)),
            jnp.where(wanted, pltpu.roll(one, wide_head, 1), two),
        )

    def by_heads(ref):
        blocks = [[], []]
        for h in range(0, HEADS, 2):
            pair = halves(ref[h * copies_of].astype(F32), ref[(h + 1) * copies_of].astype(F32))
            for layer in range(LAYERS):
                blocks[layer].append(pair[layer])
        return [jnp.concatenate(blocks[layer], axis=1) for layer in range(LAYERS)]

    dq_sent = []

    @op("dq1")
    def _():
        for k in range(1, 4):
            ref = dq_in.at[grp]
            dq_sent.append(remote(ref, ref, seq, lax.rem(grp + k, 4)))

    @op("dq2")
    def _():
        for copy in dq_sent:
            copy.wait_recv()
        total = dq_in[0].astype(F32)
        for k in range(1, 4):
            total = total + dq_in[k].astype(F32)
        dq_out[...] = total
        dq_all[seq] = total
        dq_begin()

    @op("dq3")
    def _():
        dq_finish()
        total = by_heads(dq_all)
        for layer in range(LAYERS):
            dquery_ref[layer] = total[layer]

    @op("he5")
    def _():
        small_finish()
        at_finish()

        full = by_heads(small_in)
        pieces = []
        for layer in range(LAYERS):
            pieces += hops["sides"][layer]
            pieces += [hops["dpooled"][layer], full[layer][layer : layer + 1]]
        pieces.append(jnp.zeros((16 - len(pieces), channels), F32))
        wide[grp] = jnp.concatenate(pieces, axis=0).astype(BF)
        at = lax.broadcasted_iota(jnp.int32, (rows, 128), 1)
        thin = jnp.where(at >= 66, at_in[seq].astype(F32), 0.0)
        for h in range(0, HEADS, 2):
            one, two = at_in[h * copies_of].astype(F32), at_in[(h + 1) * copies_of].astype(F32)
            pair = jnp.where(at < wide_head, one, pltpu.roll(two, wide_head, 1))
            bundle[grp, :, h * wide_head : (h + 2) * wide_head] = pair.astype(BF)
            for k, value in ((h, one), (h + 1, two)):
                turned = pltpu.roll(value, wide_head + 2 * k, 1)
                thin = jnp.where(lax.div(at, 2) == k, turned, thin)
        bundle[grp, :, channels : channels + 128] = thin.astype(BF)

    bundles = []

    @op("bundle")
    def _():
        for k in range(1, 4):
            for ref in (bundle.at[grp], wide.at[grp]):
                bundles.append(remote(ref, ref, seq, lax.rem(grp + k, 4)))

    @op("low")
    def _():
        for copy in bundles:
            copy.wait_recv()
        mask = head_mask()
        at = lax.broadcasted_iota(jnp.int32, (8, channels), 0)
        probe = bundle[0, :, 0:channels].astype(F32)
        for k in range(1, 4):
            probe = probe + bundle[k, :, 0:channels].astype(F32)
        probe = probe.astype(BF)
        blank = jnp.zeros((number, channels), F32)
        column = lax.div(lax.broadcasted_iota(jnp.int32, (number, channels), 1), wide_head)
        for layer in range(LAYERS):
            side = []
            for h in range(HEADS):
                one = jnp.where(column == h, queries_ref[layer], 0.0)
                side += [blank, one] if layer else [one, blank]
            low_ref[layer, 0] = mm(probe, jnp.concatenate(side, axis=0).astype(BF)).astype(BF)
            total = None
            for k in range(4):
                right = wide[k].astype(F32)[6 * layer : 6 * layer + 6]
                dmixed = jnp.where(mask, right[5:6], 0.0)
                nothing = jnp.zeros((1, channels), F32)
                rows_of = []
                for h in range(HEADS):
                    one = dmixed[h : h + 1]
                    rows_of += [nothing, one] if layer else [one, nothing]
                value = jnp.concatenate(rows_of, axis=0)
                gap = jnp.zeros((48, channels), F32)
                rest = jnp.zeros((56, channels), F32)
                pieces = [jnp.concatenate([value, gap, jnp.zeros((64, channels), F32)], axis=0)]
                for i, row in ((4, 2), (0, 4), (1, 4), (2, 6), (3, 6)):
                    row = row + (layer if row < 6 else 0)
                    one = jnp.where(at == row, right[i : i + 1], 0.0)
                    pieces.append(
                        jnp.concatenate([jnp.zeros((64, channels), F32), one, rest], axis=0)
                    )
                term = mm(
                    bundle[k, :, channels : channels + 128],
                    jnp.concatenate(pieces, axis=1).astype(BF),
                )
                total = term if total is None else total + term
            for i in range(6):
                low_ref[layer, 1 + i] = total[:, i * channels : (i + 1) * channels].astype(BF)

    @op("end")
    def _():
        for copies in lasts.values():
            for copy in copies[1:]:
                copy.wait_recv()
        if LAST_DIRECT:
            lasts[0][0].wait_recv()
        for copy in outs:
            copy.wait()
        for copy in halos:
            copy.wait_send()
        gathered()
        for copy in waits:
            copy.wait_send()

    local_in[0].wait()
    for key in ORDER:
        ops[key if isinstance(key, tuple) else (key,)]()


def train_step(
    n_seq, owners, dilations, lengths, pairing, step_embed, queries, master, prompts,
    frames_in, cond_frames, grad_out, grad_skip,
):
    _, own, channels = frames_in.shape
    rows = master.shape[1]
    number = queries.shape[1]
    grid_rows = own + 2 * HALO
    nz = n_seq // 2
    v = pltpu.VMEM
    dma = pltpu.SemaphoreType.DMA
    frame_out = jax.ShapeDtypeStruct((1, own, channels), F32)
    film = FILM * LAYERS
    copies = 52 + 24 * nz
    return pl.pallas_call(
        functools.partial(step_kernel, n_seq),
        out_shape=(
            frame_out,
            frame_out,
            frame_out,
            jax.ShapeDtypeStruct((LAYERS, 4, 5, rows, WIDE), BF),
            jax.ShapeDtypeStruct((LAYERS, LOW_RANK, rows, channels), BF),
            jax.ShapeDtypeStruct((LAYERS, number, channels), F32),
        ),
        in_specs=[smem_spec()] * 4 + [vmem_spec()] * 2 + [any_spec()] * 6,
        out_specs=(any_spec(),) * 4 + (vmem_spec(),) * 2,
        scratch_shapes=[
            v((BLOCKS, nz, 2, rows, WIDE), BF),
            v((10, nz, 2, rows, WIDE), BF),
            v((BLOCKS, rows, WIDE), BF),
            v((BLOCKS // 2, rows, WIDE), BF),
            v((BLOCKS // 4, rows, WIDE), BF),
            v((film, rows, WIDE), BF),
            v((film // 2, rows, WIDE), BF),
            v((film // 2, rows, WIDE), BF),
            v((film, rows, WIDE), BF),
            v((LAYERS, 10, nz, 2, rows, WIDE), BF),
            v((LAYERS, nz, 2, 5, rows, WIDE), BF),
            v((LAYERS, nz, 5, rows, WIDE), BF),
            v((LAYERS, nz - 1, 5, rows, WIDE), BF),
            v((LAYERS, 5, rows, WIDE), BF),
            v((grid_rows, channels), BF),
            v((grid_rows, 6 * channels), BF),
            v((LAYERS, grid_rows, 2 * channels), BF),
            v((grid_rows, channels), BF),
            v((grid_rows, channels), F32),
            v((grid_rows // 8 + 4, 8, channels), F32),
            v((grid_rows, 2 * channels), BF),
            v((LAYERS, channels, own), BF),
            v((channels, own), BF),
            v((LAYERS, channels, own), BF),
            v((grid_rows, channels), F32),
            v((own, channels), F32),
            v(master.shape, F32),
            v(prompts.shape[1:], BF),
            v((LAYERS * number, prompts.shape[1]), F32),
            v((16, channels), F32),
            v((LAYERS, 8, channels), F32),
            v((LAYERS, 8, channels), F32),
            v((4, rows, channels + 128), BF),
            v((4, 16, channels), BF),
            v((4, number, 128), BF),
            v((HEADS, rows, WIDE), BF),
            v((n_seq, rows, WIDE), BF),
            v((n_seq, rows, 128), BF),
            v((n_seq, rows, 128), BF),
            v((16, 128), BF),
            v((n_seq, 16, 128), BF),
            v((number, 128), F32),
            v((n_seq, number, 128), F32),
            v((sum(HOP_ROWS), 128), F32),
            v((n_seq, sum(HOP_ROWS), 128), F32),
            dma((5,)),
            dma((4,)),
            dma((8,)),
            dma((8,)),
            dma((8,)),
            dma((copies,)),
            dma((copies,)),
            dma((len(HOP_ROWS), n_seq)),
            dma((len(HOP_ROWS), n_seq)),
            dma((4, n_seq)),
            dma((4, n_seq)),
        ],
        compiler_params=pltpu.CompilerParams(
            collective_id=0, has_side_effects=True, vmem_limit_bytes=MEM
        ),
        name="train_step",
    )(
        owners, dilations, lengths, pairing, step_embed, queries, master, prompts,
        frames_in, cond_frames, grad_out, grad_skip,
    )


def adam_update(weight, moment_one, moment_two, gradient, step_rate):
    moment_one = BETA_ONE * moment_one + (1.0 - BETA_ONE) * gradient
    moment_two = BETA_TWO * moment_two + (1.0 - BETA_TWO) * gradient * gradient
    normal = (
        moment_one
        * (1.0 / (1.0 - BETA_ONE**STEP))
        / (jnp.sqrt(moment_two * (1.0 / (1.0 - BETA_TWO**STEP))) + EPSILON)
    )
    return (moment_one, moment_two, weight - step_rate * (normal + WEIGHT_DECAY * weight))


def update_kernel(
    owners_ref, master_hbm, first_hbm, second_hbm, grad_hbm, low_hbm,
    queries_ref, qfirst_ref, qsecond_ref, dq_ref, block_in, skip_in, gframes_in,
    nfirst_hbm, nsecond_hbm, nmaster_hbm, ncopy_hbm, nqfirst_ref, nqsecond_ref, nqueries_ref,
    block_out, skip_out, gframes_out,
    master, first, second, grad, low, three, one, two, copied, frames,
    tile_of, grad_sem, in_sem, out_sem, frame_sem,
):
    grp = lax.axis_index("grp")
    grads_in = [
        pltpu.make_async_copy(a, b, grad_sem.at[i])
        for i, (a, b) in enumerate(((grad_hbm, grad), (low_hbm, low)))
    ]
    spots = [pl.ds(start, count) for start, count in CHUNKS]
    slots_in = [
        [
            pltpu.make_async_copy(a.at[spot], b.at[spot], in_sem.at[i, j])
            for j, (a, b) in enumerate(
                ((master_hbm, master), (first_hbm, first), (second_hbm, second))
            )
        ]
        for i, spot in enumerate(spots)
    ]
    frames_in = [
        pltpu.make_async_copy(a, frames.at[i], frame_sem.at[0, i])
        for i, a in enumerate((block_in, skip_in, gframes_in))
    ]
    for copy in grads_in + slots_in[0]:
        copy.start()
    for copies in slots_in[1:]:
        for copy in copies:
            copy.start()
    for copy in frames_in:
        copy.start()

    for slot in range(CAP + 1):
        tile_of[slot] = TILES
    count = jnp.int32(0)
    for tile in range(TILES):
        own = owners_ref[tile] == grp

        @pl.when(own)
        def _(count=count, tile=tile):
            tile_of[jnp.minimum(count, CAP)] = tile

        count = count + own.astype(jnp.int32)
    news = adam_update(
        queries_ref[...], qfirst_ref[...], qsecond_ref[...], dq_ref[...], QUERY_RATE
    )
    nqfirst_ref[...], nqsecond_ref[...], nqueries_ref[...] = news

    def slot_update(slot, carry):
        tile = tile_of[slot]
        used = (tile < TILES).astype(jnp.int32)
        tile = jnp.minimum(tile, TILES - 1)
        layer, kind = lax.div(tile, PER_LAYER), lax.rem(tile, PER_LAYER)
        plain = kind < 8
        pair = jnp.where(plain, lax.rem(kind, 2), (kind == 16).astype(jnp.int32))
        tap = jnp.where(plain, lax.div(kind, 2), 4)
        full = jnp.concatenate([grad[layer, 2 * pair, tap], grad[layer, 2 * pair + 1, tap]], axis=1)
        place = jnp.where(kind < 10, kind - 3, kind - 10)
        thin = low[layer, jnp.clip(place, 0, LOW_RANK - 1)]
        is_thin = ((kind >= 8) & (kind <= 14)).astype(jnp.int32)
        gradient = jnp.where(
            jnp.broadcast_to(is_thin, full.shape) > 0, thin.astype(F32), full.astype(F32)
        )
        old, old_first, old_second = master[slot], first[slot], second[slot]
        new_first, new_second, new = adam_update(old, old_first, old_second, gradient, LEARN_RATE)
        keep = jnp.broadcast_to(used, old.shape) > 0
        new = jnp.where(keep, new, old)
        one[slot] = jnp.where(keep, new_first, old_first)
        two[slot] = jnp.where(keep, new_second, old_second)
        three[slot] = new
        copied[slot] = new.astype(BF)
        return carry

    for copy in grads_in:
        copy.wait()
    outs = []
    for i, (start, number) in enumerate(CHUNKS):
        for copy in slots_in[i]:
            copy.wait()
        lax.fori_loop(start, start + number, slot_update, 0)
        for j, (a, b) in enumerate(
            ((one, nfirst_hbm), (two, nsecond_hbm), (three, nmaster_hbm), (copied, ncopy_hbm))
        ):
            copy = pltpu.make_async_copy(a.at[spots[i]], b.at[spots[i]], out_sem.at[i, j])
            copy.start()
            outs.append(copy)
    for i, target in enumerate((block_out, skip_out, gframes_out)):
        frames_in[i].wait()
        copy = pltpu.make_async_copy(frames.at[i], target, frame_sem.at[1, i])
        copy.start()
        outs.append(copy)
    for copy in outs:
        copy.wait()


CHUNKS = ((0, 2), (2, 3), (5, 4), (9, 4))


def update(owners, master, first, second, grads, low, queries, qfirst, qsecond, dq, *frames):
    any_, whole = any_spec(), vmem_spec()
    query = jax.ShapeDtypeStruct(queries.shape, F32)
    full = jax.ShapeDtypeStruct(master.shape, F32)
    passed = jax.ShapeDtypeStruct(frames[0].shape, F32)
    v = pltpu.VMEM
    slots = v(master.shape, F32)
    return pl.pallas_call(
        update_kernel,
        out_shape=(full, full, full, jax.ShapeDtypeStruct(master.shape, BF), query, query, query)
        + (passed,) * 3,
        in_specs=[smem_spec()] + [any_] * 5 + [whole] * 4 + [any_] * 3,
        out_specs=(any_,) * 4 + (whole,) * 3 + (any_,) * 3,
        scratch_shapes=[
            slots, slots, slots, v(grads.shape, BF), v(low.shape, BF),
            slots, slots, slots, v(master.shape, BF), v((3,) + passed.shape, F32),
            pltpu.SMEM((CAP + 1,), jnp.int32),
            pltpu.SemaphoreType.DMA((2,)),
            pltpu.SemaphoreType.DMA((len(CHUNKS), 3)),
            pltpu.SemaphoreType.DMA((len(CHUNKS), 4)),
            pltpu.SemaphoreType.DMA((2, 3)),
        ],
        compiler_params=pltpu.CompilerParams(vmem_limit_bytes=MEM),
        name="update",
    )(owners, master, first, second, grads, low, queries, qfirst, qsecond, dq, *frames)


def on_device(
    n_seq,
    frames_in,
    cond_frames,
    step_embed,
    prompts,
    prompt_lengths,
    pairing,
    dilations,
    owners,
    master,
    first_moment,
    second_moment,
    queries,
    query_first,
    query_second,
    grad_out,
    grad_skip,
):
    block, skip, gframes, own_grads, low, dq = train_step(
        n_seq, owners, dilations, prompt_lengths, pairing, step_embed, queries, master, prompts,
        frames_in, cond_frames, grad_out, grad_skip,
    )
    (
        new_first, new_second, new_master, new_copy, nqf, nqs, nq,
        block_out, skip_out, grad_frames,
    ) = update(
        owners, master, first_moment, second_moment, own_grads, low,
        queries, query_first, query_second, dq, block, skip, gframes,
    )
    return (
        new_first, new_second, new_master, new_copy, nqf, nqs, nq,
        block_out, skip_out, grad_frames,
    )


def solution(mesh):
    shard = P("grp", "seq", None)
    placed = (
        shard, shard, P("grp", None), P(), P(), P("grp"), P(), P(),
        shard, shard, shard, P(), P(), P(), shard, shard,
    )
    return jax.shard_map(
        functools.partial(on_device, mesh.shape["seq"]),
        mesh=mesh,
        in_specs=placed,
        out_specs=(shard, shard, shard, shard, P(), P(), P(), shard, shard, shard),
        check_vma=False,
    )
```

```python
import functools

import jax
import jax.numpy as jnp
from jax import lax
from jax.experimental import pallas as pl
from jax.experimental.pallas import tpu as pltpu
from jax.sharding import PartitionSpec as P

HEADS = 8
LAYERS = 2
DMAX = 8
CAP = 13
STEP = 10
PER_LAYER = 17
TILES = PER_LAYER * LAYERS

BETA_ONE = 0.9
BETA_TWO = 0.999
EPSILON = 1e-08
WEIGHT_DECAY = 0.01
LEARN_RATE = 0.02
QUERY_RATE = 0.4
HALF_ROOT = 0.7071067811865476
NEGATIVE = -1e30

BF = jnp.bfloat16
F32 = jnp.float32
HALO = 32
WIDE = 256
MAIN = 20
BLOCKS = MAIN * LAYERS
PHASES = (None, (0, MAIN), (MAIN, MAIN))
FILM_ORDER = (10, 11, 12, 13, 14, 8, 9)
FILM = 2 * len(FILM_ORDER)
LOW_RANK = len(FILM_ORDER)
KEY_VALUE = 4 * LAYERS
HOP_ROWS = (24, 16, 32, 8, 8)
IN_SPLIT = (2, 2, 2)
OUT_SPLIT = (2, 2)
EACH = 5
LAST_DIRECT = True
ORDER = (
    "fcK", ("prep", 2), ("pr", 0), ("prep", 1), ("pr", 1), "fxK", ("cross", 1), ("cross", 2),
    "fcR", "flK", ("pr", 2), ("end", 1), ("first", 1, 0), "hsK", ("end", 2), "fxR",
    ("first", 2, 0), "condt", ("second", 1, 0), ("first", 1, 2), ("first", 1, 3), ("first", 1, 1),
    ("second", 2, 0), ("pr", 3), "flR", ("second", 1, 2), "heK", ("second", 1, 3), "att", "hsB",
    ("second", 1, 1), ("first", 2, 3), ("first", 2, 2), "heB", "hsC", ("third", 1, 2),
    ("third", 1, 0), ("first", 2, 1), ("second", 2, 3), ("third", 1, 1), ("second", 2, 2),
    ("third", 1, 3), ("third", 2, 0), "heC", "win0", ("second", 2, 1), "gates0a", ("third", 2, 3),
    "gates0b", ("third", 2, 2), ("third", 2, 1), "res0", "skip0", "gatt0", "win1", "gates1a",
    "gates1b", "gg1a", "gatt1", "gg1b", "winb1", ("give", 1, 0), ("give", 1, 1), "fg1b",
    ("keep", 1, 0), ("one", 1, 3), "fg1a", ("one", 1, 1), ("one", 1, 0), "out1", ("keep", 1, 1),
    ("onb", 1, 1), ("one", 1, 2), "gg0a", "gg0b", ("onb", 1, 0), "winb0", "fg0b", ("onb", 1, 3),
    ("give", 0, 0), ("give", 0, 1), ("onb", 1, 2), "fg0a", "hs3", ("two", 1, 1), ("keep", 0, 0),
    ("two", 1, 3), ("one", 0, 0), ("two", 1, 2), "he3", ("one", 0, 2), "hs4", ("keep", 0, 1),
    ("three", 1, 1), ("onb", 0, 2), ("one", 0, 3), ("one", 0, 1), ("three", 1, 3), ("onb", 0, 0),
    ("onb", 0, 3), ("three", 1, 2), ("two", 0, 2), ("two", 1, 0), ("onb", 0, 1), "he4", "fb",
    "hs5", ("two", 0, 3), ("three", 0, 2), ("three", 1, 0), ("two", 0, 1), "he5", "dq1",
    ("two", 0, 0), ("three", 0, 3), ("three", 0, 1), ("four", 1), "dq2", "bundle",
    ("three", 0, 0), ("four", 0), "low", "dq3", ("five", 1), "end",
)

MEM = 64 * 1024 * 1024 - 256 * 1024
MESH = pl.DeviceIdType.MESH


def block_table():
    table = {}
    for layer in range(LAYERS):
        base = PER_LAYER * layer
        start = MAIN * layer
        for part in range(4):
            for tap in range(4):
                table[base + 2 * tap + part // 2, part % 2] = start + 5 * part + tap
            table[base + 15 + part // 2, part % 2] = start + 5 * part + 4
    return table


BLOCK_OF = block_table()
FILM_OF = {
    (PER_LAYER * layer + tile, side): (
        4 * layer + 2 * place + side
        if place < 2
        else KEY_VALUE + (FILM - 4) * layer + 2 * (place - 2) + side
    )
    for layer in range(LAYERS)
    for place, tile in enumerate(FILM_ORDER)
    for side in range(2)
}


def mm(a, b):
    return lax.dot_general(a, b, (((1,), (0,)), ((), ())), preferred_element_type=F32)


def mm_nt(a, b):
    return lax.dot_general(a, b, (((1,), (1,)), ((), ())), preferred_element_type=F32)


def mm_nt_fine(a, b):
    high = a.astype(BF)
    return mm_nt(high, b) + mm_nt((a - high.astype(F32)).astype(BF), b)


def mm_low(a, b):
    return mm(a.astype(BF), b)


def mm_nt_low(a, b):
    return mm_nt(a.astype(BF), b)


def mm_nt_pairs(a, blocks):
    total = None
    for place, block in enumerate(blocks):
        term = mm_nt_fine(a[:, place * WIDE : (place + 1) * WIDE], block)
        total = term if total is None else total + term
    return total


def window(ref, start, count, width):
    group, rest = lax.div(start, 8), lax.rem(start, 8)
    groups = ref[pl.ds(group, count // 8 + 1), :, 0:width]
    turned = pltpu.roll(groups, lax.rem(8 - rest, 8), 1)
    row = lax.broadcasted_iota(jnp.int32, (1, 8, 1), 1)
    return jnp.where(row < 8 - rest, turned[:-1], turned[1:]).reshape(count, width)


def in_eights(value):
    return value.reshape(value.shape[0] // 8, 8, value.shape[1])


def place_of(n_seq):
    seq, grp = lax.axis_index("seq"), lax.axis_index("grp")
    z, y = lax.div(seq, 2), lax.rem(seq, 2)
    x, c = lax.div(grp, 2), lax.rem(grp, 2)
    return seq, grp, z, y, x, c


def greet(n_seq, seq, grp, groups):
    barrier = pltpu.get_barrier_semaphore()

    def one(k, carry):
        pl.semaphore_signal(
            barrier, inc=1, device_id={"seq": lax.rem(seq + k, n_seq), "grp": grp}, device_id_type=MESH
        )
        return carry

    lax.fori_loop(1, n_seq, one, 0)
    for k in range(1, groups):
        pl.semaphore_signal(
            barrier, inc=1, device_id={"seq": seq, "grp": lax.rem(grp + k, groups)}, device_id_type=MESH
        )
    pl.semaphore_wait(barrier, n_seq - 1 + groups - 1)


def any_spec():
    return pl.BlockSpec(memory_space=pl.ANY)


def vmem_spec():
    return pl.BlockSpec(memory_space=pltpu.VMEM)


def smem_spec():
    return pl.BlockSpec(memory_space=pltpu.SMEM)


def head_mask():
    row = lax.broadcasted_iota(jnp.int32, (HEADS, 512), 0)
    column = lax.broadcasted_iota(jnp.int32, (HEADS, 512), 1)
    return lax.div(column, 512 // HEADS) == row


def block_diagonal(rows):
    column = lax.div(lax.broadcasted_iota(jnp.int32, rows.shape, 1), 512 // HEADS)
    return jnp.concatenate([jnp.where(column == h, rows, 0.0) for h in range(HEADS)], axis=0)


def same_rows(row):
    return jnp.broadcast_to(row, (8, row.shape[1]))


def pack(vectors):
    pieces = [v[:, 128 * i : 128 * (i + 1)] for v in vectors for i in range(v.shape[1] // 128)]
    spare = -len(pieces) % 8
    if spare:
        pieces.append(jnp.zeros((spare, 128), pieces[0].dtype))
    return jnp.concatenate(pieces, axis=0)


def unpack(rows, place, pieces=4):
    return jnp.concatenate(
        [rows[pieces * place + i : pieces * place + i + 1] for i in range(pieces)], axis=1
    )


def step_kernel(
    n_seq, owners_ref, dil_ref, lengths_ref, pairing_ref, embed_ref, queries_ref, master_hbm,
    prompts_hbm, frames_hbm, cond_hbm, gout_hbm, gskip_hbm,
    block_hbm, skip_hbm, gframes_hbm, out_hbm, low_ref, dquery_ref,
    w, gs, prep, core_in, x_in, fr, fr_in, fx, ff, red_in, one_in, two_in, z_in, ze_in, xe_in, fin,
    xe, cat, slopes, gated, x1, bh, bb, sht, condt, gatt, bx, sk,
    master, prompt, probs, left, vec, sums, bundle, wide, dq_in,
    kv_out, kv_in, at_out, at_in, small_out, small_in, dq_out, dq_all, hop_src, hop_in,
    in_sem, prompt_sem, out_sem, hsend, hrecv, send, recv, hop_send, hop_recv, each_send, each_recv,
):
    seq, grp, z, y, x, c = place_of(n_seq)
    nz = n_seq // 2
    rows = prep.shape[1]
    own = frames_hbm.shape[1]
    grid_rows = own + 2 * HALO
    top = HALO + own
    channels = 512
    number = queries_ref.shape[1]
    sib, across, other_y = x * 2 + 1 - c, (1 - x) * 2 + c, z * 2 + 1 - y
    mine, theirs = 2 * c + x, 2 * c + 1 - x

    local_in = [
        pltpu.make_async_copy(a, b, in_sem.at[i])
        for i, (a, b) in enumerate(
            (
                (master_hbm, master),
                (frames_hbm.at[0], xe.at[pl.ds(HALO, own)]),
                (cond_hbm.at[0], cat.at[pl.ds(HALO, own), pl.ds(1536, channels)]),
                (gout_hbm.at[0], bb.at[pl.ds(HALO, own), pl.ds(0, channels)]),
                (gskip_hbm.at[0], bb.at[pl.ds(HALO, own), pl.ds(channels, channels)]),
            )
        )
    ]
    for copy in local_in:
        copy.start()

    def prompt_copy(turn, i):
        rows_now, columns = pl.ds(0, prompt.shape[0]), pl.ds((i % 2) * channels, channels)
        return pltpu.make_async_copy(
            prompts_hbm.at[4 * turn + i], slopes.at[i // 2, rows_now, columns], prompt_sem.at[i]
        )

    for i in range(4):
        prompt_copy(0, i).start()

    greet(n_seq, seq, grp, 4)

    waits = []
    used = [0]

    def remote(src, dst, to_seq, to_grp, sent=None, start=True):
        place = used[0]
        used[0] += 1
        copy = pltpu.make_async_remote_copy(
            src_ref=src,
            dst_ref=dst,
            send_sem=send.at[place],
            recv_sem=recv.at[place],
            device_id={"seq": to_seq, "grp": to_grp},
            device_id_type=MESH,
        )
        if start:
            copy.start()
        (waits if sent is None else sent).append(copy)
        return copy

    after, before = lax.rem(seq + 1, n_seq), lax.rem(seq + n_seq - 1, n_seq)
    halos = []
    for ref, buffer, column in (
        (frames_hbm, xe, 0),
        (cond_hbm, cat, 1536),
        (gout_hbm, bb, 0),
        (gskip_hbm, bb, channels),
    ):
        for start, at, target in ((own - HALO, 0, after), (0, top, before)):
            place = len(halos)
            copy = pltpu.make_async_remote_copy(
                src_ref=ref.at[0, pl.ds(start, HALO)],
                dst_ref=buffer.at[pl.ds(at, HALO), pl.ds(column, channels)],
                send_sem=hsend.at[place],
                recv_sem=hrecv.at[place],
                device_id={"seq": target, "grp": grp},
                device_id_type=MESH,
            )
            copy.start()
            halos.append(copy)

    slots, flags = [], []
    count = jnp.int32(0)
    for tile in range(TILES):
        flag = (owners_ref[tile] == grp).astype(jnp.int32)
        slots.append(jnp.minimum(count, CAP - 1))
        flags.append(flag.astype(F32))
        count = count + flag

    def rounded(tile):
        return (master[slots[tile]] * flags[tile]).astype(BF)

    def ready(tiles, buffer, table):
        for tile in tiles:
            value = rounded(tile)
            buffer[table[tile, 0]] = value[:, :WIDE]
            buffer[table[tile, 1]] = value[:, WIDE:]

    def merge_start(phase):
        base, blocks = PHASES[phase]
        each = blocks // 4
        return remote(
            prep.at[pl.ds(base + 2 * (1 - c) * each, 2 * each)],
            core_in.at[pl.ds(base // 2, 2 * each)],
            seq, sib,
        )

    def merge_cross(phase, copy):
        base, blocks = PHASES[phase]
        each = blocks // 4
        copy.wait_recv()

        def add(i, carry):
            place = base // 2 + i
            core_in[place] = core_in[place] + prep[base + 2 * c * each + i]
            return carry

        lax.fori_loop(0, 2 * each, add, 0)
        return remote(
            core_in.at[pl.ds(base // 2 + (1 - x) * each, each)],
            x_in.at[pl.ds(base // 4, each)],
            seq, across,
        )

    def view(phase, quarter, zz, yy):
        base, blocks = PHASES[phase]
        return w.at[pl.ds(base + quarter * (blocks // 4), EACH), zz, yy]

    def side_view(phase, quarter, *place):
        base, blocks = PHASES[phase]
        spot = pl.ds(base + quarter * (blocks // 4) + EACH, 5 - EACH)
        return w.at[(spot,) + place]

    gathering, legs = [], {}

    def spread(ref, to_seq, to_grp):
        return remote(ref, ref, to_seq, to_grp, gathering)

    def merge_end(phase, copy):
        base, blocks = PHASES[phase]
        each = blocks // 4
        copy.wait_recv()

        def settle(i, carry):
            w[base + mine * each + i, z, y] = (
                core_in[base // 2 + x * each + i] + x_in[base // 4 + i]
            )
            return carry

        lax.fori_loop(0, each, settle, 0)

    def y_first(zz, quarters):
        return 1 - jnp.minimum(lax.div(4 * zz, quarters * nz), 1)

    def spread_z(phase):
        ref = view(phase, mine, z, y)
        for k in range(1, nz):
            legs[phase, k] = spread(ref, lax.rem(z + k, nz) * 2 + y, grp)

    core_legs = {phase: [] for phase in (1, 2)}

    def first(phase, k):
        zs = lax.rem(z - k + nz, nz)
        a = y_first(zs, IN_SPLIT[phase])
        b = 1 - a
        if k:
            legs[phase, k].wait_recv()
        ref = view(phase, mine, zs, y)
        one = spread(ref, a * other_y + b * seq, a * grp + b * across)
        two = spread(ref, a * seq + b * other_y, a * across + b * grp)
        core_legs[phase].append(spread(ref, seq, sib))
        legs[phase, k] = (zs, a, one, two)

    def second(phase, k):
        zs, a, one, two = legs[phase, k]
        b = 1 - a
        one.wait_recv()
        ref = view(phase, a * mine + b * theirs, zs, a * (1 - y) + b * y)
        last = spread(ref, a * seq + b * other_y, a * across + b * grp)
        core_legs[phase].append(spread(ref, seq, sib))
        legs[phase, k] = (zs, a, two, last)

    def third(phase, k):
        zs, a, two, last = legs[phase, k]
        b = 1 - a
        two.wait_recv()
        ref = view(phase, a * theirs + b * mine, zs, a * y + b * (1 - y))
        core_legs[phase].append(spread(ref, seq, sib))
        last.wait_recv()
        core_legs[phase].append(spread(view(phase, theirs, zs, 1 - y), seq, sib))

    side_legs = {}

    def side_first(phase):
        ref = side_view(phase, mine, z, y)
        side_legs[phase] = [
            spread(ref, other_y, grp), spread(ref, seq, across), spread(ref, other_y, across)
        ]

    def side_second(phase):
        for copy in side_legs[phase]:
            copy.wait_recv()
        for k in range(1, nz):
            for q in (mine, theirs):
                ref = side_view(phase, q, z)
                side_legs[phase, k, q is mine] = spread(ref, lax.rem(z + k, nz) * 2 + y, grp)
        for q in (mine, theirs):
            core_legs[phase].append(spread(side_view(phase, q, z), seq, sib))

    def side_third(phase):
        for k in range(1, nz):
            for q in (mine, theirs):
                side_legs[phase, k, q is mine].wait_recv()
                ref = side_view(phase, q, lax.rem(z - k + nz, nz))
                core_legs[phase].append(spread(ref, seq, sib))

    def arrived(phase):
        for copy in core_legs[phase]:
            copy.wait_recv()

    def hop_refs(j):
        start = sum(HOP_ROWS[:j])
        spot = pl.ds(start, HOP_ROWS[j])
        return hop_src.at[spot], hop_in.at[seq, spot], hop_in.at[:, spot]

    def hop_copy(j, k):
        src, dst, _ = hop_refs(j)
        return pltpu.make_async_remote_copy(
            src_ref=src,
            dst_ref=dst,
            send_sem=hop_send.at[j, k],
            recv_sem=hop_recv.at[j, k],
            device_id={"seq": lax.rem(seq + k, n_seq), "grp": grp},
            device_id_type=MESH,
        )

    def hop_start(j, value):
        src, dst, _ = hop_refs(j)
        value = value.astype(src.dtype)
        src[...] = value
        dst[...] = value

        def one(k, carry):
            hop_copy(j, k).start()
            return carry

        lax.fori_loop(1, n_seq, one, 0)

    def hop_end(j):
        def one(k, carry):
            hop_copy(j, k).wait()
            return carry

        lax.fori_loop(1, n_seq, one, 0)
        _, _, whole = hop_refs(j)

        def add(i, total):
            return total + whole[i].astype(F32)

        return lax.fori_loop(0, n_seq, add, jnp.zeros((HOP_ROWS[j], 128), F32))

    position = lax.broadcasted_iota(jnp.int32, (channels, rows), 0)
    column = lax.broadcasted_iota(jnp.int32, (channels, rows), 1)
    chosen = jnp.where(position == column + seq * rows, 1.0, 0.0).astype(BF)

    def pick(v):
        return mm_low(v, chosen)

    def film_block(layer, place):
        if place < 4:
            return ff[4 * layer + place]
        return ff[KEY_VALUE + (FILM - 4) * layer + place - 4]

    def film_rows(layer, v, places):
        return jnp.concatenate([mm_low(v, film_block(layer, i)) for i in places], axis=1)

    def film_back(layer, v, places):
        total = None
        for i, place in enumerate(places):
            term = mm_nt_low(v[:, i * WIDE : (i + 1) * WIDE], film_block(layer, place))
            total = term if total is None else total + term
        return mm_nt_low(total, chosen)

    wide_head = channels // HEADS
    copies_of = n_seq // HEADS
    head = lax.div(seq, copies_of)
    lane = lax.broadcasted_iota(jnp.int32, (channels, 128), 1)
    at_row = lax.broadcasted_iota(jnp.int32, (channels, 128), 0)
    of_head = at_row == head * wide_head + lax.rem(lane, wide_head)
    head_columns = jnp.where(of_head, 1.0, 0.0).astype(BF)
    own_half = lax.div(lax.broadcasted_iota(jnp.int32, (8, 128), 1), wide_head) == (
        lax.broadcasted_iota(jnp.int32, (8, 128), 0)
    )

    def exchange(index, source, target):
        def copy(k):
            dest = lax.rem(seq + k, n_seq)
            return pltpu.make_async_remote_copy(
                src_ref=source(dest),
                dst_ref=target,
                send_sem=each_send.at[index, k],
                recv_sem=each_recv.at[index, k],
                device_id={"seq": dest, "grp": grp},
                device_id_type=MESH,
            )

        def begin():
            def one(k, carry):
                copy(k).start()
                return carry

            lax.fori_loop(1, n_seq, one, 0)

        def finish():
            def one(k, carry):
                copy(k).wait()
                return carry

            lax.fori_loop(1, n_seq, one, 0)

        return begin, finish

    kv_begin, kv_finish = exchange(
        0, lambda dest: kv_out.at[lax.div(dest, copies_of)], kv_in.at[seq]
    )
    at_begin, at_finish = exchange(1, lambda dest: at_out.at[dest], at_in.at[seq])
    dq_begin, dq_finish = exchange(3, lambda dest: dq_out, dq_all.at[seq])
    small_begin, small_finish = exchange(2, lambda dest: small_out, small_in.at[seq])

    def head_weights():
        value = kv_in[...].reshape(channels, WIDE)
        return value[:, 0:128], value[:, 128:256]

    def attention():
        keys, values = head_weights()
        pieces = []
        for layer in range(LAYERS):
            high = queries_ref[layer].astype(BF)
            rest = (queries_ref[layer] - high.astype(F32)).astype(BF)
            both = mm(high, head_columns) + mm(rest, head_columns)
            half = lax.div(lax.broadcasted_iota(jnp.int32, both.shape, 1), wide_head)
            pieces.append(jnp.where(half == layer, both, 0.0))
        probe = mm_nt_fine(jnp.concatenate(pieces, axis=0), keys)
        pr = prompt[...]
        scores = mm_nt_fine(probe, pr) * 0.125
        live = lax.broadcasted_iota(jnp.int32, scores.shape, 1) < lengths_ref[pairing_ref[0]]
        scores = jnp.where(live, scores, NEGATIVE)
        weight = jnp.exp(scores - jnp.max(scores, axis=1, keepdims=True))
        value = weight / jnp.sum(weight, axis=1, keepdims=True)
        probs[...] = value
        mean = jnp.concatenate(
            [
                jnp.mean(value[l * number : (l + 1) * number], axis=0, keepdims=True)
                for l in range(LAYERS)
            ]
            + [jnp.zeros((8 - LAYERS, value.shape[1]), F32)],
            axis=0,
        )
        seen = mm_low(mean, pr)
        mixed = jnp.where(own_half, mm_low(seen, values), 0.0)
        left[0:8] = seen
        left[8:16] = mm_nt_low(mixed, head_columns)

    def wblock(layer, place):
        return w[MAIN * layer + place].reshape(channels, WIDE)

    def inside(low, count):
        row = lax.broadcasted_iota(jnp.int32, (count, 1), 0) + (low - HALO) + seq * own
        return (row >= 0) & (row < n_seq * own)

    def windows_forward(layer):
        low = 16 * layer
        high = grid_rows - low
        scale, shift = 1.0 + vec[layer, 0:1], vec[layer, 1:2]
        here = xe[...].astype(F32) if layer == 0 else x1[...]
        shifted = (here * scale + shift).astype(BF).astype(F32)
        shifted = jnp.where(inside(0, grid_rows), shifted, 0.0)
        groups = grid_rows // 8
        bh[0] = jnp.zeros((8, channels), F32)
        bh[1 : 1 + groups] = in_eights(shifted)
        bh[1 + groups :] = jnp.zeros((3, 8, channels), F32)
        sht[layer] = jnp.transpose(shifted[HALO:top]).astype(BF)
        cat[low:high, channels : 2 * channels] = shifted[low:high].astype(BF)
        for tap in (0, 2):
            start = 8 + low + (tap - 1) * dil_ref[layer]
            cat[low:high, tap * channels : (tap + 1) * channels] = window(
                bh, start, high - low, channels
            ).astype(BF)

    def gates(layer, first_row, rows_now):
        spot = slice(first_row, first_row + rows_now)
        value = cat[spot, 0:2048]
        for part in range(2):
            columns = slice(part * WIDE, (part + 1) * WIDE)
            base = MAIN * layer + 5 * part
            lhs = mm(value, w[base : base + 4].reshape(2048, WIDE))
            tangent = jnp.tanh(lhs + vec[layer, 2:3, columns])
            rhs = mm(value, w[base + 10 : base + 14].reshape(2048, WIDE))
            opening = jax.nn.sigmoid(rhs + vec[layer, 3:4, columns])
            gate = tangent * opening
            gated[spot, columns] = gate.astype(BF)
            slopes[layer, spot, columns] = (opening * (1.0 - tangent * tangent)).astype(BF)
            other = slice(channels + part * WIDE, channels + (part + 1) * WIDE)
            slopes[layer, spot, other] = (gate * (1.0 - opening)).astype(BF)

    def residual(layer, first_row, rows_now):
        value = gated[first_row : first_row + rows_now]
        for part in range(2):
            columns = slice(part * WIDE, (part + 1) * WIDE)
            term = mm(value, wblock(layer, 5 * part + 4))
            if layer == 0:
                base = xe[first_row : first_row + rows_now, columns].astype(F32)
                x1[first_row : first_row + rows_now, columns] = (base + term) * HALF_ROOT
            else:
                base = x1[first_row : first_row + rows_now, columns]
                x1[first_row : first_row + rows_now, columns] = (base + term) * HALF_ROOT

    def skipped(layer, first_row, rows_now):
        value = gated[first_row : first_row + rows_now]
        spot = slice(first_row - HALO, first_row - HALO + rows_now)
        for part in range(2):
            columns = slice(part * WIDE, (part + 1) * WIDE)
            term = mm(value, wblock(layer, 5 * part + 14))
            if layer == 0:
                sk[spot, columns] = term
            else:
                sk[spot, columns] = sk[spot, columns] + term

    low, high = 16, grid_rows - 16

    def gate_grads(layer, first_row, rows_now):
        spot = slice(first_row, first_row + rows_now)
        bb[spot, 0:channels] = (bx[spot] * HALF_ROOT).astype(BF)
        branch = jnp.concatenate([wblock(layer, 5 * part + 4) for part in range(4)], axis=1)
        back = mm_nt(bb[spot], branch)
        keep = inside(first_row, rows_now)
        for side in range(2):
            columns = slice(side * channels, (side + 1) * channels)
            value = back * slopes[layer, spot, columns].astype(F32)
            middle = slice((2 + side) * channels, (3 + side) * channels)
            cat[spot, middle] = jnp.where(keep, value, 0.0).astype(BF)

    def windows_backward(layer):
        reach, limit = (low, high) if layer else (HALO, top)
        edge = 1 + low // 8
        bh[0:edge] = jnp.zeros((edge, 8, channels), F32)
        bh[1 + high // 8 :] = jnp.zeros((edge + 2, 8, channels), F32)
        for side in range(2):
            middle = slice((2 + side) * channels, (3 + side) * channels)
            value = cat[low:high, middle].astype(F32)
            bh[edge : 1 + high // 8] = in_eights(value)
            total = jnp.sum(value[HALO - low : top - low], axis=0, keepdims=True)
            sums[layer, 2 + side : 3 + side] = total
            for tap in (0, 2):
                start = 8 + reach - (tap - 1) * dil_ref[layer]
                columns = slice((2 * tap + side) * channels, (2 * tap + side + 1) * channels)
                cat[reach:limit, columns] = window(bh, start, limit - reach, channels).astype(BF)

    def frame_grads(layer, first_row, rows_now):
        spot = slice(first_row, first_row + rows_now)
        taps = jnp.concatenate(
            [wblock(layer, 5 * part + tap) for tap in range(3) for part in range(4)], axis=1
        )
        back = mm_nt(cat[spot], taps)
        if layer:
            here = x1[spot]
            row = lax.broadcasted_iota(jnp.int32, (rows_now, 1), 0) + first_row
            kept = jnp.where((row >= HALO) & (row < top), back, 0.0)
        else:
            here = xe[spot].astype(F32)
            kept = back
        sums[layer, 0:1] += jnp.sum(kept * here, axis=0, keepdims=True)
        sums[layer, 1:2] += jnp.sum(kept, axis=0, keepdims=True)
        bx[spot] = bx[spot] * HALF_ROOT + back * (1.0 + vec[layer, 0:1])

    def weight_grad(layer, part, i):
        if i < 4:
            tap = i if i < 3 else 1
            start = pl.multiple_of(tap * 1024 + part * WIDE, WIDE)
            lhs = sht[layer] if i < 3 else condt[...]
            return mm(lhs, cat[HALO:top, pl.ds(start, WIDE)])
        start = pl.multiple_of(part * WIDE, WIDE)
        return mm(gatt[layer], bb[HALO:top, pl.ds(start, WIDE)])

    core_sent = {}

    def x_of(turn):
        return x if turn else 1 - x

    def give(layer, turn):
        xx = x_of(turn)
        part = 2 * (1 - c) + xx
        buffer, base = (gs, 0) if layer else (w, MAIN)
        for i in range(5):
            value = weight_grad(layer, part, i).astype(BF)
            spot = 5 * xx + i
            buffer[base + spot] = value.reshape(nz, 2, rows, WIDE)
            core_sent[layer, turn, i] = remote(
                buffer.at[base + spot], red_in.at[layer, spot], seq, sib
            )

    def keep(layer, turn):
        xx = x_of(turn)
        part = 2 * c + xx
        for i in range(5):
            value = weight_grad(layer, part, i).reshape(nz, 2, rows, WIDE)
            spot = 5 * xx + i
            core_sent[layer, turn, i].wait_recv()
            red_in[layer, spot] = (red_in[layer, spot].astype(F32) + value).astype(BF)

    ones, twos, zs, targets = {}, {}, {}, {}
    for layer in range(LAYERS):
        for k in range(nz):
            zd = lax.rem(z + k, nz)
            targets[layer, k] = (zd, y_first(zd, OUT_SPLIT[layer]))

    def one_copy(layer, k, turn):
        zd, a = targets[layer, k]
        b = 1 - a
        if turn:
            xi, yi, j = a * (1 - x) + b * x, a + b * (1 - y), a + b * x
        else:
            xi, yi, j = 1 - x, b * (1 - y), b * (1 - x)
        return remote(
            red_in.at[layer, pl.ds(5 * xi, EACH), zd, yi],
            one_in.at[layer, k, j],
            a * seq + b * other_y, a * across + b * grp, start=not turn,
        )

    def red_one(layer, k):
        ones[layer, k] = [one_copy(layer, k, turn) for turn in range(2)]
        pl.when(targets[layer, k][1] == 1)(ones[layer, k][1].start)

    def red_one_more(layer, k):
        pl.when(targets[layer, k][1] == 0)(ones[layer, k][1].start)

    def red_two(layer, k):
        zd, a = targets[layer, k]
        b = 1 - a
        you = a * y + b * x
        for copy in ones[layer, k]:
            copy.wait_recv()
        for j in range(2):
            xi, yi = a * x + b * j, a * j + b * y

            def body(i, carry, j=j, xi=xi, yi=yi):
                one_in[layer, k, j, i] = (
                    one_in[layer, k, j, i] + red_in[layer, 5 * xi + i, zd, yi]
                )
                return carry

            lax.fori_loop(0, EACH, body, 0)
        twos[layer, k] = remote(
            one_in.at[layer, k, 1 - you], two_in.at[layer, k],
            a * other_y + b * seq, a * grp + b * across,
        )

    def red_three(layer, k):
        zd, a = targets[layer, k]
        you = a * y + (1 - a) * x
        twos[layer, k].wait_recv()

        def body(i, carry):
            two_in[layer, k, i] = two_in[layer, k, i] + one_in[layer, k, you, i]
            return carry

        lax.fori_loop(0, EACH, body, 0)
        if k:
            zs[layer, k] = remote(two_in.at[layer, k], z_in.at[layer, k - 1], zd * 2 + y, grp)

    side_sent = {}

    def red_side_one(layer):
        side_sent[layer] = [
            remote(
                red_in.at[layer, pl.ds(5 * xx + EACH, 5 - EACH), targets[layer, k][0]],
                ze_in.at[layer, k - 1, xx],
                targets[layer, k][0] * 2 + y, grp,
            )
            for k in range(1, nz)
            for xx in range(2)
        ]

    def red_side_two(layer):
        for copy in side_sent[layer]:
            copy.wait_recv()
        for xx in range(2):
            for i in range(5 - EACH):
                spot = 5 * xx + EACH + i
                total = red_in[layer, spot, z].astype(F32)
                for k in range(1, nz):
                    total = total + ze_in[layer, k - 1, xx, i].astype(F32)
                red_in[layer, spot, z] = total.astype(BF)
        side_sent[layer] = [
            remote(
                red_in.at[layer, pl.ds(5 * xx + EACH, 5 - EACH), z, yy], xe_in.at[layer, place],
                to_seq, to_grp,
            )
            for place, (xx, yy, to_seq, to_grp) in enumerate(
                (
                    (1 - x, y, seq, across), (x, 1 - y, other_y, grp),
                    (1 - x, 1 - y, other_y, across),
                )
            )
        ]

    def red_side_three(layer):
        for copy in side_sent[layer]:
            copy.wait_recv()
        for i in range(5 - EACH):
            total = red_in[layer, 5 * x + EACH + i, z, y].astype(F32)
            for place in range(3):
                total = total + xe_in[layer, place, i].astype(F32)
            fin[layer, EACH + i] = total.astype(BF)

    lasts = {}
    outs = []

    def local_out(src, dst):
        copy = pltpu.make_async_copy(src, dst, out_sem.at[len(outs)])
        copy.start()
        outs.append(copy)

    def red_four(layer):
        for k in range(1, nz):
            zs[layer, k].wait_recv()

        def body(i, carry):
            total = two_in[layer, 0, i].astype(F32)
            for k in range(1, nz):
                total = total + z_in[layer, k - 1, i].astype(F32)
            fin[layer, i] = total.astype(BF)
            return carry

        lax.fori_loop(0, EACH, body, 0)
        src, dst = fin.at[layer], out_hbm.at[layer, mine]
        lasts[layer] = [remote(src, dst, seq, across), remote(src, dst, seq, sib)]
        if not layer and LAST_DIRECT:
            lasts[layer].append(remote(src, dst, seq, (1 - x) * 2 + 1 - c))
        local_out(src, dst)

    def red_five(layer):
        lasts[layer][0].wait_recv()
        ref = out_hbm.at[layer, theirs]
        lasts[layer].append(remote(ref, ref, seq, sib))

    ops = {}

    def op(*key):
        def keep_op(body):
            ops[key] = body
            return body

        return keep_op

    main_tiles = (0, 1, 2, 3, 4, 5, 6, 7, 15, 16)
    merges, crosses, film_sent, seen, hops = {}, {}, {}, {}, {}
    size_all, size_mid, size_own = grid_rows // 2, (high - low) // 2, own // 2
    embed = same_rows(embed_ref[...].astype(F32))

    for phase in (1, 2):

        @op("prep", phase)
        def _(phase=phase):
            ready([PER_LAYER * (phase - 1) + t for t in main_tiles], prep, BLOCK_OF)
            merges[phase] = merge_start(phase)

        @op("cross", phase)
        def _(phase=phase):
            crosses[phase] = merge_cross(phase, merges[phase])

        @op("end", phase)
        def _(phase=phase):
            merge_end(phase, crosses[phase])
            spread_z(phase)

    def quarter(j):
        return range(j * nz // 4, (j + 1) * nz // 4)

    for phase in (1, 2):
        for name, body in (("e1", side_first), ("e2", side_second), ("e3", side_third)):

            @op(name, phase)
            def _(phase=phase, body=body):
                body(phase)

        for j in range(4):
            for name, body in (("first", first), ("second", second), ("third", third)):

                @op(name, phase, j)
                def _(phase=phase, j=j, body=body):
                    for k in quarter(j):
                        body(phase, k)

    parts = {"K": (0, KEY_VALUE), "R": (KEY_VALUE, FILM * LAYERS - KEY_VALUE)}
    for name, (begin, blocks) in parts.items():
        half = blocks // 2
        own_half_at = begin + c * half

        @op("fc" + name)
        def _(name=name, begin=begin, half=half):
            order = FILM_ORDER[:2] if name == "K" else FILM_ORDER[2:]
            for layer in range(LAYERS):
                ready([PER_LAYER * layer + t for t in order], fr, FILM_OF)
            film_sent[name, 0] = remote(
                fr.at[pl.ds(begin + (1 - c) * half, half)],
                fr_in.at[pl.ds(begin // 2, half)],
                seq, sib,
            )

        @op("fx" + name)
        def _(name=name, begin=begin, half=half, own_half_at=own_half_at):
            film_sent[name, 0].wait_recv()
            spot = slice(begin // 2, begin // 2 + half)
            fr_in[spot] = fr_in[spot] + fr[pl.ds(own_half_at, half)]
            ref = pl.ds(begin // 2, half)
            film_sent[name, 1] = remote(fr_in.at[ref], fx.at[ref], seq, across)

        @op("fl" + name)
        def _(name=name, begin=begin, half=half, own_half_at=own_half_at):
            film_sent[name, 1].wait_recv()
            spot = slice(begin // 2, begin // 2 + half)
            ref = pl.ds(own_half_at, half)
            ff[ref] = fr_in[spot] + fx[spot]
            film_sent[name, 2] = remote(ff.at[ref], ff.at[ref], seq, sib)

    for turn in range(4):

        @op("pr", turn)
        def _(turn=turn):
            total = prompt[...] if turn else None
            for i in range(4):
                prompt_copy(turn, i).wait()
                flag = (pairing_ref[0] == 4 * turn + i).astype(F32).astype(BF)
                part = slice((i % 2) * channels, (i % 2 + 1) * channels)
                term = slopes[i // 2, 0 : prompt.shape[0], part] * flag
                total = term if total is None else total + term
            prompt[...] = total
            if turn < 3:
                for i in range(4):
                    prompt_copy(turn + 1, i).start()

    def gathered():
        while gathering:
            gathering.pop().wait_send()

    @op("condt")
    def _():
        local_in[2].wait()
        condt[...] = jnp.transpose(cat[HALO:top, 1536:2048].astype(F32)).astype(BF)

    @op("hsK")
    def _():
        film_sent["K", 2].wait_recv()
        for h in range(HEADS):
            columns = slice((h % 4) * wide_head, (h % 4 + 1) * wide_head)
            pieces = [
                film_block(layer, place + h // 4).astype(F32)[:, columns]
                for place in (0, 2)
                for layer in range(LAYERS)
            ]
            kv_out[h] = jnp.concatenate(pieces, axis=1).astype(BF)
        kv_in[seq] = kv_out[head]
        kv_begin()

    @op("heK")
    def _():
        kv_finish()

    @op("att")
    def _():
        attention()

    @op("hsB")
    def _():
        film_sent["R", 2].wait_recv()
        vectors = []
        embed_here, mixed = pick(embed), pick(left[8:16])
        for layer in range(LAYERS):
            vectors.append(film_rows(layer, mixed, (4, 5))[layer : layer + 1])
            steps = film_rows(layer, embed_here, (10, 11, 12, 13))
            vectors += [steps[0:1, :channels], steps[0:1, channels:]]
        hop_start(0, pack(vectors))

    @op("heB")
    def _():
        total = hop_end(0)
        hops["pooled"] = [unpack(total, 3 * layer) for layer in range(LAYERS)]
        for layer in range(LAYERS):
            vec[layer, 2:3] = unpack(total, 3 * layer + 1)
            vec[layer, 3:4] = unpack(total, 3 * layer + 2)

    @op("hsC")
    def _():
        vectors = []
        for layer in range(LAYERS):
            pooled = hops["pooled"][layer]
            film = film_rows(layer, pick(same_rows(pooled)), (6, 7, 8, 9))
            vectors += [film[0:1, :channels], film[0:1, channels:]]
        hop_start(1, pack(vectors))

    @op("heC")
    def _():
        total = hop_end(1)
        for layer in range(LAYERS):
            vec[layer, 0:1] = unpack(total, 2 * layer)
            vec[layer, 1:2] = unpack(total, 2 * layer + 1)

    @op("win0")
    def _():
        local_in[1].wait()
        for copy in halos[:4]:
            copy.wait_recv()
        windows_forward(0)

    @op("win1")
    def _():
        local_in[3].wait()
        local_in[4].wait()
        for copy in halos[4:]:
            copy.wait_recv()
        bx[...] = bb[:, 0:channels].astype(F32)
        windows_forward(1)

    for layer in range(LAYERS):
        start, size = (low, size_mid) if layer else (0, size_all)
        for part, name in enumerate("ab"):
            first_row = start + part * size

            @op(f"gates{layer}{name}")
            def _(layer=layer, first_row=first_row, size=size, part=part):
                if not part:
                    arrived(1 + layer)
                gates(layer, first_row, size)

        @op(f"gatt{layer}")
        def _(layer=layer):
            gatt[layer] = jnp.transpose(gated[HALO:top].astype(F32)).astype(BF)

    @op("res0")
    def _():
        for part in range(2):
            residual(0, part * size_all, size_all)

    @op("skip0")
    def _():
        for part in range(2):
            skipped(0, HALO + part * size_own, size_own)

    @op("out1")
    def _():
        for part in range(2):
            residual(1, HALO + part * size_own, size_own)
            skipped(1, HALO + part * size_own, size_own)
        local_out(x1.at[pl.ds(HALO, own)], block_hbm.at[0])
        local_out(sk, skip_hbm.at[0])

    for layer in range(LAYERS):
        for part, name in enumerate("ab"):

            @op(f"gg{layer}{name}")
            def _(layer=layer, part=part):
                if layer and not part:
                    sums[...] = jnp.zeros_like(sums)
                gate_grads(layer, low + part * size_mid, size_mid)

            @op(f"fg{layer}{name}")
            def _(layer=layer, part=part):
                if layer:
                    frame_grads(1, low + part * size_mid, size_mid)
                else:
                    frame_grads(0, HALO + part * size_own, size_own)

        @op(f"winb{layer}")
        def _(layer=layer):
            windows_backward(layer)

        for xx in range(2):

            @op("give", layer, xx)
            def _(layer=layer, xx=xx):
                if not layer:
                    gathered()
                give(layer, xx)

            @op("keep", layer, xx)
            def _(layer=layer, xx=xx):
                keep(layer, xx)

        for j in range(4):
            for name, body in (
                ("one", red_one), ("onb", red_one_more), ("two", red_two), ("three", red_three)
            ):

                @op(name, layer, j)
                def _(layer=layer, j=j, body=body):
                    for k in quarter(j):
                        body(layer, k)

        for name, body in (("r1", red_side_one), ("r2", red_side_two), ("r3", red_side_three)):

            @op(name, layer)
            def _(layer=layer, body=body):
                body(layer)

        @op("four", layer)
        def _(layer=layer):
            red_four(layer)

        @op("five", layer)
        def _(layer=layer):
            red_five(layer)

    @op("hs3")
    def _():
        local_out(bx.at[pl.ds(HALO, own)], gframes_hbm.at[0])
        hop_start(2, pack([sums[l, i : i + 1] for l in range(LAYERS) for i in range(4)]))

    @op("he3")
    def _():
        total = hop_end(2)
        hops["sides"] = [[unpack(total, 4 * l + i) for i in range(4)] for l in range(LAYERS)]

    @op("hs4")
    def _():
        vectors = []
        for layer in range(LAYERS):
            dfilm = same_rows(jnp.concatenate(hops["sides"][layer][0:2], axis=1))
            vectors.append(film_back(layer, dfilm, (6, 7, 8, 9))[0:1])
        hop_start(3, pack(vectors))

    @op("he4")
    def _():
        total = hop_end(3)
        hops["dpooled"] = [unpack(total, layer) for layer in range(LAYERS)]


    @op("fb")
    def _():
        vectors = [
            film_back(l, same_rows(hops["dpooled"][l]), (4, 5))[0:1] for l in range(LAYERS)
        ]
        if copies_of > 1:
            hop_start(4, pack(vectors))
            total = hop_end(4)
            vectors = [unpack(total, layer) for layer in range(LAYERS)]
        dmixed = jnp.concatenate(vectors + [jnp.zeros((8 - LAYERS, channels), F32)], axis=0)
        dmixed = jnp.where(own_half, mm_low(dmixed, head_columns), 0.0)
        keys, values = head_weights()
        pr = prompt[...]
        dmean = mm_nt_low(mm_nt_low(dmixed, values), pr) * (1.0 / number)
        dprobs = jnp.concatenate(
            [jnp.broadcast_to(dmean[l : l + 1], (number, channels)) for l in range(LAYERS)], axis=0
        )
        value = probs[...]
        inner = jnp.sum(dprobs * value, axis=1, keepdims=True)
        dprobe = mm_low(value * (dprobs - inner) * 0.125, pr)
        dqueries = mm_low(dprobe, keys)
        half = lax.div(lax.broadcasted_iota(jnp.int32, (number, 128), 1), wide_head)
        dquery = jnp.where(half == 0, dqueries[0:number], dqueries[number : 2 * number])
        dq_in[grp] = dquery.astype(BF)
        small_out[...] = jnp.concatenate([dmixed, jnp.zeros((8, 128), F32)], axis=0).astype(BF)
        lefts = jnp.concatenate(
            [dprobe, left[0:2], left[8:10]]
            + [hops["pooled"][layer] for layer in range(LAYERS)]
            + [embed[0:1], jnp.zeros((128 - 2 * number - 7, channels), F32)],
            axis=0,
        )
        at_out[...] = jnp.transpose(lefts).astype(BF).reshape(n_seq, rows, 128)

    @op("hs5")
    def _():
        small_in[seq] = small_out[...]
        at_in[seq] = at_out[seq]
        small_begin()
        at_begin()

    def halves(one, two):
        wanted = lax.broadcasted_iota(jnp.int32, one.shape, 1) < wide_head
        return (
            jnp.where(wanted, one, pltpu.roll(two, wide_head, 1)),
            jnp.where(wanted, pltpu.roll(one, wide_head, 1), two),
        )

    def by_heads(ref):
        blocks = [[], []]
        for h in range(0, HEADS, 2):
            pair = halves(ref[h * copies_of].astype(F32), ref[(h + 1) * copies_of].astype(F32))
            for layer in range(LAYERS):
                blocks[layer].append(pair[layer])
        return [jnp.concatenate(blocks[layer], axis=1) for layer in range(LAYERS)]

    dq_sent = []

    @op("dq1")
    def _():
        for k in range(1, 4):
            ref = dq_in.at[grp]
            dq_sent.append(remote(ref, ref, seq, lax.rem(grp + k, 4)))

    @op("dq2")
    def _():
        for copy in dq_sent:
            copy.wait_recv()
        total = dq_in[0].astype(F32)
        for k in range(1, 4):
            total = total + dq_in[k].astype(F32)
        dq_out[...] = total
        dq_all[seq] = total
        dq_begin()

    @op("dq3")
    def _():
        dq_finish()
        total = by_heads(dq_all)
        for layer in range(LAYERS):
            dquery_ref[layer] = total[layer]

    @op("he5")
    def _():
        small_finish()
        at_finish()

        full = by_heads(small_in)
        pieces = []
        for layer in range(LAYERS):
            pieces += hops["sides"][layer]
            pieces += [hops["dpooled"][layer], full[layer][layer : layer + 1]]
        pieces.append(jnp.zeros((16 - len(pieces), channels), F32))
        wide[grp] = jnp.concatenate(pieces, axis=0).astype(BF)
        at = lax.broadcasted_iota(jnp.int32, (rows, 128), 1)
        thin = jnp.where(at >= 66, at_in[seq].astype(F32), 0.0)
        for h in range(0, HEADS, 2):
            one, two = at_in[h * copies_of].astype(F32), at_in[(h + 1) * copies_of].astype(F32)
            pair = jnp.where(at < wide_head, one, pltpu.roll(two, wide_head, 1))
            bundle[grp, :, h * wide_head : (h + 2) * wide_head] = pair.astype(BF)
            for k, value in ((h, one), (h + 1, two)):
                turned = pltpu.roll(value, wide_head + 2 * k, 1)
                thin = jnp.where(lax.div(at, 2) == k, turned, thin)
        bundle[grp, :, channels : channels + 128] = thin.astype(BF)

    bundles = []

    @op("bundle")
    def _():
        for k in range(1, 4):
            for ref in (bundle.at[grp], wide.at[grp]):
                bundles.append(remote(ref, ref, seq, lax.rem(grp + k, 4)))

    @op("low")
    def _():
        for copy in bundles:
            copy.wait_recv()
        mask = head_mask()
        at = lax.broadcasted_iota(jnp.int32, (8, channels), 0)
        probe = bundle[0, :, 0:channels].astype(F32)
        for k in range(1, 4):
            probe = probe + bundle[k, :, 0:channels].astype(F32)
        probe = probe.astype(BF)
        blank = jnp.zeros((number, channels), F32)
        column = lax.div(lax.broadcasted_iota(jnp.int32, (number, channels), 1), wide_head)
        for layer in range(LAYERS):
            side = []
            for h in range(HEADS):
                one = jnp.where(column == h, queries_ref[layer], 0.0)
                side += [blank, one] if layer else [one, blank]
            low_ref[layer, 0] = mm(probe, jnp.concatenate(side, axis=0).astype(BF)).astype(BF)
            total = None
            for k in range(4):
                right = wide[k].astype(F32)[6 * layer : 6 * layer + 6]
                dmixed = jnp.where(mask, right[5:6], 0.0)
                nothing = jnp.zeros((1, channels), F32)
                rows_of = []
                for h in range(HEADS):
                    one = dmixed[h : h + 1]
                    rows_of += [nothing, one] if layer else [one, nothing]
                value = jnp.concatenate(rows_of, axis=0)
                gap = jnp.zeros((48, channels), F32)
                rest = jnp.zeros((56, channels), F32)
                pieces = [jnp.concatenate([value, gap, jnp.zeros((64, channels), F32)], axis=0)]
                for i, row in ((4, 2), (0, 4), (1, 4), (2, 6), (3, 6)):
                    row = row + (layer if row < 6 else 0)
                    one = jnp.where(at == row, right[i : i + 1], 0.0)
                    pieces.append(
                        jnp.concatenate([jnp.zeros((64, channels), F32), one, rest], axis=0)
                    )
                term = mm(
                    bundle[k, :, channels : channels + 128],
                    jnp.concatenate(pieces, axis=1).astype(BF),
                )
                total = term if total is None else total + term
            for i in range(6):
                low_ref[layer, 1 + i] = total[:, i * channels : (i + 1) * channels].astype(BF)

    @op("end")
    def _():
        for copies in lasts.values():
            for copy in copies[1:]:
                copy.wait_recv()
        if LAST_DIRECT:
            lasts[0][0].wait_recv()
        for copy in outs:
            copy.wait()
        for copy in halos:
            copy.wait_send()
        gathered()
        for copy in waits:
            copy.wait_send()

    local_in[0].wait()
    for key in ORDER:
        ops[key if isinstance(key, tuple) else (key,)]()


def train_step(
    n_seq, owners, dilations, lengths, pairing, step_embed, queries, master, prompts,
    frames_in, cond_frames, grad_out, grad_skip,
):
    _, own, channels = frames_in.shape
    rows = master.shape[1]
    number = queries.shape[1]
    grid_rows = own + 2 * HALO
    nz = n_seq // 2
    v = pltpu.VMEM
    dma = pltpu.SemaphoreType.DMA
    frame_out = jax.ShapeDtypeStruct((1, own, channels), F32)
    film = FILM * LAYERS
    copies = 96 + 34 * nz
    return pl.pallas_call(
        functools.partial(step_kernel, n_seq),
        out_shape=(
            frame_out,
            frame_out,
            frame_out,
            jax.ShapeDtypeStruct((LAYERS, 4, 5, rows, WIDE), BF),
            jax.ShapeDtypeStruct((LAYERS, LOW_RANK, rows, channels), BF),
            jax.ShapeDtypeStruct((LAYERS, number, channels), F32),
        ),
        in_specs=[smem_spec()] * 4 + [vmem_spec()] * 2 + [any_spec()] * 6,
        out_specs=(any_spec(),) * 4 + (vmem_spec(),) * 2,
        scratch_shapes=[
            v((BLOCKS, nz, 2, rows, WIDE), BF),
            v((10, nz, 2, rows, WIDE), BF),
            v((BLOCKS, rows, WIDE), BF),
            v((BLOCKS // 2, rows, WIDE), BF),
            v((BLOCKS // 4, rows, WIDE), BF),
            v((film, rows, WIDE), BF),
            v((film // 2, rows, WIDE), BF),
            v((film // 2, rows, WIDE), BF),
            v((film, rows, WIDE), BF),
            v((LAYERS, 10, nz, 2, rows, WIDE), BF),
            v((LAYERS, nz, 2, EACH, rows, WIDE), BF),
            v((LAYERS, nz, EACH, rows, WIDE), BF),
            v((LAYERS, nz - 1, EACH, rows, WIDE), BF),
            v((LAYERS, nz - 1, 2, max(5 - EACH, 1), 2, rows, WIDE), BF),
            v((LAYERS, 3, max(5 - EACH, 1), rows, WIDE), BF),
            v((LAYERS, 5, rows, WIDE), BF),
            v((grid_rows, channels), BF),
            v((grid_rows, 6 * channels), BF),
            v((LAYERS, grid_rows, 2 * channels), BF),
            v((grid_rows, channels), BF),
            v((grid_rows, channels), F32),
            v((grid_rows // 8 + 4, 8, channels), F32),
            v((grid_rows, 2 * channels), BF),
            v((LAYERS, channels, own), BF),
            v((channels, own), BF),
            v((LAYERS, channels, own), BF),
            v((grid_rows, channels), F32),
            v((own, channels), F32),
            v(master.shape, F32),
            v(prompts.shape[1:], BF),
            v((LAYERS * number, prompts.shape[1]), F32),
            v((16, channels), F32),
            v((LAYERS, 8, channels), F32),
            v((LAYERS, 8, channels), F32),
            v((4, rows, channels + 128), BF),
            v((4, 16, channels), BF),
            v((4, number, 128), BF),
            v((HEADS, rows, WIDE), BF),
            v((n_seq, rows, WIDE), BF),
            v((n_seq, rows, 128), BF),
            v((n_seq, rows, 128), BF),
            v((16, 128), BF),
            v((n_seq, 16, 128), BF),
            v((number, 128), F32),
            v((n_seq, number, 128), F32),
            v((sum(HOP_ROWS), 128), F32),
            v((n_seq, sum(HOP_ROWS), 128), F32),
            dma((5,)),
            dma((4,)),
            dma((8,)),
            dma((8,)),
            dma((8,)),
            dma((copies,)),
            dma((copies,)),
            dma((len(HOP_ROWS), n_seq)),
            dma((len(HOP_ROWS), n_seq)),
            dma((4, n_seq)),
            dma((4, n_seq)),
        ],
        compiler_params=pltpu.CompilerParams(
            collective_id=0, has_side_effects=True, vmem_limit_bytes=MEM
        ),
        name="train_step",
    )(
        owners, dilations, lengths, pairing, step_embed, queries, master, prompts,
        frames_in, cond_frames, grad_out, grad_skip,
    )


def adam_update(weight, moment_one, moment_two, gradient, step_rate):
    moment_one = BETA_ONE * moment_one + (1.0 - BETA_ONE) * gradient
    moment_two = BETA_TWO * moment_two + (1.0 - BETA_TWO) * gradient * gradient
    normal = (
        moment_one
        * (1.0 / (1.0 - BETA_ONE**STEP))
        / (jnp.sqrt(moment_two * (1.0 / (1.0 - BETA_TWO**STEP))) + EPSILON)
    )
    return (moment_one, moment_two, weight - step_rate * (normal + WEIGHT_DECAY * weight))


def update_kernel(
    owners_ref, master_hbm, first_hbm, second_hbm, grad_hbm, low_hbm,
    queries_hbm, qfirst_hbm, qsecond_hbm, dq_hbm, block_in, skip_in, gframes_in,
    nfirst_hbm, nsecond_hbm, nmaster_hbm, ncopy_hbm, nqfirst_hbm, nqsecond_hbm, nqueries_hbm,
    block_out, skip_out, gframes_out,
    master, first, second, grad, low, three, one, two, copied, frames, asked,
    tile_of, grad_sem, in_sem, out_sem, frame_sem, asked_sem,
):
    grp = lax.axis_index("grp")
    grads_in = [
        pltpu.make_async_copy(a, b, grad_sem.at[i])
        for i, (a, b) in enumerate(((grad_hbm, grad), (low_hbm, low)))
    ]
    spots = [pl.ds(start, count) for start, count in CHUNKS]
    slots_in = [
        [
            pltpu.make_async_copy(a.at[spot], b.at[spot], in_sem.at[i, j])
            for j, (a, b) in enumerate(
                ((master_hbm, master), (first_hbm, first), (second_hbm, second))
            )
        ]
        for i, spot in enumerate(spots)
    ]
    frames_in = [
        pltpu.make_async_copy(a, frames.at[i], frame_sem.at[0, i])
        for i, a in enumerate((block_in, skip_in, gframes_in))
    ]
    asked_in = [
        pltpu.make_async_copy(a, asked.at[i], asked_sem.at[i])
        for i, a in enumerate((queries_hbm, qfirst_hbm, qsecond_hbm, dq_hbm))
    ]
    for copy in grads_in + slots_in[0] + asked_in + frames_in[:1] + slots_in[1] + frames_in[1:]:
        copy.start()
    for copies in slots_in[2:]:
        for copy in copies:
            copy.start()

    for slot in range(CAP + 1):
        tile_of[slot] = TILES
    count = jnp.int32(0)
    for tile in range(TILES):
        own = owners_ref[tile] == grp

        @pl.when(own)
        def _(count=count, tile=tile):
            tile_of[jnp.minimum(count, CAP)] = tile

        count = count + own.astype(jnp.int32)
    outs = []

    def send(a, b, sem):
        copy = pltpu.make_async_copy(a, b, sem)
        copy.start()
        outs.append(copy)

    def pass_frames(i, target):
        frames_in[i].wait()
        send(frames.at[i], target, frame_sem.at[1, i])

    def slot_update(slot, carry):
        tile = tile_of[slot]
        used = (tile < TILES).astype(jnp.int32)
        tile = jnp.minimum(tile, TILES - 1)
        layer, kind = lax.div(tile, PER_LAYER), lax.rem(tile, PER_LAYER)
        plain = kind < 8
        pair = jnp.where(plain, lax.rem(kind, 2), (kind == 16).astype(jnp.int32))
        tap = jnp.where(plain, lax.div(kind, 2), 4)
        full = jnp.concatenate([grad[layer, 2 * pair, tap], grad[layer, 2 * pair + 1, tap]], axis=1)
        place = jnp.where(kind < 10, kind - 3, kind - 10)
        thin = low[layer, jnp.clip(place, 0, LOW_RANK - 1)]
        is_thin = ((kind >= 8) & (kind <= 14)).astype(jnp.int32)
        gradient = jnp.where(
            jnp.broadcast_to(is_thin, full.shape) > 0, thin.astype(F32), full.astype(F32)
        )
        old, old_first, old_second = master[slot], first[slot], second[slot]
        new_first, new_second, new = adam_update(old, old_first, old_second, gradient, LEARN_RATE)
        keep = jnp.broadcast_to(used, old.shape) > 0
        new = jnp.where(keep, new, old)
        one[slot] = jnp.where(keep, new_first, old_first)
        two[slot] = jnp.where(keep, new_second, old_second)
        three[slot] = new
        copied[slot] = new.astype(BF)
        return carry

    for copy in grads_in:
        copy.wait()
    passed = (block_out, skip_out, gframes_out)
    for i, (start, number) in enumerate(CHUNKS):
        for copy in slots_in[i]:
            copy.wait()
        lax.fori_loop(start, start + number, slot_update, 0)
        for j, (a, b) in enumerate(
            ((one, nfirst_hbm), (two, nsecond_hbm), (three, nmaster_hbm), (copied, ncopy_hbm))
        ):
            send(a.at[spots[i]], b.at[spots[i]], out_sem.at[i, j])
        if i < len(passed):
            pass_frames(i, passed[i])
        if i == 1:
            for copy in asked_in:
                copy.wait()
            news = adam_update(asked[0], asked[1], asked[2], asked[3], QUERY_RATE)
            for j, (value, target) in enumerate(
                zip(news, (nqfirst_hbm, nqsecond_hbm, nqueries_hbm))
            ):
                asked[4 + j] = value
                send(asked.at[4 + j], target, asked_sem.at[4 + j])
    for copy in outs:
        copy.wait()


CHUNKS = ((0, 2), (2, 3), (5, 4), (9, 4))


def update(owners, master, first, second, grads, low, queries, qfirst, qsecond, dq, *frames):
    any_ = any_spec()
    query = jax.ShapeDtypeStruct(queries.shape, F32)
    full = jax.ShapeDtypeStruct(master.shape, F32)
    passed = jax.ShapeDtypeStruct(frames[0].shape, F32)
    v = pltpu.VMEM
    slots = v(master.shape, F32)
    return pl.pallas_call(
        update_kernel,
        out_shape=(full, full, full, jax.ShapeDtypeStruct(master.shape, BF), query, query, query)
        + (passed,) * 3,
        in_specs=[smem_spec()] + [any_] * 12,
        out_specs=(any_,) * 10,
        scratch_shapes=[
            slots, slots, slots, v(grads.shape, BF), v(low.shape, BF),
            slots, slots, slots, v(master.shape, BF), v((3,) + passed.shape, F32),
            v((7,) + queries.shape, F32),
            pltpu.SMEM((CAP + 1,), jnp.int32),
            pltpu.SemaphoreType.DMA((2,)),
            pltpu.SemaphoreType.DMA((len(CHUNKS), 3)),
            pltpu.SemaphoreType.DMA((len(CHUNKS), 4)),
            pltpu.SemaphoreType.DMA((2, 3)),
            pltpu.SemaphoreType.DMA((7,)),
        ],
        compiler_params=pltpu.CompilerParams(vmem_limit_bytes=MEM),
        name="update",
    )(owners, master, first, second, grads, low, queries, qfirst, qsecond, dq, *frames)


def on_device(
    n_seq,
    frames_in,
    cond_frames,
    step_embed,
    prompts,
    prompt_lengths,
    pairing,
    dilations,
    owners,
    master,
    first_moment,
    second_moment,
    queries,
    query_first,
    query_second,
    grad_out,
    grad_skip,
):
    block, skip, gframes, own_grads, low, dq = train_step(
        n_seq, owners, dilations, prompt_lengths, pairing, step_embed, queries, master, prompts,
        frames_in, cond_frames, grad_out, grad_skip,
    )
    (
        new_first, new_second, new_master, new_copy, nqf, nqs, nq,
        block_out, skip_out, grad_frames,
    ) = update(
        owners, master, first_moment, second_moment, own_grads, low,
        queries, query_first, query_second, dq, block, skip, gframes,
    )
    return (
        new_first, new_second, new_master, new_copy, nqf, nqs, nq,
        block_out, skip_out, grad_frames,
    )


def solution(mesh):
    shard = P("grp", "seq", None)
    placed = (
        shard, shard, P("grp", None), P(), P(), P("grp"), P(), P(),
        shard, shard, shard, P(), P(), P(), shard, shard,
    )
    return jax.shard_map(
        functools.partial(on_device, mesh.shape["seq"]),
        mesh=mesh,
        in_specs=placed,
        out_specs=(shard, shard, shard, shard, P(), P(), P(), shard, shard, shard),
        check_vma=False,
    )
```

```python
import functools

import jax
import jax.numpy as jnp
from jax import lax
from jax.experimental import pallas as pl
from jax.experimental.pallas import tpu as pltpu
from jax.sharding import PartitionSpec as P

HEADS = 8
LAYERS = 2
DMAX = 8
CAP = 13
STEP = 10
PER_LAYER = 17
TILES = PER_LAYER * LAYERS

BETA_ONE = 0.9
BETA_TWO = 0.999
EPSILON = 1e-08
WEIGHT_DECAY = 0.01
LEARN_RATE = 0.02
QUERY_RATE = 0.4
HALF_ROOT = 0.7071067811865476
NEGATIVE = -1e30

BF = jnp.bfloat16
F32 = jnp.float32
HALO = 32
WIDE = 256
MAIN = 20
BLOCKS = MAIN * LAYERS
PHASES = (None, (0, MAIN), (MAIN, MAIN))
FILM_ORDER = (10, 11, 12, 13, 14, 8, 9)
FILM = 2 * len(FILM_ORDER)
LOW_RANK = len(FILM_ORDER)
KEY_VALUE = 4 * LAYERS
HOP_ROWS = (24, 16, 32, 8, 8)
IN_SPLIT = (2, 2, 2)
OUT_SPLIT = (2, 2)
LAST_DIRECT = True
ORDER = (
    ("prep", 1), "fcK", "fcR", ("pr", 0), ("prep", 2), ("cross", 1), "fxK", ("pr", 1),
    ("cross", 2), "fxR", ("end", 1), ("first", 1, 0), "flK", ("pr", 2), "hsK", ("end", 2),
    ("first", 2, 0), ("first", 1, 2), ("first", 1, 1), ("pr", 3), ("first", 1, 3), "flR",
    ("second", 1, 2), ("second", 1, 0), "heK", ("second", 2, 0), "att", ("second", 1, 1), "hsB",
    ("second", 1, 3), ("first", 2, 2), ("first", 2, 3), ("third", 1, 3), ("third", 2, 0), "heB",
    ("third", 1, 2), "hsC", ("third", 1, 1), ("third", 1, 0), ("first", 2, 1), ("second", 2, 2),
    "heC", ("second", 2, 3), "win0", "condt", ("second", 2, 1), "gates0a", "gates0b",
    ("third", 2, 2), "res0", ("third", 2, 3), ("third", 2, 1), "gatt0", "skip0", "win1",
    "gates1a", "gates1b", "gatt1", "gg1a", "gg1b", "winb1", ("give", 1, 1), ("give", 1, 0),
    "fg1a", ("keep", 1, 1), "fg1b", ("keep", 1, 0), ("one", 1, 3), "gg0a", ("one", 1, 1), "gg0b",
    "winb0", "out1", "fg0b", ("one", 1, 0), ("one", 1, 2), ("give", 0, 0), "fg0a", "hs3",
    ("two", 1, 3), ("give", 0, 1), ("two", 1, 1), ("keep", 0, 0), ("two", 1, 2), ("two", 1, 0),
    ("keep", 0, 1), "he3", ("one", 0, 2), ("one", 0, 0), "hs4", ("three", 1, 1), ("one", 0, 1),
    ("three", 1, 2), ("one", 0, 3), ("three", 1, 3), ("two", 0, 2), "he4", "fb", "dq1", "hs5",
    ("two", 0, 0), ("three", 1, 0), ("two", 0, 1), ("two", 0, 3), ("three", 0, 2),
    ("three", 0, 0), ("three", 0, 1), ("three", 0, 3), "he5", "bundle", ("four", 1), "dq2",
    ("four", 0), ("five", 1), "dq3", "low", "end",
)

MEM = 64 * 1024 * 1024 - 256 * 1024
MESH = pl.DeviceIdType.MESH


def block_table():
    table = {}
    for layer in range(LAYERS):
        base = PER_LAYER * layer
        start = MAIN * layer
        for part in range(4):
            for tap in range(4):
                table[base + 2 * tap + part // 2, part % 2] = start + 5 * part + tap
            table[base + 15 + part // 2, part % 2] = start + 5 * part + 4
    return table


BLOCK_OF = block_table()
FILM_OF = {
    (PER_LAYER * layer + tile, side): (
        4 * layer + 2 * place + side
        if place < 2
        else KEY_VALUE + (FILM - 4) * layer + 2 * (place - 2) + side
    )
    for layer in range(LAYERS)
    for place, tile in enumerate(FILM_ORDER)
    for side in range(2)
}


def mm(a, b):
    return lax.dot_general(a, b, (((1,), (0,)), ((), ())), preferred_element_type=F32)


def mm_nt(a, b):
    return lax.dot_general(a, b, (((1,), (1,)), ((), ())), preferred_element_type=F32)


def mm_nt_fine(a, b):
    high = a.astype(BF)
    return mm_nt(high, b) + mm_nt((a - high.astype(F32)).astype(BF), b)


def mm_low(a, b):
    return mm(a.astype(BF), b)


def mm_nt_low(a, b):
    return mm_nt(a.astype(BF), b)


def mm_nt_pairs(a, blocks):
    total = None
    for place, block in enumerate(blocks):
        term = mm_nt_fine(a[:, place * WIDE : (place + 1) * WIDE], block)
        total = term if total is None else total + term
    return total


def window(ref, start, count, width):
    group, rest = lax.div(start, 8), lax.rem(start, 8)
    groups = ref[pl.ds(group, count // 8 + 1), :, 0:width]
    turned = pltpu.roll(groups, lax.rem(8 - rest, 8), 1)
    row = lax.broadcasted_iota(jnp.int32, (1, 8, 1), 1)
    return jnp.where(row < 8 - rest, turned[:-1], turned[1:]).reshape(count, width)


def in_eights(value):
    return value.reshape(value.shape[0] // 8, 8, value.shape[1])


def place_of(n_seq):
    seq, grp = lax.axis_index("seq"), lax.axis_index("grp")
    z, y = lax.div(seq, 2), lax.rem(seq, 2)
    x, c = lax.div(grp, 2), lax.rem(grp, 2)
    return seq, grp, z, y, x, c


def greet(n_seq, seq, grp, groups):
    barrier = pltpu.get_barrier_semaphore()

    def one(k, carry):
        pl.semaphore_signal(
            barrier, inc=1, device_id={"seq": lax.rem(seq + k, n_seq), "grp": grp}, device_id_type=MESH
        )
        return carry

    lax.fori_loop(1, n_seq, one, 0)
    for k in range(1, groups):
        pl.semaphore_signal(
            barrier, inc=1, device_id={"seq": seq, "grp": lax.rem(grp + k, groups)}, device_id_type=MESH
        )
    pl.semaphore_wait(barrier, n_seq - 1 + groups - 1)


def any_spec():
    return pl.BlockSpec(memory_space=pl.ANY)


def vmem_spec():
    return pl.BlockSpec(memory_space=pltpu.VMEM)


def smem_spec():
    return pl.BlockSpec(memory_space=pltpu.SMEM)


def head_mask():
    row = lax.broadcasted_iota(jnp.int32, (HEADS, 512), 0)
    column = lax.broadcasted_iota(jnp.int32, (HEADS, 512), 1)
    return lax.div(column, 512 // HEADS) == row


def block_diagonal(rows):
    column = lax.div(lax.broadcasted_iota(jnp.int32, rows.shape, 1), 512 // HEADS)
    return jnp.concatenate([jnp.where(column == h, rows, 0.0) for h in range(HEADS)], axis=0)


def same_rows(row):
    return jnp.broadcast_to(row, (8, row.shape[1]))


def pack(vectors):
    pieces = [v[:, 128 * i : 128 * (i + 1)] for v in vectors for i in range(v.shape[1] // 128)]
    spare = -len(pieces) % 8
    if spare:
        pieces.append(jnp.zeros((spare, 128), pieces[0].dtype))
    return jnp.concatenate(pieces, axis=0)


def unpack(rows, place, pieces=4):
    return jnp.concatenate(
        [rows[pieces * place + i : pieces * place + i + 1] for i in range(pieces)], axis=1
    )


def step_kernel(
    n_seq, owners_ref, dil_ref, lengths_ref, pairing_ref, embed_ref, queries_ref, master_hbm,
    prompts_hbm, frames_hbm, cond_hbm, gout_hbm, gskip_hbm,
    block_hbm, skip_hbm, gframes_hbm, out_hbm, low_ref, dquery_ref,
    w, gs, prep, core_in, x_in, fr, fr_in, fx, ff, red_in, one_in, two_in, z_in, fin,
    xe, cat, slopes, gated, x1, bh, bb, sht, condt, gatt, bx, sk,
    master, prompt, probs, left, vec, sums, bundle, wide, dq_in,
    kv_out, kv_in, at_out, at_in, small_out, small_in, dq_out, dq_all, hop_src, hop_in,
    in_sem, prompt_sem, out_sem, hsend, hrecv, send, recv, hop_send, hop_recv, each_send, each_recv,
):
    seq, grp, z, y, x, c = place_of(n_seq)
    nz = n_seq // 2
    rows = prep.shape[1]
    own = frames_hbm.shape[1]
    grid_rows = own + 2 * HALO
    top = HALO + own
    channels = 512
    number = queries_ref.shape[1]
    sib, across, other_y = x * 2 + 1 - c, (1 - x) * 2 + c, z * 2 + 1 - y
    mine, theirs = 2 * c + x, 2 * c + 1 - x

    local_in = [
        pltpu.make_async_copy(a, b, in_sem.at[i])
        for i, (a, b) in enumerate(
            (
                (master_hbm, master),
                (frames_hbm.at[0], xe.at[pl.ds(HALO, own)]),
                (cond_hbm.at[0], cat.at[pl.ds(HALO, own), pl.ds(1536, channels)]),
                (gout_hbm.at[0], bb.at[pl.ds(HALO, own), pl.ds(0, channels)]),
                (gskip_hbm.at[0], bb.at[pl.ds(HALO, own), pl.ds(channels, channels)]),
            )
        )
    ]
    for copy in local_in:
        copy.start()

    def prompt_copy(turn, i):
        rows_now, columns = pl.ds(0, prompt.shape[0]), pl.ds((i % 2) * channels, channels)
        return pltpu.make_async_copy(
            prompts_hbm.at[4 * turn + i], slopes.at[i // 2, rows_now, columns], prompt_sem.at[i]
        )

    for i in range(4):
        prompt_copy(0, i).start()

    greet(n_seq, seq, grp, 4)

    waits = []
    used = [0]

    def remote(src, dst, to_seq, to_grp, sent=None):
        place = used[0]
        used[0] += 1
        copy = pltpu.make_async_remote_copy(
            src_ref=src,
            dst_ref=dst,
            send_sem=send.at[place],
            recv_sem=recv.at[place],
            device_id={"seq": to_seq, "grp": to_grp},
            device_id_type=MESH,
        )
        copy.start()
        (waits if sent is None else sent).append(copy)
        return copy

    after, before = lax.rem(seq + 1, n_seq), lax.rem(seq + n_seq - 1, n_seq)
    halos = []
    for ref, buffer, column in (
        (frames_hbm, xe, 0),
        (cond_hbm, cat, 1536),
        (gout_hbm, bb, 0),
        (gskip_hbm, bb, channels),
    ):
        for start, at, target in ((own - HALO, 0, after), (0, top, before)):
            place = len(halos)
            copy = pltpu.make_async_remote_copy(
                src_ref=ref.at[0, pl.ds(start, HALO)],
                dst_ref=buffer.at[pl.ds(at, HALO), pl.ds(column, channels)],
                send_sem=hsend.at[place],
                recv_sem=hrecv.at[place],
                device_id={"seq": target, "grp": grp},
                device_id_type=MESH,
            )
            copy.start()
            halos.append(copy)

    slots, flags = [], []
    count = jnp.int32(0)
    for tile in range(TILES):
        flag = (owners_ref[tile] == grp).astype(jnp.int32)
        slots.append(jnp.minimum(count, CAP - 1))
        flags.append(flag.astype(F32))
        count = count + flag

    def rounded(tile):
        return (master[slots[tile]] * flags[tile]).astype(BF)

    def ready(tiles, buffer, table):
        for tile in tiles:
            value = rounded(tile)
            buffer[table[tile, 0]] = value[:, :WIDE]
            buffer[table[tile, 1]] = value[:, WIDE:]

    def merge_start(phase):
        base, blocks = PHASES[phase]
        each = blocks // 4
        return remote(
            prep.at[pl.ds(base + 2 * (1 - c) * each, 2 * each)],
            core_in.at[pl.ds(base // 2, 2 * each)],
            seq, sib,
        )

    def merge_cross(phase, copy):
        base, blocks = PHASES[phase]
        each = blocks // 4
        copy.wait_recv()

        def add(i, carry):
            place = base // 2 + i
            core_in[place] = core_in[place] + prep[base + 2 * c * each + i]
            return carry

        lax.fori_loop(0, 2 * each, add, 0)
        return remote(
            core_in.at[pl.ds(base // 2 + (1 - x) * each, each)],
            x_in.at[pl.ds(base // 4, each)],
            seq, across,
        )

    def view(phase, quarter, zz, yy):
        base, blocks = PHASES[phase]
        each = blocks // 4
        return w.at[pl.ds(base + quarter * each, each), zz, yy]

    gathering, legs = [], {}

    def spread(ref, to_seq, to_grp):
        return remote(ref, ref, to_seq, to_grp, gathering)

    def merge_end(phase, copy):
        base, blocks = PHASES[phase]
        each = blocks // 4
        copy.wait_recv()

        def settle(i, carry):
            w[base + mine * each + i, z, y] = (
                core_in[base // 2 + x * each + i] + x_in[base // 4 + i]
            )
            return carry

        lax.fori_loop(0, each, settle, 0)

    def y_first(zz, quarters):
        return 1 - jnp.minimum(lax.div(4 * zz, quarters * nz), 1)

    def spread_z(phase):
        ref = view(phase, mine, z, y)
        for k in range(1, nz):
            legs[phase, k] = spread(ref, lax.rem(z + k, nz) * 2 + y, grp)

    core_legs = {phase: [] for phase in (1, 2)}

    def first(phase, k):
        zs = lax.rem(z - k + nz, nz)
        a = y_first(zs, IN_SPLIT[phase])
        b = 1 - a
        if k:
            legs[phase, k].wait_recv()
        ref = view(phase, mine, zs, y)
        one = spread(ref, a * other_y + b * seq, a * grp + b * across)
        two = spread(ref, a * seq + b * other_y, a * across + b * grp)
        core_legs[phase].append(spread(ref, seq, sib))
        legs[phase, k] = (zs, a, one, two)

    def second(phase, k):
        zs, a, one, two = legs[phase, k]
        b = 1 - a
        one.wait_recv()
        ref = view(phase, a * mine + b * theirs, zs, a * (1 - y) + b * y)
        last = spread(ref, a * seq + b * other_y, a * across + b * grp)
        core_legs[phase].append(spread(ref, seq, sib))
        legs[phase, k] = (zs, a, two, last)

    def third(phase, k):
        zs, a, two, last = legs[phase, k]
        b = 1 - a
        two.wait_recv()
        ref = view(phase, a * theirs + b * mine, zs, a * y + b * (1 - y))
        core_legs[phase].append(spread(ref, seq, sib))
        last.wait_recv()
        core_legs[phase].append(spread(view(phase, theirs, zs, 1 - y), seq, sib))

    def arrived(phase):
        for copy in core_legs[phase]:
            copy.wait_recv()

    def hop_refs(j):
        start = sum(HOP_ROWS[:j])
        spot = pl.ds(start, HOP_ROWS[j])
        return hop_src.at[spot], hop_in.at[seq, spot], hop_in.at[:, spot]

    def hop_copy(j, k):
        src, dst, _ = hop_refs(j)
        return pltpu.make_async_remote_copy(
            src_ref=src,
            dst_ref=dst,
            send_sem=hop_send.at[j, k],
            recv_sem=hop_recv.at[j, k],
            device_id={"seq": lax.rem(seq + k, n_seq), "grp": grp},
            device_id_type=MESH,
        )

    def hop_start(j, value):
        src, dst, _ = hop_refs(j)
        value = value.astype(src.dtype)
        src[...] = value
        dst[...] = value

        def one(k, carry):
            hop_copy(j, k).start()
            return carry

        lax.fori_loop(1, n_seq, one, 0)

    def hop_end(j):
        def one(k, carry):
            hop_copy(j, k).wait()
            return carry

        lax.fori_loop(1, n_seq, one, 0)
        _, _, whole = hop_refs(j)

        def add(i, total):
            return total + whole[i].astype(F32)

        return lax.fori_loop(0, n_seq, add, jnp.zeros((HOP_ROWS[j], 128), F32))

    position = lax.broadcasted_iota(jnp.int32, (channels, rows), 0)
    column = lax.broadcasted_iota(jnp.int32, (channels, rows), 1)
    chosen = jnp.where(position == column + seq * rows, 1.0, 0.0).astype(BF)

    def pick(v):
        return mm_low(v, chosen)

    def film_block(layer, place):
        if place < 4:
            return ff[4 * layer + place]
        return ff[KEY_VALUE + (FILM - 4) * layer + place - 4]

    def film_rows(layer, v, places):
        return jnp.concatenate([mm_low(v, film_block(layer, i)) for i in places], axis=1)

    def film_back(layer, v, places):
        total = None
        for i, place in enumerate(places):
            term = mm_nt_low(v[:, i * WIDE : (i + 1) * WIDE], film_block(layer, place))
            total = term if total is None else total + term
        return mm_nt_low(total, chosen)

    wide_head = channels // HEADS
    copies_of = n_seq // HEADS
    head = lax.div(seq, copies_of)
    lane = lax.broadcasted_iota(jnp.int32, (channels, 128), 1)
    at_row = lax.broadcasted_iota(jnp.int32, (channels, 128), 0)
    of_head = at_row == head * wide_head + lax.rem(lane, wide_head)
    head_columns = jnp.where(of_head, 1.0, 0.0).astype(BF)
    own_half = lax.div(lax.broadcasted_iota(jnp.int32, (8, 128), 1), wide_head) == (
        lax.broadcasted_iota(jnp.int32, (8, 128), 0)
    )

    def exchange(index, source, target):
        def copy(k):
            dest = lax.rem(seq + k, n_seq)
            return pltpu.make_async_remote_copy(
                src_ref=source(dest),
                dst_ref=target,
                send_sem=each_send.at[index, k],
                recv_sem=each_recv.at[index, k],
                device_id={"seq": dest, "grp": grp},
                device_id_type=MESH,
            )

        def begin():
            def one(k, carry):
                copy(k).start()
                return carry

            lax.fori_loop(1, n_seq, one, 0)

        def finish():
            def one(k, carry):
                copy(k).wait()
                return carry

            lax.fori_loop(1, n_seq, one, 0)

        return begin, finish

    kv_begin, kv_finish = exchange(
        0, lambda dest: kv_out.at[lax.div(dest, copies_of)], kv_in.at[seq]
    )
    at_begin, at_finish = exchange(1, lambda dest: at_out.at[dest], at_in.at[seq])
    dq_begin, dq_finish = exchange(3, lambda dest: dq_out, dq_all.at[seq])
    small_begin, small_finish = exchange(2, lambda dest: small_out, small_in.at[seq])

    def head_weights():
        value = kv_in[...].reshape(channels, WIDE)
        return value[:, 0:128], value[:, 128:256]

    def attention():
        keys, values = head_weights()
        pieces = []
        for layer in range(LAYERS):
            high = queries_ref[layer].astype(BF)
            rest = (queries_ref[layer] - high.astype(F32)).astype(BF)
            both = mm(high, head_columns) + mm(rest, head_columns)
            half = lax.div(lax.broadcasted_iota(jnp.int32, both.shape, 1), wide_head)
            pieces.append(jnp.where(half == layer, both, 0.0))
        probe = mm_nt_fine(jnp.concatenate(pieces, axis=0), keys)
        pr = prompt[...]
        scores = mm_nt_fine(probe, pr) * 0.125
        live = lax.broadcasted_iota(jnp.int32, scores.shape, 1) < lengths_ref[pairing_ref[0]]
        scores = jnp.where(live, scores, NEGATIVE)
        weight = jnp.exp(scores - jnp.max(scores, axis=1, keepdims=True))
        value = weight / jnp.sum(weight, axis=1, keepdims=True)
        probs[...] = value
        mean = jnp.concatenate(
            [
                jnp.mean(value[l * number : (l + 1) * number], axis=0, keepdims=True)
                for l in range(LAYERS)
            ]
            + [jnp.zeros((8 - LAYERS, value.shape[1]), F32)],
            axis=0,
        )
        seen = mm_low(mean, pr)
        mixed = jnp.where(own_half, mm_low(seen, values), 0.0)
        left[0:8] = seen
        left[8:16] = mm_nt_low(mixed, head_columns)

    def wblock(layer, place):
        return w[MAIN * layer + place].reshape(channels, WIDE)

    def inside(low, count):
        row = lax.broadcasted_iota(jnp.int32, (count, 1), 0) + (low - HALO) + seq * own
        return (row >= 0) & (row < n_seq * own)

    def windows_forward(layer):
        low = 16 * layer
        high = grid_rows - low
        scale, shift = 1.0 + vec[layer, 0:1], vec[layer, 1:2]
        here = xe[...].astype(F32) if layer == 0 else x1[...]
        shifted = (here * scale + shift).astype(BF).astype(F32)
        shifted = jnp.where(inside(0, grid_rows), shifted, 0.0)
        groups = grid_rows // 8
        bh[0] = jnp.zeros((8, channels), F32)
        bh[1 : 1 + groups] = in_eights(shifted)
        bh[1 + groups :] = jnp.zeros((3, 8, channels), F32)
        sht[layer] = jnp.transpose(shifted[HALO:top]).astype(BF)
        cat[low:high, channels : 2 * channels] = shifted[low:high].astype(BF)
        for tap in (0, 2):
            start = 8 + low + (tap - 1) * dil_ref[layer]
            cat[low:high, tap * channels : (tap + 1) * channels] = window(
                bh, start, high - low, channels
            ).astype(BF)

    def gates(layer, first_row, rows_now):
        spot = slice(first_row, first_row + rows_now)
        value = cat[spot, 0:2048]
        for part in range(2):
            columns = slice(part * WIDE, (part + 1) * WIDE)
            base = MAIN * layer + 5 * part
            lhs = mm(value, w[base : base + 4].reshape(2048, WIDE))
            tangent = jnp.tanh(lhs + vec[layer, 2:3, columns])
            rhs = mm(value, w[base + 10 : base + 14].reshape(2048, WIDE))
            opening = jax.nn.sigmoid(rhs + vec[layer, 3:4, columns])
            gate = tangent * opening
            gated[spot, columns] = gate.astype(BF)
            slopes[layer, spot, columns] = (opening * (1.0 - tangent * tangent)).astype(BF)
            other = slice(channels + part * WIDE, channels + (part + 1) * WIDE)
            slopes[layer, spot, other] = (gate * (1.0 - opening)).astype(BF)

    def residual(layer, first_row, rows_now):
        value = gated[first_row : first_row + rows_now]
        for part in range(2):
            columns = slice(part * WIDE, (part + 1) * WIDE)
            term = mm(value, wblock(layer, 5 * part + 4))
            if layer == 0:
                base = xe[first_row : first_row + rows_now, columns].astype(F32)
                x1[first_row : first_row + rows_now, columns] = (base + term) * HALF_ROOT
            else:
                base = x1[first_row : first_row + rows_now, columns]
                x1[first_row : first_row + rows_now, columns] = (base + term) * HALF_ROOT

    def skipped(layer, first_row, rows_now):
        value = gated[first_row : first_row + rows_now]
        spot = slice(first_row - HALO, first_row - HALO + rows_now)
        for part in range(2):
            columns = slice(part * WIDE, (part + 1) * WIDE)
            term = mm(value, wblock(layer, 5 * part + 14))
            if layer == 0:
                sk[spot, columns] = term
            else:
                sk[spot, columns] = sk[spot, columns] + term

    low, high = 16, grid_rows - 16

    def gate_grads(layer, first_row, rows_now):
        spot = slice(first_row, first_row + rows_now)
        bb[spot, 0:channels] = (bx[spot] * HALF_ROOT).astype(BF)
        branch = jnp.concatenate([wblock(layer, 5 * part + 4) for part in range(4)], axis=1)
        back = mm_nt(bb[spot], branch)
        keep = inside(first_row, rows_now)
        for side in range(2):
            columns = slice(side * channels, (side + 1) * channels)
            value = back * slopes[layer, spot, columns].astype(F32)
            middle = slice((2 + side) * channels, (3 + side) * channels)
            cat[spot, middle] = jnp.where(keep, value, 0.0).astype(BF)

    def windows_backward(layer):
        reach, limit = (low, high) if layer else (HALO, top)
        edge = 1 + low // 8
        bh[0:edge] = jnp.zeros((edge, 8, channels), F32)
        bh[1 + high // 8 :] = jnp.zeros((edge + 2, 8, channels), F32)
        for side in range(2):
            middle = slice((2 + side) * channels, (3 + side) * channels)
            value = cat[low:high, middle].astype(F32)
            bh[edge : 1 + high // 8] = in_eights(value)
            total = jnp.sum(value[HALO - low : top - low], axis=0, keepdims=True)
            sums[layer, 2 + side : 3 + side] = total
            for tap in (0, 2):
                start = 8 + reach - (tap - 1) * dil_ref[layer]
                columns = slice((2 * tap + side) * channels, (2 * tap + side + 1) * channels)
                cat[reach:limit, columns] = window(bh, start, limit - reach, channels).astype(BF)

    def frame_grads(layer, first_row, rows_now):
        spot = slice(first_row, first_row + rows_now)
        taps = jnp.concatenate(
            [wblock(layer, 5 * part + tap) for tap in range(3) for part in range(4)], axis=1
        )
        back = mm_nt(cat[spot], taps)
        if layer:
            here = x1[spot]
            row = lax.broadcasted_iota(jnp.int32, (rows_now, 1), 0) + first_row
            kept = jnp.where((row >= HALO) & (row < top), back, 0.0)
        else:
            here = xe[spot].astype(F32)
            kept = back
        sums[layer, 0:1] += jnp.sum(kept * here, axis=0, keepdims=True)
        sums[layer, 1:2] += jnp.sum(kept, axis=0, keepdims=True)
        bx[spot] = bx[spot] * HALF_ROOT + back * (1.0 + vec[layer, 0:1])

    def weight_grad(layer, part, i):
        if i < 4:
            tap = i if i < 3 else 1
            start = pl.multiple_of(tap * 1024 + part * WIDE, WIDE)
            lhs = sht[layer] if i < 3 else condt[...]
            return mm(lhs, cat[HALO:top, pl.ds(start, WIDE)])
        start = pl.multiple_of(part * WIDE, WIDE)
        return mm(gatt[layer], bb[HALO:top, pl.ds(start, WIDE)])

    core_sent = {}

    def give(layer, xx):
        part = 2 * (1 - c) + xx
        buffer, base = (gs, 0) if layer else (w, MAIN)
        for i in range(5):
            value = weight_grad(layer, part, i).astype(BF)
            buffer[base + 5 * xx + i] = value.reshape(nz, 2, rows, WIDE)
        core_sent[layer, xx] = remote(
            buffer.at[pl.ds(base + 5 * xx, 5)], red_in.at[layer, pl.ds(5 * xx, 5)], seq, sib
        )

    def keep(layer, xx):
        part = 2 * c + xx
        core_sent[layer, xx].wait_recv()
        for i in range(5):
            value = weight_grad(layer, part, i).reshape(nz, 2, rows, WIDE)
            spot = 5 * xx + i
            red_in[layer, spot] = (red_in[layer, spot].astype(F32) + value).astype(BF)

    ones, twos, zs, targets = {}, {}, {}, {}
    for layer in range(LAYERS):
        for k in range(nz):
            zd = lax.rem(z + k, nz)
            targets[layer, k] = (zd, y_first(zd, OUT_SPLIT[layer]))

    def red_one(layer, k):
        zd, a = targets[layer, k]
        b = 1 - a
        ones[layer, k] = []
        for j in range(2):
            xi, yi = a * (1 - x) + b * j, a * j + b * (1 - y)
            ones[layer, k].append(
                remote(
                    red_in.at[layer, pl.ds(5 * xi, 5), zd, yi],
                    one_in.at[layer, k, j],
                    a * seq + b * other_y, a * across + b * grp,
                )
            )

    def red_two(layer, k):
        zd, a = targets[layer, k]
        b = 1 - a
        you = a * y + b * x
        for j in range(2):
            ones[layer, k][j].wait_recv()
            xi, yi = a * x + b * j, a * j + b * y

            def body(i, carry, j=j, xi=xi, yi=yi):
                one_in[layer, k, j, i] = (
                    one_in[layer, k, j, i] + red_in[layer, 5 * xi + i, zd, yi]
                )
                return carry

            lax.fori_loop(0, 5, body, 0)
        twos[layer, k] = remote(
            one_in.at[layer, k, 1 - you], two_in.at[layer, k],
            a * other_y + b * seq, a * grp + b * across,
        )

    def red_three(layer, k):
        zd, a = targets[layer, k]
        you = a * y + (1 - a) * x
        twos[layer, k].wait_recv()

        def body(i, carry):
            two_in[layer, k, i] = two_in[layer, k, i] + one_in[layer, k, you, i]
            return carry

        lax.fori_loop(0, 5, body, 0)
        if k:
            zs[layer, k] = remote(two_in.at[layer, k], z_in.at[layer, k - 1], zd * 2 + y, grp)

    lasts = {}
    outs = []

    def local_out(src, dst):
        copy = pltpu.make_async_copy(src, dst, out_sem.at[len(outs)])
        copy.start()
        outs.append(copy)

    def red_four(layer):
        for k in range(1, nz):
            zs[layer, k].wait_recv()

        def body(i, carry):
            total = two_in[layer, 0, i].astype(F32)
            for k in range(1, nz):
                total = total + z_in[layer, k - 1, i].astype(F32)
            fin[layer, i] = total.astype(BF)
            return carry

        lax.fori_loop(0, 5, body, 0)
        src, dst = fin.at[layer], out_hbm.at[layer, mine]
        lasts[layer] = [remote(src, dst, seq, across), remote(src, dst, seq, sib)]
        if not layer and LAST_DIRECT:
            lasts[layer].append(remote(src, dst, seq, (1 - x) * 2 + 1 - c))
        local_out(src, dst)

    def red_five(layer):
        lasts[layer][0].wait_recv()
        ref = out_hbm.at[layer, theirs]
        lasts[layer].append(remote(ref, ref, seq, sib))

    ops = {}

    def op(*key):
        def keep_op(body):
            ops[key] = body
            return body

        return keep_op

    main_tiles = (0, 1, 2, 3, 4, 5, 6, 7, 15, 16)
    merges, crosses, film_sent, seen, hops = {}, {}, {}, {}, {}
    size_all, size_mid, size_own = grid_rows // 2, (high - low) // 2, own // 2
    embed = same_rows(embed_ref[...].astype(F32))

    for phase in (1, 2):

        @op("prep", phase)
        def _(phase=phase):
            ready([PER_LAYER * (phase - 1) + t for t in main_tiles], prep, BLOCK_OF)
            merges[phase] = merge_start(phase)

        @op("cross", phase)
        def _(phase=phase):
            crosses[phase] = merge_cross(phase, merges[phase])

        @op("end", phase)
        def _(phase=phase):
            merge_end(phase, crosses[phase])
            spread_z(phase)

    def quarter(j):
        return range(j * nz // 4, (j + 1) * nz // 4)

    for phase in (1, 2):
        for j in range(4):
            for name, body in (("first", first), ("second", second), ("third", third)):

                @op(name, phase, j)
                def _(phase=phase, j=j, body=body):
                    for k in quarter(j):
                        body(phase, k)

    parts = {"K": (0, KEY_VALUE), "R": (KEY_VALUE, FILM * LAYERS - KEY_VALUE)}
    for name, (begin, blocks) in parts.items():
        half = blocks // 2
        own_half_at = begin + c * half

        @op("fc" + name)
        def _(name=name, begin=begin, half=half):
            order = FILM_ORDER[:2] if name == "K" else FILM_ORDER[2:]
            for layer in range(LAYERS):
                ready([PER_LAYER * layer + t for t in order], fr, FILM_OF)
            film_sent[name, 0] = remote(
                fr.at[pl.ds(begin + (1 - c) * half, half)],
                fr_in.at[pl.ds(begin // 2, half)],
                seq, sib,
            )

        @op("fx" + name)
        def _(name=name, begin=begin, half=half, own_half_at=own_half_at):
            film_sent[name, 0].wait_recv()
            spot = slice(begin // 2, begin // 2 + half)
            fr_in[spot] = fr_in[spot] + fr[pl.ds(own_half_at, half)]
            ref = pl.ds(begin // 2, half)
            film_sent[name, 1] = remote(fr_in.at[ref], fx.at[ref], seq, across)

        @op("fl" + name)
        def _(name=name, begin=begin, half=half, own_half_at=own_half_at):
            film_sent[name, 1].wait_recv()
            spot = slice(begin // 2, begin // 2 + half)
            ref = pl.ds(own_half_at, half)
            ff[ref] = fr_in[spot] + fx[spot]
            film_sent[name, 2] = remote(ff.at[ref], ff.at[ref], seq, sib)

    for turn in range(4):

        @op("pr", turn)
        def _(turn=turn):
            total = prompt[...] if turn else None
            for i in range(4):
                prompt_copy(turn, i).wait()
                flag = (pairing_ref[0] == 4 * turn + i).astype(F32).astype(BF)
                part = slice((i % 2) * channels, (i % 2 + 1) * channels)
                term = slopes[i // 2, 0 : prompt.shape[0], part] * flag
                total = term if total is None else total + term
            prompt[...] = total
            if turn < 3:
                for i in range(4):
                    prompt_copy(turn + 1, i).start()

    def gathered():
        while gathering:
            gathering.pop().wait_send()

    @op("condt")
    def _():
        local_in[2].wait()
        condt[...] = jnp.transpose(cat[HALO:top, 1536:2048].astype(F32)).astype(BF)

    @op("hsK")
    def _():
        film_sent["K", 2].wait_recv()
        for h in range(HEADS):
            columns = slice((h % 4) * wide_head, (h % 4 + 1) * wide_head)
            pieces = [
                film_block(layer, place + h // 4).astype(F32)[:, columns]
                for place in (0, 2)
                for layer in range(LAYERS)
            ]
            kv_out[h] = jnp.concatenate(pieces, axis=1).astype(BF)
        kv_in[seq] = kv_out[head]
        kv_begin()

    @op("heK")
    def _():
        kv_finish()

    @op("att")
    def _():
        attention()

    @op("hsB")
    def _():
        film_sent["R", 2].wait_recv()
        vectors = []
        embed_here, mixed = pick(embed), pick(left[8:16])
        for layer in range(LAYERS):
            vectors.append(film_rows(layer, mixed, (4, 5))[layer : layer + 1])
            steps = film_rows(layer, embed_here, (10, 11, 12, 13))
            vectors += [steps[0:1, :channels], steps[0:1, channels:]]
        hop_start(0, pack(vectors))

    @op("heB")
    def _():
        total = hop_end(0)
        hops["pooled"] = [unpack(total, 3 * layer) for layer in range(LAYERS)]
        for layer in range(LAYERS):
            vec[layer, 2:3] = unpack(total, 3 * layer + 1)
            vec[layer, 3:4] = unpack(total, 3 * layer + 2)

    @op("hsC")
    def _():
        vectors = []
        for layer in range(LAYERS):
            pooled = hops["pooled"][layer]
            film = film_rows(layer, pick(same_rows(pooled)), (6, 7, 8, 9))
            vectors += [film[0:1, :channels], film[0:1, channels:]]
        hop_start(1, pack(vectors))

    @op("heC")
    def _():
        total = hop_end(1)
        for layer in range(LAYERS):
            vec[layer, 0:1] = unpack(total, 2 * layer)
            vec[layer, 1:2] = unpack(total, 2 * layer + 1)

    @op("win0")
    def _():
        local_in[1].wait()
        for copy in halos[:4]:
            copy.wait_recv()
        windows_forward(0)

    @op("win1")
    def _():
        local_in[3].wait()
        local_in[4].wait()
        for copy in halos[4:]:
            copy.wait_recv()
        bx[...] = bb[:, 0:channels].astype(F32)
        windows_forward(1)

    for layer in range(LAYERS):
        start, size = (low, size_mid) if layer else (0, size_all)
        for part, name in enumerate("ab"):
            first_row = start + part * size

            @op(f"gates{layer}{name}")
            def _(layer=layer, first_row=first_row, size=size, part=part):
                if not part:
                    arrived(1 + layer)
                gates(layer, first_row, size)

        @op(f"gatt{layer}")
        def _(layer=layer):
            gatt[layer] = jnp.transpose(gated[HALO:top].astype(F32)).astype(BF)

    @op("res0")
    def _():
        for part in range(2):
            residual(0, part * size_all, size_all)

    @op("skip0")
    def _():
        for part in range(2):
            skipped(0, HALO + part * size_own, size_own)

    @op("out1")
    def _():
        for part in range(2):
            residual(1, HALO + part * size_own, size_own)
            skipped(1, HALO + part * size_own, size_own)
        local_out(x1.at[pl.ds(HALO, own)], block_hbm.at[0])
        local_out(sk, skip_hbm.at[0])

    for layer in range(LAYERS):
        for part, name in enumerate("ab"):

            @op(f"gg{layer}{name}")
            def _(layer=layer, part=part):
                if layer and not part:
                    sums[...] = jnp.zeros_like(sums)
                gate_grads(layer, low + part * size_mid, size_mid)

            @op(f"fg{layer}{name}")
            def _(layer=layer, part=part):
                if layer:
                    frame_grads(1, low + part * size_mid, size_mid)
                else:
                    frame_grads(0, HALO + part * size_own, size_own)

        @op(f"winb{layer}")
        def _(layer=layer):
            windows_backward(layer)

        for xx in range(2):

            @op("give", layer, xx)
            def _(layer=layer, xx=xx):
                if not layer:
                    gathered()
                give(layer, xx)

            @op("keep", layer, xx)
            def _(layer=layer, xx=xx):
                keep(layer, xx)

        for j in range(4):
            for name, body in (("one", red_one), ("two", red_two), ("three", red_three)):

                @op(name, layer, j)
                def _(layer=layer, j=j, body=body):
                    for k in quarter(j):
                        body(layer, k)

        @op("four", layer)
        def _(layer=layer):
            red_four(layer)

        @op("five", layer)
        def _(layer=layer):
            red_five(layer)

    @op("hs3")
    def _():
        local_out(bx.at[pl.ds(HALO, own)], gframes_hbm.at[0])
        hop_start(2, pack([sums[l, i : i + 1] for l in range(LAYERS) for i in range(4)]))

    @op("he3")
    def _():
        total = hop_end(2)
        hops["sides"] = [[unpack(total, 4 * l + i) for i in range(4)] for l in range(LAYERS)]

    @op("hs4")
    def _():
        vectors = []
        for layer in range(LAYERS):
            dfilm = same_rows(jnp.concatenate(hops["sides"][layer][0:2], axis=1))
            vectors.append(film_back(layer, dfilm, (6, 7, 8, 9))[0:1])
        hop_start(3, pack(vectors))

    @op("he4")
    def _():
        total = hop_end(3)
        hops["dpooled"] = [unpack(total, layer) for layer in range(LAYERS)]


    @op("fb")
    def _():
        vectors = [
            film_back(l, same_rows(hops["dpooled"][l]), (4, 5))[0:1] for l in range(LAYERS)
        ]
        if copies_of > 1:
            hop_start(4, pack(vectors))
            total = hop_end(4)
            vectors = [unpack(total, layer) for layer in range(LAYERS)]
        dmixed = jnp.concatenate(vectors + [jnp.zeros((8 - LAYERS, channels), F32)], axis=0)
        dmixed = jnp.where(own_half, mm_low(dmixed, head_columns), 0.0)
        keys, values = head_weights()
        pr = prompt[...]
        dmean = mm_nt_low(mm_nt_low(dmixed, values), pr) * (1.0 / number)
        dprobs = jnp.concatenate(
            [jnp.broadcast_to(dmean[l : l + 1], (number, channels)) for l in range(LAYERS)], axis=0
        )
        value = probs[...]
        inner = jnp.sum(dprobs * value, axis=1, keepdims=True)
        dprobe = mm_low(value * (dprobs - inner) * 0.125, pr)
        dqueries = mm_low(dprobe, keys)
        half = lax.div(lax.broadcasted_iota(jnp.int32, (number, 128), 1), wide_head)
        dquery = jnp.where(half == 0, dqueries[0:number], dqueries[number : 2 * number])
        dq_in[grp] = dquery.astype(BF)
        small_out[...] = jnp.concatenate([dmixed, jnp.zeros((8, 128), F32)], axis=0).astype(BF)
        lefts = jnp.concatenate(
            [dprobe, left[0:2], left[8:10]]
            + [hops["pooled"][layer] for layer in range(LAYERS)]
            + [embed[0:1], jnp.zeros((128 - 2 * number - 7, channels), F32)],
            axis=0,
        )
        at_out[...] = jnp.transpose(lefts).astype(BF).reshape(n_seq, rows, 128)

    @op("hs5")
    def _():
        small_in[seq] = small_out[...]
        at_in[seq] = at_out[seq]
        small_begin()
        at_begin()

    def halves(one, two):
        wanted = lax.broadcasted_iota(jnp.int32, one.shape, 1) < wide_head
        return (
            jnp.where(wanted, one, pltpu.roll(two, wide_head, 1)),
            jnp.where(wanted, pltpu.roll(one, wide_head, 1), two),
        )

    def by_heads(ref):
        blocks = [[], []]
        for h in range(0, HEADS, 2):
            pair = halves(ref[h * copies_of].astype(F32), ref[(h + 1) * copies_of].astype(F32))
            for layer in range(LAYERS):
                blocks[layer].append(pair[layer])
        return [jnp.concatenate(blocks[layer], axis=1) for layer in range(LAYERS)]

    dq_sent = []

    @op("dq1")
    def _():
        for k in range(1, 4):
            ref = dq_in.at[grp]
            dq_sent.append(remote(ref, ref, seq, lax.rem(grp + k, 4)))

    @op("dq2")
    def _():
        for copy in dq_sent:
            copy.wait_recv()
        total = dq_in[0].astype(F32)
        for k in range(1, 4):
            total = total + dq_in[k].astype(F32)
        dq_out[...] = total
        dq_all[seq] = total
        dq_begin()

    @op("dq3")
    def _():
        dq_finish()
        total = by_heads(dq_all)
        for layer in range(LAYERS):
            dquery_ref[layer] = total[layer]

    @op("he5")
    def _():
        small_finish()
        at_finish()

        full = by_heads(small_in)
        pieces = []
        for layer in range(LAYERS):
            pieces += hops["sides"][layer]
            pieces += [hops["dpooled"][layer], full[layer][layer : layer + 1]]
        pieces.append(jnp.zeros((16 - len(pieces), channels), F32))
        wide[grp] = jnp.concatenate(pieces, axis=0).astype(BF)
        at = lax.broadcasted_iota(jnp.int32, (rows, 128), 1)
        thin = jnp.where(at >= 66, at_in[seq].astype(F32), 0.0)
        for h in range(0, HEADS, 2):
            one, two = at_in[h * copies_of].astype(F32), at_in[(h + 1) * copies_of].astype(F32)
            pair = jnp.where(at < wide_head, one, pltpu.roll(two, wide_head, 1))
            bundle[grp, :, h * wide_head : (h + 2) * wide_head] = pair.astype(BF)
            for k, value in ((h, one), (h + 1, two)):
                turned = pltpu.roll(value, wide_head + 2 * k, 1)
                thin = jnp.where(lax.div(at, 2) == k, turned, thin)
        bundle[grp, :, channels : channels + 128] = thin.astype(BF)

    bundles = []

    @op("bundle")
    def _():
        for k in range(1, 4):
            for ref in (bundle.at[grp], wide.at[grp]):
                bundles.append(remote(ref, ref, seq, lax.rem(grp + k, 4)))

    @op("low")
    def _():
        for copy in bundles:
            copy.wait_recv()
        mask = head_mask()
        at = lax.broadcasted_iota(jnp.int32, (8, channels), 0)
        probe = bundle[0, :, 0:channels].astype(F32)
        for k in range(1, 4):
            probe = probe + bundle[k, :, 0:channels].astype(F32)
        probe = probe.astype(BF)
        blank = jnp.zeros((number, channels), F32)
        column = lax.div(lax.broadcasted_iota(jnp.int32, (number, channels), 1), wide_head)
        for layer in range(LAYERS):
            side = []
            for h in range(HEADS):
                one = jnp.where(column == h, queries_ref[layer], 0.0)
                side += [blank, one] if layer else [one, blank]
            low_ref[layer, 0] = mm(probe, jnp.concatenate(side, axis=0).astype(BF)).astype(BF)
            total = None
            for k in range(4):
                right = wide[k].astype(F32)[6 * layer : 6 * layer + 6]
                dmixed = jnp.where(mask, right[5:6], 0.0)
                nothing = jnp.zeros((1, channels), F32)
                rows_of = []
                for h in range(HEADS):
                    one = dmixed[h : h + 1]
                    rows_of += [nothing, one] if layer else [one, nothing]
                value = jnp.concatenate(rows_of, axis=0)
                gap = jnp.zeros((48, channels), F32)
                rest = jnp.zeros((56, channels), F32)
                pieces = [jnp.concatenate([value, gap, jnp.zeros((64, channels), F32)], axis=0)]
                for i, row in ((4, 2), (0, 4), (1, 4), (2, 6), (3, 6)):
                    row = row + (layer if row < 6 else 0)
                    one = jnp.where(at == row, right[i : i + 1], 0.0)
                    pieces.append(
                        jnp.concatenate([jnp.zeros((64, channels), F32), one, rest], axis=0)
                    )
                term = mm(
                    bundle[k, :, channels : channels + 128],
                    jnp.concatenate(pieces, axis=1).astype(BF),
                )
                total = term if total is None else total + term
            for i in range(6):
                low_ref[layer, 1 + i] = total[:, i * channels : (i + 1) * channels].astype(BF)

    @op("end")
    def _():
        for copies in lasts.values():
            for copy in copies[1:]:
                copy.wait_recv()
        if LAST_DIRECT:
            lasts[0][0].wait_recv()
        for copy in outs:
            copy.wait()
        for copy in halos:
            copy.wait_send()
        gathered()
        for copy in waits:
            copy.wait_send()

    local_in[0].wait()
    for key in ORDER:
        ops[key if isinstance(key, tuple) else (key,)]()


def train_step(
    n_seq, owners, dilations, lengths, pairing, step_embed, queries, master, prompts,
    frames_in, cond_frames, grad_out, grad_skip,
):
    _, own, channels = frames_in.shape
    rows = master.shape[1]
    number = queries.shape[1]
    grid_rows = own + 2 * HALO
    nz = n_seq // 2
    v = pltpu.VMEM
    dma = pltpu.SemaphoreType.DMA
    frame_out = jax.ShapeDtypeStruct((1, own, channels), F32)
    film = FILM * LAYERS
    copies = 52 + 24 * nz
    return pl.pallas_call(
        functools.partial(step_kernel, n_seq),
        out_shape=(
            frame_out,
            frame_out,
            frame_out,
            jax.ShapeDtypeStruct((LAYERS, 4, 5, rows, WIDE), BF),
            jax.ShapeDtypeStruct((LAYERS, LOW_RANK, rows, channels), BF),
            jax.ShapeDtypeStruct((LAYERS, number, channels), F32),
        ),
        in_specs=[smem_spec()] * 4 + [vmem_spec()] * 2 + [any_spec()] * 6,
        out_specs=(any_spec(),) * 4 + (vmem_spec(),) * 2,
        scratch_shapes=[
            v((BLOCKS, nz, 2, rows, WIDE), BF),
            v((10, nz, 2, rows, WIDE), BF),
            v((BLOCKS, rows, WIDE), BF),
            v((BLOCKS // 2, rows, WIDE), BF),
            v((BLOCKS // 4, rows, WIDE), BF),
            v((film, rows, WIDE), BF),
            v((film // 2, rows, WIDE), BF),
            v((film // 2, rows, WIDE), BF),
            v((film, rows, WIDE), BF),
            v((LAYERS, 10, nz, 2, rows, WIDE), BF),
            v((LAYERS, nz, 2, 5, rows, WIDE), BF),
            v((LAYERS, nz, 5, rows, WIDE), BF),
            v((LAYERS, nz - 1, 5, rows, WIDE), BF),
            v((LAYERS, 5, rows, WIDE), BF),
            v((grid_rows, channels), BF),
            v((grid_rows, 6 * channels), BF),
            v((LAYERS, grid_rows, 2 * channels), BF),
            v((grid_rows, channels), BF),
            v((grid_rows, channels), F32),
            v((grid_rows // 8 + 4, 8, channels), F32),
            v((grid_rows, 2 * channels), BF),
            v((LAYERS, channels, own), BF),
            v((channels, own), BF),
            v((LAYERS, channels, own), BF),
            v((grid_rows, channels), F32),
            v((own, channels), F32),
            v(master.shape, F32),
            v(prompts.shape[1:], BF),
            v((LAYERS * number, prompts.shape[1]), F32),
            v((16, channels), F32),
            v((LAYERS, 8, channels), F32),
            v((LAYERS, 8, channels), F32),
            v((4, rows, channels + 128), BF),
            v((4, 16, channels), BF),
            v((4, number, 128), BF),
            v((HEADS, rows, WIDE), BF),
            v((n_seq, rows, WIDE), BF),
            v((n_seq, rows, 128), BF),
            v((n_seq, rows, 128), BF),
            v((16, 128), BF),
            v((n_seq, 16, 128), BF),
            v((number, 128), F32),
            v((n_seq, number, 128), F32),
            v((sum(HOP_ROWS), 128), F32),
            v((n_seq, sum(HOP_ROWS), 128), F32),
            dma((5,)),
            dma((4,)),
            dma((8,)),
            dma((8,)),
            dma((8,)),
            dma((copies,)),
            dma((copies,)),
            dma((len(HOP_ROWS), n_seq)),
            dma((len(HOP_ROWS), n_seq)),
            dma((4, n_seq)),
            dma((4, n_seq)),
        ],
        compiler_params=pltpu.CompilerParams(
            collective_id=0, has_side_effects=True, vmem_limit_bytes=MEM
        ),
        name="train_step",
    )(
        owners, dilations, lengths, pairing, step_embed, queries, master, prompts,
        frames_in, cond_frames, grad_out, grad_skip,
    )


def adam_update(weight, moment_one, moment_two, gradient, step_rate):
    moment_one = BETA_ONE * moment_one + (1.0 - BETA_ONE) * gradient
    moment_two = BETA_TWO * moment_two + (1.0 - BETA_TWO) * gradient * gradient
    normal = (
        moment_one
        * (1.0 / (1.0 - BETA_ONE**STEP))
        / (jnp.sqrt(moment_two * (1.0 / (1.0 - BETA_TWO**STEP))) + EPSILON)
    )
    return (moment_one, moment_two, weight - step_rate * (normal + WEIGHT_DECAY * weight))


def update_kernel(
    owners_ref, master_hbm, first_hbm, second_hbm, grad_hbm, low_hbm,
    queries_hbm, qfirst_hbm, qsecond_hbm, dq_hbm, block_in, skip_in, gframes_in,
    nfirst_hbm, nsecond_hbm, nmaster_hbm, ncopy_hbm, nqfirst_hbm, nqsecond_hbm, nqueries_hbm,
    block_out, skip_out, gframes_out,
    master, first, second, grad, low, three, one, two, copied, frames, asked,
    tile_of, grad_sem, in_sem, out_sem, frame_sem, asked_sem,
):
    grp = lax.axis_index("grp")
    grads_in = [
        pltpu.make_async_copy(a, b, grad_sem.at[i])
        for i, (a, b) in enumerate(((grad_hbm, grad), (low_hbm, low)))
    ]
    spots = [pl.ds(start, count) for start, count in CHUNKS]
    slots_in = [
        [
            pltpu.make_async_copy(a.at[spot], b.at[spot], in_sem.at[i, j])
            for j, (a, b) in enumerate(
                ((master_hbm, master), (first_hbm, first), (second_hbm, second))
            )
        ]
        for i, spot in enumerate(spots)
    ]
    frames_in = [
        pltpu.make_async_copy(a, frames.at[i], frame_sem.at[0, i])
        for i, a in enumerate((block_in, skip_in, gframes_in))
    ]
    asked_in = [
        pltpu.make_async_copy(a, asked.at[i], asked_sem.at[i])
        for i, a in enumerate((queries_hbm, qfirst_hbm, qsecond_hbm, dq_hbm))
    ]
    for copy in grads_in + slots_in[0] + asked_in + frames_in[:1] + slots_in[1] + frames_in[1:]:
        copy.start()
    for copies in slots_in[2:]:
        for copy in copies:
            copy.start()

    for slot in range(CAP + 1):
        tile_of[slot] = TILES
    count = jnp.int32(0)
    for tile in range(TILES):
        own = owners_ref[tile] == grp

        @pl.when(own)
        def _(count=count, tile=tile):
            tile_of[jnp.minimum(count, CAP)] = tile

        count = count + own.astype(jnp.int32)
    outs = []

    def send(a, b, sem):
        copy = pltpu.make_async_copy(a, b, sem)
        copy.start()
        outs.append(copy)

    def pass_frames(i, target):
        frames_in[i].wait()
        send(frames.at[i], target, frame_sem.at[1, i])

    def slot_update(slot, carry):
        tile = tile_of[slot]
        used = (tile < TILES).astype(jnp.int32)
        tile = jnp.minimum(tile, TILES - 1)
        layer, kind = lax.div(tile, PER_LAYER), lax.rem(tile, PER_LAYER)
        plain = kind < 8
        pair = jnp.where(plain, lax.rem(kind, 2), (kind == 16).astype(jnp.int32))
        tap = jnp.where(plain, lax.div(kind, 2), 4)
        full = jnp.concatenate([grad[layer, 2 * pair, tap], grad[layer, 2 * pair + 1, tap]], axis=1)
        place = jnp.where(kind < 10, kind - 3, kind - 10)
        thin = low[layer, jnp.clip(place, 0, LOW_RANK - 1)]
        is_thin = ((kind >= 8) & (kind <= 14)).astype(jnp.int32)
        gradient = jnp.where(
            jnp.broadcast_to(is_thin, full.shape) > 0, thin.astype(F32), full.astype(F32)
        )
        old, old_first, old_second = master[slot], first[slot], second[slot]
        new_first, new_second, new = adam_update(old, old_first, old_second, gradient, LEARN_RATE)
        keep = jnp.broadcast_to(used, old.shape) > 0
        new = jnp.where(keep, new, old)
        one[slot] = jnp.where(keep, new_first, old_first)
        two[slot] = jnp.where(keep, new_second, old_second)
        three[slot] = new
        copied[slot] = new.astype(BF)
        return carry

    for copy in grads_in:
        copy.wait()
    passed = (block_out, skip_out, gframes_out)
    for i, (start, number) in enumerate(CHUNKS):
        for copy in slots_in[i]:
            copy.wait()
        lax.fori_loop(start, start + number, slot_update, 0)
        for j, (a, b) in enumerate(
            ((one, nfirst_hbm), (two, nsecond_hbm), (three, nmaster_hbm), (copied, ncopy_hbm))
        ):
            send(a.at[spots[i]], b.at[spots[i]], out_sem.at[i, j])
        if i < len(passed):
            pass_frames(i, passed[i])
        if i == 1:
            for copy in asked_in:
                copy.wait()
            news = adam_update(asked[0], asked[1], asked[2], asked[3], QUERY_RATE)
            for j, (value, target) in enumerate(
                zip(news, (nqfirst_hbm, nqsecond_hbm, nqueries_hbm))
            ):
                asked[4 + j] = value
                send(asked.at[4 + j], target, asked_sem.at[4 + j])
    for copy in outs:
        copy.wait()


CHUNKS = ((0, 2), (2, 3), (5, 4), (9, 4))


def update(owners, master, first, second, grads, low, queries, qfirst, qsecond, dq, *frames):
    any_ = any_spec()
    query = jax.ShapeDtypeStruct(queries.shape, F32)
    full = jax.ShapeDtypeStruct(master.shape, F32)
    passed = jax.ShapeDtypeStruct(frames[0].shape, F32)
    v = pltpu.VMEM
    slots = v(master.shape, F32)
    return pl.pallas_call(
        update_kernel,
        out_shape=(full, full, full, jax.ShapeDtypeStruct(master.shape, BF), query, query, query)
        + (passed,) * 3,
        in_specs=[smem_spec()] + [any_] * 12,
        out_specs=(any_,) * 10,
        scratch_shapes=[
            slots, slots, slots, v(grads.shape, BF), v(low.shape, BF),
            slots, slots, slots, v(master.shape, BF), v((3,) + passed.shape, F32),
            v((7,) + queries.shape, F32),
            pltpu.SMEM((CAP + 1,), jnp.int32),
            pltpu.SemaphoreType.DMA((2,)),
            pltpu.SemaphoreType.DMA((len(CHUNKS), 3)),
            pltpu.SemaphoreType.DMA((len(CHUNKS), 4)),
            pltpu.SemaphoreType.DMA((2, 3)),
            pltpu.SemaphoreType.DMA((7,)),
        ],
        compiler_params=pltpu.CompilerParams(vmem_limit_bytes=MEM),
        name="update",
    )(owners, master, first, second, grads, low, queries, qfirst, qsecond, dq, *frames)


def on_device(
    n_seq,
    frames_in,
    cond_frames,
    step_embed,
    prompts,
    prompt_lengths,
    pairing,
    dilations,
    owners,
    master,
    first_moment,
    second_moment,
    queries,
    query_first,
    query_second,
    grad_out,
    grad_skip,
):
    block, skip, gframes, own_grads, low, dq = train_step(
        n_seq, owners, dilations, prompt_lengths, pairing, step_embed, queries, master, prompts,
        frames_in, cond_frames, grad_out, grad_skip,
    )
    (
        new_first, new_second, new_master, new_copy, nqf, nqs, nq,
        block_out, skip_out, grad_frames,
    ) = update(
        owners, master, first_moment, second_moment, own_grads, low,
        queries, query_first, query_second, dq, block, skip, gframes,
    )
    return (
        new_first, new_second, new_master, new_copy, nqf, nqs, nq,
        block_out, skip_out, grad_frames,
    )


def solution(mesh):
    shard = P("grp", "seq", None)
    placed = (
        shard, shard, P("grp", None), P(), P(), P("grp"), P(), P(),
        shard, shard, shard, P(), P(), P(), shard, shard,
    )
    return jax.shard_map(
        functools.partial(on_device, mesh.shape["seq"]),
        mesh=mesh,
        in_specs=placed,
        out_specs=(shard, shard, shard, shard, P(), P(), P(), shard, shard, shard),
        check_vma=False,
    )
```

```python
import functools

import jax
import jax.numpy as jnp
from jax import lax
from jax.experimental import pallas as pl
from jax.experimental.pallas import tpu as pltpu
from jax.sharding import PartitionSpec as P

HEADS = 8
LAYERS = 2
DMAX = 8
CAP = 13
STEP = 10
PER_LAYER = 17
TILES = PER_LAYER * LAYERS

BETA_ONE = 0.9
BETA_TWO = 0.999
EPSILON = 1e-08
WEIGHT_DECAY = 0.01
LEARN_RATE = 0.02
QUERY_RATE = 0.4
HALF_ROOT = 0.7071067811865476
NEGATIVE = -1e30

BF = jnp.bfloat16
F32 = jnp.float32
HALO = 32
WIDE = 256
MAIN = 20
BLOCKS = MAIN * LAYERS
PHASES = (None, (0, MAIN), (MAIN, MAIN))
FILM_ORDER = (10, 11, 12, 13, 14, 8, 9)
FILM = 2 * len(FILM_ORDER)
LOW_RANK = len(FILM_ORDER)
KEY_VALUE = 4 * LAYERS
HOP_ROWS = (24, 16, 32, 8, 8)
IN_SPLIT = (2, 2, 2)
OUT_SPLIT = (2, 2)
EACH = 5
LAST_DIRECT = True
ORDER = (
    ("prep", 1), "fcK", "fcR", ("pr", 0), ("prep", 2), ("cross", 1), "fxK", ("pr", 1),
    ("cross", 2), "fxR", ("end", 1), ("first", 1, 0), "flK", ("pr", 2), "hsK", ("end", 2),
    ("first", 2, 0), ("first", 1, 2), ("first", 1, 1), ("pr", 3), ("first", 1, 3), "flR",
    ("second", 1, 2), ("second", 1, 0), "heK", ("second", 2, 0), "att", ("second", 1, 1), "hsB",
    ("second", 1, 3), ("first", 2, 2), ("first", 2, 3), ("third", 1, 3), ("third", 2, 0), "heB",
    ("third", 1, 2), "hsC", ("third", 1, 1), ("third", 1, 0), ("first", 2, 1), ("second", 2, 2),
    "heC", ("second", 2, 3), "win0", "condt", ("second", 2, 1), "gates0a", "gates0b",
    ("third", 2, 2), "res0", ("third", 2, 3), ("third", 2, 1), "gatt0", "skip0", "win1",
    "gates1a", "gates1b", "gatt1", "gg1a", "gg1b", "winb1", ("give", 1, 0), ("give", 1, 1),
    "fg1a", ("keep", 1, 0), ("one", 1, 3), ("one", 1, 1), ("one", 1, 0), ("one", 1, 2), "fg1b",
    ("keep", 1, 1), ("onb", 1, 3), "gg0a", ("onb", 1, 1), "gg0b", "winb0", "out1", "fg0b",
    ("onb", 1, 0), ("onb", 1, 2), ("give", 0, 0), "fg0a", "hs3", ("two", 1, 3), ("give", 0, 1),
    ("two", 1, 1), ("keep", 0, 0), ("one", 0, 2), ("one", 0, 0), ("one", 0, 1), ("one", 0, 3),
    ("two", 1, 2), ("two", 1, 0), ("keep", 0, 1), "he3", ("onb", 0, 2), ("onb", 0, 0), "hs4",
    ("three", 1, 1), ("onb", 0, 1), ("three", 1, 2), ("onb", 0, 3), ("three", 1, 3),
    ("two", 0, 2), "he4", "fb", "dq1", "hs5", ("two", 0, 0), ("three", 1, 0), ("two", 0, 1),
    ("two", 0, 3), ("three", 0, 2), ("three", 0, 0), ("three", 0, 1), ("three", 0, 3), "he5",
    "bundle", ("four", 1), "dq2", ("four", 0), ("five", 1), "dq3", "low", "end",
)

MEM = 64 * 1024 * 1024 - 256 * 1024
MESH = pl.DeviceIdType.MESH


def block_table():
    table = {}
    for layer in range(LAYERS):
        base = PER_LAYER * layer
        start = MAIN * layer
        for part in range(4):
            for tap in range(4):
                table[base + 2 * tap + part // 2, part % 2] = start + 5 * part + tap
            table[base + 15 + part // 2, part % 2] = start + 5 * part + 4
    return table


BLOCK_OF = block_table()
FILM_OF = {
    (PER_LAYER * layer + tile, side): (
        4 * layer + 2 * place + side
        if place < 2
        else KEY_VALUE + (FILM - 4) * layer + 2 * (place - 2) + side
    )
    for layer in range(LAYERS)
    for place, tile in enumerate(FILM_ORDER)
    for side in range(2)
}


def mm(a, b):
    return lax.dot_general(a, b, (((1,), (0,)), ((), ())), preferred_element_type=F32)


def mm_nt(a, b):
    return lax.dot_general(a, b, (((1,), (1,)), ((), ())), preferred_element_type=F32)


def mm_nt_fine(a, b):
    high = a.astype(BF)
    return mm_nt(high, b) + mm_nt((a - high.astype(F32)).astype(BF), b)


def mm_low(a, b):
    return mm(a.astype(BF), b)


def mm_nt_low(a, b):
    return mm_nt(a.astype(BF), b)


def mm_nt_pairs(a, blocks):
    total = None
    for place, block in enumerate(blocks):
        term = mm_nt_fine(a[:, place * WIDE : (place + 1) * WIDE], block)
        total = term if total is None else total + term
    return total


def window(ref, start, count, width):
    group, rest = lax.div(start, 8), lax.rem(start, 8)
    groups = ref[pl.ds(group, count // 8 + 1), :, 0:width]
    turned = pltpu.roll(groups, lax.rem(8 - rest, 8), 1)
    row = lax.broadcasted_iota(jnp.int32, (1, 8, 1), 1)
    return jnp.where(row < 8 - rest, turned[:-1], turned[1:]).reshape(count, width)


def in_eights(value):
    return value.reshape(value.shape[0] // 8, 8, value.shape[1])


def place_of(n_seq):
    seq, grp = lax.axis_index("seq"), lax.axis_index("grp")
    z, y = lax.div(seq, 2), lax.rem(seq, 2)
    x, c = lax.div(grp, 2), lax.rem(grp, 2)
    return seq, grp, z, y, x, c


def greet(n_seq, seq, grp, groups):
    barrier = pltpu.get_barrier_semaphore()

    def one(k, carry):
        pl.semaphore_signal(
            barrier, inc=1, device_id={"seq": lax.rem(seq + k, n_seq), "grp": grp}, device_id_type=MESH
        )
        return carry

    lax.fori_loop(1, n_seq, one, 0)
    for k in range(1, groups):
        pl.semaphore_signal(
            barrier, inc=1, device_id={"seq": seq, "grp": lax.rem(grp + k, groups)}, device_id_type=MESH
        )
    pl.semaphore_wait(barrier, n_seq - 1 + groups - 1)


def any_spec():
    return pl.BlockSpec(memory_space=pl.ANY)


def vmem_spec():
    return pl.BlockSpec(memory_space=pltpu.VMEM)


def smem_spec():
    return pl.BlockSpec(memory_space=pltpu.SMEM)


def head_mask():
    row = lax.broadcasted_iota(jnp.int32, (HEADS, 512), 0)
    column = lax.broadcasted_iota(jnp.int32, (HEADS, 512), 1)
    return lax.div(column, 512 // HEADS) == row


def block_diagonal(rows):
    column = lax.div(lax.broadcasted_iota(jnp.int32, rows.shape, 1), 512 // HEADS)
    return jnp.concatenate([jnp.where(column == h, rows, 0.0) for h in range(HEADS)], axis=0)


def same_rows(row):
    return jnp.broadcast_to(row, (8, row.shape[1]))


def pack(vectors):
    pieces = [v[:, 128 * i : 128 * (i + 1)] for v in vectors for i in range(v.shape[1] // 128)]
    spare = -len(pieces) % 8
    if spare:
        pieces.append(jnp.zeros((spare, 128), pieces[0].dtype))
    return jnp.concatenate(pieces, axis=0)


def unpack(rows, place, pieces=4):
    return jnp.concatenate(
        [rows[pieces * place + i : pieces * place + i + 1] for i in range(pieces)], axis=1
    )


def step_kernel(
    n_seq, owners_ref, dil_ref, lengths_ref, pairing_ref, embed_ref, queries_ref, master_hbm,
    prompts_hbm, frames_hbm, cond_hbm, gout_hbm, gskip_hbm,
    block_hbm, skip_hbm, gframes_hbm, out_hbm, low_ref, dquery_ref,
    w, gs, prep, core_in, x_in, fr, fr_in, fx, ff, red_in, one_in, two_in, z_in, ze_in, xe_in, fin,
    xe, cat, slopes, gated, x1, bh, bb, sht, condt, gatt, bx, sk,
    master, prompt, probs, left, vec, sums, bundle, wide, dq_in,
    kv_out, kv_in, at_out, at_in, small_out, small_in, dq_out, dq_all, hop_src, hop_in,
    in_sem, prompt_sem, out_sem, hsend, hrecv, send, recv, hop_send, hop_recv, each_send, each_recv,
):
    seq, grp, z, y, x, c = place_of(n_seq)
    nz = n_seq // 2
    rows = prep.shape[1]
    own = frames_hbm.shape[1]
    grid_rows = own + 2 * HALO
    top = HALO + own
    channels = 512
    number = queries_ref.shape[1]
    sib, across, other_y = x * 2 + 1 - c, (1 - x) * 2 + c, z * 2 + 1 - y
    mine, theirs = 2 * c + x, 2 * c + 1 - x

    local_in = [
        pltpu.make_async_copy(a, b, in_sem.at[i])
        for i, (a, b) in enumerate(
            (
                (master_hbm, master),
                (frames_hbm.at[0], xe.at[pl.ds(HALO, own)]),
                (cond_hbm.at[0], cat.at[pl.ds(HALO, own), pl.ds(1536, channels)]),
                (gout_hbm.at[0], bb.at[pl.ds(HALO, own), pl.ds(0, channels)]),
                (gskip_hbm.at[0], bb.at[pl.ds(HALO, own), pl.ds(channels, channels)]),
            )
        )
    ]
    for copy in local_in:
        copy.start()

    def prompt_copy(turn, i):
        rows_now, columns = pl.ds(0, prompt.shape[0]), pl.ds((i % 2) * channels, channels)
        return pltpu.make_async_copy(
            prompts_hbm.at[4 * turn + i], slopes.at[i // 2, rows_now, columns], prompt_sem.at[i]
        )

    for i in range(4):
        prompt_copy(0, i).start()

    greet(n_seq, seq, grp, 4)

    waits = []
    used = [0]

    def remote(src, dst, to_seq, to_grp, sent=None, start=True):
        place = used[0]
        used[0] += 1
        copy = pltpu.make_async_remote_copy(
            src_ref=src,
            dst_ref=dst,
            send_sem=send.at[place],
            recv_sem=recv.at[place],
            device_id={"seq": to_seq, "grp": to_grp},
            device_id_type=MESH,
        )
        if start:
            copy.start()
        (waits if sent is None else sent).append(copy)
        return copy

    after, before = lax.rem(seq + 1, n_seq), lax.rem(seq + n_seq - 1, n_seq)
    halos = []
    for ref, buffer, column in (
        (frames_hbm, xe, 0),
        (cond_hbm, cat, 1536),
        (gout_hbm, bb, 0),
        (gskip_hbm, bb, channels),
    ):
        for start, at, target in ((own - HALO, 0, after), (0, top, before)):
            place = len(halos)
            copy = pltpu.make_async_remote_copy(
                src_ref=ref.at[0, pl.ds(start, HALO)],
                dst_ref=buffer.at[pl.ds(at, HALO), pl.ds(column, channels)],
                send_sem=hsend.at[place],
                recv_sem=hrecv.at[place],
                device_id={"seq": target, "grp": grp},
                device_id_type=MESH,
            )
            copy.start()
            halos.append(copy)

    slots, flags = [], []
    count = jnp.int32(0)
    for tile in range(TILES):
        flag = (owners_ref[tile] == grp).astype(jnp.int32)
        slots.append(jnp.minimum(count, CAP - 1))
        flags.append(flag.astype(F32))
        count = count + flag

    def rounded(tile):
        return (master[slots[tile]] * flags[tile]).astype(BF)

    def ready(tiles, buffer, table):
        for tile in tiles:
            value = rounded(tile)
            buffer[table[tile, 0]] = value[:, :WIDE]
            buffer[table[tile, 1]] = value[:, WIDE:]

    def merge_start(phase):
        base, blocks = PHASES[phase]
        each = blocks // 4
        return remote(
            prep.at[pl.ds(base + 2 * (1 - c) * each, 2 * each)],
            core_in.at[pl.ds(base // 2, 2 * each)],
            seq, sib,
        )

    def merge_cross(phase, copy):
        base, blocks = PHASES[phase]
        each = blocks // 4
        copy.wait_recv()

        def add(i, carry):
            place = base // 2 + i
            core_in[place] = core_in[place] + prep[base + 2 * c * each + i]
            return carry

        lax.fori_loop(0, 2 * each, add, 0)
        return remote(
            core_in.at[pl.ds(base // 2 + (1 - x) * each, each)],
            x_in.at[pl.ds(base // 4, each)],
            seq, across,
        )

    def view(phase, quarter, zz, yy):
        base, blocks = PHASES[phase]
        return w.at[pl.ds(base + quarter * (blocks // 4), EACH), zz, yy]

    def side_view(phase, quarter, *place):
        base, blocks = PHASES[phase]
        spot = pl.ds(base + quarter * (blocks // 4) + EACH, 5 - EACH)
        return w.at[(spot,) + place]

    gathering, legs = [], {}

    def spread(ref, to_seq, to_grp):
        return remote(ref, ref, to_seq, to_grp, gathering)

    def merge_end(phase, copy):
        base, blocks = PHASES[phase]
        each = blocks // 4
        copy.wait_recv()

        def settle(i, carry):
            w[base + mine * each + i, z, y] = (
                core_in[base // 2 + x * each + i] + x_in[base // 4 + i]
            )
            return carry

        lax.fori_loop(0, each, settle, 0)

    def y_first(zz, quarters):
        return 1 - jnp.minimum(lax.div(4 * zz, quarters * nz), 1)

    def spread_z(phase):
        ref = view(phase, mine, z, y)
        for k in range(1, nz):
            legs[phase, k] = spread(ref, lax.rem(z + k, nz) * 2 + y, grp)

    core_legs = {phase: [] for phase in (1, 2)}

    def first(phase, k):
        zs = lax.rem(z - k + nz, nz)
        a = y_first(zs, IN_SPLIT[phase])
        b = 1 - a
        if k:
            legs[phase, k].wait_recv()
        ref = view(phase, mine, zs, y)
        one = spread(ref, a * other_y + b * seq, a * grp + b * across)
        two = spread(ref, a * seq + b * other_y, a * across + b * grp)
        core_legs[phase].append(spread(ref, seq, sib))
        legs[phase, k] = (zs, a, one, two)

    def second(phase, k):
        zs, a, one, two = legs[phase, k]
        b = 1 - a
        one.wait_recv()
        ref = view(phase, a * mine + b * theirs, zs, a * (1 - y) + b * y)
        last = spread(ref, a * seq + b * other_y, a * across + b * grp)
        core_legs[phase].append(spread(ref, seq, sib))
        legs[phase, k] = (zs, a, two, last)

    def third(phase, k):
        zs, a, two, last = legs[phase, k]
        b = 1 - a
        two.wait_recv()
        ref = view(phase, a * theirs + b * mine, zs, a * y + b * (1 - y))
        core_legs[phase].append(spread(ref, seq, sib))
        last.wait_recv()
        core_legs[phase].append(spread(view(phase, theirs, zs, 1 - y), seq, sib))

    side_legs = {}

    def side_first(phase):
        ref = side_view(phase, mine, z, y)
        side_legs[phase] = [
            spread(ref, other_y, grp), spread(ref, seq, across), spread(ref, other_y, across)
        ]

    def side_second(phase):
        for copy in side_legs[phase]:
            copy.wait_recv()
        for k in range(1, nz):
            for q in (mine, theirs):
                ref = side_view(phase, q, z)
                side_legs[phase, k, q is mine] = spread(ref, lax.rem(z + k, nz) * 2 + y, grp)
        for q in (mine, theirs):
            core_legs[phase].append(spread(side_view(phase, q, z), seq, sib))

    def side_third(phase):
        for k in range(1, nz):
            for q in (mine, theirs):
                side_legs[phase, k, q is mine].wait_recv()
                ref = side_view(phase, q, lax.rem(z - k + nz, nz))
                core_legs[phase].append(spread(ref, seq, sib))

    def arrived(phase):
        for copy in core_legs[phase]:
            copy.wait_recv()

    def hop_refs(j):
        start = sum(HOP_ROWS[:j])
        spot = pl.ds(start, HOP_ROWS[j])
        return hop_src.at[spot], hop_in.at[seq, spot], hop_in.at[:, spot]

    def hop_copy(j, k):
        src, dst, _ = hop_refs(j)
        return pltpu.make_async_remote_copy(
            src_ref=src,
            dst_ref=dst,
            send_sem=hop_send.at[j, k],
            recv_sem=hop_recv.at[j, k],
            device_id={"seq": lax.rem(seq + k, n_seq), "grp": grp},
            device_id_type=MESH,
        )

    def hop_start(j, value):
        src, dst, _ = hop_refs(j)
        value = value.astype(src.dtype)
        src[...] = value
        dst[...] = value

        def one(k, carry):
            hop_copy(j, k).start()
            return carry

        lax.fori_loop(1, n_seq, one, 0)

    def hop_end(j):
        def one(k, carry):
            hop_copy(j, k).wait()
            return carry

        lax.fori_loop(1, n_seq, one, 0)
        _, _, whole = hop_refs(j)

        def add(i, total):
            return total + whole[i].astype(F32)

        return lax.fori_loop(0, n_seq, add, jnp.zeros((HOP_ROWS[j], 128), F32))

    position = lax.broadcasted_iota(jnp.int32, (channels, rows), 0)
    column = lax.broadcasted_iota(jnp.int32, (channels, rows), 1)
    chosen = jnp.where(position == column + seq * rows, 1.0, 0.0).astype(BF)

    def pick(v):
        return mm_low(v, chosen)

    def film_block(layer, place):
        if place < 4:
            return ff[4 * layer + place]
        return ff[KEY_VALUE + (FILM - 4) * layer + place - 4]

    def film_rows(layer, v, places):
        return jnp.concatenate([mm_low(v, film_block(layer, i)) for i in places], axis=1)

    def film_back(layer, v, places):
        total = None
        for i, place in enumerate(places):
            term = mm_nt_low(v[:, i * WIDE : (i + 1) * WIDE], film_block(layer, place))
            total = term if total is None else total + term
        return mm_nt_low(total, chosen)

    wide_head = channels // HEADS
    copies_of = n_seq // HEADS
    head = lax.div(seq, copies_of)
    lane = lax.broadcasted_iota(jnp.int32, (channels, 128), 1)
    at_row = lax.broadcasted_iota(jnp.int32, (channels, 128), 0)
    of_head = at_row == head * wide_head + lax.rem(lane, wide_head)
    head_columns = jnp.where(of_head, 1.0, 0.0).astype(BF)
    own_half = lax.div(lax.broadcasted_iota(jnp.int32, (8, 128), 1), wide_head) == (
        lax.broadcasted_iota(jnp.int32, (8, 128), 0)
    )

    def exchange(index, source, target):
        def copy(k):
            dest = lax.rem(seq + k, n_seq)
            return pltpu.make_async_remote_copy(
                src_ref=source(dest),
                dst_ref=target,
                send_sem=each_send.at[index, k],
                recv_sem=each_recv.at[index, k],
                device_id={"seq": dest, "grp": grp},
                device_id_type=MESH,
            )

        def begin():
            def one(k, carry):
                copy(k).start()
                return carry

            lax.fori_loop(1, n_seq, one, 0)

        def finish():
            def one(k, carry):
                copy(k).wait()
                return carry

            lax.fori_loop(1, n_seq, one, 0)

        return begin, finish

    kv_begin, kv_finish = exchange(
        0, lambda dest: kv_out.at[lax.div(dest, copies_of)], kv_in.at[seq]
    )
    at_begin, at_finish = exchange(1, lambda dest: at_out.at[dest], at_in.at[seq])
    dq_begin, dq_finish = exchange(3, lambda dest: dq_out, dq_all.at[seq])
    small_begin, small_finish = exchange(2, lambda dest: small_out, small_in.at[seq])

    def head_weights():
        value = kv_in[...].reshape(channels, WIDE)
        return value[:, 0:128], value[:, 128:256]

    def attention():
        keys, values = head_weights()
        pieces = []
        for layer in range(LAYERS):
            high = queries_ref[layer].astype(BF)
            rest = (queries_ref[layer] - high.astype(F32)).astype(BF)
            both = mm(high, head_columns) + mm(rest, head_columns)
            half = lax.div(lax.broadcasted_iota(jnp.int32, both.shape, 1), wide_head)
            pieces.append(jnp.where(half == layer, both, 0.0))
        probe = mm_nt_fine(jnp.concatenate(pieces, axis=0), keys)
        pr = prompt[...]
        scores = mm_nt_fine(probe, pr) * 0.125
        live = lax.broadcasted_iota(jnp.int32, scores.shape, 1) < lengths_ref[pairing_ref[0]]
        scores = jnp.where(live, scores, NEGATIVE)
        weight = jnp.exp(scores - jnp.max(scores, axis=1, keepdims=True))
        value = weight / jnp.sum(weight, axis=1, keepdims=True)
        probs[...] = value
        mean = jnp.concatenate(
            [
                jnp.mean(value[l * number : (l + 1) * number], axis=0, keepdims=True)
                for l in range(LAYERS)
            ]
            + [jnp.zeros((8 - LAYERS, value.shape[1]), F32)],
            axis=0,
        )
        seen = mm_low(mean, pr)
        mixed = jnp.where(own_half, mm_low(seen, values), 0.0)
        left[0:8] = seen
        left[8:16] = mm_nt_low(mixed, head_columns)

    def wblock(layer, place):
        return w[MAIN * layer + place].reshape(channels, WIDE)

    def inside(low, count):
        row = lax.broadcasted_iota(jnp.int32, (count, 1), 0) + (low - HALO) + seq * own
        return (row >= 0) & (row < n_seq * own)

    def windows_forward(layer):
        low = 16 * layer
        high = grid_rows - low
        scale, shift = 1.0 + vec[layer, 0:1], vec[layer, 1:2]
        here = xe[...].astype(F32) if layer == 0 else x1[...]
        shifted = (here * scale + shift).astype(BF).astype(F32)
        shifted = jnp.where(inside(0, grid_rows), shifted, 0.0)
        groups = grid_rows // 8
        bh[0] = jnp.zeros((8, channels), F32)
        bh[1 : 1 + groups] = in_eights(shifted)
        bh[1 + groups :] = jnp.zeros((3, 8, channels), F32)
        sht[layer] = jnp.transpose(shifted[HALO:top]).astype(BF)
        cat[low:high, channels : 2 * channels] = shifted[low:high].astype(BF)
        for tap in (0, 2):
            start = 8 + low + (tap - 1) * dil_ref[layer]
            cat[low:high, tap * channels : (tap + 1) * channels] = window(
                bh, start, high - low, channels
            ).astype(BF)

    def gates(layer, first_row, rows_now):
        spot = slice(first_row, first_row + rows_now)
        value = cat[spot, 0:2048]
        for part in range(2):
            columns = slice(part * WIDE, (part + 1) * WIDE)
            base = MAIN * layer + 5 * part
            lhs = mm(value, w[base : base + 4].reshape(2048, WIDE))
            tangent = jnp.tanh(lhs + vec[layer, 2:3, columns])
            rhs = mm(value, w[base + 10 : base + 14].reshape(2048, WIDE))
            opening = jax.nn.sigmoid(rhs + vec[layer, 3:4, columns])
            gate = tangent * opening
            gated[spot, columns] = gate.astype(BF)
            slopes[layer, spot, columns] = (opening * (1.0 - tangent * tangent)).astype(BF)
            other = slice(channels + part * WIDE, channels + (part + 1) * WIDE)
            slopes[layer, spot, other] = (gate * (1.0 - opening)).astype(BF)

    def residual(layer, first_row, rows_now):
        value = gated[first_row : first_row + rows_now]
        for part in range(2):
            columns = slice(part * WIDE, (part + 1) * WIDE)
            term = mm(value, wblock(layer, 5 * part + 4))
            if layer == 0:
                base = xe[first_row : first_row + rows_now, columns].astype(F32)
                x1[first_row : first_row + rows_now, columns] = (base + term) * HALF_ROOT
            else:
                base = x1[first_row : first_row + rows_now, columns]
                x1[first_row : first_row + rows_now, columns] = (base + term) * HALF_ROOT

    def skipped(layer, first_row, rows_now):
        value = gated[first_row : first_row + rows_now]
        spot = slice(first_row - HALO, first_row - HALO + rows_now)
        for part in range(2):
            columns = slice(part * WIDE, (part + 1) * WIDE)
            term = mm(value, wblock(layer, 5 * part + 14))
            if layer == 0:
                sk[spot, columns] = term
            else:
                sk[spot, columns] = sk[spot, columns] + term

    low, high = 16, grid_rows - 16

    def gate_grads(layer, first_row, rows_now):
        spot = slice(first_row, first_row + rows_now)
        bb[spot, 0:channels] = (bx[spot] * HALF_ROOT).astype(BF)
        branch = jnp.concatenate([wblock(layer, 5 * part + 4) for part in range(4)], axis=1)
        back = mm_nt(bb[spot], branch)
        keep = inside(first_row, rows_now)
        for side in range(2):
            columns = slice(side * channels, (side + 1) * channels)
            value = back * slopes[layer, spot, columns].astype(F32)
            middle = slice((2 + side) * channels, (3 + side) * channels)
            cat[spot, middle] = jnp.where(keep, value, 0.0).astype(BF)

    def windows_backward(layer):
        reach, limit = (low, high) if layer else (HALO, top)
        edge = 1 + low // 8
        bh[0:edge] = jnp.zeros((edge, 8, channels), F32)
        bh[1 + high // 8 :] = jnp.zeros((edge + 2, 8, channels), F32)
        for side in range(2):
            middle = slice((2 + side) * channels, (3 + side) * channels)
            value = cat[low:high, middle].astype(F32)
            bh[edge : 1 + high // 8] = in_eights(value)
            total = jnp.sum(value[HALO - low : top - low], axis=0, keepdims=True)
            sums[layer, 2 + side : 3 + side] = total
            for tap in (0, 2):
                start = 8 + reach - (tap - 1) * dil_ref[layer]
                columns = slice((2 * tap + side) * channels, (2 * tap + side + 1) * channels)
                cat[reach:limit, columns] = window(bh, start, limit - reach, channels).astype(BF)

    def frame_grads(layer, first_row, rows_now):
        spot = slice(first_row, first_row + rows_now)
        taps = jnp.concatenate(
            [wblock(layer, 5 * part + tap) for tap in range(3) for part in range(4)], axis=1
        )
        back = mm_nt(cat[spot], taps)
        if layer:
            here = x1[spot]
            row = lax.broadcasted_iota(jnp.int32, (rows_now, 1), 0) + first_row
            kept = jnp.where((row >= HALO) & (row < top), back, 0.0)
        else:
            here = xe[spot].astype(F32)
            kept = back
        sums[layer, 0:1] += jnp.sum(kept * here, axis=0, keepdims=True)
        sums[layer, 1:2] += jnp.sum(kept, axis=0, keepdims=True)
        bx[spot] = bx[spot] * HALF_ROOT + back * (1.0 + vec[layer, 0:1])

    def weight_grad(layer, part, i):
        if i < 4:
            tap = i if i < 3 else 1
            start = pl.multiple_of(tap * 1024 + part * WIDE, WIDE)
            lhs = sht[layer] if i < 3 else condt[...]
            return mm(lhs, cat[HALO:top, pl.ds(start, WIDE)])
        start = pl.multiple_of(part * WIDE, WIDE)
        return mm(gatt[layer], bb[HALO:top, pl.ds(start, WIDE)])

    core_sent = {}

    def x_of(turn):
        return x if turn else 1 - x

    def give(layer, turn):
        xx = x_of(turn)
        part = 2 * (1 - c) + xx
        buffer, base = (gs, 0) if layer else (w, MAIN)
        for i in range(5):
            value = weight_grad(layer, part, i).astype(BF)
            buffer[base + 5 * xx + i] = value.reshape(nz, 2, rows, WIDE)
        core_sent[layer, turn] = remote(
            buffer.at[pl.ds(base + 5 * xx, 5)], red_in.at[layer, pl.ds(5 * xx, 5)], seq, sib
        )

    def keep(layer, turn):
        xx = x_of(turn)
        part = 2 * c + xx
        core_sent[layer, turn].wait_recv()
        for i in range(5):
            value = weight_grad(layer, part, i).reshape(nz, 2, rows, WIDE)
            spot = 5 * xx + i
            red_in[layer, spot] = (red_in[layer, spot].astype(F32) + value).astype(BF)

    ones, twos, zs, targets = {}, {}, {}, {}
    for layer in range(LAYERS):
        for k in range(nz):
            zd = lax.rem(z + k, nz)
            targets[layer, k] = (zd, y_first(zd, OUT_SPLIT[layer]))

    def one_copy(layer, k, turn):
        zd, a = targets[layer, k]
        b = 1 - a
        if turn:
            xi, yi, j = a * (1 - x) + b * x, a + b * (1 - y), a + b * x
        else:
            xi, yi, j = 1 - x, b * (1 - y), b * (1 - x)
        return remote(
            red_in.at[layer, pl.ds(5 * xi, EACH), zd, yi],
            one_in.at[layer, k, j],
            a * seq + b * other_y, a * across + b * grp, start=not turn,
        )

    def red_one(layer, k):
        ones[layer, k] = [one_copy(layer, k, turn) for turn in range(2)]
        pl.when(targets[layer, k][1] == 1)(ones[layer, k][1].start)

    def red_one_more(layer, k):
        pl.when(targets[layer, k][1] == 0)(ones[layer, k][1].start)

    def red_two(layer, k):
        zd, a = targets[layer, k]
        b = 1 - a
        you = a * y + b * x
        for copy in ones[layer, k]:
            copy.wait_recv()
        for j in range(2):
            xi, yi = a * x + b * j, a * j + b * y

            def body(i, carry, j=j, xi=xi, yi=yi):
                one_in[layer, k, j, i] = (
                    one_in[layer, k, j, i] + red_in[layer, 5 * xi + i, zd, yi]
                )
                return carry

            lax.fori_loop(0, EACH, body, 0)
        twos[layer, k] = remote(
            one_in.at[layer, k, 1 - you], two_in.at[layer, k],
            a * other_y + b * seq, a * grp + b * across,
        )

    def red_three(layer, k):
        zd, a = targets[layer, k]
        you = a * y + (1 - a) * x
        twos[layer, k].wait_recv()

        def body(i, carry):
            two_in[layer, k, i] = two_in[layer, k, i] + one_in[layer, k, you, i]
            return carry

        lax.fori_loop(0, EACH, body, 0)
        if k:
            zs[layer, k] = remote(two_in.at[layer, k], z_in.at[layer, k - 1], zd * 2 + y, grp)

    side_sent = {}

    def red_side_one(layer):
        side_sent[layer] = [
            remote(
                red_in.at[layer, pl.ds(5 * xx + EACH, 5 - EACH), targets[layer, k][0]],
                ze_in.at[layer, k - 1, xx],
                targets[layer, k][0] * 2 + y, grp,
            )
            for k in range(1, nz)
            for xx in range(2)
        ]

    def red_side_two(layer):
        for copy in side_sent[layer]:
            copy.wait_recv()
        for xx in range(2):
            for i in range(5 - EACH):
                spot = 5 * xx + EACH + i
                total = red_in[layer, spot, z].astype(F32)
                for k in range(1, nz):
                    total = total + ze_in[layer, k - 1, xx, i].astype(F32)
                red_in[layer, spot, z] = total.astype(BF)
        side_sent[layer] = [
            remote(
                red_in.at[layer, pl.ds(5 * xx + EACH, 5 - EACH), z, yy], xe_in.at[layer, place],
                to_seq, to_grp,
            )
            for place, (xx, yy, to_seq, to_grp) in enumerate(
                (
                    (1 - x, y, seq, across), (x, 1 - y, other_y, grp),
                    (1 - x, 1 - y, other_y, across),
                )
            )
        ]

    def red_side_three(layer):
        for copy in side_sent[layer]:
            copy.wait_recv()
        for i in range(5 - EACH):
            total = red_in[layer, 5 * x + EACH + i, z, y].astype(F32)
            for place in range(3):
                total = total + xe_in[layer, place, i].astype(F32)
            fin[layer, EACH + i] = total.astype(BF)

    lasts = {}
    outs = []

    def local_out(src, dst):
        copy = pltpu.make_async_copy(src, dst, out_sem.at[len(outs)])
        copy.start()
        outs.append(copy)

    def red_four(layer):
        for k in range(1, nz):
            zs[layer, k].wait_recv()

        def body(i, carry):
            total = two_in[layer, 0, i].astype(F32)
            for k in range(1, nz):
                total = total + z_in[layer, k - 1, i].astype(F32)
            fin[layer, i] = total.astype(BF)
            return carry

        lax.fori_loop(0, EACH, body, 0)
        src, dst = fin.at[layer], out_hbm.at[layer, mine]
        lasts[layer] = [remote(src, dst, seq, across), remote(src, dst, seq, sib)]
        if not layer and LAST_DIRECT:
            lasts[layer].append(remote(src, dst, seq, (1 - x) * 2 + 1 - c))
        local_out(src, dst)

    def red_five(layer):
        lasts[layer][0].wait_recv()
        ref = out_hbm.at[layer, theirs]
        lasts[layer].append(remote(ref, ref, seq, sib))

    ops = {}

    def op(*key):
        def keep_op(body):
            ops[key] = body
            return body

        return keep_op

    main_tiles = (0, 1, 2, 3, 4, 5, 6, 7, 15, 16)
    merges, crosses, film_sent, seen, hops = {}, {}, {}, {}, {}
    size_all, size_mid, size_own = grid_rows // 2, (high - low) // 2, own // 2
    embed = same_rows(embed_ref[...].astype(F32))

    for phase in (1, 2):

        @op("prep", phase)
        def _(phase=phase):
            ready([PER_LAYER * (phase - 1) + t for t in main_tiles], prep, BLOCK_OF)
            merges[phase] = merge_start(phase)

        @op("cross", phase)
        def _(phase=phase):
            crosses[phase] = merge_cross(phase, merges[phase])

        @op("end", phase)
        def _(phase=phase):
            merge_end(phase, crosses[phase])
            spread_z(phase)

    def quarter(j):
        return range(j * nz // 4, (j + 1) * nz // 4)

    for phase in (1, 2):
        for name, body in (("e1", side_first), ("e2", side_second), ("e3", side_third)):

            @op(name, phase)
            def _(phase=phase, body=body):
                body(phase)

        for j in range(4):
            for name, body in (("first", first), ("second", second), ("third", third)):

                @op(name, phase, j)
                def _(phase=phase, j=j, body=body):
                    for k in quarter(j):
                        body(phase, k)

    parts = {"K": (0, KEY_VALUE), "R": (KEY_VALUE, FILM * LAYERS - KEY_VALUE)}
    for name, (begin, blocks) in parts.items():
        half = blocks // 2
        own_half_at = begin + c * half

        @op("fc" + name)
        def _(name=name, begin=begin, half=half):
            order = FILM_ORDER[:2] if name == "K" else FILM_ORDER[2:]
            for layer in range(LAYERS):
                ready([PER_LAYER * layer + t for t in order], fr, FILM_OF)
            film_sent[name, 0] = remote(
                fr.at[pl.ds(begin + (1 - c) * half, half)],
                fr_in.at[pl.ds(begin // 2, half)],
                seq, sib,
            )

        @op("fx" + name)
        def _(name=name, begin=begin, half=half, own_half_at=own_half_at):
            film_sent[name, 0].wait_recv()
            spot = slice(begin // 2, begin // 2 + half)
            fr_in[spot] = fr_in[spot] + fr[pl.ds(own_half_at, half)]
            ref = pl.ds(begin // 2, half)
            film_sent[name, 1] = remote(fr_in.at[ref], fx.at[ref], seq, across)

        @op("fl" + name)
        def _(name=name, begin=begin, half=half, own_half_at=own_half_at):
            film_sent[name, 1].wait_recv()
            spot = slice(begin // 2, begin // 2 + half)
            ref = pl.ds(own_half_at, half)
            ff[ref] = fr_in[spot] + fx[spot]
            film_sent[name, 2] = remote(ff.at[ref], ff.at[ref], seq, sib)

    for turn in range(4):

        @op("pr", turn)
        def _(turn=turn):
            total = prompt[...] if turn else None
            for i in range(4):
                prompt_copy(turn, i).wait()
                flag = (pairing_ref[0] == 4 * turn + i).astype(F32).astype(BF)
                part = slice((i % 2) * channels, (i % 2 + 1) * channels)
                term = slopes[i // 2, 0 : prompt.shape[0], part] * flag
                total = term if total is None else total + term
            prompt[...] = total
            if turn < 3:
                for i in range(4):
                    prompt_copy(turn + 1, i).start()

    def gathered():
        while gathering:
            gathering.pop().wait_send()

    @op("condt")
    def _():
        local_in[2].wait()
        condt[...] = jnp.transpose(cat[HALO:top, 1536:2048].astype(F32)).astype(BF)

    @op("hsK")
    def _():
        film_sent["K", 2].wait_recv()
        for h in range(HEADS):
            columns = slice((h % 4) * wide_head, (h % 4 + 1) * wide_head)
            pieces = [
                film_block(layer, place + h // 4).astype(F32)[:, columns]
                for place in (0, 2)
                for layer in range(LAYERS)
            ]
            kv_out[h] = jnp.concatenate(pieces, axis=1).astype(BF)
        kv_in[seq] = kv_out[head]
        kv_begin()

    @op("heK")
    def _():
        kv_finish()

    @op("att")
    def _():
        attention()

    @op("hsB")
    def _():
        film_sent["R", 2].wait_recv()
        vectors = []
        embed_here, mixed = pick(embed), pick(left[8:16])
        for layer in range(LAYERS):
            vectors.append(film_rows(layer, mixed, (4, 5))[layer : layer + 1])
            steps = film_rows(layer, embed_here, (10, 11, 12, 13))
            vectors += [steps[0:1, :channels], steps[0:1, channels:]]
        hop_start(0, pack(vectors))

    @op("heB")
    def _():
        total = hop_end(0)
        hops["pooled"] = [unpack(total, 3 * layer) for layer in range(LAYERS)]
        for layer in range(LAYERS):
            vec[layer, 2:3] = unpack(total, 3 * layer + 1)
            vec[layer, 3:4] = unpack(total, 3 * layer + 2)

    @op("hsC")
    def _():
        vectors = []
        for layer in range(LAYERS):
            pooled = hops["pooled"][layer]
            film = film_rows(layer, pick(same_rows(pooled)), (6, 7, 8, 9))
            vectors += [film[0:1, :channels], film[0:1, channels:]]
        hop_start(1, pack(vectors))

    @op("heC")
    def _():
        total = hop_end(1)
        for layer in range(LAYERS):
            vec[layer, 0:1] = unpack(total, 2 * layer)
            vec[layer, 1:2] = unpack(total, 2 * layer + 1)

    @op("win0")
    def _():
        local_in[1].wait()
        for copy in halos[:4]:
            copy.wait_recv()
        windows_forward(0)

    @op("win1")
    def _():
        local_in[3].wait()
        local_in[4].wait()
        for copy in halos[4:]:
            copy.wait_recv()
        bx[...] = bb[:, 0:channels].astype(F32)
        windows_forward(1)

    for layer in range(LAYERS):
        start, size = (low, size_mid) if layer else (0, size_all)
        for part, name in enumerate("ab"):
            first_row = start + part * size

            @op(f"gates{layer}{name}")
            def _(layer=layer, first_row=first_row, size=size, part=part):
                if not part:
                    arrived(1 + layer)
                gates(layer, first_row, size)

        @op(f"gatt{layer}")
        def _(layer=layer):
            gatt[layer] = jnp.transpose(gated[HALO:top].astype(F32)).astype(BF)

    @op("res0")
    def _():
        for part in range(2):
            residual(0, part * size_all, size_all)

    @op("skip0")
    def _():
        for part in range(2):
            skipped(0, HALO + part * size_own, size_own)

    @op("out1")
    def _():
        for part in range(2):
            residual(1, HALO + part * size_own, size_own)
            skipped(1, HALO + part * size_own, size_own)
        local_out(x1.at[pl.ds(HALO, own)], block_hbm.at[0])
        local_out(sk, skip_hbm.at[0])

    for layer in range(LAYERS):
        for part, name in enumerate("ab"):

            @op(f"gg{layer}{name}")
            def _(layer=layer, part=part):
                if layer and not part:
                    sums[...] = jnp.zeros_like(sums)
                gate_grads(layer, low + part * size_mid, size_mid)

            @op(f"fg{layer}{name}")
            def _(layer=layer, part=part):
                if layer:
                    frame_grads(1, low + part * size_mid, size_mid)
                else:
                    frame_grads(0, HALO + part * size_own, size_own)

        @op(f"winb{layer}")
        def _(layer=layer):
            windows_backward(layer)

        for xx in range(2):

            @op("give", layer, xx)
            def _(layer=layer, xx=xx):
                if not layer:
                    gathered()
                give(layer, xx)

            @op("keep", layer, xx)
            def _(layer=layer, xx=xx):
                keep(layer, xx)

        for j in range(4):
            for name, body in (
                ("one", red_one), ("onb", red_one_more), ("two", red_two), ("three", red_three)
            ):

                @op(name, layer, j)
                def _(layer=layer, j=j, body=body):
                    for k in quarter(j):
                        body(layer, k)

        for name, body in (("r1", red_side_one), ("r2", red_side_two), ("r3", red_side_three)):

            @op(name, layer)
            def _(layer=layer, body=body):
                body(layer)

        @op("four", layer)
        def _(layer=layer):
            red_four(layer)

        @op("five", layer)
        def _(layer=layer):
            red_five(layer)

    @op("hs3")
    def _():
        local_out(bx.at[pl.ds(HALO, own)], gframes_hbm.at[0])
        hop_start(2, pack([sums[l, i : i + 1] for l in range(LAYERS) for i in range(4)]))

    @op("he3")
    def _():
        total = hop_end(2)
        hops["sides"] = [[unpack(total, 4 * l + i) for i in range(4)] for l in range(LAYERS)]

    @op("hs4")
    def _():
        vectors = []
        for layer in range(LAYERS):
            dfilm = same_rows(jnp.concatenate(hops["sides"][layer][0:2], axis=1))
            vectors.append(film_back(layer, dfilm, (6, 7, 8, 9))[0:1])
        hop_start(3, pack(vectors))

    @op("he4")
    def _():
        total = hop_end(3)
        hops["dpooled"] = [unpack(total, layer) for layer in range(LAYERS)]


    @op("fb")
    def _():
        vectors = [
            film_back(l, same_rows(hops["dpooled"][l]), (4, 5))[0:1] for l in range(LAYERS)
        ]
        if copies_of > 1:
            hop_start(4, pack(vectors))
            total = hop_end(4)
            vectors = [unpack(total, layer) for layer in range(LAYERS)]
        dmixed = jnp.concatenate(vectors + [jnp.zeros((8 - LAYERS, channels), F32)], axis=0)
        dmixed = jnp.where(own_half, mm_low(dmixed, head_columns), 0.0)
        keys, values = head_weights()
        pr = prompt[...]
        dmean = mm_nt_low(mm_nt_low(dmixed, values), pr) * (1.0 / number)
        dprobs = jnp.concatenate(
            [jnp.broadcast_to(dmean[l : l + 1], (number, channels)) for l in range(LAYERS)], axis=0
        )
        value = probs[...]
        inner = jnp.sum(dprobs * value, axis=1, keepdims=True)
        dprobe = mm_low(value * (dprobs - inner) * 0.125, pr)
        dqueries = mm_low(dprobe, keys)
        half = lax.div(lax.broadcasted_iota(jnp.int32, (number, 128), 1), wide_head)
        dquery = jnp.where(half == 0, dqueries[0:number], dqueries[number : 2 * number])
        dq_in[grp] = dquery.astype(BF)
        small_out[...] = jnp.concatenate([dmixed, jnp.zeros((8, 128), F32)], axis=0).astype(BF)
        lefts = jnp.concatenate(
            [dprobe, left[0:2], left[8:10]]
            + [hops["pooled"][layer] for layer in range(LAYERS)]
            + [embed[0:1], jnp.zeros((128 - 2 * number - 7, channels), F32)],
            axis=0,
        )
        at_out[...] = jnp.transpose(lefts).astype(BF).reshape(n_seq, rows, 128)

    @op("hs5")
    def _():
        small_in[seq] = small_out[...]
        at_in[seq] = at_out[seq]
        small_begin()
        at_begin()

    def halves(one, two):
        wanted = lax.broadcasted_iota(jnp.int32, one.shape, 1) < wide_head
        return (
            jnp.where(wanted, one, pltpu.roll(two, wide_head, 1)),
            jnp.where(wanted, pltpu.roll(one, wide_head, 1), two),
        )

    def by_heads(ref):
        blocks = [[], []]
        for h in range(0, HEADS, 2):
            pair = halves(ref[h * copies_of].astype(F32), ref[(h + 1) * copies_of].astype(F32))
            for layer in range(LAYERS):
                blocks[layer].append(pair[layer])
        return [jnp.concatenate(blocks[layer], axis=1) for layer in range(LAYERS)]

    dq_sent = []

    @op("dq1")
    def _():
        for k in range(1, 4):
            ref = dq_in.at[grp]
            dq_sent.append(remote(ref, ref, seq, lax.rem(grp + k, 4)))

    @op("dq2")
    def _():
        for copy in dq_sent:
            copy.wait_recv()
        total = dq_in[0].astype(F32)
        for k in range(1, 4):
            total = total + dq_in[k].astype(F32)
        dq_out[...] = total
        dq_all[seq] = total
        dq_begin()

    @op("dq3")
    def _():
        dq_finish()
        total = by_heads(dq_all)
        for layer in range(LAYERS):
            dquery_ref[layer] = total[layer]

    @op("he5")
    def _():
        small_finish()
        at_finish()

        full = by_heads(small_in)
        pieces = []
        for layer in range(LAYERS):
            pieces += hops["sides"][layer]
            pieces += [hops["dpooled"][layer], full[layer][layer : layer + 1]]
        pieces.append(jnp.zeros((16 - len(pieces), channels), F32))
        wide[grp] = jnp.concatenate(pieces, axis=0).astype(BF)
        at = lax.broadcasted_iota(jnp.int32, (rows, 128), 1)
        thin = jnp.where(at >= 66, at_in[seq].astype(F32), 0.0)
        for h in range(0, HEADS, 2):
            one, two = at_in[h * copies_of].astype(F32), at_in[(h + 1) * copies_of].astype(F32)
            pair = jnp.where(at < wide_head, one, pltpu.roll(two, wide_head, 1))
            bundle[grp, :, h * wide_head : (h + 2) * wide_head] = pair.astype(BF)
            for k, value in ((h, one), (h + 1, two)):
                turned = pltpu.roll(value, wide_head + 2 * k, 1)
                thin = jnp.where(lax.div(at, 2) == k, turned, thin)
        bundle[grp, :, channels : channels + 128] = thin.astype(BF)

    bundles = []

    @op("bundle")
    def _():
        for k in range(1, 4):
            for ref in (bundle.at[grp], wide.at[grp]):
                bundles.append(remote(ref, ref, seq, lax.rem(grp + k, 4)))

    @op("low")
    def _():
        for copy in bundles:
            copy.wait_recv()
        mask = head_mask()
        at = lax.broadcasted_iota(jnp.int32, (8, channels), 0)
        probe = bundle[0, :, 0:channels].astype(F32)
        for k in range(1, 4):
            probe = probe + bundle[k, :, 0:channels].astype(F32)
        probe = probe.astype(BF)
        blank = jnp.zeros((number, channels), F32)
        column = lax.div(lax.broadcasted_iota(jnp.int32, (number, channels), 1), wide_head)
        for layer in range(LAYERS):
            side = []
            for h in range(HEADS):
                one = jnp.where(column == h, queries_ref[layer], 0.0)
                side += [blank, one] if layer else [one, blank]
            low_ref[layer, 0] = mm(probe, jnp.concatenate(side, axis=0).astype(BF)).astype(BF)
            total = None
            for k in range(4):
                right = wide[k].astype(F32)[6 * layer : 6 * layer + 6]
                dmixed = jnp.where(mask, right[5:6], 0.0)
                nothing = jnp.zeros((1, channels), F32)
                rows_of = []
                for h in range(HEADS):
                    one = dmixed[h : h + 1]
                    rows_of += [nothing, one] if layer else [one, nothing]
                value = jnp.concatenate(rows_of, axis=0)
                gap = jnp.zeros((48, channels), F32)
                rest = jnp.zeros((56, channels), F32)
                pieces = [jnp.concatenate([value, gap, jnp.zeros((64, channels), F32)], axis=0)]
                for i, row in ((4, 2), (0, 4), (1, 4), (2, 6), (3, 6)):
                    row = row + (layer if row < 6 else 0)
                    one = jnp.where(at == row, right[i : i + 1], 0.0)
                    pieces.append(
                        jnp.concatenate([jnp.zeros((64, channels), F32), one, rest], axis=0)
                    )
                term = mm(
                    bundle[k, :, channels : channels + 128],
                    jnp.concatenate(pieces, axis=1).astype(BF),
                )
                total = term if total is None else total + term
            for i in range(6):
                low_ref[layer, 1 + i] = total[:, i * channels : (i + 1) * channels].astype(BF)

    @op("end")
    def _():
        for copies in lasts.values():
            for copy in copies[1:]:
                copy.wait_recv()
        if LAST_DIRECT:
            lasts[0][0].wait_recv()
        for copy in outs:
            copy.wait()
        for copy in halos:
            copy.wait_send()
        gathered()
        for copy in waits:
            copy.wait_send()

    local_in[0].wait()
    for key in ORDER:
        ops[key if isinstance(key, tuple) else (key,)]()


def train_step(
    n_seq, owners, dilations, lengths, pairing, step_embed, queries, master, prompts,
    frames_in, cond_frames, grad_out, grad_skip,
):
    _, own, channels = frames_in.shape
    rows = master.shape[1]
    number = queries.shape[1]
    grid_rows = own + 2 * HALO
    nz = n_seq // 2
    v = pltpu.VMEM
    dma = pltpu.SemaphoreType.DMA
    frame_out = jax.ShapeDtypeStruct((1, own, channels), F32)
    film = FILM * LAYERS
    copies = 96 + 34 * nz
    return pl.pallas_call(
        functools.partial(step_kernel, n_seq),
        out_shape=(
            frame_out,
            frame_out,
            frame_out,
            jax.ShapeDtypeStruct((LAYERS, 4, 5, rows, WIDE), BF),
            jax.ShapeDtypeStruct((LAYERS, LOW_RANK, rows, channels), BF),
            jax.ShapeDtypeStruct((LAYERS, number, channels), F32),
        ),
        in_specs=[smem_spec()] * 4 + [vmem_spec()] * 2 + [any_spec()] * 6,
        out_specs=(any_spec(),) * 4 + (vmem_spec(),) * 2,
        scratch_shapes=[
            v((BLOCKS, nz, 2, rows, WIDE), BF),
            v((10, nz, 2, rows, WIDE), BF),
            v((BLOCKS, rows, WIDE), BF),
            v((BLOCKS // 2, rows, WIDE), BF),
            v((BLOCKS // 4, rows, WIDE), BF),
            v((film, rows, WIDE), BF),
            v((film // 2, rows, WIDE), BF),
            v((film // 2, rows, WIDE), BF),
            v((film, rows, WIDE), BF),
            v((LAYERS, 10, nz, 2, rows, WIDE), BF),
            v((LAYERS, nz, 2, EACH, rows, WIDE), BF),
            v((LAYERS, nz, EACH, rows, WIDE), BF),
            v((LAYERS, nz - 1, EACH, rows, WIDE), BF),
            v((LAYERS, nz - 1, 2, max(5 - EACH, 1), 2, rows, WIDE), BF),
            v((LAYERS, 3, max(5 - EACH, 1), rows, WIDE), BF),
            v((LAYERS, 5, rows, WIDE), BF),
            v((grid_rows, channels), BF),
            v((grid_rows, 6 * channels), BF),
            v((LAYERS, grid_rows, 2 * channels), BF),
            v((grid_rows, channels), BF),
            v((grid_rows, channels), F32),
            v((grid_rows // 8 + 4, 8, channels), F32),
            v((grid_rows, 2 * channels), BF),
            v((LAYERS, channels, own), BF),
            v((channels, own), BF),
            v((LAYERS, channels, own), BF),
            v((grid_rows, channels), F32),
            v((own, channels), F32),
            v(master.shape, F32),
            v(prompts.shape[1:], BF),
            v((LAYERS * number, prompts.shape[1]), F32),
            v((16, channels), F32),
            v((LAYERS, 8, channels), F32),
            v((LAYERS, 8, channels), F32),
            v((4, rows, channels + 128), BF),
            v((4, 16, channels), BF),
            v((4, number, 128), BF),
            v((HEADS, rows, WIDE), BF),
            v((n_seq, rows, WIDE), BF),
            v((n_seq, rows, 128), BF),
            v((n_seq, rows, 128), BF),
            v((16, 128), BF),
            v((n_seq, 16, 128), BF),
            v((number, 128), F32),
            v((n_seq, number, 128), F32),
            v((sum(HOP_ROWS), 128), F32),
            v((n_seq, sum(HOP_ROWS), 128), F32),
            dma((5,)),
            dma((4,)),
            dma((8,)),
            dma((8,)),
            dma((8,)),
            dma((copies,)),
            dma((copies,)),
            dma((len(HOP_ROWS), n_seq)),
            dma((len(HOP_ROWS), n_seq)),
            dma((4, n_seq)),
            dma((4, n_seq)),
        ],
        compiler_params=pltpu.CompilerParams(
            collective_id=0, has_side_effects=True, vmem_limit_bytes=MEM
        ),
        name="train_step",
    )(
        owners, dilations, lengths, pairing, step_embed, queries, master, prompts,
        frames_in, cond_frames, grad_out, grad_skip,
    )


def adam_update(weight, moment_one, moment_two, gradient, step_rate):
    moment_one = BETA_ONE * moment_one + (1.0 - BETA_ONE) * gradient
    moment_two = BETA_TWO * moment_two + (1.0 - BETA_TWO) * gradient * gradient
    normal = (
        moment_one
        * (1.0 / (1.0 - BETA_ONE**STEP))
        / (jnp.sqrt(moment_two * (1.0 / (1.0 - BETA_TWO**STEP))) + EPSILON)
    )
    return (moment_one, moment_two, weight - step_rate * (normal + WEIGHT_DECAY * weight))


def update_kernel(
    owners_ref, master_hbm, first_hbm, second_hbm, grad_hbm, low_hbm,
    queries_hbm, qfirst_hbm, qsecond_hbm, dq_hbm, block_in, skip_in, gframes_in,
    nfirst_hbm, nsecond_hbm, nmaster_hbm, ncopy_hbm, nqfirst_hbm, nqsecond_hbm, nqueries_hbm,
    block_out, skip_out, gframes_out,
    master, first, second, grad, low, three, one, two, copied, frames, asked,
    tile_of, grad_sem, in_sem, out_sem, frame_sem, asked_sem,
):
    grp = lax.axis_index("grp")
    grads_in = [
        pltpu.make_async_copy(a, b, grad_sem.at[i])
        for i, (a, b) in enumerate(((grad_hbm, grad), (low_hbm, low)))
    ]
    spots = [pl.ds(start, count) for start, count in CHUNKS]
    slots_in = [
        [
            pltpu.make_async_copy(a.at[spot], b.at[spot], in_sem.at[i, j])
            for j, (a, b) in enumerate(
                ((master_hbm, master), (first_hbm, first), (second_hbm, second))
            )
        ]
        for i, spot in enumerate(spots)
    ]
    frames_in = [
        pltpu.make_async_copy(a, frames.at[i], frame_sem.at[0, i])
        for i, a in enumerate((block_in, skip_in, gframes_in))
    ]
    asked_in = [
        pltpu.make_async_copy(a, asked.at[i], asked_sem.at[i])
        for i, a in enumerate((queries_hbm, qfirst_hbm, qsecond_hbm, dq_hbm))
    ]
    for copy in grads_in + slots_in[0] + asked_in + frames_in[:1] + slots_in[1] + frames_in[1:]:
        copy.start()
    for copies in slots_in[2:]:
        for copy in copies:
            copy.start()

    for slot in range(CAP + 1):
        tile_of[slot] = TILES
    count = jnp.int32(0)
    for tile in range(TILES):
        own = owners_ref[tile] == grp

        @pl.when(own)
        def _(count=count, tile=tile):
            tile_of[jnp.minimum(count, CAP)] = tile

        count = count + own.astype(jnp.int32)
    outs = []

    def send(a, b, sem):
        copy = pltpu.make_async_copy(a, b, sem)
        copy.start()
        outs.append(copy)

    def pass_frames(i, target):
        frames_in[i].wait()
        send(frames.at[i], target, frame_sem.at[1, i])

    def slot_update(slot, carry):
        tile = tile_of[slot]
        used = (tile < TILES).astype(jnp.int32)
        tile = jnp.minimum(tile, TILES - 1)
        layer, kind = lax.div(tile, PER_LAYER), lax.rem(tile, PER_LAYER)
        plain = kind < 8
        pair = jnp.where(plain, lax.rem(kind, 2), (kind == 16).astype(jnp.int32))
        tap = jnp.where(plain, lax.div(kind, 2), 4)
        full = jnp.concatenate([grad[layer, 2 * pair, tap], grad[layer, 2 * pair + 1, tap]], axis=1)
        place = jnp.where(kind < 10, kind - 3, kind - 10)
        thin = low[layer, jnp.clip(place, 0, LOW_RANK - 1)]
        is_thin = ((kind >= 8) & (kind <= 14)).astype(jnp.int32)
        gradient = jnp.where(
            jnp.broadcast_to(is_thin, full.shape) > 0, thin.astype(F32), full.astype(F32)
        )
        old, old_first, old_second = master[slot], first[slot], second[slot]
        new_first, new_second, new = adam_update(old, old_first, old_second, gradient, LEARN_RATE)
        keep = jnp.broadcast_to(used, old.shape) > 0
        new = jnp.where(keep, new, old)
        one[slot] = jnp.where(keep, new_first, old_first)
        two[slot] = jnp.where(keep, new_second, old_second)
        three[slot] = new
        copied[slot] = new.astype(BF)
        return carry

    for copy in grads_in:
        copy.wait()
    passed = (block_out, skip_out, gframes_out)
    for i, (start, number) in enumerate(CHUNKS):
        for copy in slots_in[i]:
            copy.wait()
        lax.fori_loop(start, start + number, slot_update, 0)
        for j, (a, b) in enumerate(
            ((one, nfirst_hbm), (two, nsecond_hbm), (three, nmaster_hbm), (copied, ncopy_hbm))
        ):
            send(a.at[spots[i]], b.at[spots[i]], out_sem.at[i, j])
        if i < len(passed):
            pass_frames(i, passed[i])
        if i == 1:
            for copy in asked_in:
                copy.wait()
            news = adam_update(asked[0], asked[1], asked[2], asked[3], QUERY_RATE)
            for j, (value, target) in enumerate(
                zip(news, (nqfirst_hbm, nqsecond_hbm, nqueries_hbm))
            ):
                asked[4 + j] = value
                send(asked.at[4 + j], target, asked_sem.at[4 + j])
    for copy in outs:
        copy.wait()


CHUNKS = ((0, 2), (2, 3), (5, 4), (9, 4))


def update(owners, master, first, second, grads, low, queries, qfirst, qsecond, dq, *frames):
    any_ = any_spec()
    query = jax.ShapeDtypeStruct(queries.shape, F32)
    full = jax.ShapeDtypeStruct(master.shape, F32)
    passed = jax.ShapeDtypeStruct(frames[0].shape, F32)
    v = pltpu.VMEM
    slots = v(master.shape, F32)
    return pl.pallas_call(
        update_kernel,
        out_shape=(full, full, full, jax.ShapeDtypeStruct(master.shape, BF), query, query, query)
        + (passed,) * 3,
        in_specs=[smem_spec()] + [any_] * 12,
        out_specs=(any_,) * 10,
        scratch_shapes=[
            slots, slots, slots, v(grads.shape, BF), v(low.shape, BF),
            slots, slots, slots, v(master.shape, BF), v((3,) + passed.shape, F32),
            v((7,) + queries.shape, F32),
            pltpu.SMEM((CAP + 1,), jnp.int32),
            pltpu.SemaphoreType.DMA((2,)),
            pltpu.SemaphoreType.DMA((len(CHUNKS), 3)),
            pltpu.SemaphoreType.DMA((len(CHUNKS), 4)),
            pltpu.SemaphoreType.DMA((2, 3)),
            pltpu.SemaphoreType.DMA((7,)),
        ],
        compiler_params=pltpu.CompilerParams(vmem_limit_bytes=MEM),
        name="update",
    )(owners, master, first, second, grads, low, queries, qfirst, qsecond, dq, *frames)


def on_device(
    n_seq,
    frames_in,
    cond_frames,
    step_embed,
    prompts,
    prompt_lengths,
    pairing,
    dilations,
    owners,
    master,
    first_moment,
    second_moment,
    queries,
    query_first,
    query_second,
    grad_out,
    grad_skip,
):
    block, skip, gframes, own_grads, low, dq = train_step(
        n_seq, owners, dilations, prompt_lengths, pairing, step_embed, queries, master, prompts,
        frames_in, cond_frames, grad_out, grad_skip,
    )
    (
        new_first, new_second, new_master, new_copy, nqf, nqs, nq,
        block_out, skip_out, grad_frames,
    ) = update(
        owners, master, first_moment, second_moment, own_grads, low,
        queries, query_first, query_second, dq, block, skip, gframes,
    )
    return (
        new_first, new_second, new_master, new_copy, nqf, nqs, nq,
        block_out, skip_out, grad_frames,
    )


def solution(mesh):
    shard = P("grp", "seq", None)
    placed = (
        shard, shard, P("grp", None), P(), P(), P("grp"), P(), P(),
        shard, shard, shard, P(), P(), P(), shard, shard,
    )
    return jax.shard_map(
        functools.partial(on_device, mesh.shape["seq"]),
        mesh=mesh,
        in_specs=placed,
        out_specs=(shard, shard, shard, shard, P(), P(), P(), shard, shard, shard),
        check_vma=False,
    )
```
